256 devices in a mesh: ctx: 64 (over x, z_lo, y), dp: 4 (over z_hi, core).
Axes of the slice: x: 4, y: 4, z: 8 (z_hi: 2, z_lo: 4; z = z_hi * 4 + z_lo), core: 2. Of those that a mesh axis runs over, the one named last changes fastest.
Arguments:
- tokens: bfloat16 [4, 8192, 1536], P('dp', 'ctx'), may hold values from -6 to 6
- w_in: bfloat16 [1536, 2880], replicated, may hold values from -0.15625 to 0.15625
- conv_taps: float32 [7, 2880], replicated, may hold values from -2.4 to 2.4
- residues: float32 [960, 16], P('ctx'), may hold values from -1.5 to 1.5
- rates: float32 [960, 16], P('ctx'), may hold values from 3.6621094e-05 to 0.08
- cotangent: bfloat16 [4, 8192, 960], P('dp', 'ctx'), may hold values from -6 to 6
Outputs:
- output: bfloat16 [4, 8192, 960], P('dp', 'ctx')
- grad_tokens: bfloat16 [4, 8192, 1536], P('dp', 'ctx')
- grad_weight: bfloat16 [1536, 2880], P('ctx', 'dp')
- grad_taps: float32 [7, 2880], replicated
- grad_residues: float32 [960, 16], P('ctx')
The draws below stay inside these ranges and needn't reach their ends.
All inputs are finite; a program needn't handle non-finite values.
Results may differ from the reference program's by a relative error of at most 0.02.
Values may be sent and summed in bfloat16 or wider, within the bound.
No kernel may reach another device: no remote copies, remote signals or barrier semaphores. Data moves between devices by JAX's collectives and lax.ppermute only.
A program may use at most 192 MiB of HBM per device.

```python
import math
import jax
import jax.numpy as jnp
from jax import lax

D = 1536
CH = 960
ORDER = 16
TAPS = 7
SEQ_LEN = 8192
SEQS = 4
C = 2880


def draw_rates(key, part):
    key = jax.random.fold_in(key, 11)
    key_pick, key_slow, key_fast = jax.random.split(key, 3)
    share = 0.5
    pick = jax.random.uniform(key_pick, (CH, ORDER), jnp.float32) < share
    slow = jnp.exp(jax.random.uniform(key_slow, (CH, ORDER), jnp.float32, jnp.log(0.3 / SEQ_LEN), jnp.log(2.0 / SEQ_LEN)))
    fast = jnp.exp(jax.random.uniform(key_fast, (CH, ORDER), jnp.float32, jnp.log(0.02), jnp.log(0.08)))
    return jnp.where(pick, slow, fast).astype(jnp.float32)


def shard_levels(key, extent, pieces, low, top_value):
    def one(dim, blocks):
        heights = jax.random.uniform(jax.random.fold_in(jax.random.fold_in(key, 6), dim), (blocks,), jnp.float32, low / len(pieces), top_value / len(pieces))
        return jnp.repeat(jnp.exp(heights), extent[dim] // blocks).reshape((-1,) + (1,) * (len(extent) - dim - 1))

    level = one(*pieces[0])
    for cut in pieces[1:]:
        level = level * one(*cut)
    return level


def bell_draw(key, dims, scale, most, cuts=(), held_as=jnp.bfloat16):
    entries = jax.random.normal(key, dims, jnp.float32) * scale
    if len(cuts) > 0:
        entries = shard_levels(key, dims, cuts, -0.22, 0.18) * entries
    return jnp.clip(entries, min=-most, max=most).astype(held_as)


def setup_inputs(seed: int = 0) -> dict:
    keys = jax.random.split(jax.random.key(seed), 7)
    tokens = bell_draw(keys[0], (SEQS, SEQ_LEN, D), 1.0, 6.0, ((0, 4), (1, 64)))
    w_in = bell_draw(keys[1], (D, C), D ** -0.5, 0.15625)
    conv_taps = bell_draw(keys[2], (TAPS, C), 0.4, 2.4, (), jnp.float32)
    residues = bell_draw(keys[3], (CH, ORDER), 0.25, 1.5, ((0, 64),), jnp.float32)
    rates = draw_rates(jax.random.fold_in(keys[6], 71), 0)
    cotangent = bell_draw(keys[5], (SEQS, SEQ_LEN, CH), 1.0, 6.0, ((0, 4), (1, 64)))
    return {"tokens": tokens, "w_in": w_in, "conv_taps": conv_taps, "residues": residues, "rates": rates, "cotangent": cotangent}


def reference(tokens, w_in, conv_taps, residues, rates, cotangent):
    scale = 1.0 / math.sqrt(SEQS * SEQ_LEN)
    flat = tokens.reshape(-1, D)
    z = jnp.dot(flat, w_in, preferred_element_type=jnp.float32).astype(jnp.bfloat16)
    z = z.reshape(SEQS, SEQ_LEN, 3 * CH)
    zpad = jnp.pad(z, ((0, 0), (TAPS - 1, 0), (0, 0)))
    mixed = jnp.zeros((SEQS, SEQ_LEN, 3 * CH), jnp.float32)
    for j in range(TAPS):
        mixed = mixed + conv_taps[j] * zpad[:, TAPS - 1 - j:TAPS - 1 - j + SEQ_LEN].astype(jnp.float32)
    query = mixed[..., :CH]
    keyed = mixed[..., CH:2 * CH]
    valued = mixed[..., 2 * CH:]
    product = (keyed * valued).astype(jnp.bfloat16)
    amp = jnp.sqrt(-jnp.expm1(-2.0 * rates))
    reff = residues * amp
    steps = jnp.arange(SEQ_LEN).astype(jnp.float32)
    filt = jnp.zeros((CH, SEQ_LEN), jnp.float32)
    for k in range(ORDER):
        filt = filt + reff[:, k, None] * jnp.exp(-rates[:, k, None] * steps)
    filt_f = jnp.fft.rfft(filt, n=2 * SEQ_LEN)

    def conv_one(seq):
        spec_seq = jnp.fft.rfft(seq.T, n=2 * SEQ_LEN)
        return jnp.fft.irfft(spec_seq * filt_f, n=2 * SEQ_LEN)[:, :SEQ_LEN].T
    long_out = lax.map(conv_one, product.astype(jnp.float32)).astype(jnp.bfloat16)
    output = (query * long_out.astype(jnp.float32)).astype(jnp.bfloat16)
    upstream = cotangent.astype(jnp.float32)
    dquery = upstream * long_out.astype(jnp.float32)
    dlong = (upstream * query).astype(jnp.bfloat16)

    def back_one(seq):
        return jnp.flip(conv_one(jnp.flip(seq, 0)), 0)
    dproduct = lax.map(back_one, dlong.astype(jnp.float32)).astype(jnp.bfloat16)

    def corr_one(pair):
        left = jnp.fft.rfft(pair[0].T, n=2 * SEQ_LEN)
        right = jnp.fft.rfft(pair[1].T, n=2 * SEQ_LEN)
        return jnp.fft.irfft(jnp.conj(left) * right, n=2 * SEQ_LEN)[:, :SEQ_LEN]
    corr = lax.optimization_barrier(jnp.sum(lax.map(corr_one, (product.astype(jnp.float32), dlong.astype(jnp.float32))), axis=0))
    columns = []
    for k in range(ORDER):
        columns.append(lax.optimization_barrier(jnp.sum(corr * jnp.exp(-rates[:, k, None] * steps), axis=1)))
    grad_residues = amp * jnp.stack(columns, axis=1) * scale
    dprod32 = dproduct.astype(jnp.float32)
    dmixed = jnp.concatenate([dquery, dprod32 * valued, dprod32 * keyed], axis=-1).astype(jnp.bfloat16)
    dm32 = dmixed.astype(jnp.float32)
    tap_rows = []
    for j in range(TAPS):
        tap_rows.append(lax.optimization_barrier(jnp.sum(dm32 * zpad[:, TAPS - 1 - j:TAPS - 1 - j + SEQ_LEN].astype(jnp.float32), axis=(0, 1))))
    grad_taps = jnp.stack(tap_rows, axis=0) * scale
    dpad = jnp.pad(dmixed, ((0, 0), (0, TAPS - 1), (0, 0)))
    dz = jnp.zeros((SEQS, SEQ_LEN, 3 * CH), jnp.float32)
    for j in range(TAPS):
        dz = dz + conv_taps[j] * dpad[:, j:j + SEQ_LEN].astype(jnp.float32)
    dz = dz.astype(jnp.bfloat16).reshape(-1, 3 * CH)
    grad_tokens = jnp.dot(dz, w_in.T, preferred_element_type=jnp.float32).astype(jnp.bfloat16)
    grad_tokens = grad_tokens.reshape(SEQS, SEQ_LEN, D)
    grad_weight = (jnp.dot(flat.T, dz, preferred_element_type=jnp.float32) * scale).astype(jnp.bfloat16)
    return (output, grad_tokens, grad_weight, grad_taps, grad_residues)
```

```python
import functools
import math

import jax
import jax.numpy as jnp
from jax import lax
from jax.experimental import pallas as pl
from jax.experimental.pallas import tpu as pltpu
from jax.sharding import Mesh, PartitionSpec as P

F32 = jnp.float32
BF16 = jnp.bfloat16
HALO = 16
EXT = 136
SEG = 17
PADC = 1024
MODES = 16


def rounded(a):
    return a.astype(BF16).astype(F32)


def kernel_a(tp, tk, tn, w, taps, rates, cot, cotn, zf, mix, es, ends, acc, cots, us, dls):
    step = pl.program_id(0)
    rows = jnp.concatenate([tp[...], tk[...], tn[...]], axis=0)
    part = jnp.dot(rows, w[...], preferred_element_type=F32)

    @pl.when(step == 0)
    def _():
        acc[...] = part

    @pl.when(step > 0)
    def _():
        acc[...] += part

    @pl.when(step == pl.num_programs(0) - 1)
    def _():
        width = cot.shape[1]
        own = cot.shape[0]
        for g in range(3):
            zf[:, g * PADC : g * PADC + width] = rounded(acc[:, g * width : (g + 1) * width])
            zf[:, g * PADC + width : (g + 1) * PADC] = jnp.zeros((zf.shape[0], PADC - width), F32)
        cots[...] = jnp.zeros(cots.shape, F32)
        cots[0:own, 0:width] = cot[...].astype(F32)
        cots[own : own + HALO, 0:width] = cotn[...].astype(F32)
        sub = lax.broadcasted_iota(jnp.int32, (8, 128), 0)
        subf = sub.astype(F32)
        fdepth = jnp.where(sub == 7, 0.0, (EXT - 8 - SEG) - SEG * subf)
        bdepth = jnp.where(sub == 0, 0.0, SEG * subf - 8.0)

        def tile(ct, carry):
            lane = pl.multiple_of(ct * 128, 128)
            lanes = pl.ds(lane, 128)
            mixed = []
            for g in range(3):
                cols = pl.ds(pl.multiple_of(g * PADC + lane, 128), 128)
                total = taps[0:1, cols] * zf[pl.ds(HALO, EXT), cols]
                for j in range(1, 7):
                    total = total + taps[j : j + 1, cols] * zf[pl.ds(HALO - j, EXT), cols]
                mix[g, :, lanes] = total
                mixed.append(total)
            us[...] = rounded(mixed[1] * mixed[2])
            dls[...] = rounded(cots[0:EXT, lanes] * mixed[0])
            rate = rates[:, lanes]
            decay = jnp.exp(-rate)
            for half in range(2):
                ks = range(half * 8, half * 8 + 8)
                al = [jnp.broadcast_to(decay[k : k + 1, :], (8, 128)) for k in ks]
                rl = [jnp.broadcast_to(rate[k : k + 1, :], (8, 128)) for k in ks]
                st = [jnp.zeros((8, 128), F32)] * 8
                snap = st
                for t in range(SEG):
                    uv = us[pl.ds(t, 8, stride=SEG), :]
                    st = [a * s + uv for a, s in zip(al, st)]
                    if t == 8:
                        snap = st
                for i, k in enumerate(ks):
                    es[0, k, :, lanes] = st[i]
                    full = jnp.where(sub == 7, snap[i], st[i]) * jnp.exp(-rl[i] * fdepth)
                    ends[k : k + 1, lanes] = jnp.sum(full, axis=0, keepdims=True)
                st = [jnp.zeros((8, 128), F32)] * 8
                for t in range(SEG - 1, -1, -1):
                    dv = dls[pl.ds(t, 8, stride=SEG), :]
                    st = [a * s + dv for a, s in zip(al, st)]
                    if t == 8:
                        snap = st
                for i, k in enumerate(ks):
                    es[1, k, :, lanes] = st[i]
                    full = jnp.where(sub == 0, snap[i], st[i]) * jnp.exp(-rl[i] * bdepth)
                    ends[MODES + k : MODES + k + 1, lanes] = jnp.sum(full, axis=0, keepdims=True)
            return carry

        lax.fori_loop(0, PADC // 128, tile, 0)


def kernel_b(
    zf, mix, es, inc, taps, rates, reff, cot, cotn,
    out, dz, dzb, sums, cots, us, dls, longs, dps, dms, outs, dzs, packed,
):
    width = cot.shape[1]
    own = cot.shape[0]
    cots[...] = jnp.zeros(cots.shape, F32)
    cots[0:own, 0:width] = cot[...].astype(F32)
    cots[own : own + HALO, 0:width] = cotn[...].astype(F32)
    sub = lax.broadcasted_iota(jnp.int32, (8, 128), 0)

    def tile(ct, carry):
        lane = pl.multiple_of(ct * 128, 128)
        lanes = pl.ds(lane, 128)
        us[...] = rounded(mix[1, :, lanes] * mix[2, :, lanes])
        dls[...] = rounded(cots[0:EXT, lanes] * mix[0, :, lanes])
        rate = rates[:, lanes]
        decay = jnp.exp(-rate)
        gain = reff[:, lanes]
        for half in range(2):
            ks = range(half * 8, half * 8 + 8)
            al = [jnp.broadcast_to(decay[k : k + 1, :], (8, 128)) for k in ks]
            gl = [jnp.broadcast_to(gain[k : k + 1, :], (8, 128)) for k in ks]
            rl = [jnp.broadcast_to(rate[k : k + 1, :], (8, 128)) for k in ks]
            fwd = []
            bwd = []
            for i, k in enumerate(ks):
                jump = [jnp.exp(-float(SEG * m) * rl[i]) for m in (1, 2, 4)]
                x = jnp.where(sub == 0, inc[k : k + 1, lanes], pltpu.roll(es[0, k, :, lanes], 1, 0))
                for m, d in zip((1, 2, 4), jump):
                    x = x + jnp.where(sub >= m, pltpu.roll(x, m, 0) * d, 0.0)
                fwd.append(x)
                x = jnp.where(
                    sub == 7, inc[MODES + k : MODES + k + 1, lanes], pltpu.roll(es[1, k, :, lanes], 7, 0)
                )
                for m, d in zip((1, 2, 4), jump):
                    x = x + jnp.where(sub < 8 - m, pltpu.roll(x, 8 - m, 0) * d, 0.0)
                bwd.append(x)
            gr = [jnp.zeros((8, 128), F32)] * 8
            st = fwd
            for t in range(SEG):
                uv = us[pl.ds(t, 8, stride=SEG), :]
                dv = dls[pl.ds(t, 8, stride=SEG), :]
                if t >= 9:
                    dv = jnp.where(sub < 7, dv, 0.0)
                st = [a * s + uv for a, s in zip(al, st)]
                gr = [q + dv * s for q, s in zip(gr, st)]
                total = sum(g * s for g, s in zip(gl, st))
                if half:
                    total = total + longs[pl.ds(t, 8, stride=SEG), :]
                longs[pl.ds(t, 8, stride=SEG), :] = total
            for i, k in enumerate(ks):
                sums[24 + k : 25 + k, lanes] = jnp.sum(gr[i], axis=0, keepdims=True)
            st = bwd
            for t in range(SEG - 1, -1, -1):
                dv = dls[pl.ds(t, 8, stride=SEG), :]
                st = [a * s + dv for a, s in zip(al, st)]
                total = sum(g * s for g, s in zip(gl, st))
                if half:
                    total = total + dps[pl.ds(t, 8, stride=SEG), :]
                dps[pl.ds(t, 8, stride=SEG), :] = total
        long_out = rounded(longs[...])
        dprod = rounded(dps[...])
        outs[:, lanes] = mix[0, 0:own, lanes] * long_out[0:own]
        dms[0] = rounded(cots[0:EXT, lanes] * long_out)
        dms[1] = rounded(dprod * mix[2, :, lanes])
        dms[2] = rounded(dprod * mix[1, :, lanes])
        for g in range(3):
            cols = pl.ds(pl.multiple_of(g * PADC + lane, 128), 128)
            mine = dms[g, 0:own, :]
            total = taps[0:1, cols] * mine
            sums[8 * g : 8 * g + 1, lanes] = jnp.sum(
                mine * zf[pl.ds(HALO, own), cols], axis=0, keepdims=True
            )
            for j in range(1, 7):
                total = total + taps[j : j + 1, cols] * dms[g, pl.ds(j, own), :]
                sums[8 * g + j : 8 * g + j + 1, lanes] = jnp.sum(
                    mine * zf[pl.ds(HALO - j, own), cols], axis=0, keepdims=True
                )
            sums[8 * g + 7 : 8 * g + 8, lanes] = jnp.zeros((1, 128), F32)
            dzs[:, cols] = total
        return carry

    lax.fori_loop(0, PADC // 128, tile, 0)
    out[...] = outs[:, 0:width].astype(BF16)
    for g in range(3):
        packed[:, g * width : (g + 1) * width] = dzs[:, g * PADC : g * PADC + width]
    dz[...] = packed[...].astype(BF16)
    piece = dzb.shape[2] // 2
    for b in range(8):
        for h in range(2):
            off = h * 8 * piece + (b % 2) * 4 * piece + (b // 2) * piece
            dzb[b, :, h * piece : (h + 1) * piece] = packed[:, off : off + piece].astype(BF16)


def ring(a, ax, d, n=4):
    return lax.ppermute(a, ax, [(i, (i + d) % n) for i in range(n)])


def gathered(a, ax, d):
    return ring(a, ax, d)


def local(tokens, w_in, conv_taps, residues, rates, cotangent):
    feats = tokens[0]
    cot = cotangent[0]
    own, width = cot.shape
    chans = 3 * width
    xi, zi, yi = lax.axis_index("x"), lax.axis_index("zl"), lax.axis_index("y")
    ctx = ("x", "zl", "y")
    count = 64
    scale = 1.0 / math.sqrt(4 * count * own)
    tprev = lax.ppermute(feats[own - HALO :], ctx, [(i, i + 1) for i in range(count - 1)])
    firsts = jnp.concatenate([feats[:HALO], cot[:HALO]], axis=1)
    nexts = lax.ppermute(firsts, ctx, [(i, i - 1) for i in range(1, count)])
    tnext = nexts[:, : feats.shape[1]]
    cnext = nexts[:, feats.shape[1] :]
    amp_mine = jnp.sqrt(-jnp.expm1(-2.0 * rates))
    held = jnp.concatenate([rates, residues * amp_mine], axis=1)[None]
    for ax in ("y", "zl", "x"):
        held = jnp.concatenate([held] + [ring(held, ax, d) for d in (1, 2, 3)], axis=0)
    slots = jnp.arange(count)
    sx, sz, sy = slots // 16, (slots // 4) % 4, slots % 4
    source = ((xi - sx) % 4) * 16 + ((zi - sz) % 4) * 4 + (yi - sy) % 4
    held = held[source]
    params = jnp.transpose(held, (2, 0, 1)).reshape(2 * MODES, width)
    params = jnp.pad(params, ((0, 0), (0, PADC - width)))
    rate, gain = params[:MODES], params[MODES:]
    taps = jnp.pad(conv_taps.reshape(7, 3, width), ((0, 1), (0, 0), (0, PADC - width)))
    taps = taps.reshape(8, 3 * PADC)

    depth = feats.shape[1]
    kblk = 256
    vmem = pltpu.CompilerParams(vmem_limit_bytes=48 * 1024 * 1024)

    def whole(shape):
        return pl.BlockSpec(shape, lambda k: (0,) * len(shape))

    ext_rows = own + 2 * HALO
    zf, mix, es, ends = pl.pallas_call(
        kernel_a,
        grid=(depth // kblk,),
        in_specs=[
            pl.BlockSpec((HALO, kblk), lambda k: (0, k)),
            pl.BlockSpec((own, kblk), lambda k: (0, k)),
            pl.BlockSpec((HALO, kblk), lambda k: (0, k)),
            pl.BlockSpec((kblk, chans), lambda k: (k, 0)),
            whole((8, 3 * PADC)),
            whole((MODES, PADC)),
            whole((own, width)),
            whole((HALO, width)),
        ],
        out_specs=[
            whole((ext_rows, 3 * PADC)),
            whole((3, EXT, PADC)),
            whole((2, MODES, 8, PADC)),
            whole((2 * MODES, PADC)),
        ],
        out_shape=[
            jax.ShapeDtypeStruct((ext_rows, 3 * PADC), F32),
            jax.ShapeDtypeStruct((3, EXT, PADC), F32),
            jax.ShapeDtypeStruct((2, MODES, 8, PADC), F32),
            jax.ShapeDtypeStruct((2 * MODES, PADC), F32),
        ],
        scratch_shapes=[
            pltpu.VMEM((ext_rows, chans), F32),
            pltpu.VMEM((own + HALO, PADC), F32),
            pltpu.VMEM((EXT, 128), F32),
            pltpu.VMEM((EXT, 128), F32),
        ],
        compiler_params=vmem,
        cost_estimate=pl.CostEstimate(flops=1500000000, bytes_accessed=14000000, transcendentals=0),
    )(tprev, feats, tnext, w_in, taps, rate, cot, cnext)

    rate2 = jnp.concatenate([rate, rate], axis=0)
    ahead = (jnp.arange(2 * MODES) < MODES)[:, None]
    total = ends
    incoming = None
    reach = []
    for ax, me, span in (("y", yi, own), ("zl", zi, 4 * own), ("x", xi, 16 * own)):
        prefix = jnp.zeros_like(total)
        whole_sum = jnp.zeros_like(total)
        for d in range(4):
            other = total if d == 0 else ring(total, ax, d)
            m = (me - d) % 4
            gap = jnp.where(ahead, me - 1 - m, m - me - 1)
            far = jnp.where(ahead, 3 - m, m)
            if d > 0:
                weight = jnp.exp(-rate2 * (span * jnp.maximum(gap, 0)).astype(F32))
                prefix = prefix + jnp.where(gap >= 0, weight * other, 0.0)
            whole_sum = whole_sum + jnp.exp(-rate2 * (span * far).astype(F32)) * other
        reach.append((prefix, jnp.exp(-rate2 * (span * jnp.where(ahead, me, 3 - me)).astype(F32))))
        total = whole_sum
    incoming = reach[0][0] + reach[0][1] * (reach[1][0] + reach[1][1] * reach[2][0])

    piece = chans // 16
    out, dz, dzb, sums = pl.pallas_call(
        kernel_b,
        out_shape=[
            jax.ShapeDtypeStruct((own, width), BF16),
            jax.ShapeDtypeStruct((own, chans), BF16),
            jax.ShapeDtypeStruct((8, own, 2 * piece), BF16),
            jax.ShapeDtypeStruct((40, PADC), F32),
        ],
        scratch_shapes=[
            pltpu.VMEM((own + HALO, PADC), F32),
            pltpu.VMEM((EXT, 128), F32),
            pltpu.VMEM((EXT, 128), F32),
            pltpu.VMEM((EXT, 128), F32),
            pltpu.VMEM((EXT, 128), F32),
            pltpu.VMEM((3, EXT, 128), F32),
            pltpu.VMEM((own, PADC), F32),
            pltpu.VMEM((own, 3 * PADC), F32),
            pltpu.VMEM((own, chans), F32),
        ],
        compiler_params=vmem,
        cost_estimate=pl.CostEstimate(flops=200000000, bytes_accessed=10000000, transcendentals=0),
    )(zf, mix, es, incoming, taps, rate, gain, cot, cnext)

    fblk = depth // count
    shuffled = feats.reshape(own, 4, 4, 4, fblk).transpose(0, 3, 1, 2, 4).reshape(own, depth)
    ours = jnp.stack([shuffled] + [ring(shuffled, "x", d) for d in (1, 2, 3)], axis=0)
    theirs = lax.ppermute(ours, "core", [(0, 1), (1, 0)])
    tok_all = jnp.stack([ours, theirs], axis=0).reshape(8 * own, depth)

    def summed(a, ax):
        return a + ring(a, ax, 1) + ring(a, ax, 2) + ring(a, ax, 3)

    for ax in ("y", "zl", "x", ("zh", "core")):
        sums = summed(sums, ax)
    grad_taps = sums[:24].reshape(3, 8, PADC)[:, :7, :width].transpose(1, 0, 2).reshape(7, chans)
    grad_taps = grad_taps * scale
    index = (xi * 4 + zi) * 4 + yi
    held_chans = width // count
    mine = lax.dynamic_slice_in_dim(sums[24:, :width], index * held_chans, held_chans, axis=1)
    grad_residues = amp_mine * mine.T * scale

    arrived = lax.all_to_all(dzb, ("x", "core"), split_axis=0, concat_axis=0, tiled=True)
    ci = lax.axis_index("core")
    order = jnp.arange(8)
    want = ((xi - order % 4) % 4) * 2 + jnp.where(order < 4, ci, 1 - ci)
    arrived = arrived[want].reshape(8 * own, 2 * piece)
    term = lax.dot_general(
        tok_all, arrived, (((0,), (0,)), ((), ())), preferred_element_type=F32
    ).astype(BF16)
    got = lax.all_to_all(term.reshape(4, depth // 4, 2 * piece), "y", 0, 0, tiled=True)
    got = jnp.sum(got.astype(F32), axis=0).astype(BF16)
    got = got.reshape(16, fblk, 2, piece).transpose(0, 2, 1, 3).reshape(32, fblk, piece)
    last = lax.all_to_all(got, ("x", "zl", "zh"), 0, 0, tiled=True)
    last = jnp.sum(last.reshape(4, 8, fblk, piece).astype(F32), axis=1) * scale
    grad_weight = last.transpose(1, 0, 2).reshape(fblk, 4 * piece).astype(BF16)

    grad_feats = lax.dot_general(
        dz, w_in, (((1,), (1,)), ((), ())), preferred_element_type=F32
    ).astype(BF16)
    return (out[None], grad_feats[None], grad_weight, grad_taps, grad_residues)


def solution(mesh):
    fine = Mesh(mesh.devices.reshape(4, 4, 4, 2, 2), ("x", "zl", "y", "zh", "core"))
    ctx = ("x", "zl", "y")
    dp = ("zh", "core")
    in_specs = (P(dp, ctx, None), P(), P(), P(ctx, None), P(ctx, None), P(dp, ctx, None))
    out_specs = (P(dp, ctx, None), P(dp, ctx, None), P(ctx, dp), P(), P(ctx, None))
    return jax.shard_map(local, mesh=fine, in_specs=in_specs, out_specs=out_specs, check_vma=False)
```

```python
import math

import jax
import jax.numpy as jnp
from jax import lax
from jax.experimental import pallas as pl
from jax.experimental.pallas import tpu as pltpu
from jax.sharding import Mesh, PartitionSpec as P

F32 = jnp.float32
BF16 = jnp.bfloat16
HALO = 16
EXT = 136
SEG = 17
PADC = 1024
MODES = 16
NT = (((1,), (1,)), ((), ()))


def rounded(a):
    return a.astype(BF16).astype(F32)


def project(tp, tk, tn, wt, taps, cott, cotnt, zf, mix, cots, us, dls, acc, turn):
    step = pl.program_id(0)
    rows = jnp.concatenate([tp[...], tk[...], tn[...]], axis=0)
    part = lax.dot_general(rows, wt[...], NT, preferred_element_type=F32)

    @pl.when(step == 0)
    def _():
        acc[...] = part

    @pl.when(step > 0)
    def _():
        acc[...] += part

    @pl.when(step == pl.num_programs(0) - 1)
    def _():
        width, own = cott.shape
        for g in range(3):
            zf[:, g * PADC : g * PADC + width] = rounded(acc[:, g * width : (g + 1) * width])
            zf[:, g * PADC + width : (g + 1) * PADC] = jnp.zeros((zf.shape[0], PADC - width), F32)
        turn[...] = jnp.zeros(turn.shape, F32)
        turn[0:width, 0:own] = cott[...].astype(F32)
        turn[0:width, own : own + HALO] = cotnt[...].astype(F32)

        def tile(ct, carry):
            lane = pl.multiple_of(ct * 128, 128)
            lanes = pl.ds(lane, 128)
            mixed = []
            for g in range(3):
                cols = pl.ds(pl.multiple_of(g * PADC + lane, 128), 128)
                total = taps[0:1, cols] * zf[pl.ds(HALO, EXT), cols]
                for j in range(1, 7):
                    total = total + taps[j : j + 1, cols] * zf[pl.ds(HALO - j, EXT), cols]
                mix[g, :, lanes] = total
                mixed.append(total)
            cot = jnp.concatenate(
                [turn[lanes, 0:128].T, turn[lanes, 128:256].T[0 : EXT - 128]], axis=0
            )
            cots[:, lanes] = cot
            us[:, lanes] = rounded(mixed[1] * mixed[2])
            dls[:, lanes] = rounded(cot * mixed[0])
            return carry

        lax.fori_loop(0, PADC // 128, tile, 0)


def first_params(rates, residues, amp, out, held):
    count = rates.shape[0]
    held[...] = jnp.zeros(held.shape, F32)
    held[0:count, 0:MODES] = rates[...]
    held[0:count, MODES : 2 * MODES] = residues[...] * amp[...]
    out[...] = held[...].T[0 : 2 * MODES, 0:count]


def placed(place, refs, held, goal):
    me = place[0]
    wide = refs[0].shape[1]
    total = None
    for d, ref in enumerate(refs):
        held[...] = jnp.zeros(held.shape, F32)
        held[:, 0:wide] = ref[...]
        part = pltpu.roll(held[...], lax.rem(me + (4 - d), 4) * wide, 1)
        total = part if total is None else total + part
    return total[:, 0:goal]


def join_params(place, r0, r1, r2, r3, out, held):
    out[...] = placed(place, (r0, r1, r2, r3), held, out.shape[1])


def end_states(place, r0, r1, r2, r3, us, dls, rates, gains, es, ends, endb, ut, dt, held):
    joined = placed(place, (r0, r1, r2, r3), held, PADC)
    rates[...] = joined[0:MODES]
    gains[...] = joined[MODES : 2 * MODES]
    sub = lax.broadcasted_iota(jnp.int32, (8, 128), 0)
    subf = sub.astype(F32)
    fdepth = jnp.where(sub == 7, 0.0, (EXT - 8 - SEG) - SEG * subf)
    bdepth = jnp.where(sub == 0, 0.0, SEG * subf - 8.0)

    def tile(ct, carry):
        lanes = pl.ds(pl.multiple_of(ct * 128, 128), 128)
        ut[...] = us[:, lanes]
        dt[...] = dls[:, lanes]
        rate = rates[:, lanes]
        decay = jnp.exp(-rate)
        for half in range(2):
            ks = range(half * 8, half * 8 + 8)
            al = [jnp.broadcast_to(decay[k : k + 1, :], (8, 128)) for k in ks]
            rl = [jnp.broadcast_to(rate[k : k + 1, :], (8, 128)) for k in ks]
            st = [jnp.zeros((8, 128), F32)] * 8
            snap = st
            for t in range(SEG):
                uv = ut[pl.ds(t, 8, stride=SEG), :]
                st = [a * s + uv for a, s in zip(al, st)]
                if t == 8:
                    snap = st
            for i, k in enumerate(ks):
                es[0, k, :, lanes] = st[i]
                full = jnp.where(sub == 7, snap[i], st[i]) * jnp.exp(-rl[i] * fdepth)
                ends[k : k + 1, lanes] = jnp.sum(full, axis=0, keepdims=True)
            st = [jnp.zeros((8, 128), F32)] * 8
            for t in range(SEG - 1, -1, -1):
                dv = dt[pl.ds(t, 8, stride=SEG), :]
                st = [a * s + dv for a, s in zip(al, st)]
                if t == 8:
                    snap = st
            for i, k in enumerate(ks):
                es[1, k, :, lanes] = st[i]
                full = jnp.where(sub == 0, snap[i], st[i]) * jnp.exp(-rl[i] * bdepth)
                ends[MODES + k : MODES + k + 1, lanes] = jnp.sum(full, axis=0, keepdims=True)
        return carry

    lax.fori_loop(0, PADC // 128, tile, 0)
    endb[...] = ends[...].astype(BF16)


def make_level(span):
    def level(place, own, r1, r2, r3, rates, total, totalb, prefix):
        me = place[0]
        rate = rates[...] * float(span)
        before = jnp.zeros((MODES, PADC), F32)
        after = before
        whole_f = before
        whole_b = before
        for d, ref in enumerate((own, r1, r2, r3)):
            m = lax.rem(me + (4 - d), 4)
            f = ref[0:MODES, :].astype(F32)
            b = ref[MODES : 2 * MODES, :].astype(F32)
            whole_f = whole_f + f * jnp.exp(-rate * (3 - m).astype(F32))
            whole_b = whole_b + b * jnp.exp(-rate * m.astype(F32))
            if d > 0:
                gf = me - 1 - m
                gb = m - me - 1
                wf = jnp.exp(-rate * jnp.maximum(gf, 0).astype(F32))
                wb = jnp.exp(-rate * jnp.maximum(gb, 0).astype(F32))
                before = before + jnp.where(gf >= 0, 1.0, 0.0) * (wf * f)
                after = after + jnp.where(gb >= 0, 1.0, 0.0) * (wb * b)
        prefix[0:MODES, :] = before
        prefix[MODES : 2 * MODES, :] = after
        total[0:MODES, :] = whole_f
        total[MODES : 2 * MODES, :] = whole_b
        totalb[0:MODES, :] = whole_f.astype(BF16)
        totalb[MODES : 2 * MODES, :] = whole_b.astype(BF16)

    return level


def finish(
    place, zf, mix, es, py, pz, px, taps, rates, reff, cots, us, dls,
    outt, dz, dzb, sums, inc, ut, dt, longs, dps, dms, outs, dzs, dzt, packed,
):
    width, own = outt.shape
    rate_all = rates[...] * float(own)
    for back in range(2):
        part = pl.ds(back * MODES, MODES)
        near, mid = place[2], place[1]
        if back:
            near, mid = 3 - near, 3 - mid
        far = pz[part, :] + jnp.exp(-rate_all * (4 * mid).astype(F32)) * px[part, :]
        inc[part, :] = py[part, :] + jnp.exp(-rate_all * near.astype(F32)) * far
    sub = lax.broadcasted_iota(jnp.int32, (8, 128), 0)

    def tile(ct, carry):
        lane = pl.multiple_of(ct * 128, 128)
        lanes = pl.ds(lane, 128)
        ut[...] = us[:, lanes]
        dt[...] = dls[:, lanes]
        rate = rates[:, lanes]
        decay = jnp.exp(-rate)
        gain = reff[:, lanes]
        for half in range(2):
            ks = range(half * 8, half * 8 + 8)
            al = [jnp.broadcast_to(decay[k : k + 1, :], (8, 128)) for k in ks]
            gl = [jnp.broadcast_to(gain[k : k + 1, :], (8, 128)) for k in ks]
            rl = [jnp.broadcast_to(rate[k : k + 1, :], (8, 128)) for k in ks]
            fwd = []
            bwd = []
            for i, k in enumerate(ks):
                jump = [jnp.exp(-float(SEG * m) * rl[i]) for m in (1, 2, 4)]
                x = jnp.where(sub == 0, inc[k : k + 1, lanes], pltpu.roll(es[0, k, :, lanes], 1, 0))
                for m, d in zip((1, 2, 4), jump):
                    x = x + jnp.where(sub >= m, pltpu.roll(x, m, 0) * d, 0.0)
                fwd.append(x)
                x = jnp.where(
                    sub == 7, inc[MODES + k : MODES + k + 1, lanes], pltpu.roll(es[1, k, :, lanes], 7, 0)
                )
                for m, d in zip((1, 2, 4), jump):
                    x = x + jnp.where(sub < 8 - m, pltpu.roll(x, 8 - m, 0) * d, 0.0)
                bwd.append(x)
            gr = [jnp.zeros((8, 128), F32)] * 8
            st = fwd
            for t in range(SEG):
                uv = ut[pl.ds(t, 8, stride=SEG), :]
                dv = dt[pl.ds(t, 8, stride=SEG), :]
                if t >= 9:
                    dv = jnp.where(sub < 7, dv, 0.0)
                st = [a * s + uv for a, s in zip(al, st)]
                gr = [q + dv * s for q, s in zip(gr, st)]
                total = sum(g * s for g, s in zip(gl, st))
                if half:
                    total = total + longs[pl.ds(t, 8, stride=SEG), :]
                longs[pl.ds(t, 8, stride=SEG), :] = total
            for i, k in enumerate(ks):
                sums[24 + k : 25 + k, lanes] = jnp.sum(gr[i], axis=0, keepdims=True)
            st = bwd
            for t in range(SEG - 1, -1, -1):
                dv = dt[pl.ds(t, 8, stride=SEG), :]
                st = [a * s + dv for a, s in zip(al, st)]
                total = sum(g * s for g, s in zip(gl, st))
                if half:
                    total = total + dps[pl.ds(t, 8, stride=SEG), :]
                dps[pl.ds(t, 8, stride=SEG), :] = total
        long_out = rounded(longs[...])
        dprod = rounded(dps[...])
        outs[lanes, :] = (mix[0, 0:own, lanes] * long_out[0:own]).T
        dms[0] = rounded(cots[:, lanes] * long_out)
        dms[1] = rounded(dprod * mix[2, :, lanes])
        dms[2] = rounded(dprod * mix[1, :, lanes])
        for g in range(3):
            cols = pl.ds(pl.multiple_of(g * PADC + lane, 128), 128)
            mine = dms[g, 0:own, :]
            total = taps[0:1, cols] * mine
            sums[8 * g : 8 * g + 1, lanes] = jnp.sum(
                mine * zf[pl.ds(HALO, own), cols], axis=0, keepdims=True
            )
            for j in range(1, 7):
                total = total + taps[j : j + 1, cols] * dms[g, pl.ds(j, own), :]
                sums[8 * g + j : 8 * g + j + 1, lanes] = jnp.sum(
                    mine * zf[pl.ds(HALO - j, own), cols], axis=0, keepdims=True
                )
            sums[8 * g + 7 : 8 * g + 8, lanes] = jnp.zeros((1, 128), F32)
            dzs[:, cols] = total
            dzt[cols, :] = total.T
        return carry

    lax.fori_loop(0, PADC // 128, tile, 0)
    outt[...] = outs[0:width, :].astype(BF16)
    for g in range(3):
        dz[:, g * width : (g + 1) * width] = dzs[:, g * PADC : g * PADC + width].astype(BF16)
        packed[g * width : (g + 1) * width, :] = dzt[g * PADC : g * PADC + width, :]
    piece = dzb.shape[1] // 2
    for b in range(8):
        offs = [h * 8 * piece + (b % 2) * 4 * piece + (b // 2) * piece for h in range(2)]
        both = [packed[off : off + piece, :] for off in offs]
        dzb[b] = jnp.concatenate(both, axis=0).astype(BF16)


def weight_term(place, arrived, ours, theirs, term):
    me = place[0]
    core = place[1]
    chunk = term.shape[2]
    slots = (me, lax.bitwise_xor(me, 1), 3 - me, lax.bitwise_xor(3 - me, 1))
    pairs = []
    for ref, c in ((ours, core), (theirs, 1 - core)):
        for p in range(2):
            left = [arrived[slots[2 * p + i] * 2 + c] for i in range(2)]
            pairs.append((jnp.concatenate(left, axis=1), ref, p))
    for j in range(4):
        total = None
        for left, ref, p in pairs:
            right = ref[p, :, j * chunk : (j + 1) * chunk]
            part = jnp.dot(left, right, preferred_element_type=F32)
            total = part if total is None else total + part
        term[j] = total.astype(BF16)


def split_rows(got, blocks, turn):
    chans = got.shape[1]
    fblk = blocks.shape[1]
    piece = blocks.shape[2]
    turn[0:chans, :] = (
        got[0].astype(F32) + got[1].astype(F32) + got[2].astype(F32) + got[3].astype(F32)
    )
    turn[chans:, :] = jnp.zeros((turn.shape[0] - chans, turn.shape[1]), F32)
    flipped = turn[...].T
    for q in range(16):
        for h in range(2):
            part = flipped[q * fblk : (q + 1) * fblk, h * piece : (h + 1) * piece]
            blocks[2 * q + h] = part.astype(BF16)


def ring(a, ax, d):
    return lax.ppermute(a, ax, [(i, (i + d) % 4) for i in range(4)])


def params(mb):
    return pltpu.CompilerParams(vmem_limit_bytes=mb * 1024 * 1024)


def local(tokens, w_in, conv_taps, residues, rates, cotangent):
    feats = tokens[0]
    cot = cotangent[0]
    own, width = cot.shape
    depth = feats.shape[1]
    chans = 3 * width
    count = 64
    piece = chans // 16
    fblk = depth // count
    xi, zi, yi = lax.axis_index("x"), lax.axis_index("zl"), lax.axis_index("y")
    ci = lax.axis_index("core")
    ctx = ("x", "zl", "y")
    scale = 1.0 / math.sqrt(4 * count * own)
    smem = pl.BlockSpec(memory_space=pltpu.SMEM)
    vm = pl.BlockSpec(memory_space=pltpu.VMEM)
    each = width // count
    amp_mine = jnp.sqrt(-jnp.expm1(-2.0 * rates))
    held = pl.pallas_call(
        first_params,
        in_specs=[vm] * 3,
        out_specs=vm,
        out_shape=jax.ShapeDtypeStruct((2 * MODES, each), F32),
        scratch_shapes=[pltpu.VMEM((128, 128), F32)],
        compiler_params=params(4),
        name="first_params",
    )(rates, residues, amp_mine)
    early = None
    for ax, me in (("y", yi), ("zl", zi)):
        blocks = [held] + [ring(held, ax, d) for d in (1, 2, 3)]
        each = 4 * each
        held = pl.pallas_call(
            join_params,
            in_specs=[smem] + [vm] * 4,
            out_specs=vm,
            out_shape=jax.ShapeDtypeStruct((2 * MODES, each), F32),
            scratch_shapes=[pltpu.VMEM((2 * MODES, 256), F32)],
            compiler_params=params(4),
            name="join_params",
        )(me.reshape(1), *blocks)
        if early is None:
            early = held
    blocks = [held] + [ring(held, "x", d) for d in (1, 2, 3)]
    taps = jnp.pad(conv_taps.reshape(7, 3, width), ((0, 1), (0, 0), (0, PADC - width)))
    taps = taps.reshape(8, 3 * PADC)
    tprev = lax.ppermute(feats[own - HALO :], ctx, [(i, i + 1) for i in range(count - 1)])
    firsts = jnp.concatenate([feats[:HALO], cot[:HALO]], axis=1)
    nexts = lax.ppermute(firsts, ctx, [(i, i - 1) for i in range(1, count)])
    tnext = nexts[:, :depth]
    cnext = nexts[:, depth:].T

    kblk = 256

    def whole(shape):
        return pl.BlockSpec(shape, lambda k: (0,) * len(shape))

    ext_rows = own + 2 * HALO
    shapes = [(ext_rows, 3 * PADC), (3, EXT, PADC), (EXT, PADC), (EXT, PADC), (EXT, PADC)]
    zf, mix, cots, us, dls = pl.pallas_call(
        project,
        grid=(depth // kblk,),
        in_specs=[
            pl.BlockSpec((HALO, kblk), lambda k: (0, k)),
            pl.BlockSpec((own, kblk), lambda k: (0, k)),
            pl.BlockSpec((HALO, kblk), lambda k: (0, k)),
            pl.BlockSpec((chans, kblk), lambda k: (0, k)),
            whole((8, 3 * PADC)),
            whole((width, own)),
            whole((width, HALO)),
        ],
        out_specs=[whole(s) for s in shapes],
        out_shape=[jax.ShapeDtypeStruct(s, F32) for s in shapes],
        scratch_shapes=[pltpu.VMEM((ext_rows, chans), F32), pltpu.VMEM((PADC, 256), F32)],
        compiler_params=params(24),
        cost_estimate=pl.CostEstimate(flops=1500000000, bytes_accessed=14000000, transcendentals=0),
        name="project",
    )(tprev, feats, tnext, w_in.T, taps, cot.T, cnext)

    *blocks, us, dls = lax.optimization_barrier((*blocks, us, dls))
    rate, gain, es, ends, endb = pl.pallas_call(
        end_states,
        in_specs=[smem] + [vm] * 6,
        out_specs=[vm] * 5,
        out_shape=[
            jax.ShapeDtypeStruct((MODES, PADC), F32),
            jax.ShapeDtypeStruct((MODES, PADC), F32),
            jax.ShapeDtypeStruct((2, MODES, 8, PADC), F32),
            jax.ShapeDtypeStruct((2 * MODES, PADC), F32),
            jax.ShapeDtypeStruct((2 * MODES, PADC), BF16),
        ],
        scratch_shapes=[
            pltpu.VMEM((EXT, 128), F32),
            pltpu.VMEM((EXT, 128), F32),
            pltpu.VMEM((2 * MODES, PADC), F32),
        ],
        compiler_params=params(12),
        cost_estimate=pl.CostEstimate(flops=20000000, bytes_accessed=3000000, transcendentals=0),
        name="end_states",
    )(xi.reshape(1), *blocks, us, dls)

    mine, _ = lax.optimization_barrier((feats, early))
    pair = lax.ppermute(mine, "y", [(i, i ^ 1) for i in range(4)])
    two = jnp.stack([mine, pair], axis=0)

    prefixes = []
    total, sent = ends, endb
    for ax, me, span in (("y", yi, own), ("zl", zi, 4 * own), ("x", xi, 16 * own)):
        near = [ring(sent, ax, d) for d in (1, 2, 3)]
        total, sent, prefix = pl.pallas_call(
            make_level(span),
            in_specs=[smem] + [vm] * 5,
            out_specs=[vm] * 3,
            out_shape=[
                jax.ShapeDtypeStruct((2 * MODES, PADC), F32),
                jax.ShapeDtypeStruct((2 * MODES, PADC), BF16),
                jax.ShapeDtypeStruct((2 * MODES, PADC), F32),
            ],
            compiler_params=params(8),
            name="level",
        )(me.reshape(1), total, *near, rate)
        prefixes.append(prefix)
        if ax == "y":
            two, _ = lax.optimization_barrier((two, sent))
            other = lax.ppermute(two, "y", [(i, 3 - i) for i in range(4)])
    other, prefixes[2] = lax.optimization_barrier((other, prefixes[2]))
    ours = jnp.concatenate([two, other], axis=0)
    theirs = lax.ppermute(ours, "core", [(0, 1), (1, 0)])

    outt, dz, dzb, sums = pl.pallas_call(
        finish,
        in_specs=[smem] + [vm] * 12,
        out_specs=[vm] * 4,
        out_shape=[
            jax.ShapeDtypeStruct((width, own), BF16),
            jax.ShapeDtypeStruct((own, chans), BF16),
            jax.ShapeDtypeStruct((8, 2 * piece, own), BF16),
            jax.ShapeDtypeStruct((40, PADC), F32),
        ],
        scratch_shapes=[
            pltpu.VMEM((2 * MODES, PADC), F32),
            pltpu.VMEM((EXT, 128), F32),
            pltpu.VMEM((EXT, 128), F32),
            pltpu.VMEM((EXT, 128), F32),
            pltpu.VMEM((EXT, 128), F32),
            pltpu.VMEM((3, EXT, 128), F32),
            pltpu.VMEM((PADC, own), F32),
            pltpu.VMEM((own, 3 * PADC), F32),
            pltpu.VMEM((3 * PADC, own), F32),
            pltpu.VMEM((chans, own), F32),
        ],
        compiler_params=params(24),
        cost_estimate=pl.CostEstimate(flops=200000000, bytes_accessed=10000000, transcendentals=0),
        name="finish",
    )(jnp.stack([xi, zi, yi]), zf, mix, es, *prefixes, taps, rate, gain, cots, us, dls)
    output = outt.T

    arrived = lax.all_to_all(dzb, ("y", "core"), split_axis=0, concat_axis=0, tiled=True)
    term = pl.pallas_call(
        weight_term,
        in_specs=[smem] + [vm] * 3,
        out_specs=vm,
        out_shape=jax.ShapeDtypeStruct((4, 2 * piece, depth // 4), BF16),
        compiler_params=params(24),
        cost_estimate=pl.CostEstimate(flops=1200000000, bytes_accessed=6000000, transcendentals=0),
        name="weight_term",
    )(jnp.stack([yi, ci]), arrived, ours.reshape(2, 2 * own, depth), theirs.reshape(2, 2 * own, depth))
    got = lax.all_to_all(term, "x", 0, 0, tiled=True)
    blocks = pl.pallas_call(
        split_rows,
        in_specs=[vm],
        out_specs=vm,
        out_shape=jax.ShapeDtypeStruct((32, fblk, piece), BF16),
        scratch_shapes=[pltpu.VMEM((384, depth // 4), F32)],
        compiler_params=params(12),
        name="split_rows",
    )(got)
    last = lax.all_to_all(blocks, ("zl", "y", "zh"), 0, 0, tiled=True)
    last = jnp.sum(last.reshape(4, 4, 2, fblk, piece).astype(F32), axis=(0, 2)) * scale
    grad_weight = last.transpose(1, 0, 2).reshape(fblk, 4 * piece).astype(BF16)

    for ax, behind in (("zl", term), ("y", got), ("x", None), (("zh", "core"), None)):
        short = sums.astype(BF16)
        parts = [short] + [ring(short, ax, d) for d in (1, 2, 3)]
        if behind is not None:
            *parts, _ = lax.optimization_barrier((*parts, behind))
        sums = sum(p.astype(F32) for p in parts)
    grad_taps = sums[:24].reshape(3, 8, PADC)[:, :7, :width].transpose(1, 0, 2).reshape(7, chans)
    grad_taps = grad_taps * scale
    index = (xi * 4 + zi) * 4 + yi
    held_chans = width // count
    chosen = lax.dynamic_slice_in_dim(sums[24:, :width], index * held_chans, held_chans, axis=1)
    grad_residues = amp_mine * chosen.T * scale

    dz, _ = lax.optimization_barrier((dz, term))
    grad_feats = lax.dot_general(dz, w_in, NT, preferred_element_type=F32).astype(BF16)
    return (output[None], grad_feats[None], grad_weight, grad_taps, grad_residues)


def solution(mesh):
    fine = Mesh(mesh.devices.reshape(4, 4, 4, 2, 2), ("x", "zl", "y", "zh", "core"))
    ctx = ("x", "zl", "y")
    dp = ("zh", "core")
    in_specs = (P(dp, ctx, None), P(), P(), P(ctx, None), P(ctx, None), P(dp, ctx, None))
    out_specs = (P(dp, ctx, None), P(dp, ctx, None), P(ctx, dp), P(), P(ctx, None))
    return jax.shard_map(local, mesh=fine, in_specs=in_specs, out_specs=out_specs, check_vma=False)
```

```python
import math

import jax
import jax.numpy as jnp
from jax import lax
from jax.experimental import pallas as pl
from jax.experimental.pallas import tpu as pltpu
from jax.sharding import Mesh, PartitionSpec as P

F32 = jnp.float32
BF16 = jnp.bfloat16
HALO = 16
EXT = 136
SEG = 17
PADC = 1024
MODES = 16
NT = (((1,), (1,)), ((), ()))


def rounded(a):
    return a.astype(BF16).astype(F32)


def project(
    tp, tk, tn, wt, taps, cott, cotnt, zf, mix, cots, us, dls, acc, turn, wbuf, sems,
):
    steps, _, kblk = wbuf.shape
    copies = [
        pltpu.make_async_copy(wt.at[:, pl.ds(k * kblk, kblk)], wbuf.at[k], sems.at[k])
        for k in range(steps)
    ]
    for copy in copies:
        copy.start()
    width, own = cott.shape
    turn[...] = jnp.zeros(turn.shape, F32)
    turn[0:width, 0:own] = cott[...].astype(F32)
    turn[0:width, own : own + HALO] = cotnt[0:width, :].astype(F32)
    for k in range(steps):
        cols = slice(k * kblk, (k + 1) * kblk)
        rows = jnp.concatenate([tp[:, cols], tk[:, cols], tn[:, cols]], axis=0)
        copies[k].wait()
        part = lax.dot_general(rows, wbuf[k], NT, preferred_element_type=F32)
        if k == 0:
            acc[...] = part
        else:
            acc[...] += part
    if True:
        for g in range(3):
            zf[:, g * PADC : g * PADC + width] = rounded(acc[:, g * width : (g + 1) * width])
            zf[:, g * PADC + width : (g + 1) * PADC] = jnp.zeros((zf.shape[0], PADC - width), F32)

        def tile(ct, carry):
            lane = pl.multiple_of(ct * 128, 128)
            lanes = pl.ds(lane, 128)
            mixed = []
            for g in range(3):
                cols = pl.ds(pl.multiple_of(g * PADC + lane, 128), 128)
                total = taps[0:1, cols] * zf[pl.ds(HALO, EXT), cols]
                for j in range(1, 7):
                    total = total + taps[j : j + 1, cols] * zf[pl.ds(HALO - j, EXT), cols]
                mix[g, :, lanes] = total
                mixed.append(total)
            cot = jnp.concatenate(
                [turn[lanes, 0:128].T, turn[lanes, 128:256].T[0 : EXT - 128]], axis=0
            )
            cots[:, lanes] = cot
            us[:, lanes] = rounded(mixed[1] * mixed[2])
            dls[:, lanes] = rounded(cot * mixed[0])
            return carry

        lax.fori_loop(0, PADC // 128, tile, 0)


def prepare(feats, cott, rates, residues, amp, conv, head, tail, block, taps, held, turn):
    count = rates.shape[0]
    width, own = cott.shape
    depth = feats.shape[1]
    head[:, 0:depth] = feats[0:HALO, :]
    turn[...] = jnp.zeros(turn.shape, F32)
    turn[0:width, :] = cott[...].astype(F32)
    for c in range(PADC // 128):
        part = turn[c * 128 : (c + 1) * 128, :].T[0:HALO]
        head[:, depth + c * 128 : depth + (c + 1) * 128] = part.astype(BF16)
    tail[...] = feats[own - HALO :, :]
    held[...] = jnp.zeros(held.shape, F32)
    for j in range(count):
        row, lane = j // 4, (j % 4) * 2 * MODES
        held[row : row + 1, lane : lane + MODES] = rates[j : j + 1, :]
        held[row : row + 1, lane + MODES : lane + 2 * MODES] = residues[j : j + 1, :] * amp[j : j + 1, :]
    block[...] = jnp.broadcast_to(held[...][None], block.shape)
    taps[...] = jnp.zeros(taps.shape, F32)
    for g in range(3):
        taps[0:7, g * PADC : g * PADC + width] = conv[:, g * width : (g + 1) * width]


def joined_params(blocks, order, left):
    row = lax.broadcasted_iota(jnp.int32, (PADC, PADC), 0)
    col = lax.broadcasted_iota(jnp.int32, (PADC, PADC), 1)
    goal = 15 * lax.bitwise_and(row, 63) + lax.shift_right_logical(row, 6)
    order[...] = jnp.where((goal == col) & (row < 960), 1.0, 0.0).astype(BF16)
    left[...] = jnp.zeros(left.shape, F32)
    count = blocks.shape[0]
    for c in range(4):
        flipped = blocks[:, c, :].T
        for p in range(4):
            j = 4 * c + p
            if j < 15:
                left[:, j * count : (j + 1) * count] = flipped[p * 2 * MODES : (p + 1) * 2 * MODES, :]
    rest = left[...]
    parts = []
    for _ in range(3):
        part = rest.astype(BF16)
        parts.append(part)
        rest = rest - part.astype(F32)
    out = jnp.dot(jnp.concatenate(parts, axis=0), order[...], preferred_element_type=F32)
    size = 2 * MODES
    return out[0:size] + out[size : 2 * size] + out[2 * size : 3 * size]


def end_states(blocks, us, dls, rates, gains, es, ends, endb, ut, dt, left, order):
    joined = joined_params(blocks, order, left)
    rates[...] = joined[0:MODES]
    gains[...] = joined[MODES : 2 * MODES]
    sub = lax.broadcasted_iota(jnp.int32, (8, 128), 0)
    subf = sub.astype(F32)
    fdepth = jnp.where(sub == 7, 0.0, (EXT - 8 - SEG) - SEG * subf)
    bdepth = jnp.where(sub == 0, 0.0, SEG * subf - 8.0)

    def tile(ct, carry):
        lanes = pl.ds(pl.multiple_of(ct * 128, 128), 128)
        ut[...] = us[:, lanes]
        dt[...] = dls[:, lanes]
        rate = rates[:, lanes]
        decay = jnp.exp(-rate)
        for half in range(2):
            ks = range(half * 8, half * 8 + 8)
            al = [jnp.broadcast_to(decay[k : k + 1, :], (8, 128)) for k in ks]
            rl = [jnp.broadcast_to(rate[k : k + 1, :], (8, 128)) for k in ks]
            st = [jnp.zeros((8, 128), F32)] * 8
            snap = st
            for t in range(SEG):
                uv = ut[pl.ds(t, 8, stride=SEG), :]
                st = [a * s + uv for a, s in zip(al, st)]
                if t == 8:
                    snap = st
            for i, k in enumerate(ks):
                es[0, k, :, lanes] = st[i]
                full = jnp.where(sub == 7, snap[i], st[i]) * jnp.exp(-rl[i] * fdepth)
                ends[k : k + 1, lanes] = jnp.sum(full, axis=0, keepdims=True)
            st = [jnp.zeros((8, 128), F32)] * 8
            for t in range(SEG - 1, -1, -1):
                dv = dt[pl.ds(t, 8, stride=SEG), :]
                st = [a * s + dv for a, s in zip(al, st)]
                if t == 8:
                    snap = st
            for i, k in enumerate(ks):
                es[1, k, :, lanes] = st[i]
                full = jnp.where(sub == 0, snap[i], st[i]) * jnp.exp(-rl[i] * bdepth)
                ends[MODES + k : MODES + k + 1, lanes] = jnp.sum(full, axis=0, keepdims=True)
        return carry

    lax.fori_loop(0, PADC // 128, tile, 0)
    endb[...] = ends[...].astype(BF16)


def make_level(span):
    def level(place, own, r1, r2, r3, rates, total, totalb, prefix):
        me = place[0]
        rate = rates[...] * float(span)
        before = jnp.zeros((MODES, PADC), F32)
        after = before
        whole_f = before
        whole_b = before
        for d, ref in enumerate((own, r1, r2, r3)):
            m = lax.rem(me + (4 - d), 4)
            f = ref[0:MODES, :].astype(F32)
            b = ref[MODES : 2 * MODES, :].astype(F32)
            whole_f = whole_f + f * jnp.exp(-rate * (3 - m).astype(F32))
            whole_b = whole_b + b * jnp.exp(-rate * m.astype(F32))
            if d > 0:
                gf = me - 1 - m
                gb = m - me - 1
                wf = jnp.exp(-rate * jnp.maximum(gf, 0).astype(F32))
                wb = jnp.exp(-rate * jnp.maximum(gb, 0).astype(F32))
                before = before + jnp.where(gf >= 0, 1.0, 0.0) * (wf * f)
                after = after + jnp.where(gb >= 0, 1.0, 0.0) * (wb * b)
        prefix[0:MODES, :] = before
        prefix[MODES : 2 * MODES, :] = after
        total[0:MODES, :] = whole_f
        total[MODES : 2 * MODES, :] = whole_b
        totalb[0:MODES, :] = whole_f.astype(BF16)
        totalb[MODES : 2 * MODES, :] = whole_b.astype(BF16)

    return level


def finish(
    place, zf, mix, es, py, pz, px, taps, rates, reff, cots, us, dls,
    outt, dz, dzb, sums, inc, ut, dt, longs, dps, dms, outs, dzs, dzt, packed,
):
    width, own = outt.shape
    rate_all = rates[...] * float(own)
    for back in range(2):
        part = pl.ds(back * MODES, MODES)
        near, mid = place[2], place[1]
        if back:
            near, mid = 3 - near, 3 - mid
        far = pz[part, :] + jnp.exp(-rate_all * (4 * mid).astype(F32)) * px[part, :]
        inc[part, :] = py[part, :] + jnp.exp(-rate_all * near.astype(F32)) * far
    sub = lax.broadcasted_iota(jnp.int32, (8, 128), 0)

    def tile(ct, carry):
        lane = pl.multiple_of(ct * 128, 128)
        lanes = pl.ds(lane, 128)
        ut[...] = us[:, lanes]
        dt[...] = dls[:, lanes]
        rate = rates[:, lanes]
        decay = jnp.exp(-rate)
        gain = reff[:, lanes]
        for half in range(2):
            ks = range(half * 8, half * 8 + 8)
            al = [jnp.broadcast_to(decay[k : k + 1, :], (8, 128)) for k in ks]
            gl = [jnp.broadcast_to(gain[k : k + 1, :], (8, 128)) for k in ks]
            rl = [jnp.broadcast_to(rate[k : k + 1, :], (8, 128)) for k in ks]
            fwd = []
            bwd = []
            for i, k in enumerate(ks):
                jump = [jnp.exp(-float(SEG * m) * rl[i]) for m in (1, 2, 4)]
                x = jnp.where(sub == 0, inc[k : k + 1, lanes], pltpu.roll(es[0, k, :, lanes], 1, 0))
                for m, d in zip((1, 2, 4), jump):
                    x = x + jnp.where(sub >= m, pltpu.roll(x, m, 0) * d, 0.0)
                fwd.append(x)
                x = jnp.where(
                    sub == 7, inc[MODES + k : MODES + k + 1, lanes], pltpu.roll(es[1, k, :, lanes], 7, 0)
                )
                for m, d in zip((1, 2, 4), jump):
                    x = x + jnp.where(sub < 8 - m, pltpu.roll(x, 8 - m, 0) * d, 0.0)
                bwd.append(x)
            gr = [jnp.zeros((8, 128), F32)] * 8
            st = fwd
            for t in range(SEG):
                uv = ut[pl.ds(t, 8, stride=SEG), :]
                dv = dt[pl.ds(t, 8, stride=SEG), :]
                if t >= 9:
                    dv = jnp.where(sub < 7, dv, 0.0)
                st = [a * s + uv for a, s in zip(al, st)]
                gr = [q + dv * s for q, s in zip(gr, st)]
                total = sum(g * s for g, s in zip(gl, st))
                if half:
                    total = total + longs[pl.ds(t, 8, stride=SEG), :]
                longs[pl.ds(t, 8, stride=SEG), :] = total
            for i, k in enumerate(ks):
                sums[24 + k : 25 + k, lanes] = jnp.sum(gr[i], axis=0, keepdims=True)
            st = bwd
            for t in range(SEG - 1, -1, -1):
                dv = dt[pl.ds(t, 8, stride=SEG), :]
                st = [a * s + dv for a, s in zip(al, st)]
                total = sum(g * s for g, s in zip(gl, st))
                if half:
                    total = total + dps[pl.ds(t, 8, stride=SEG), :]
                dps[pl.ds(t, 8, stride=SEG), :] = total
        long_out = rounded(longs[...])
        dprod = rounded(dps[...])
        outs[lanes, :] = (mix[0, 0:own, lanes] * long_out[0:own]).T
        dms[0] = rounded(cots[:, lanes] * long_out)
        dms[1] = rounded(dprod * mix[2, :, lanes])
        dms[2] = rounded(dprod * mix[1, :, lanes])
        for g in range(3):
            cols = pl.ds(pl.multiple_of(g * PADC + lane, 128), 128)
            mine = dms[g, 0:own, :]
            total = taps[0:1, cols] * mine
            sums[8 * g : 8 * g + 1, lanes] = jnp.sum(
                mine * zf[pl.ds(HALO, own), cols], axis=0, keepdims=True
            )
            for j in range(1, 7):
                total = total + taps[j : j + 1, cols] * dms[g, pl.ds(j, own), :]
                sums[8 * g + j : 8 * g + j + 1, lanes] = jnp.sum(
                    mine * zf[pl.ds(HALO - j, own), cols], axis=0, keepdims=True
                )
            sums[8 * g + 7 : 8 * g + 8, lanes] = jnp.zeros((1, 128), F32)
            dzs[:, cols] = total
            dzt[cols, :] = total.T
        return carry

    lax.fori_loop(0, PADC // 128, tile, 0)
    outt[...] = outs[0:width, :].astype(BF16)
    for g in range(3):
        dz[:, g * width : (g + 1) * width] = dzs[:, g * PADC : g * PADC + width].astype(BF16)
        packed[g * width : (g + 1) * width, :] = dzt[g * PADC : g * PADC + width, :]
    piece = dzb.shape[1] // 2
    for b in range(8):
        offs = [h * 8 * piece + (b % 2) * 4 * piece + (b // 2) * piece for h in range(2)]
        both = [packed[off : off + piece, :] for off in offs]
        dzb[b] = jnp.concatenate(both, axis=0).astype(BF16)


def weight_term(place, arrived, ours, theirs, term):
    me = place[0]
    core = place[1]
    chunk = term.shape[2]
    slots = (me, lax.bitwise_xor(me, 1), 3 - me, lax.bitwise_xor(3 - me, 1))
    pairs = []
    for ref, c in ((ours, core), (theirs, 1 - core)):
        for p in range(2):
            left = [arrived[slots[2 * p + i] * 2 + c] for i in range(2)]
            pairs.append((jnp.concatenate(left, axis=1), ref, p))
    for j in range(4):
        total = None
        for left, ref, p in pairs:
            right = ref[p, :, j * chunk : (j + 1) * chunk]
            part = jnp.dot(left, right, preferred_element_type=F32)
            total = part if total is None else total + part
        term[j] = total.astype(BF16)


def split_rows(got, blocks, turn):
    chans = got.shape[1]
    fblk = blocks.shape[1]
    piece = blocks.shape[2]
    turn[0:chans, :] = (
        got[0].astype(F32) + got[1].astype(F32) + got[2].astype(F32) + got[3].astype(F32)
    )
    turn[chans:, :] = jnp.zeros((turn.shape[0] - chans, turn.shape[1]), F32)
    flipped = turn[...].T
    for q in range(16):
        for h in range(2):
            part = flipped[q * fblk : (q + 1) * fblk, h * piece : (h + 1) * piece]
            blocks[2 * q + h] = part.astype(BF16)


def ring(a, ax, d):
    return lax.ppermute(a, ax, [(i, (i + d) % 4) for i in range(4)])


def params(mb):
    return pltpu.CompilerParams(vmem_limit_bytes=mb * 1024 * 1024)


def local(tokens, w_in, conv_taps, residues, rates, cotangent):
    feats = tokens[0]
    cot = cotangent[0]
    own, width = cot.shape
    depth = feats.shape[1]
    chans = 3 * width
    count = 64
    piece = chans // 16
    fblk = depth // count
    xi, zi, yi = lax.axis_index("x"), lax.axis_index("zl"), lax.axis_index("y")
    ci = lax.axis_index("core")
    ctx = ("x", "zl", "y")
    scale = 1.0 / math.sqrt(4 * count * own)
    smem = pl.BlockSpec(memory_space=pltpu.SMEM)
    vm = pl.BlockSpec(memory_space=pltpu.VMEM)
    amp_mine = jnp.sqrt(-jnp.expm1(-2.0 * rates))
    head, tail, block, taps = pl.pallas_call(
        prepare,
        in_specs=[vm] * 6,
        out_specs=[vm] * 4,
        out_shape=[
            jax.ShapeDtypeStruct((HALO, depth + PADC), BF16),
            jax.ShapeDtypeStruct((HALO, depth), BF16),
            jax.ShapeDtypeStruct((count, 8, 128), F32),
            jax.ShapeDtypeStruct((8, 3 * PADC), F32),
        ],
        scratch_shapes=[pltpu.VMEM((8, 128), F32), pltpu.VMEM((PADC, own), F32)],
        compiler_params=params(8),
        name="prepare",
    )(feats, cot.T, rates, residues, amp_mine, conv_taps)
    blocks = lax.all_to_all(block, ctx, split_axis=0, concat_axis=0, tiled=True)
    tprev = lax.ppermute(tail, ctx, [(i, i + 1) for i in range(count - 1)])
    nexts = lax.ppermute(head, ctx, [(i, i - 1) for i in range(1, count)])
    tnext = nexts[:, :depth]
    cnext = nexts[:, depth:].T

    kblk = 256

    ext_rows = own + 2 * HALO
    shapes = [(ext_rows, 3 * PADC), (3, EXT, PADC), (EXT, PADC), (EXT, PADC), (EXT, PADC)]
    zf, mix, cots, us, dls = pl.pallas_call(
        project,
        in_specs=[vm] * 3 + [pl.BlockSpec(memory_space=pl.ANY)] + [vm] * 3,
        out_specs=[vm] * 5,
        out_shape=[jax.ShapeDtypeStruct(s, F32) for s in shapes],
        scratch_shapes=[
            pltpu.VMEM((ext_rows, chans), F32),
            pltpu.VMEM((PADC, 256), F32),
            pltpu.VMEM((depth // kblk, chans, kblk), BF16),
            pltpu.SemaphoreType.DMA((depth // kblk,)),
        ],
        compiler_params=params(46),
        cost_estimate=pl.CostEstimate(flops=1500000000, bytes_accessed=14000000, transcendentals=0),
        name="project",
    )(tprev, feats, tnext, w_in.T, taps, cot.T, cnext)

    blocks, us, dls = lax.optimization_barrier((blocks, us, dls))
    rate, gain, es, ends, endb = pl.pallas_call(
        end_states,
        in_specs=[vm] * 3,
        out_specs=[vm] * 5,
        out_shape=[
            jax.ShapeDtypeStruct((MODES, PADC), F32),
            jax.ShapeDtypeStruct((MODES, PADC), F32),
            jax.ShapeDtypeStruct((2, MODES, 8, PADC), F32),
            jax.ShapeDtypeStruct((2 * MODES, PADC), F32),
            jax.ShapeDtypeStruct((2 * MODES, PADC), BF16),
        ],
        scratch_shapes=[
            pltpu.VMEM((EXT, 128), F32),
            pltpu.VMEM((EXT, 128), F32),
            pltpu.VMEM((2 * MODES, PADC), F32),
            pltpu.VMEM((PADC, PADC), BF16),
        ],
        compiler_params=params(16),
        cost_estimate=pl.CostEstimate(flops=20000000, bytes_accessed=3000000, transcendentals=0),
        name="end_states",
    )(blocks, us, dls)

    mine, _ = lax.optimization_barrier((feats, tprev))
    pair = lax.ppermute(mine, "y", [(i, i ^ 1) for i in range(4)])
    two = jnp.stack([mine, pair], axis=0)

    prefixes = []
    total, sent = ends, endb
    for ax, me, span in (("y", yi, own), ("zl", zi, 4 * own), ("x", xi, 16 * own)):
        near = [ring(sent, ax, d) for d in (1, 2, 3)]
        total, sent, prefix = pl.pallas_call(
            make_level(span),
            in_specs=[smem] + [vm] * 5,
            out_specs=[vm] * 3,
            out_shape=[
                jax.ShapeDtypeStruct((2 * MODES, PADC), F32),
                jax.ShapeDtypeStruct((2 * MODES, PADC), BF16),
                jax.ShapeDtypeStruct((2 * MODES, PADC), F32),
            ],
            compiler_params=params(8),
            name="level",
        )(me.reshape(1), total, *near, rate)
        prefixes.append(prefix)
        if ax == "y":
            two, _ = lax.optimization_barrier((two, sent))
            other = lax.ppermute(two, "y", [(i, 3 - i) for i in range(4)])
    other, prefixes[2] = lax.optimization_barrier((other, prefixes[2]))
    ours = jnp.concatenate([two, other], axis=0)
    theirs = lax.ppermute(ours, "core", [(0, 1), (1, 0)])

    outt, dz, dzb, sums = pl.pallas_call(
        finish,
        in_specs=[smem] + [vm] * 12,
        out_specs=[vm] * 4,
        out_shape=[
            jax.ShapeDtypeStruct((width, own), BF16),
            jax.ShapeDtypeStruct((own, chans), BF16),
            jax.ShapeDtypeStruct((8, 2 * piece, own), BF16),
            jax.ShapeDtypeStruct((40, PADC), F32),
        ],
        scratch_shapes=[
            pltpu.VMEM((2 * MODES, PADC), F32),
            pltpu.VMEM((EXT, 128), F32),
            pltpu.VMEM((EXT, 128), F32),
            pltpu.VMEM((EXT, 128), F32),
            pltpu.VMEM((EXT, 128), F32),
            pltpu.VMEM((3, EXT, 128), F32),
            pltpu.VMEM((PADC, own), F32),
            pltpu.VMEM((own, 3 * PADC), F32),
            pltpu.VMEM((3 * PADC, own), F32),
            pltpu.VMEM((chans, own), F32),
        ],
        compiler_params=params(24),
        cost_estimate=pl.CostEstimate(flops=200000000, bytes_accessed=10000000, transcendentals=0),
        name="finish",
    )(jnp.stack([xi, zi, yi]), zf, mix, es, *prefixes, taps, rate, gain, cots, us, dls)
    output = outt.T

    def summed(a, ax):
        short = a.astype(BF16)
        parts = [short] + [ring(short, ax, d) for d in (1, 2, 3)]
        return sum(p.astype(F32) for p in parts)

    arrived = lax.all_to_all(dzb, ("y", "core"), split_axis=0, concat_axis=0, tiled=True)
    sums = summed(sums, "x")
    arrived, sums = lax.optimization_barrier((arrived, sums))
    term = pl.pallas_call(
        weight_term,
        in_specs=[smem] + [vm] * 3,
        out_specs=vm,
        out_shape=jax.ShapeDtypeStruct((4, 2 * piece, depth // 4), BF16),
        compiler_params=params(24),
        cost_estimate=pl.CostEstimate(flops=1200000000, bytes_accessed=6000000, transcendentals=0),
        name="weight_term",
    )(jnp.stack([yi, ci]), arrived, ours.reshape(2, 2 * own, depth), theirs.reshape(2, 2 * own, depth))
    got = lax.all_to_all(term, "x", 0, 0, tiled=True)
    dz, sums, _ = lax.optimization_barrier((dz, sums, term))
    sums = summed(sums, "zl")
    grad_feats = lax.dot_general(dz, w_in, NT, preferred_element_type=F32).astype(BF16)
    got, sums, grad_feats = lax.optimization_barrier((got, sums, grad_feats))
    blocks = pl.pallas_call(
        split_rows,
        in_specs=[vm],
        out_specs=vm,
        out_shape=jax.ShapeDtypeStruct((32, fblk, piece), BF16),
        scratch_shapes=[pltpu.VMEM((384, depth // 4), F32)],
        compiler_params=params(12),
        name="split_rows",
    )(got)
    last = lax.all_to_all(blocks, ("zl", "y", "zh"), 0, 0, tiled=True)
    sums, _ = lax.optimization_barrier((sums, blocks))
    sums = summed(summed(sums, "y"), ("zh", "core"))
    last = jnp.sum(last.reshape(4, 4, 2, fblk, piece).astype(F32), axis=(0, 2)) * scale
    grad_weight = last.transpose(1, 0, 2).reshape(fblk, 4 * piece).astype(BF16)

    grad_taps = sums[:24].reshape(3, 8, PADC)[:, :7, :width].transpose(1, 0, 2).reshape(7, chans)
    grad_taps = grad_taps * scale
    index = (xi * 4 + zi) * 4 + yi
    held_chans = width // count
    chosen = lax.dynamic_slice_in_dim(sums[24:, :width], index * held_chans, held_chans, axis=1)
    grad_residues = amp_mine * chosen.T * scale

    return (output[None], grad_feats[None], grad_weight, grad_taps, grad_residues)


def solution(mesh):
    fine = Mesh(mesh.devices.reshape(4, 4, 4, 2, 2), ("x", "zl", "y", "zh", "core"))
    ctx = ("x", "zl", "y")
    dp = ("zh", "core")
    in_specs = (P(dp, ctx, None), P(), P(), P(ctx, None), P(ctx, None), P(dp, ctx, None))
    out_specs = (P(dp, ctx, None), P(dp, ctx, None), P(ctx, dp), P(), P(ctx, None))
    return jax.shard_map(local, mesh=fine, in_specs=in_specs, out_specs=out_specs, check_vma=False)
```

```python
import math

import jax
import jax.numpy as jnp
from jax import lax
from jax.experimental import pallas as pl
from jax.experimental.pallas import tpu as pltpu
from jax.sharding import Mesh, PartitionSpec as P

F32 = jnp.float32
BF16 = jnp.bfloat16
HALO = 16
EXT = 136
SEG = 17
PADC = 1024
MODES = 16
NT = (((1,), (1,)), ((), ()))


def rounded(a):
    return a.astype(BF16).astype(F32)


def project(
    tp, tk, nexts, wt, taps, cott, zf_out, mix_out, cots_out, us, dls,
    acc, turn, wbuf, zf, mix, cots, sems, zsem, tsems,
):
    steps, _, kblk = wbuf.shape
    copies = [
        pltpu.make_async_copy(wt.at[:, pl.ds(k * kblk, kblk)], wbuf.at[k], sems.at[k])
        for k in range(steps)
    ]
    for copy in copies:
        copy.start()
    width, own = cott.shape
    depth = tk.shape[1]
    turn[...] = jnp.zeros(turn.shape, F32)
    turn[0:width, :] = cott[...].astype(F32)
    for g in range(3):
        zf[g, :, width:] = jnp.zeros((zf.shape[1], PADC - width), F32)
    for k in range(steps):
        cols = slice(k * kblk, (k + 1) * kblk)
        rows = jnp.concatenate([tp[:, cols], tk[:, cols], nexts[:, cols]], axis=0)
        copies[k].wait()
        part = lax.dot_general(rows, wbuf[k], NT, preferred_element_type=F32)
        if k == 0:
            acc[...] = part
        elif k < steps - 1:
            acc[...] += part
        else:
            total = acc[...] + part
            for g in range(3):
                zf[g, :, 0:width] = rounded(total[:, g * width : (g + 1) * width])
    zcopy = pltpu.make_async_copy(zf, zf_out, zsem)
    zcopy.start()

    def out_copies(ct):
        lanes = pl.ds(pl.multiple_of(ct * 128, 128), 128)
        return (
            pltpu.make_async_copy(mix.at[:, :, lanes], mix_out.at[:, :, lanes], tsems.at[0, ct]),
            pltpu.make_async_copy(cots.at[:, lanes], cots_out.at[:, lanes], tsems.at[1, ct]),
        )

    def tile(ct, carry):
        lane = pl.multiple_of(ct * 128, 128)
        lanes = pl.ds(lane, 128)
        mixed = []
        for g in range(3):
            total = taps[g, 0:1, lanes] * zf[g, pl.ds(HALO, EXT), lanes]
            for j in range(1, 7):
                total = total + taps[g, j : j + 1, lanes] * zf[g, pl.ds(HALO - j, EXT), lanes]
            mix[g, :, lanes] = total
            mixed.append(total)
        after = nexts[:, pl.ds(pl.multiple_of(depth + lane, 128), 128)].astype(F32)
        cot = jnp.concatenate([turn[lanes, :].T, after[0 : EXT - 128]], axis=0)
        cots[:, lanes] = cot
        us[:, lanes] = rounded(mixed[1] * mixed[2])
        dls[:, lanes] = rounded(cot * mixed[0])
        for copy in out_copies(ct):
            copy.start()
        return carry

    lax.fori_loop(0, PADC // 128, tile, 0)
    zcopy.wait()
    for ct in range(PADC // 128):
        for copy in out_copies(ct):
            copy.wait()


def one_minus_exp(x):
    series = jnp.ones_like(x)
    for n in range(13, 1, -1):
        series = 1.0 - series * x * (1.0 / n)
    return jnp.where(x < 0.5, x * series, 1.0 - jnp.exp(-x))


def prepare(
    feats, cott, rates, residues, conv, head, tail, block, taps, amp,
    held, turn, cbuf, rbuf, sbuf, vbuf, sems,
):
    count = rates.shape[0]
    width, own = cott.shape
    depth = feats.shape[1]
    copies = [
        pltpu.make_async_copy(rates, rbuf, sems.at[0]),
        pltpu.make_async_copy(residues, sbuf, sems.at[1]),
        pltpu.make_async_copy(cott, cbuf, sems.at[2]),
        pltpu.make_async_copy(conv, vbuf, sems.at[3]),
        pltpu.make_async_copy(feats.at[pl.ds(0, HALO)], head.at[:, pl.ds(0, depth)], sems.at[4]),
        pltpu.make_async_copy(feats.at[pl.ds(own - HALO, HALO)], tail, sems.at[5]),
    ]
    for copy in copies:
        copy.start()
    held[...] = jnp.zeros(held.shape, F32)
    turn[...] = jnp.zeros(turn.shape, F32)
    taps[...] = jnp.zeros(taps.shape, F32)
    copies[0].wait()
    copies[1].wait()
    size = jnp.sqrt(one_minus_exp(2.0 * rbuf[...]))
    amp[...] = size
    rate = rbuf[...]
    gain = sbuf[...] * size
    for j in range(count):
        row, lane = j // 4, (j % 4) * 2 * MODES
        held[row : row + 1, lane : lane + MODES] = rate[j : j + 1, :]
        held[row : row + 1, lane + MODES : lane + 2 * MODES] = gain[j : j + 1, :]
    block[...] = jnp.broadcast_to(held[...][None], block.shape)
    copies[2].wait()
    turn[0:width, :] = cbuf[...].astype(F32)
    for c in range(PADC // 128):
        part = turn[c * 128 : (c + 1) * 128, :].T[0:HALO]
        head[:, depth + c * 128 : depth + (c + 1) * 128] = part.astype(BF16)
    copies[3].wait()
    for g in range(3):
        taps[g, 0:7, 0:width] = vbuf[:, g * width : (g + 1) * width]
    copies[4].wait()
    copies[5].wait()


def joined_params(blocks, order, left):
    row = lax.broadcasted_iota(jnp.int32, (PADC, PADC), 0)
    col = lax.broadcasted_iota(jnp.int32, (PADC, PADC), 1)
    goal = 15 * lax.bitwise_and(row, 63) + lax.shift_right_logical(row, 6)
    order[...] = jnp.where((goal == col) & (row < 960), 1.0, 0.0).astype(BF16)
    left[...] = jnp.zeros(left.shape, F32)
    count = blocks.shape[0]
    for c in range(4):
        flipped = blocks[:, c, :].T
        for p in range(4):
            j = 4 * c + p
            if j < 15:
                left[:, j * count : (j + 1) * count] = flipped[p * 2 * MODES : (p + 1) * 2 * MODES, :]
    rest = left[...]
    parts = []
    for _ in range(3):
        part = rest.astype(BF16)
        parts.append(part)
        rest = rest - part.astype(F32)
    out = jnp.dot(jnp.concatenate(parts, axis=0), order[...], preferred_element_type=F32)
    size = 2 * MODES
    return out[0:size] + out[size : 2 * size] + out[2 * size : 3 * size]


def end_states(blocks, us, dls, rates, gains, es, ends, endb, ut, dt, left, order):
    joined = joined_params(blocks, order, left)
    rates[...] = joined[0:MODES]
    gains[...] = joined[MODES : 2 * MODES]
    sub = lax.broadcasted_iota(jnp.int32, (8, 128), 0)
    subf = sub.astype(F32)
    fdepth = jnp.where(sub == 7, 0.0, (EXT - 8 - SEG) - SEG * subf)
    bdepth = jnp.where(sub == 0, 0.0, SEG * subf - 8.0)

    def tile(ct, carry):
        lanes = pl.ds(pl.multiple_of(ct * 128, 128), 128)
        ut[...] = us[:, lanes]
        dt[...] = dls[:, lanes]
        rate = rates[:, lanes]
        decay = jnp.exp(-rate)
        for half in range(2):
            ks = range(half * 8, half * 8 + 8)
            al = [jnp.broadcast_to(decay[k : k + 1, :], (8, 128)) for k in ks]
            rl = [jnp.broadcast_to(rate[k : k + 1, :], (8, 128)) for k in ks]
            st = [jnp.zeros((8, 128), F32)] * 8
            snap = st
            for t in range(SEG):
                uv = ut[pl.ds(t, 8, stride=SEG), :]
                st = [a * s + uv for a, s in zip(al, st)]
                if t == 8:
                    snap = st
            for i, k in enumerate(ks):
                es[0, k, :, lanes] = st[i]
                full = jnp.where(sub == 7, snap[i], st[i]) * jnp.exp(-rl[i] * fdepth)
                ends[k : k + 1, lanes] = jnp.sum(full, axis=0, keepdims=True)
            st = [jnp.zeros((8, 128), F32)] * 8
            for t in range(SEG - 1, -1, -1):
                dv = dt[pl.ds(t, 8, stride=SEG), :]
                st = [a * s + dv for a, s in zip(al, st)]
                if t == 8:
                    snap = st
            for i, k in enumerate(ks):
                es[1, k, :, lanes] = st[i]
                full = jnp.where(sub == 0, snap[i], st[i]) * jnp.exp(-rl[i] * bdepth)
                ends[MODES + k : MODES + k + 1, lanes] = jnp.sum(full, axis=0, keepdims=True)
        return carry

    lax.fori_loop(0, PADC // 128, tile, 0)
    endb[...] = ends[...].astype(BF16)


def make_level(span):
    def level(place, own, r1, r2, r3, rates, total, totalb, prefix):
        me = place[0]
        rate = rates[...] * float(span)
        before = jnp.zeros((MODES, PADC), F32)
        after = before
        whole_f = before
        whole_b = before
        for d, ref in enumerate((own, r1, r2, r3)):
            m = lax.rem(me + (4 - d), 4)
            f = ref[0:MODES, :].astype(F32)
            b = ref[MODES : 2 * MODES, :].astype(F32)
            whole_f = whole_f + f * jnp.exp(-rate * (3 - m).astype(F32))
            whole_b = whole_b + b * jnp.exp(-rate * m.astype(F32))
            if d > 0:
                gf = me - 1 - m
                gb = m - me - 1
                wf = jnp.exp(-rate * jnp.maximum(gf, 0).astype(F32))
                wb = jnp.exp(-rate * jnp.maximum(gb, 0).astype(F32))
                before = before + jnp.where(gf >= 0, 1.0, 0.0) * (wf * f)
                after = after + jnp.where(gb >= 0, 1.0, 0.0) * (wb * b)
        prefix[0:MODES, :] = before
        prefix[MODES : 2 * MODES, :] = after
        total[0:MODES, :] = whole_f
        total[MODES : 2 * MODES, :] = whole_b
        totalb[0:MODES, :] = whole_f.astype(BF16)
        totalb[MODES : 2 * MODES, :] = whole_b.astype(BF16)

    return level


def finish(
    place, zf, mix, es, py, pz, px, taps, rates, reff, cots,
    outt, dz, dzb, sums, inc, ut, dt, longs, dps, dms, dzt,
):
    own = dz.shape[1]
    rate = rates[...]
    for back in range(2):
        part = pl.ds(back * MODES, MODES)
        near, mid = place[2], place[1]
        if back:
            near, mid = 3 - near, 3 - mid
        far = pz[part, :] + jnp.exp(-rate * (4 * own * mid).astype(F32)) * px[part, :]
        inc[part, :] = py[part, :] + jnp.exp(-rate * (own * near).astype(F32)) * far
    sub = lax.broadcasted_iota(jnp.int32, (8, 128), 0)
    ut[...] = rounded(mix[1] * mix[2])
    dt[...] = rounded(cots[...] * mix[0])
    decay = jnp.exp(-rate)
    gain = reff[...]
    for half in range(2):
        ks = range(half * 8, half * 8 + 8)
        al = [jnp.broadcast_to(decay[k : k + 1, :], (8, 128)) for k in ks]
        gl = [jnp.broadcast_to(gain[k : k + 1, :], (8, 128)) for k in ks]
        rl = [jnp.broadcast_to(rate[k : k + 1, :], (8, 128)) for k in ks]
        fwd = []
        bwd = []
        for i, k in enumerate(ks):
            jump = [jnp.exp(-float(SEG * m) * rl[i]) for m in (1, 2, 4)]
            x = jnp.where(sub == 0, inc[k : k + 1, :], pltpu.roll(es[0, k], 1, 0))
            for m, d in zip((1, 2, 4), jump):
                x = x + jnp.where(sub >= m, pltpu.roll(x, m, 0) * d, 0.0)
            fwd.append(x)
            x = jnp.where(
                sub == 7, inc[MODES + k : MODES + k + 1, :], pltpu.roll(es[1, k], 7, 0)
            )
            for m, d in zip((1, 2, 4), jump):
                x = x + jnp.where(sub < 8 - m, pltpu.roll(x, 8 - m, 0) * d, 0.0)
            bwd.append(x)
        gr = [jnp.zeros((8, 128), F32)] * 8
        st = fwd
        for t in range(SEG):
            uv = ut[pl.ds(t, 8, stride=SEG), :]
            dv = dt[pl.ds(t, 8, stride=SEG), :]
            if t >= 9:
                dv = jnp.where(sub < 7, dv, 0.0)
            st = [a * s + uv for a, s in zip(al, st)]
            gr = [q + dv * s for q, s in zip(gr, st)]
            total = sum(g * s for g, s in zip(gl, st))
            if half:
                total = total + longs[pl.ds(t, 8, stride=SEG), :]
            longs[pl.ds(t, 8, stride=SEG), :] = total
        for i, k in enumerate(ks):
            sums[24 + k : 25 + k, :] = jnp.sum(gr[i], axis=0, keepdims=True)
        st = bwd
        for t in range(SEG - 1, -1, -1):
            dv = dt[pl.ds(t, 8, stride=SEG), :]
            st = [a * s + dv for a, s in zip(al, st)]
            total = sum(g * s for g, s in zip(gl, st))
            if half:
                total = total + dps[pl.ds(t, 8, stride=SEG), :]
            dps[pl.ds(t, 8, stride=SEG), :] = total
    long_out = rounded(longs[...])
    dprod = rounded(dps[...])
    outt[...] = (mix[0, 0:own, :] * long_out[0:own]).T.astype(BF16)
    dms[0] = rounded(cots[...] * long_out)
    dms[1] = rounded(dprod * mix[2])
    dms[2] = rounded(dprod * mix[1])
    ct = pl.program_id(0)
    for g in range(3):
        mine = dms[g, 0:own, :]
        total = taps[g, 0:1, :] * mine
        sums[8 * g : 8 * g + 1, :] = jnp.sum(mine * zf[g, pl.ds(HALO, own), :], axis=0, keepdims=True)
        for j in range(1, 7):
            total = total + taps[g, j : j + 1, :] * dms[g, pl.ds(j, own), :]
            sums[8 * g + j : 8 * g + j + 1, :] = jnp.sum(
                mine * zf[g, pl.ds(HALO - j, own), :], axis=0, keepdims=True
            )
        sums[8 * g + 7 : 8 * g + 8, :] = jnp.zeros((1, 128), F32)
        dz[g] = total.astype(BF16)
        dzt[g, pl.ds(pl.multiple_of(ct * 128, 128), 128), :] = total.T

    @pl.when(ct == pl.num_programs(0) - 1)
    def _():
        piece = dzb.shape[1] // 2
        width = 16 * piece // 3
        for b in range(8):
            both = []
            for h in range(2):
                off = h * 8 * piece + (b % 2) * 4 * piece + (b // 2) * piece
                g, low = off // width, off % width
                size = min(piece, width - low)
                both.append(dzt[g, low : low + size, :])
                if size < piece:
                    both.append(dzt[g + 1, 0 : piece - size, :])
            dzb[b] = jnp.concatenate(both, axis=0).astype(BF16)


def token_grads(dz, wt, out, acc):
    g = pl.program_id(0)
    part = jnp.dot(dz[0, :, 0 : wt.shape[0]], wt[...], preferred_element_type=F32)

    @pl.when(g == 0)
    def _():
        acc[...] = part

    @pl.when(g > 0)
    def _():
        acc[...] += part

    @pl.when(g == pl.num_programs(0) - 1)
    def _():
        out[...] = acc[...].astype(BF16)


def weight_term(place, arrived, *refs):
    *tokens, term = refs
    me = place[0]
    core = place[1]
    chunk = term.shape[2]
    slots = (me, lax.bitwise_xor(me, 1), 3 - me, lax.bitwise_xor(3 - me, 1))
    pairs = []
    for half, c in ((0, core), (1, 1 - core)):
        for p in (0, 2):
            left = [arrived[slots[p + i] * 2 + c] for i in range(2)]
            pairs.append((jnp.concatenate(left, axis=1), tokens[4 * half + p : 4 * half + p + 2]))
    for j in range(4):
        total = None
        cols = slice(j * chunk, (j + 1) * chunk)
        for left, (one, two) in pairs:
            right = jnp.concatenate([one[:, cols], two[:, cols]], axis=0)
            part = jnp.dot(left, right, preferred_element_type=F32)
            total = part if total is None else total + part
        term[j] = total.astype(BF16)


def split_rows(got, blocks, turn):
    chans = got.shape[1]
    fblk = blocks.shape[1]
    piece = blocks.shape[2]
    turn[0:chans, :] = (
        got[0].astype(F32) + got[1].astype(F32) + got[2].astype(F32) + got[3].astype(F32)
    )
    turn[chans:, :] = jnp.zeros((turn.shape[0] - chans, turn.shape[1]), F32)
    flipped = turn[...].T
    for q in range(16):
        for h in range(2):
            part = flipped[q * fblk : (q + 1) * fblk, h * piece : (h + 1) * piece]
            blocks[2 * q + h] = part.astype(BF16)


def ring(a, ax, d):
    return lax.ppermute(a, ax, [(i, (i + d) % 4) for i in range(4)])


def params(mb):
    return pltpu.CompilerParams(vmem_limit_bytes=mb * 1024 * 1024)


def local(tokens, w_in, conv_taps, residues, rates, cotangent):
    feats = tokens[0]
    cot = cotangent[0]
    own, width = cot.shape
    depth = feats.shape[1]
    chans = 3 * width
    count = 64
    piece = chans // 16
    fblk = depth // count
    xi, zi, yi = lax.axis_index("x"), lax.axis_index("zl"), lax.axis_index("y")
    ci = lax.axis_index("core")
    ctx = ("x", "zl", "y")
    scale = 1.0 / math.sqrt(4 * count * own)
    smem = pl.BlockSpec(memory_space=pltpu.SMEM)
    vm = pl.BlockSpec(memory_space=pltpu.VMEM)
    anywhere = pl.BlockSpec(memory_space=pl.ANY)
    head, tail, block, taps, amp_mine = pl.pallas_call(
        prepare,
        in_specs=[anywhere] * 5,
        out_specs=[vm] * 5,
        out_shape=[
            jax.ShapeDtypeStruct((HALO, depth + PADC), BF16),
            jax.ShapeDtypeStruct((HALO, depth), BF16),
            jax.ShapeDtypeStruct((count, 8, 128), F32),
            jax.ShapeDtypeStruct((3, 8, PADC), F32),
            jax.ShapeDtypeStruct(rates.shape, F32),
        ],
        scratch_shapes=[
            pltpu.VMEM((8, 128), F32),
            pltpu.VMEM((PADC, own), F32),
            pltpu.VMEM((width, own), BF16),
            pltpu.VMEM(rates.shape, F32),
            pltpu.VMEM(rates.shape, F32),
            pltpu.VMEM(conv_taps.shape, F32),
            pltpu.SemaphoreType.DMA((6,)),
        ],
        compiler_params=params(60),
        name="prepare",
    )(feats, cot.T, rates, residues, conv_taps)
    tprev = lax.ppermute(tail, ctx, [(i, i + 1) for i in range(count - 1)])
    nexts = lax.ppermute(head, ctx, [(i, i - 1) for i in range(1, count)])
    block, tprev, nexts = lax.optimization_barrier((block, tprev, nexts))
    blocks = lax.all_to_all(block, ctx, split_axis=0, concat_axis=0, tiled=True)

    kblk = 256
    ext_rows = own + 2 * HALO
    shapes = [(3, ext_rows, PADC), (3, EXT, PADC), (EXT, PADC), (EXT, PADC), (EXT, PADC)]
    zf, mix, cots, us, dls = pl.pallas_call(
        project,
        in_specs=[vm] * 3 + [anywhere] + [vm] * 2,
        out_specs=[anywhere] * 3 + [vm] * 2,
        out_shape=[jax.ShapeDtypeStruct(s, F32) for s in shapes],
        scratch_shapes=[
            pltpu.VMEM((ext_rows, chans), F32),
            pltpu.VMEM((PADC, own), F32),
            pltpu.VMEM((depth // kblk, chans, kblk), BF16),
            pltpu.VMEM(shapes[0], F32),
            pltpu.VMEM(shapes[1], F32),
            pltpu.VMEM(shapes[2], F32),
            pltpu.SemaphoreType.DMA((depth // kblk,)),
            pltpu.SemaphoreType.DMA,
            pltpu.SemaphoreType.DMA((2, PADC // 128)),
        ],
        compiler_params=params(48),
        cost_estimate=pl.CostEstimate(flops=1500000000, bytes_accessed=14000000, transcendentals=0),
        name="project",
    )(tprev, feats, nexts, w_in.T, taps, cot.T)

    blocks, us, dls = lax.optimization_barrier((blocks, us, dls))
    rate, gain, es, ends, endb = pl.pallas_call(
        end_states,
        in_specs=[vm] * 3,
        out_specs=[vm] * 5,
        out_shape=[
            jax.ShapeDtypeStruct((MODES, PADC), F32),
            jax.ShapeDtypeStruct((MODES, PADC), F32),
            jax.ShapeDtypeStruct((2, MODES, 8, PADC), F32),
            jax.ShapeDtypeStruct((2 * MODES, PADC), F32),
            jax.ShapeDtypeStruct((2 * MODES, PADC), BF16),
        ],
        scratch_shapes=[
            pltpu.VMEM((EXT, 128), F32),
            pltpu.VMEM((EXT, 128), F32),
            pltpu.VMEM((2 * MODES, PADC), F32),
            pltpu.VMEM((PADC, PADC), BF16),
        ],
        compiler_params=params(16),
        cost_estimate=pl.CostEstimate(flops=20000000, bytes_accessed=3000000, transcendentals=0),
        name="end_states",
    )(blocks, us, dls)

    prefixes = []
    total, sent = ends, endb
    for ax, me, span in (("y", yi, own), ("zl", zi, 4 * own), ("x", xi, 16 * own)):
        near = [ring(sent, ax, d) for d in (1, 2, 3)]
        total, sent, prefix = pl.pallas_call(
            make_level(span),
            in_specs=[smem] + [vm] * 5,
            out_specs=[vm] * 3,
            out_shape=[
                jax.ShapeDtypeStruct((2 * MODES, PADC), F32),
                jax.ShapeDtypeStruct((2 * MODES, PADC), BF16),
                jax.ShapeDtypeStruct((2 * MODES, PADC), F32),
            ],
            compiler_params=params(8),
            name="level",
        )(me.reshape(1), total, *near, rate)
        prefixes.append(prefix)
        if ax == "y":
            mine, _ = lax.optimization_barrier((feats, sent))
            pair = lax.ppermute(mine, "y", [(i, i ^ 1) for i in range(4)])
            opposite = lax.ppermute(mine, "y", [(i, 3 - i) for i in range(4)])
        elif ax == "zl":
            pair, opposite, _ = lax.optimization_barrier((pair, opposite, sent))
            far = lax.ppermute(pair, "y", [(i, 3 - i) for i in range(4)])

    def tiles(shape):
        lead = len(shape) - 1
        return pl.BlockSpec(shape, lambda k: (0,) * lead + (k,))

    outt, dz, dzb, sums = pl.pallas_call(
        finish,
        grid=(PADC // 128,),
        in_specs=[
            smem,
            tiles((3, ext_rows, 128)),
            tiles((3, EXT, 128)),
            tiles((2, MODES, 8, 128)),
            tiles((2 * MODES, 128)),
            tiles((2 * MODES, 128)),
            tiles((2 * MODES, 128)),
            tiles((3, 8, 128)),
            tiles((MODES, 128)),
            tiles((MODES, 128)),
            tiles((EXT, 128)),
        ],
        out_specs=[
            pl.BlockSpec((128, own), lambda k: (k, 0)),
            tiles((3, own, 128)),
            pl.BlockSpec((8, 2 * piece, own), lambda k: (0, 0, 0)),
            tiles((40, 128)),
        ],
        out_shape=[
            jax.ShapeDtypeStruct((width, own), BF16),
            jax.ShapeDtypeStruct((3, own, PADC), BF16),
            jax.ShapeDtypeStruct((8, 2 * piece, own), BF16),
            jax.ShapeDtypeStruct((40, PADC), F32),
        ],
        scratch_shapes=[
            pltpu.VMEM((2 * MODES, 128), F32),
            pltpu.VMEM((EXT, 128), F32),
            pltpu.VMEM((EXT, 128), F32),
            pltpu.VMEM((EXT, 128), F32),
            pltpu.VMEM((EXT, 128), F32),
            pltpu.VMEM((3, EXT, 128), F32),
            pltpu.VMEM((3, PADC, own), F32),
        ],
        compiler_params=params(40),
        cost_estimate=pl.CostEstimate(flops=200000000, bytes_accessed=10000000, transcendentals=0),
        name="finish",
    )(jnp.stack([xi, zi, yi]), zf, mix, es, *prefixes, taps, rate, gain, cots)
    output = outt.T
    blocks_of = [mine, pair, opposite, far]
    theirs = [lax.ppermute(a, "core", [(0, 1), (1, 0)]) for a in blocks_of]

    def summed(a, ax):
        short = a.astype(BF16)
        parts = [short] + [ring(short, ax, d) for d in (1, 2, 3)]
        return sum(p.astype(F32) for p in parts)

    arrived = lax.all_to_all(dzb, ("y", "core"), split_axis=0, concat_axis=0, tiled=True)
    sums = summed(sums, "x")
    arrived, sums = lax.optimization_barrier((arrived, sums))
    term = pl.pallas_call(
        weight_term,
        in_specs=[smem] + [vm] * 9,
        out_specs=vm,
        out_shape=jax.ShapeDtypeStruct((4, 2 * piece, depth // 4), BF16),
        compiler_params=params(24),
        cost_estimate=pl.CostEstimate(flops=1200000000, bytes_accessed=6000000, transcendentals=0),
        name="weight_term",
    )(jnp.stack([yi, ci]), arrived, *blocks_of, *theirs)
    got = lax.all_to_all(term, "x", 0, 0, tiled=True)
    sums, _ = lax.optimization_barrier((sums, term))
    sums = summed(summed(sums, "zl"), "y")
    got, sums = lax.optimization_barrier((got, sums))
    blocks = pl.pallas_call(
        split_rows,
        in_specs=[vm],
        out_specs=vm,
        out_shape=jax.ShapeDtypeStruct((32, fblk, piece), BF16),
        scratch_shapes=[pltpu.VMEM((384, depth // 4), F32)],
        compiler_params=params(12),
        name="split_rows",
    )(got)
    last = lax.all_to_all(blocks, ("zl", "y", "zh"), 0, 0, tiled=True)
    sums, dz, _ = lax.optimization_barrier((sums, dz, blocks))
    sums = summed(sums, ("zh", "core"))
    grad_feats = pl.pallas_call(
        token_grads,
        grid=(3,),
        in_specs=[
            pl.BlockSpec((1, own, PADC), lambda g: (g, 0, 0)),
            pl.BlockSpec((width, depth), lambda g: (g, 0)),
        ],
        out_specs=pl.BlockSpec((own, depth), lambda g: (0, 0)),
        out_shape=jax.ShapeDtypeStruct((own, depth), BF16),
        scratch_shapes=[pltpu.VMEM((own, depth), F32)],
        compiler_params=params(24),
        cost_estimate=pl.CostEstimate(flops=1200000000, bytes_accessed=11000000, transcendentals=0),
        name="token_grads",
    )(dz, w_in.T)
    last = jnp.sum(last.reshape(4, 4, 2, fblk, piece).astype(F32), axis=(0, 2)) * scale
    grad_weight = last.transpose(1, 0, 2).reshape(fblk, 4 * piece).astype(BF16)

    grad_taps = sums[:24].reshape(3, 8, PADC)[:, :7, :width].transpose(1, 0, 2).reshape(7, chans)
    grad_taps = grad_taps * scale
    index = (xi * 4 + zi) * 4 + yi
    held_chans = width // count
    chosen = lax.dynamic_slice_in_dim(sums[24:, :width], index * held_chans, held_chans, axis=1)
    grad_residues = amp_mine * chosen.T * scale

    return (output[None], grad_feats[None], grad_weight, grad_taps, grad_residues)


def solution(mesh):
    fine = Mesh(mesh.devices.reshape(4, 4, 4, 2, 2), ("x", "zl", "y", "zh", "core"))
    ctx = ("x", "zl", "y")
    dp = ("zh", "core")
    in_specs = (P(dp, ctx, None), P(), P(), P(ctx, None), P(ctx, None), P(dp, ctx, None))
    out_specs = (P(dp, ctx, None), P(dp, ctx, None), P(ctx, dp), P(), P(ctx, None))
    return jax.shard_map(local, mesh=fine, in_specs=in_specs, out_specs=out_specs, check_vma=False)
```

```python
import math

import jax
import jax.numpy as jnp
from jax import lax
from jax.experimental import pallas as pl
from jax.experimental.pallas import tpu as pltpu
from jax.sharding import Mesh, PartitionSpec as P

F32 = jnp.float32
BF16 = jnp.bfloat16
HALO = 16
EXT = 136
SEG = 17
PADC = 1024
MODES = 16
NT = (((1,), (1,)), ((), ()))


def rounded(a):
    return a.astype(BF16).astype(F32)


def project(
    tp, nexts, taps, feats, cott, wt, zf_out, mix_out, cots_out, us, dls,
    acc, turn, wbuf, zf, mix, cots, tk, cbuf, sems, zsem, tsems, isems,
):
    steps, _, kblk = wbuf.shape
    arrivals = [
        pltpu.make_async_copy(feats, tk, isems.at[0]),
        pltpu.make_async_copy(cott, cbuf, isems.at[1]),
    ]
    arrivals[0].start()
    copies = [
        pltpu.make_async_copy(wt.at[:, pl.ds(k * kblk, kblk)], wbuf.at[k], sems.at[k])
        for k in range(steps)
    ]
    for copy in copies:
        copy.start()
    arrivals[1].start()
    width, own = cott.shape
    depth = tk.shape[1]
    turn[...] = jnp.zeros(turn.shape, F32)
    for g in range(3):
        zf[g, :, width:] = jnp.zeros((zf.shape[1], PADC - width), F32)
    arrivals[0].wait()
    for k in range(steps):
        cols = slice(k * kblk, (k + 1) * kblk)
        rows = jnp.concatenate([tp[:, cols], tk[:, cols], nexts[:, cols]], axis=0)
        copies[k].wait()
        part = lax.dot_general(rows, wbuf[k], NT, preferred_element_type=F32)
        if k == 0:
            acc[...] = part
        elif k < steps - 1:
            acc[...] += part
        else:
            total = acc[...] + part
            for g in range(3):
                zf[g, :, 0:width] = rounded(total[:, g * width : (g + 1) * width])
    zcopy = pltpu.make_async_copy(zf, zf_out, zsem)
    zcopy.start()
    arrivals[1].wait()
    turn[0:width, :] = cbuf[...].astype(F32)

    def out_copies(ct):
        lanes = pl.ds(pl.multiple_of(ct * 128, 128), 128)
        return (
            pltpu.make_async_copy(mix.at[:, :, lanes], mix_out.at[:, :, lanes], tsems.at[0, ct]),
            pltpu.make_async_copy(cots.at[:, lanes], cots_out.at[:, lanes], tsems.at[1, ct]),
        )

    def tile(ct, carry):
        lane = pl.multiple_of(ct * 128, 128)
        lanes = pl.ds(lane, 128)
        mixed = []
        for g in range(3):
            total = taps[g, 0:1, lanes] * zf[g, pl.ds(HALO, EXT), lanes]
            for j in range(1, 7):
                total = total + taps[g, j : j + 1, lanes] * zf[g, pl.ds(HALO - j, EXT), lanes]
            mix[g, :, lanes] = total
            mixed.append(total)
        after = nexts[:, pl.ds(pl.multiple_of(depth + lane, 128), 128)].astype(F32)
        cot = jnp.concatenate([turn[lanes, :].T, after[0 : EXT - 128]], axis=0)
        cots[:, lanes] = cot
        us[:, lanes] = rounded(mixed[1] * mixed[2])
        dls[:, lanes] = rounded(cot * mixed[0])
        for copy in out_copies(ct):
            copy.start()
        return carry

    lax.fori_loop(0, PADC // 128, tile, 0)
    zcopy.wait()
    for ct in range(PADC // 128):
        for copy in out_copies(ct):
            copy.wait()


def one_minus_exp(x):
    series = jnp.ones_like(x)
    for n in range(13, 1, -1):
        series = 1.0 - series * x * (1.0 / n)
    return jnp.where(x < 0.5, x * series, 1.0 - jnp.exp(-x))


def prepare(
    feats, cott, rates, residues, conv, head, tail, block, taps, amp,
    held, turn, cbuf, rbuf, sbuf, vbuf, sems,
):
    count = rates.shape[0]
    width, own = cott.shape
    depth = feats.shape[1]
    copies = [
        pltpu.make_async_copy(rates, rbuf, sems.at[0]),
        pltpu.make_async_copy(residues, sbuf, sems.at[1]),
        pltpu.make_async_copy(cott, cbuf, sems.at[2]),
        pltpu.make_async_copy(conv, vbuf, sems.at[3]),
        pltpu.make_async_copy(feats.at[pl.ds(0, HALO)], head.at[:, pl.ds(0, depth)], sems.at[4]),
        pltpu.make_async_copy(feats.at[pl.ds(own - HALO, HALO)], tail, sems.at[5]),
    ]
    for copy in copies:
        copy.start()
    held[...] = jnp.zeros(held.shape, F32)
    turn[...] = jnp.zeros(turn.shape, F32)
    taps[...] = jnp.zeros(taps.shape, F32)
    copies[0].wait()
    copies[1].wait()
    size = jnp.sqrt(one_minus_exp(2.0 * rbuf[...]))
    amp[...] = size
    held[0:count, 0:MODES] = rbuf[...]
    held[0:count, MODES : 2 * MODES] = sbuf[...] * size
    block[...] = held[...].T[0 : 2 * MODES, 0:count]
    copies[2].wait()
    turn[0:width, :] = cbuf[...].astype(F32)
    for c in range(PADC // 128):
        part = turn[c * 128 : (c + 1) * 128, :].T[0:HALO]
        head[:, depth + c * 128 : depth + (c + 1) * 128] = part.astype(BF16)
    copies[3].wait()
    for g in range(3):
        taps[g, 0:7, 0:width] = vbuf[:, g * width : (g + 1) * width]
    copies[4].wait()
    copies[5].wait()


def placed(me, refs, held, goal):
    wide = refs[0].shape[1]
    total = None
    for d, ref in enumerate(refs):
        held[...] = jnp.zeros(held.shape, F32)
        held[:, 0:wide] = ref[...]
        part = pltpu.roll(held[...], lax.rem(me + (4 - d), 4) * wide, 1)
        total = part if total is None else total + part
    return total[:, 0:goal]


def make_join(axis):
    def join_params(place, r0, r1, r2, r3, out, held):
        out[...] = placed(place[axis], (r0, r1, r2, r3), held, out.shape[1])

    return join_params


def end_states(place, r0, r1, r2, r3, us, dls, rates, gains, es, ends, endb, ut, dt, held):
    joined = placed(place[0], (r0, r1, r2, r3), held, PADC)
    rates[...] = joined[0:MODES]
    gains[...] = joined[MODES : 2 * MODES]
    sub = lax.broadcasted_iota(jnp.int32, (8, 128), 0)
    subf = sub.astype(F32)
    fdepth = jnp.where(sub == 7, 0.0, (EXT - 8 - SEG) - SEG * subf)
    bdepth = jnp.where(sub == 0, 0.0, SEG * subf - 8.0)

    def tile(ct, carry):
        lanes = pl.ds(pl.multiple_of(ct * 128, 128), 128)
        ut[...] = us[:, lanes]
        dt[...] = dls[:, lanes]
        rate = rates[:, lanes]
        decay = jnp.exp(-rate)
        for half in range(2):
            ks = range(half * 8, half * 8 + 8)
            al = [jnp.broadcast_to(decay[k : k + 1, :], (8, 128)) for k in ks]
            rl = [jnp.broadcast_to(rate[k : k + 1, :], (8, 128)) for k in ks]
            st = [jnp.zeros((8, 128), F32)] * 8
            snap = st
            for t in range(SEG):
                uv = ut[pl.ds(t, 8, stride=SEG), :]
                st = [a * s + uv for a, s in zip(al, st)]
                if t == 8:
                    snap = st
            for i, k in enumerate(ks):
                es[0, k, :, lanes] = st[i]
                full = jnp.where(sub == 7, snap[i], st[i]) * jnp.exp(-rl[i] * fdepth)
                ends[k : k + 1, lanes] = jnp.sum(full, axis=0, keepdims=True)
            st = [jnp.zeros((8, 128), F32)] * 8
            for t in range(SEG - 1, -1, -1):
                dv = dt[pl.ds(t, 8, stride=SEG), :]
                st = [a * s + dv for a, s in zip(al, st)]
                if t == 8:
                    snap = st
            for i, k in enumerate(ks):
                es[1, k, :, lanes] = st[i]
                full = jnp.where(sub == 0, snap[i], st[i]) * jnp.exp(-rl[i] * bdepth)
                ends[MODES + k : MODES + k + 1, lanes] = jnp.sum(full, axis=0, keepdims=True)
        return carry

    lax.fori_loop(0, PADC // 128, tile, 0)
    endb[...] = ends[...].astype(BF16)


def make_level(axis, span):
    def level(place, own, r1, r2, r3, rates, total, totalb, prefix):
        me = place[axis]
        rate = rates[...] * float(span)
        before = jnp.zeros((MODES, PADC), F32)
        after = before
        whole_f = before
        whole_b = before
        for d, ref in enumerate((own, r1, r2, r3)):
            m = lax.rem(me + (4 - d), 4)
            f = ref[0:MODES, :].astype(F32)
            b = ref[MODES : 2 * MODES, :].astype(F32)
            whole_f = whole_f + f * jnp.exp(-rate * (3 - m).astype(F32))
            whole_b = whole_b + b * jnp.exp(-rate * m.astype(F32))
            if d > 0:
                gf = me - 1 - m
                gb = m - me - 1
                wf = jnp.exp(-rate * jnp.maximum(gf, 0).astype(F32))
                wb = jnp.exp(-rate * jnp.maximum(gb, 0).astype(F32))
                before = before + jnp.where(gf >= 0, 1.0, 0.0) * (wf * f)
                after = after + jnp.where(gb >= 0, 1.0, 0.0) * (wb * b)
        prefix[0:MODES, :] = before
        prefix[MODES : 2 * MODES, :] = after
        total[0:MODES, :] = whole_f
        total[MODES : 2 * MODES, :] = whole_b
        totalb[0:MODES, :] = whole_f.astype(BF16)
        totalb[MODES : 2 * MODES, :] = whole_b.astype(BF16)

    return level


def finish(
    place, zf, mix, es, py, pz, px, taps, rates, reff, cots,
    outt, dz, dzb, sumb, sums, inc, ut, dt, longs, dps, dms, dzt,
):
    own = dz.shape[1]
    rate = rates[...]
    for back in range(2):
        part = pl.ds(back * MODES, MODES)
        near, mid = place[2], place[1]
        if back:
            near, mid = 3 - near, 3 - mid
        far = pz[part, :] + jnp.exp(-rate * (4 * own * mid).astype(F32)) * px[part, :]
        inc[part, :] = py[part, :] + jnp.exp(-rate * (own * near).astype(F32)) * far
    sub = lax.broadcasted_iota(jnp.int32, (8, 128), 0)
    ut[...] = rounded(mix[1] * mix[2])
    dt[...] = rounded(cots[...] * mix[0])
    decay = jnp.exp(-rate)
    gain = reff[...]
    for half in range(2):
        ks = range(half * 8, half * 8 + 8)
        al = [jnp.broadcast_to(decay[k : k + 1, :], (8, 128)) for k in ks]
        gl = [jnp.broadcast_to(gain[k : k + 1, :], (8, 128)) for k in ks]
        rl = [jnp.broadcast_to(rate[k : k + 1, :], (8, 128)) for k in ks]
        fwd = []
        bwd = []
        for i, k in enumerate(ks):
            jump = [jnp.exp(-float(SEG * m) * rl[i]) for m in (1, 2, 4)]
            x = jnp.where(sub == 0, inc[k : k + 1, :], pltpu.roll(es[0, k], 1, 0))
            for m, d in zip((1, 2, 4), jump):
                x = x + jnp.where(sub >= m, pltpu.roll(x, m, 0) * d, 0.0)
            fwd.append(x)
            x = jnp.where(
                sub == 7, inc[MODES + k : MODES + k + 1, :], pltpu.roll(es[1, k], 7, 0)
            )
            for m, d in zip((1, 2, 4), jump):
                x = x + jnp.where(sub < 8 - m, pltpu.roll(x, 8 - m, 0) * d, 0.0)
            bwd.append(x)
        gr = [jnp.zeros((8, 128), F32)] * 8
        st = fwd
        for t in range(SEG):
            uv = ut[pl.ds(t, 8, stride=SEG), :]
            dv = dt[pl.ds(t, 8, stride=SEG), :]
            if t >= 9:
                dv = jnp.where(sub < 7, dv, 0.0)
            st = [a * s + uv for a, s in zip(al, st)]
            gr = [q + dv * s for q, s in zip(gr, st)]
            total = sum(g * s for g, s in zip(gl, st))
            if half:
                total = total + longs[pl.ds(t, 8, stride=SEG), :]
            longs[pl.ds(t, 8, stride=SEG), :] = total
        for i, k in enumerate(ks):
            sums[24 + k : 25 + k, :] = jnp.sum(gr[i], axis=0, keepdims=True)
        st = bwd
        for t in range(SEG - 1, -1, -1):
            dv = dt[pl.ds(t, 8, stride=SEG), :]
            st = [a * s + dv for a, s in zip(al, st)]
            total = sum(g * s for g, s in zip(gl, st))
            if half:
                total = total + dps[pl.ds(t, 8, stride=SEG), :]
            dps[pl.ds(t, 8, stride=SEG), :] = total
    long_out = rounded(longs[...])
    dprod = rounded(dps[...])
    outt[...] = (mix[0, 0:own, :] * long_out[0:own]).T.astype(BF16)
    dms[0] = rounded(cots[...] * long_out)
    dms[1] = rounded(dprod * mix[2])
    dms[2] = rounded(dprod * mix[1])
    ct = pl.program_id(0)
    for g in range(3):
        mine = dms[g, 0:own, :]
        total = taps[g, 0:1, :] * mine
        sums[8 * g : 8 * g + 1, :] = jnp.sum(mine * zf[g, pl.ds(HALO, own), :], axis=0, keepdims=True)
        for j in range(1, 7):
            total = total + taps[g, j : j + 1, :] * dms[g, pl.ds(j, own), :]
            sums[8 * g + j : 8 * g + j + 1, :] = jnp.sum(
                mine * zf[g, pl.ds(HALO - j, own), :], axis=0, keepdims=True
            )
        sums[8 * g + 7 : 8 * g + 8, :] = jnp.zeros((1, 128), F32)
        dz[g] = total.astype(BF16)
        dzt[g, pl.ds(pl.multiple_of(ct * 128, 128), 128), :] = total.T

    sumb[...] = sums[...].astype(BF16)

    @pl.when(ct == pl.num_programs(0) - 1)
    def _():
        piece = dzb.shape[1] // 2
        width = 16 * piece // 3
        for b in range(8):
            both = []
            for h in range(2):
                off = h * 8 * piece + (b % 2) * 4 * piece + (b // 2) * piece
                g, low = off // width, off % width
                size = min(piece, width - low)
                both.append(dzt[g, low : low + size, :])
                if size < piece:
                    both.append(dzt[g + 1, 0 : piece - size, :])
            dzb[b] = jnp.concatenate(both, axis=0).astype(BF16)


def token_grads(dz, wt, out, acc):
    g = pl.program_id(0)
    part = jnp.dot(dz[0, :, 0 : wt.shape[0]], wt[...], preferred_element_type=F32)

    @pl.when(g == 0)
    def _():
        acc[...] = part

    @pl.when(g > 0)
    def _():
        acc[...] += part

    @pl.when(g == pl.num_programs(0) - 1)
    def _():
        out[...] = acc[...].astype(BF16)


def weight_term(place, arrived, *refs):
    *tokens, term = refs
    me = place[2]
    core = place[3]
    chunk = term.shape[2]
    slots = (me, lax.bitwise_xor(me, 1), 3 - me, lax.bitwise_xor(3 - me, 1))
    pairs = []
    for half, c in ((0, core), (1, 1 - core)):
        for p in (0, 2):
            left = [arrived[slots[p + i] * 2 + c] for i in range(2)]
            pairs.append((jnp.concatenate(left, axis=1), tokens[4 * half + p : 4 * half + p + 2]))
    for j in range(4):
        total = None
        cols = slice(j * chunk, (j + 1) * chunk)
        for left, (one, two) in pairs:
            right = jnp.concatenate([one[:, cols], two[:, cols]], axis=0)
            part = jnp.dot(left, right, preferred_element_type=F32)
            total = part if total is None else total + part
        term[j] = total.astype(BF16)


def split_rows(got, blocks, turn):
    chans = got.shape[1]
    fblk = blocks.shape[1]
    piece = blocks.shape[2]
    turn[0:chans, :] = (
        got[0].astype(F32) + got[1].astype(F32) + got[2].astype(F32) + got[3].astype(F32)
    )
    turn[chans:, :] = jnp.zeros((turn.shape[0] - chans, turn.shape[1]), F32)
    flipped = turn[...].T
    for q in range(16):
        for h in range(2):
            part = flipped[q * fblk : (q + 1) * fblk, h * piece : (h + 1) * piece]
            blocks[2 * q + h] = part.astype(BF16)


def make_sum(final):
    def add_parts(p0, p1, p2, p3, out):
        total = p0[...].astype(F32) + p1[...].astype(F32) + p2[...].astype(F32) + p3[...].astype(F32)
        out[...] = total.astype(BF16)

    def close_sums(place, amp, p0, p1, p2, p3, grad_taps, grad_res, held):
        total = p0[...].astype(F32) + p1[...].astype(F32) + p2[...].astype(F32) + p3[...].astype(F32)
        total = total * final
        width = grad_taps.shape[1] // 3
        for g in range(3):
            grad_taps[:, g * width : (g + 1) * width] = total[8 * g : 8 * g + 7, 0:width]
        count = grad_res.shape[0]
        index = (place[0] * 4 + place[1]) * 4 + place[2]
        moved = pltpu.roll(total[24:40, :], lax.rem(PADC - index * count, PADC), 1)
        held[...] = jnp.zeros(held.shape, F32)
        held[0:MODES, :] = moved[:, 0:128]
        grad_res[...] = held[...].T[0:count, 0:MODES] * amp[...]

    return close_sums if final else add_parts


def make_close(scale):
    def close_weight(last, out):
        fblk, piece = last.shape[1:]
        for y in range(4):
            total = jnp.zeros((fblk, piece), F32)
            for z in range(4):
                for h in range(2):
                    total = total + last[(z * 4 + y) * 2 + h].astype(F32)
            out[:, y * piece : (y + 1) * piece] = (total * scale).astype(BF16)

    return close_weight


def ring(a, ax, d):
    return lax.ppermute(a, ax, [(i, (i + d) % 4) for i in range(4)])


def params(mb):
    return pltpu.CompilerParams(vmem_limit_bytes=int(mb * 1024 * 1024))


def local(tokens, w_in, conv_taps, residues, rates, cotangent):
    feats = tokens[0]
    cot = cotangent[0]
    own, width = cot.shape
    depth = feats.shape[1]
    chans = 3 * width
    count = 64
    piece = chans // 16
    fblk = depth // count
    xi, zi, yi = lax.axis_index("x"), lax.axis_index("zl"), lax.axis_index("y")
    place = jnp.stack([xi, zi, yi, lax.axis_index("core")]).astype(jnp.int32)
    feats, cot, rates, place = lax.optimization_barrier((feats, cot, rates, place))
    ctx = ("x", "zl", "y")
    scale = 1.0 / math.sqrt(4 * count * own)
    smem = pl.BlockSpec(memory_space=pltpu.SMEM)
    vm = pl.BlockSpec(memory_space=pltpu.VMEM)
    anywhere = pl.BlockSpec(memory_space=pl.ANY)
    head, tail, block, taps, amp_mine = pl.pallas_call(
        prepare,
        in_specs=[anywhere] * 5,
        out_specs=[vm] * 5,
        out_shape=[
            jax.ShapeDtypeStruct((HALO, depth + PADC), BF16),
            jax.ShapeDtypeStruct((HALO, depth), BF16),
            jax.ShapeDtypeStruct((2 * MODES, width // count), F32),
            jax.ShapeDtypeStruct((3, 8, PADC), F32),
            jax.ShapeDtypeStruct(rates.shape, F32),
        ],
        scratch_shapes=[
            pltpu.VMEM((128, 128), F32),
            pltpu.VMEM((PADC, own), F32),
            pltpu.VMEM((width, own), BF16),
            pltpu.VMEM(rates.shape, F32),
            pltpu.VMEM(rates.shape, F32),
            pltpu.VMEM(conv_taps.shape, F32),
            pltpu.SemaphoreType.DMA((6,)),
        ],
        compiler_params=params(56),
        name="prepare",
    )(feats, cot.T, rates, residues, conv_taps)
    tprev = lax.ppermute(tail, ctx, [(i, i + 1) for i in range(count - 1)])
    nexts = lax.ppermute(head, ctx, [(i, i - 1) for i in range(1, count)])
    held, each = block, width // count
    for axis, ax in ((2, "y"), (1, "zl")):
        blocks = [held] + [ring(held, ax, d) for d in (1, 2, 3)]
        each = 4 * each
        held = pl.pallas_call(
            make_join(axis),
            in_specs=[smem] + [vm] * 4,
            out_specs=vm,
            out_shape=jax.ShapeDtypeStruct((2 * MODES, each), F32),
            scratch_shapes=[pltpu.VMEM((2 * MODES, 256), F32)],
            compiler_params=params(4),
            name="join_params",
        )(place, *blocks)
    blocks = [held] + [ring(held, "x", d) for d in (1, 2, 3)]

    kblk = 256
    ext_rows = own + 2 * HALO
    shapes = [(3, ext_rows, PADC), (3, EXT, PADC), (EXT, PADC), (EXT, PADC), (EXT, PADC)]
    zf, mix, cots, us, dls = pl.pallas_call(
        project,
        in_specs=[vm] * 3 + [anywhere] * 3,
        out_specs=[anywhere] * 3 + [vm] * 2,
        out_shape=[jax.ShapeDtypeStruct(s, F32) for s in shapes],
        scratch_shapes=[
            pltpu.VMEM((ext_rows, chans), F32),
            pltpu.VMEM((PADC, own), F32),
            pltpu.VMEM((depth // kblk, chans, kblk), BF16),
            pltpu.VMEM(shapes[0], F32),
            pltpu.VMEM(shapes[1], F32),
            pltpu.VMEM(shapes[2], F32),
            pltpu.VMEM((own, depth), BF16),
            pltpu.VMEM((width, own), BF16),
            pltpu.SemaphoreType.DMA((depth // kblk,)),
            pltpu.SemaphoreType.DMA,
            pltpu.SemaphoreType.DMA((2, PADC // 128)),
            pltpu.SemaphoreType.DMA((2,)),
        ],
        compiler_params=params(51),
        cost_estimate=pl.CostEstimate(flops=1500000000, bytes_accessed=14000000, transcendentals=0),
        name="project",
    )(tprev, nexts, taps, feats, cot.T, w_in.T)

    *blocks, us, dls = lax.optimization_barrier((*blocks, us, dls))
    rate, gain, es, ends, endb = pl.pallas_call(
        end_states,
        in_specs=[smem] + [vm] * 6,
        out_specs=[vm] * 5,
        out_shape=[
            jax.ShapeDtypeStruct((MODES, PADC), F32),
            jax.ShapeDtypeStruct((MODES, PADC), F32),
            jax.ShapeDtypeStruct((2, MODES, 8, PADC), F32),
            jax.ShapeDtypeStruct((2 * MODES, PADC), F32),
            jax.ShapeDtypeStruct((2 * MODES, PADC), BF16),
        ],
        scratch_shapes=[
            pltpu.VMEM((EXT, 128), F32),
            pltpu.VMEM((EXT, 128), F32),
            pltpu.VMEM((2 * MODES, PADC), F32),
        ],
        compiler_params=params(16),
        cost_estimate=pl.CostEstimate(flops=20000000, bytes_accessed=3000000, transcendentals=0),
        name="end_states",
    )(place, *blocks, us, dls)

    prefixes = []
    total, sent = ends, endb
    for axis, ax, span in ((2, "y", own), (1, "zl", 4 * own), (0, "x", 16 * own)):
        near = [ring(sent, ax, d) for d in (1, 2, 3)]
        total, sent, prefix = pl.pallas_call(
            make_level(axis, span),
            in_specs=[smem] + [vm] * 5,
            out_specs=[vm] * 3,
            out_shape=[
                jax.ShapeDtypeStruct((2 * MODES, PADC), F32),
                jax.ShapeDtypeStruct((2 * MODES, PADC), BF16),
                jax.ShapeDtypeStruct((2 * MODES, PADC), F32),
            ],
            compiler_params=params(8),
            name="level",
        )(place, total, *near, rate)
        prefixes.append(prefix)
        if ax == "y":
            mine, _ = lax.optimization_barrier((feats, sent))
            pair = lax.ppermute(mine, "y", [(i, i ^ 1) for i in range(4)])
            opposite = lax.ppermute(mine, "y", [(i, 3 - i) for i in range(4)])
        elif ax == "zl":
            pair, opposite, _ = lax.optimization_barrier((pair, opposite, sent))
            far = lax.ppermute(pair, "y", [(i, 3 - i) for i in range(4)])

    def tiles(shape):
        lead = len(shape) - 1
        return pl.BlockSpec(shape, lambda k: (0,) * lead + (k,))

    outt, dz, dzb, sums = pl.pallas_call(
        finish,
        grid=(PADC // 128,),
        in_specs=[
            smem,
            tiles((3, ext_rows, 128)),
            tiles((3, EXT, 128)),
            tiles((2, MODES, 8, 128)),
            tiles((2 * MODES, 128)),
            tiles((2 * MODES, 128)),
            tiles((2 * MODES, 128)),
            tiles((3, 8, 128)),
            tiles((MODES, 128)),
            tiles((MODES, 128)),
            tiles((EXT, 128)),
        ],
        out_specs=[
            pl.BlockSpec((128, own), lambda k: (k, 0)),
            tiles((3, own, 128)),
            pl.BlockSpec((8, 2 * piece, own), lambda k: (0, 0, 0)),
            tiles((40, 128)),
        ],
        out_shape=[
            jax.ShapeDtypeStruct((width, own), BF16),
            jax.ShapeDtypeStruct((3, own, PADC), BF16),
            jax.ShapeDtypeStruct((8, 2 * piece, own), BF16),
            jax.ShapeDtypeStruct((40, PADC), BF16),
        ],
        scratch_shapes=[
            pltpu.VMEM((40, 128), F32),
            pltpu.VMEM((2 * MODES, 128), F32),
            pltpu.VMEM((EXT, 128), F32),
            pltpu.VMEM((EXT, 128), F32),
            pltpu.VMEM((EXT, 128), F32),
            pltpu.VMEM((EXT, 128), F32),
            pltpu.VMEM((3, EXT, 128), F32),
            pltpu.VMEM((3, PADC, own), F32),
        ],
        compiler_params=params(50),
        cost_estimate=pl.CostEstimate(flops=200000000, bytes_accessed=10000000, transcendentals=0),
        name="finish",
    )(place, zf, mix, es, *prefixes, taps, rate, gain, cots)
    output = outt.T
    blocks_of = [mine, pair, opposite, far]
    theirs = [lax.ppermute(a, "core", [(0, 1), (1, 0)]) for a in blocks_of]

    def spread(a, ax):
        return [a] + [ring(a, ax, d) for d in (1, 2, 3)]

    def summed(a, ax):
        return pl.pallas_call(
            make_sum(None),
            in_specs=[vm] * 4,
            out_specs=vm,
            out_shape=jax.ShapeDtypeStruct((40, PADC), BF16),
            compiler_params=params(4),
            name="add_parts",
        )(*spread(a, ax))

    arrived = lax.all_to_all(dzb, ("y", "core"), split_axis=0, concat_axis=0, tiled=True)
    sums = summed(sums, "zl")
    arrived, sums = lax.optimization_barrier((arrived, sums))
    term = pl.pallas_call(
        weight_term,
        in_specs=[smem] + [vm] * 9,
        out_specs=vm,
        out_shape=jax.ShapeDtypeStruct((4, 2 * piece, depth // 4), BF16),
        compiler_params=params(24),
        cost_estimate=pl.CostEstimate(flops=1200000000, bytes_accessed=6000000, transcendentals=0),
        name="weight_term",
    )(place, arrived, *blocks_of, *theirs)
    got = lax.all_to_all(term, "x", 0, 0, tiled=True)
    sums, _ = lax.optimization_barrier((sums, term))
    sums = summed(summed(sums, "y"), ("zh", "core"))
    got, sums = lax.optimization_barrier((got, sums))
    blocks = pl.pallas_call(
        split_rows,
        in_specs=[vm],
        out_specs=vm,
        out_shape=jax.ShapeDtypeStruct((32, fblk, piece), BF16),
        scratch_shapes=[pltpu.VMEM((384, depth // 4), F32)],
        compiler_params=params(12),
        name="split_rows",
    )(got)
    last = lax.all_to_all(blocks, ("zl", "y", "zh"), 0, 0, tiled=True)
    sums, dz, _ = lax.optimization_barrier((sums, dz, blocks))
    parts = spread(sums, "x")
    grad_feats = pl.pallas_call(
        token_grads,
        grid=(3,),
        in_specs=[
            pl.BlockSpec((1, own, PADC), lambda g: (g, 0, 0)),
            pl.BlockSpec((width, depth), lambda g: (g, 0)),
        ],
        out_specs=pl.BlockSpec((own, depth), lambda g: (0, 0)),
        out_shape=jax.ShapeDtypeStruct((own, depth), BF16),
        scratch_shapes=[pltpu.VMEM((own, depth), F32)],
        compiler_params=params(57),
        cost_estimate=pl.CostEstimate(flops=1200000000, bytes_accessed=11000000, transcendentals=0),
        name="token_grads",
    )(dz, w_in.T)
    grad_taps, grad_residues = pl.pallas_call(
        make_sum(scale),
        in_specs=[smem] + [vm] * 5,
        out_specs=[vm] * 2,
        out_shape=[
            jax.ShapeDtypeStruct((7, chans), F32),
            jax.ShapeDtypeStruct(rates.shape, F32),
        ],
        scratch_shapes=[pltpu.VMEM((128, 128), F32)],
        compiler_params=params(4),
        name="close_sums",
    )(place, amp_mine, *parts)
    grad_weight = pl.pallas_call(
        make_close(scale),
        in_specs=[vm],
        out_specs=vm,
        out_shape=jax.ShapeDtypeStruct((fblk, 4 * piece), BF16),
        compiler_params=params(4),
        name="close_weight",
    )(last)
    return (output[None], grad_feats[None], grad_weight, grad_taps, grad_residues)


def solution(mesh):
    fine = Mesh(mesh.devices.reshape(4, 4, 4, 2, 2), ("x", "zl", "y", "zh", "core"))
    ctx = ("x", "zl", "y")
    dp = ("zh", "core")
    in_specs = (P(dp, ctx, None), P(), P(), P(ctx, None), P(ctx, None), P(dp, ctx, None))
    out_specs = (P(dp, ctx, None), P(dp, ctx, None), P(ctx, dp), P(), P(ctx, None))
    return jax.shard_map(local, mesh=fine, in_specs=in_specs, out_specs=out_specs, check_vma=False)
```

```python
import math

import jax
import jax.numpy as jnp
from jax import lax
from jax.experimental import pallas as pl
from jax.experimental.pallas import tpu as pltpu
from jax.sharding import Mesh, PartitionSpec as P

F32 = jnp.float32
BF16 = jnp.bfloat16
HALO = 16
EXT = 136
SEG = 17
PADC = 1024
MODES = 16
NT = (((1,), (1,)), ((), ()))


def rounded(a):
    return a.astype(BF16).astype(F32)


def make_project(g):
    def project(*refs):
        if g == 0:
            tp, nexts, taps, feats, wt, cott, zf, mix, cots, tk, wbuf, sems, turn, cbuf, csem = refs
        else:
            tp, nexts, taps, feats, wt, zf, mix, tk, wbuf, sems = refs
        width = wbuf.shape[0]
        depth = tk.shape[1]
        chunks = ((0, 512), (512, width - 512))
        arrival = pltpu.make_async_copy(feats, tk, sems.at[0])
        arrival.start()
        copies = [
            pltpu.make_async_copy(
                wt.at[pl.ds(g * width + low, size)], wbuf.at[pl.ds(low, size)], sems.at[1 + i]
            )
            for i, (low, size) in enumerate(chunks)
        ]
        for copy in copies:
            copy.start()
        if g == 0:
            other = pltpu.make_async_copy(cott, cbuf, csem)
            other.start()
        zf[:, width:] = jnp.zeros((zf.shape[0], PADC - width), F32)
        arrival.wait()
        rows = jnp.concatenate([tp[...], tk[...], nexts[:, 0:depth]], axis=0)
        for (low, size), copy in zip(chunks, copies):
            copy.wait()
            part = lax.dot_general(rows, wbuf[low : low + size, :], NT, preferred_element_type=F32)
            zf[:, low : low + size] = rounded(part)
        if g == 0:
            other.wait()
            turn[...] = jnp.zeros(turn.shape, F32)
            turn[0:width, :] = cbuf[...].astype(F32)

        def tile(ct, carry):
            lane = pl.multiple_of(ct * 128, 128)
            lanes = pl.ds(lane, 128)
            total = taps[g, 0:1, lanes] * zf[pl.ds(HALO, EXT), lanes]
            for j in range(1, 7):
                total = total + taps[g, j : j + 1, lanes] * zf[pl.ds(HALO - j, EXT), lanes]
            mix[:, lanes] = total
            if g == 0:
                after = nexts[:, pl.ds(pl.multiple_of(depth + lane, 128), 128)].astype(F32)
                cots[:, lanes] = jnp.concatenate([turn[lanes, :].T, after[0 : EXT - 128]], axis=0)
            return carry

        lax.fori_loop(0, PADC // 128, tile, 0)

    return project


def one_minus_exp(x):
    series = jnp.ones_like(x)
    for n in range(13, 1, -1):
        series = 1.0 - series * x * (1.0 / n)
    return jnp.where(x < 0.5, x * series, 1.0 - jnp.exp(-x))


def prepare(
    feats, cott, rates, residues, conv, head, tail, block, taps, amp,
    held, turn, cbuf, rbuf, sbuf, vbuf, sems,
):
    count = rates.shape[0]
    width, own = cott.shape
    depth = feats.shape[1]
    copies = [
        pltpu.make_async_copy(rates, rbuf, sems.at[0]),
        pltpu.make_async_copy(residues, sbuf, sems.at[1]),
        pltpu.make_async_copy(cott, cbuf, sems.at[2]),
        pltpu.make_async_copy(conv, vbuf, sems.at[3]),
        pltpu.make_async_copy(feats.at[pl.ds(0, HALO)], head.at[:, pl.ds(0, depth)], sems.at[4]),
        pltpu.make_async_copy(feats.at[pl.ds(own - HALO, HALO)], tail, sems.at[5]),
    ]
    for copy in copies:
        copy.start()
    held[...] = jnp.zeros(held.shape, F32)
    turn[...] = jnp.zeros(turn.shape, F32)
    taps[...] = jnp.zeros(taps.shape, F32)
    copies[0].wait()
    copies[1].wait()
    size = jnp.sqrt(one_minus_exp(2.0 * rbuf[...]))
    amp[...] = size
    held[0:count, 0:MODES] = rbuf[...]
    held[0:count, MODES : 2 * MODES] = sbuf[...] * size
    block[...] = held[...].T[0 : 2 * MODES, 0:count]
    copies[2].wait()
    turn[0:width, :] = cbuf[...].astype(F32)
    for c in range(PADC // 128):
        part = turn[c * 128 : (c + 1) * 128, :].T[0:HALO]
        head[:, depth + c * 128 : depth + (c + 1) * 128] = part.astype(BF16)
    copies[3].wait()
    for g in range(3):
        taps[g, 0:7, 0:width] = vbuf[:, g * width : (g + 1) * width]
    copies[4].wait()
    copies[5].wait()


def placed(me, refs, held, goal):
    wide = refs[0].shape[1]
    total = None
    for d, ref in enumerate(refs):
        held[...] = jnp.zeros(held.shape, F32)
        held[:, 0:wide] = ref[...]
        part = pltpu.roll(held[...], lax.rem(me + (4 - d), 4) * wide, 1)
        total = part if total is None else total + part
    return total[:, 0:goal]


def join_params(me, r0, r1, r2, r3, out, held):
    out[...] = placed(me[0], (r0, r1, r2, r3), held, out.shape[1])


def end_states(me, r0, r1, r2, r3, mq, mk, mv, cots, rates, gains, es, ends, endb, ut, dt, held):
    joined = placed(me[0], (r0, r1, r2, r3), held, PADC)
    rates[...] = joined[0:MODES]
    gains[...] = joined[MODES : 2 * MODES]
    sub = lax.broadcasted_iota(jnp.int32, (8, 128), 0)
    subf = sub.astype(F32)
    fdepth = jnp.where(sub == 7, 0.0, (EXT - 8 - SEG) - SEG * subf)
    bdepth = jnp.where(sub == 0, 0.0, SEG * subf - 8.0)

    def tile(ct, carry):
        lanes = pl.ds(pl.multiple_of(ct * 128, 128), 128)
        ut[...] = rounded(mk[:, lanes] * mv[:, lanes])
        dt[...] = rounded(cots[:, lanes] * mq[:, lanes])
        rate = rates[:, lanes]
        decay = jnp.exp(-rate)
        for half in range(2):
            ks = range(half * 8, half * 8 + 8)
            al = [jnp.broadcast_to(decay[k : k + 1, :], (8, 128)) for k in ks]
            rl = [jnp.broadcast_to(rate[k : k + 1, :], (8, 128)) for k in ks]
            st = [jnp.zeros((8, 128), F32)] * 8
            snap = st
            for t in range(SEG):
                uv = ut[pl.ds(t, 8, stride=SEG), :]
                st = [a * s + uv for a, s in zip(al, st)]
                if t == 8:
                    snap = st
            for i, k in enumerate(ks):
                es[0, k, :, lanes] = st[i]
                full = jnp.where(sub == 7, snap[i], st[i]) * jnp.exp(-rl[i] * fdepth)
                ends[k : k + 1, lanes] = jnp.sum(full, axis=0, keepdims=True)
            st = [jnp.zeros((8, 128), F32)] * 8
            for t in range(SEG - 1, -1, -1):
                dv = dt[pl.ds(t, 8, stride=SEG), :]
                st = [a * s + dv for a, s in zip(al, st)]
                if t == 8:
                    snap = st
            for i, k in enumerate(ks):
                es[1, k, :, lanes] = st[i]
                full = jnp.where(sub == 0, snap[i], st[i]) * jnp.exp(-rl[i] * bdepth)
                ends[MODES + k : MODES + k + 1, lanes] = jnp.sum(full, axis=0, keepdims=True)
        return carry

    lax.fori_loop(0, PADC // 128, tile, 0)
    endb[...] = ends[...].astype(BF16)


def make_level(span):
    def level(index, own, r1, r2, r3, rates, total, totalb, prefix):
        me = index[0]
        rate = rates[...] * float(span)
        before = jnp.zeros((MODES, PADC), F32)
        after = before
        whole_f = before
        whole_b = before
        for d, ref in enumerate((own, r1, r2, r3)):
            m = lax.rem(me + (4 - d), 4)
            f = ref[0:MODES, :].astype(F32)
            b = ref[MODES : 2 * MODES, :].astype(F32)
            whole_f = whole_f + f * jnp.exp(-rate * (3 - m).astype(F32))
            whole_b = whole_b + b * jnp.exp(-rate * m.astype(F32))
            if d > 0:
                gf = me - 1 - m
                gb = m - me - 1
                wf = jnp.exp(-rate * jnp.maximum(gf, 0).astype(F32))
                wb = jnp.exp(-rate * jnp.maximum(gb, 0).astype(F32))
                before = before + jnp.where(gf >= 0, 1.0, 0.0) * (wf * f)
                after = after + jnp.where(gb >= 0, 1.0, 0.0) * (wb * b)
        prefix[0:MODES, :] = before
        prefix[MODES : 2 * MODES, :] = after
        total[0:MODES, :] = whole_f
        total[MODES : 2 * MODES, :] = whole_b
        totalb[0:MODES, :] = whole_f.astype(BF16)
        totalb[MODES : 2 * MODES, :] = whole_b.astype(BF16)

    return level


def finish(
    zi, yi, zq, zk, zv, mq, mk, mv, es, py, pz, px, taps, rates, reff, cots,
    outt, dz, dzb, sumb, sums, inc, ut, dt, longs, dps, dms, dzt,
):
    own = dz.shape[1]
    rate = rates[...]
    for back in range(2):
        part = pl.ds(back * MODES, MODES)
        near, mid = yi[0], zi[0]
        if back:
            near, mid = 3 - near, 3 - mid
        far = pz[part, :] + jnp.exp(-rate * (4 * own * mid).astype(F32)) * px[part, :]
        inc[part, :] = py[part, :] + jnp.exp(-rate * (own * near).astype(F32)) * far
    sub = lax.broadcasted_iota(jnp.int32, (8, 128), 0)
    ut[...] = rounded(mk[...] * mv[...])
    dt[...] = rounded(cots[...] * mq[...])
    decay = jnp.exp(-rate)
    gain = reff[...]
    for half in range(2):
        ks = range(half * 8, half * 8 + 8)
        al = [jnp.broadcast_to(decay[k : k + 1, :], (8, 128)) for k in ks]
        gl = [jnp.broadcast_to(gain[k : k + 1, :], (8, 128)) for k in ks]
        rl = [jnp.broadcast_to(rate[k : k + 1, :], (8, 128)) for k in ks]
        fwd = []
        bwd = []
        for i, k in enumerate(ks):
            jump = [jnp.exp(-float(SEG * m) * rl[i]) for m in (1, 2, 4)]
            x = jnp.where(sub == 0, inc[k : k + 1, :], pltpu.roll(es[0, k], 1, 0))
            for m, d in zip((1, 2, 4), jump):
                x = x + jnp.where(sub >= m, pltpu.roll(x, m, 0) * d, 0.0)
            fwd.append(x)
            x = jnp.where(
                sub == 7, inc[MODES + k : MODES + k + 1, :], pltpu.roll(es[1, k], 7, 0)
            )
            for m, d in zip((1, 2, 4), jump):
                x = x + jnp.where(sub < 8 - m, pltpu.roll(x, 8 - m, 0) * d, 0.0)
            bwd.append(x)
        gr = [jnp.zeros((8, 128), F32)] * 8
        st = fwd
        for t in range(SEG):
            uv = ut[pl.ds(t, 8, stride=SEG), :]
            dv = dt[pl.ds(t, 8, stride=SEG), :]
            if t >= 9:
                dv = jnp.where(sub < 7, dv, 0.0)
            st = [a * s + uv for a, s in zip(al, st)]
            gr = [q + dv * s for q, s in zip(gr, st)]
            total = sum(g * s for g, s in zip(gl, st))
            if half:
                total = total + longs[pl.ds(t, 8, stride=SEG), :]
            longs[pl.ds(t, 8, stride=SEG), :] = total
        for i, k in enumerate(ks):
            sums[24 + k : 25 + k, :] = jnp.sum(gr[i], axis=0, keepdims=True)
        st = bwd
        for t in range(SEG - 1, -1, -1):
            dv = dt[pl.ds(t, 8, stride=SEG), :]
            st = [a * s + dv for a, s in zip(al, st)]
            total = sum(g * s for g, s in zip(gl, st))
            if half:
                total = total + dps[pl.ds(t, 8, stride=SEG), :]
            dps[pl.ds(t, 8, stride=SEG), :] = total
    long_out = rounded(longs[...])
    dprod = rounded(dps[...])
    outt[...] = (mq[0:own, :] * long_out[0:own]).T.astype(BF16)
    dms[0] = rounded(cots[...] * long_out)
    dms[1] = rounded(dprod * mv[...])
    dms[2] = rounded(dprod * mk[...])
    ct = pl.program_id(0)
    for g, zg in enumerate((zq, zk, zv)):
        mine = dms[g, 0:own, :]
        total = taps[g, 0:1, :] * mine
        sums[8 * g : 8 * g + 1, :] = jnp.sum(mine * zg[pl.ds(HALO, own), :], axis=0, keepdims=True)
        for j in range(1, 7):
            total = total + taps[g, j : j + 1, :] * dms[g, pl.ds(j, own), :]
            sums[8 * g + j : 8 * g + j + 1, :] = jnp.sum(
                mine * zg[pl.ds(HALO - j, own), :], axis=0, keepdims=True
            )
        sums[8 * g + 7 : 8 * g + 8, :] = jnp.zeros((1, 128), F32)
        dz[g] = total.astype(BF16)
        dzt[g, pl.ds(pl.multiple_of(ct * 128, 128), 128), :] = total.T

    sumb[...] = sums[...].astype(BF16)

    @pl.when(ct == pl.num_programs(0) - 1)
    def _():
        piece = dzb.shape[1] // 2
        width = 16 * piece // 3
        for b in range(8):
            both = []
            for h in range(2):
                off = h * 8 * piece + (b % 2) * 4 * piece + (b // 2) * piece
                g, low = off // width, off % width
                size = min(piece, width - low)
                both.append(dzt[g, low : low + size, :])
                if size < piece:
                    both.append(dzt[g + 1, 0 : piece - size, :])
            dzb[b] = jnp.concatenate(both, axis=0).astype(BF16)


def token_grads(dz, wt, out, acc):
    g = pl.program_id(0)
    part = jnp.dot(dz[0, :, 0 : wt.shape[0]], wt[...], preferred_element_type=F32)

    @pl.when(g == 0)
    def _():
        acc[...] = part

    @pl.when(g > 0)
    def _():
        acc[...] += part

    @pl.when(g == pl.num_programs(0) - 1)
    def _():
        out[...] = acc[...].astype(BF16)


def weight_term(yi, ci, arrived, *refs):
    *tokens, term = refs
    me = yi[0]
    core = ci[0]
    chunk = term.shape[2]
    slots = (me, lax.bitwise_xor(me, 1), 3 - me, lax.bitwise_xor(3 - me, 1))
    pairs = []
    for half, c in ((0, core), (1, 1 - core)):
        for p in (0, 2):
            left = [arrived[slots[p + i] * 2 + c] for i in range(2)]
            pairs.append((jnp.concatenate(left, axis=1), tokens[4 * half + p : 4 * half + p + 2]))
    for j in range(4):
        total = None
        cols = slice(j * chunk, (j + 1) * chunk)
        for left, (one, two) in pairs:
            right = jnp.concatenate([one[:, cols], two[:, cols]], axis=0)
            part = jnp.dot(left, right, preferred_element_type=F32)
            total = part if total is None else total + part
        term[j] = total.astype(BF16)


def split_rows(got, blocks, turn):
    chans = got.shape[1]
    fblk = blocks.shape[1]
    piece = blocks.shape[2]
    turn[0:chans, :] = (
        got[0].astype(F32) + got[1].astype(F32) + got[2].astype(F32) + got[3].astype(F32)
    )
    turn[chans:, :] = jnp.zeros((turn.shape[0] - chans, turn.shape[1]), F32)
    flipped = turn[...].T
    for q in range(16):
        for h in range(2):
            part = flipped[q * fblk : (q + 1) * fblk, h * piece : (h + 1) * piece]
            blocks[2 * q + h] = part.astype(BF16)


def added(refs):
    total = refs[0][...].astype(F32)
    for ref in refs[1:]:
        total = total + ref[...].astype(F32)
    return total


def add_parts(*refs):
    refs[-1][...] = added(refs[:-1]).astype(BF16)


def make_close_sums(scale):
    def close_sums(xi, zi, yi, amp, *refs):
        *parts, grad_taps, grad_res, held = refs
        total = added(parts) * scale
        width = grad_taps.shape[1] // 3
        for g in range(3):
            grad_taps[:, g * width : (g + 1) * width] = total[8 * g : 8 * g + 7, 0:width]
        count = grad_res.shape[0]
        index = (xi[0] * 4 + zi[0]) * 4 + yi[0]
        moved = pltpu.roll(total[24:40, :], lax.rem(PADC - index * count, PADC), 1)
        held[...] = jnp.zeros(held.shape, F32)
        held[0:MODES, :] = moved[:, 0:128]
        grad_res[...] = held[...].T[0:count, 0:MODES] * amp[...]

    return close_sums


def make_close(scale):
    def close_weight(last, out):
        fblk, piece = last.shape[1:]
        for y in range(4):
            total = jnp.zeros((fblk, piece), F32)
            for z in range(4):
                for h in range(2):
                    total = total + last[(z * 4 + y) * 2 + h].astype(F32)
            out[:, y * piece : (y + 1) * piece] = (total * scale).astype(BF16)

    return close_weight


def ring(a, ax, d):
    return lax.ppermute(a, ax, [(i, (i + d) % 4) for i in range(4)])


def params(mb):
    return pltpu.CompilerParams(vmem_limit_bytes=int(mb * 1024 * 1024))


def local(tokens, w_in, conv_taps, residues, rates, cotangent):
    feats = tokens[0]
    cot = cotangent[0]
    own, width = cot.shape
    depth = feats.shape[1]
    chans = 3 * width
    count = 64
    piece = chans // 16
    fblk = depth // count
    ctx = ("x", "zl", "y")
    scale = 1.0 / math.sqrt(4 * count * own)
    smem = pl.BlockSpec(memory_space=pltpu.SMEM)
    vm = pl.BlockSpec(memory_space=pltpu.VMEM)
    names = ("x", "zl", "y", "core")
    feats, cot, rates, *where = lax.optimization_barrier(
        (feats, cot, rates, *[lax.axis_index(n) for n in names])
    )
    xi, zi, yi, ci = [w.reshape(1) for w in where]
    anywhere = pl.BlockSpec(memory_space=pl.ANY)
    head, tail, block, taps, amp_mine = pl.pallas_call(
        prepare,
        in_specs=[anywhere] * 5,
        out_specs=[vm] * 5,
        out_shape=[
            jax.ShapeDtypeStruct((HALO, depth + PADC), BF16),
            jax.ShapeDtypeStruct((HALO, depth), BF16),
            jax.ShapeDtypeStruct((2 * MODES, width // count), F32),
            jax.ShapeDtypeStruct((3, 8, PADC), F32),
            jax.ShapeDtypeStruct(rates.shape, F32),
        ],
        scratch_shapes=[
            pltpu.VMEM((128, 128), F32),
            pltpu.VMEM((PADC, own), F32),
            pltpu.VMEM((width, own), BF16),
            pltpu.VMEM(rates.shape, F32),
            pltpu.VMEM(rates.shape, F32),
            pltpu.VMEM(conv_taps.shape, F32),
            pltpu.SemaphoreType.DMA((6,)),
        ],
        compiler_params=params(56),
        name="prepare",
    )(feats, cot.T, rates, residues, conv_taps)
    tprev = lax.ppermute(tail, ctx, [(i, i + 1) for i in range(count - 1)])
    nexts = lax.ppermute(head, ctx, [(i, i - 1) for i in range(1, count)])
    ext_rows = own + 2 * HALO
    project_out = [jax.ShapeDtypeStruct((ext_rows, PADC), F32), jax.ShapeDtypeStruct((EXT, PADC), F32)]
    project_scratch = [
        pltpu.VMEM((own, depth), BF16),
        pltpu.VMEM((width, depth), BF16),
        pltpu.SemaphoreType.DMA((3,)),
    ]
    project_cost = pl.CostEstimate(flops=500000000, bytes_accessed=4000000, transcendentals=0)
    first = [
        pltpu.VMEM((PADC, own), F32),
        pltpu.VMEM((width, own), BF16),
        pltpu.SemaphoreType.DMA,
    ]
    held, each = block, width // count
    projected = []
    for g, (me, ax) in enumerate(((yi, "y"), (zi, "zl"), (xi, "x"))):
        blocks = [held] + [ring(held, ax, d) for d in (1, 2, 3)]
        done = pl.pallas_call(
            make_project(g),
            in_specs=[vm] * 3 + [anywhere] * (3 if g == 0 else 2),
            out_specs=[vm] * (3 if g == 0 else 2),
            out_shape=project_out + project_out[1:] if g == 0 else project_out,
            scratch_shapes=project_scratch + first if g == 0 else project_scratch,
            compiler_params=params((57, 56, 52)[g]),
            cost_estimate=project_cost,
            name="project",
        )(tprev, nexts, taps, feats, w_in.T, *((cot.T,) if g == 0 else ()))
        *blocks, zg, mg = lax.optimization_barrier((*blocks, done[0], done[1]))
        projected.append((zg, mg))
        if g == 0:
            cots = done[2]
        if g == 2:
            break
        each = 4 * each
        held = pl.pallas_call(
            join_params,
            in_specs=[smem] + [vm] * 4,
            out_specs=vm,
            out_shape=jax.ShapeDtypeStruct((2 * MODES, each), F32),
            scratch_shapes=[pltpu.VMEM((2 * MODES, 256), F32)],
            compiler_params=params(4),
            name="join_params",
        )(me, *blocks)
    (zq, mq), (zk, mk), (zv, mv) = projected
    rate, gain, es, ends, endb = pl.pallas_call(
        end_states,
        in_specs=[smem] + [vm] * 8,
        out_specs=[vm] * 5,
        out_shape=[
            jax.ShapeDtypeStruct((MODES, PADC), F32),
            jax.ShapeDtypeStruct((MODES, PADC), F32),
            jax.ShapeDtypeStruct((2, MODES, 8, PADC), F32),
            jax.ShapeDtypeStruct((2 * MODES, PADC), F32),
            jax.ShapeDtypeStruct((2 * MODES, PADC), BF16),
        ],
        scratch_shapes=[
            pltpu.VMEM((EXT, 128), F32),
            pltpu.VMEM((EXT, 128), F32),
            pltpu.VMEM((2 * MODES, PADC), F32),
        ],
        compiler_params=params(16),
        cost_estimate=pl.CostEstimate(flops=20000000, bytes_accessed=3000000, transcendentals=0),
        name="end_states",
    )(xi, *blocks, mq, mk, mv, cots)

    prefixes = []
    total, sent = ends, endb
    for me, ax, span in ((yi, "y", own), (zi, "zl", 4 * own), (xi, "x", 16 * own)):
        near = [ring(sent, ax, d) for d in (1, 2, 3)]
        total, sent, prefix = pl.pallas_call(
            make_level(span),
            in_specs=[smem] + [vm] * 5,
            out_specs=[vm] * 3,
            out_shape=[
                jax.ShapeDtypeStruct((2 * MODES, PADC), F32),
                jax.ShapeDtypeStruct((2 * MODES, PADC), BF16),
                jax.ShapeDtypeStruct((2 * MODES, PADC), F32),
            ],
            compiler_params=params(8),
            name="level",
        )(me, total, *near, rate)
        prefixes.append(prefix)
        if ax == "y":
            mine, _ = lax.optimization_barrier((feats, sent))
            pair = lax.ppermute(mine, "y", [(i, i ^ 1) for i in range(4)])
            opposite = lax.ppermute(mine, "y", [(i, 3 - i) for i in range(4)])
        elif ax == "zl":
            pair, opposite, _ = lax.optimization_barrier((pair, opposite, sent))
            far = lax.ppermute(pair, "y", [(i, 3 - i) for i in range(4)])

    def swapped(a):
        return lax.ppermute(a, "core", [(0, 1), (1, 0)])

    theirs = [swapped(a) for a in (mine, pair, opposite)]
    *theirs, prefixes[2] = lax.optimization_barrier((*theirs, prefixes[2]))

    def tiles(shape):
        lead = len(shape) - 1
        return pl.BlockSpec(shape, lambda k: (0,) * lead + (k,))

    outt, dz, dzb, sums = pl.pallas_call(
        finish,
        grid=(PADC // 128,),
        in_specs=[
            smem,
            smem,
            *[tiles((ext_rows, 128))] * 3,
            *[tiles((EXT, 128))] * 3,
            tiles((2, MODES, 8, 128)),
            tiles((2 * MODES, 128)),
            tiles((2 * MODES, 128)),
            tiles((2 * MODES, 128)),
            tiles((3, 8, 128)),
            tiles((MODES, 128)),
            tiles((MODES, 128)),
            tiles((EXT, 128)),
        ],
        out_specs=[
            pl.BlockSpec((128, own), lambda k: (k, 0)),
            tiles((3, own, 128)),
            pl.BlockSpec((8, 2 * piece, own), lambda k: (0, 0, 0)),
            tiles((40, 128)),
        ],
        out_shape=[
            jax.ShapeDtypeStruct((width, own), BF16),
            jax.ShapeDtypeStruct((3, own, PADC), BF16),
            jax.ShapeDtypeStruct((8, 2 * piece, own), BF16),
            jax.ShapeDtypeStruct((40, PADC), BF16),
        ],
        scratch_shapes=[
            pltpu.VMEM((40, 128), F32),
            pltpu.VMEM((2 * MODES, 128), F32),
            pltpu.VMEM((EXT, 128), F32),
            pltpu.VMEM((EXT, 128), F32),
            pltpu.VMEM((EXT, 128), F32),
            pltpu.VMEM((EXT, 128), F32),
            pltpu.VMEM((3, EXT, 128), F32),
            pltpu.VMEM((3, PADC, own), F32),
        ],
        compiler_params=params(24),
        cost_estimate=pl.CostEstimate(flops=200000000, bytes_accessed=10000000, transcendentals=0),
        name="finish",
    )(zi, yi, zq, zk, zv, mq, mk, mv, es, *prefixes, taps, rate, gain, cots)
    output = outt.T
    blocks_of = [mine, pair, opposite, far]
    theirs.append(swapped(far))

    def spread(a, ax):
        return [a] + [ring(a, ax, d) for d in (1, 2, 3)]

    def swap(a, ax):
        return [a, lax.ppermute(a, ax, [(0, 1), (1, 0)])]

    def summed(parts):
        return pl.pallas_call(
            add_parts,
            in_specs=[vm] * len(parts),
            out_specs=vm,
            out_shape=jax.ShapeDtypeStruct((40, PADC), BF16),
            compiler_params=params(4),
            name="add_parts",
        )(*parts)

    arrived = lax.all_to_all(dzb, ("y", "core"), split_axis=0, concat_axis=0, tiled=True)
    sums = summed(spread(summed(swap(sums, "core")), "zl"))
    arrived, sums = lax.optimization_barrier((arrived, sums))
    term = pl.pallas_call(
        weight_term,
        in_specs=[smem] * 2 + [vm] * 9,
        out_specs=vm,
        out_shape=jax.ShapeDtypeStruct((4, 2 * piece, depth // 4), BF16),
        compiler_params=params(24),
        cost_estimate=pl.CostEstimate(flops=1200000000, bytes_accessed=6000000, transcendentals=0),
        name="weight_term",
    )(yi, ci, arrived, *blocks_of, *theirs)
    got = lax.all_to_all(term, "x", 0, 0, tiled=True)
    sums, _ = lax.optimization_barrier((sums, term))
    sums = summed(swap(summed(spread(sums, "y")), "zh"))
    got, sums = lax.optimization_barrier((got, sums))
    blocks = pl.pallas_call(
        split_rows,
        in_specs=[vm],
        out_specs=vm,
        out_shape=jax.ShapeDtypeStruct((32, fblk, piece), BF16),
        scratch_shapes=[pltpu.VMEM((384, depth // 4), F32)],
        compiler_params=params(12),
        name="split_rows",
    )(got)
    last = lax.all_to_all(blocks, ("zl", "y", "zh"), 0, 0, tiled=True)
    sums, dz, _ = lax.optimization_barrier((sums, dz, blocks))
    parts = spread(sums, "x")
    grad_feats = pl.pallas_call(
        token_grads,
        grid=(3,),
        in_specs=[
            pl.BlockSpec((1, own, PADC), lambda g: (g, 0, 0)),
            pl.BlockSpec((width, depth), lambda g: (g, 0)),
        ],
        out_specs=pl.BlockSpec((own, depth), lambda g: (0, 0)),
        out_shape=jax.ShapeDtypeStruct((own, depth), BF16),
        scratch_shapes=[pltpu.VMEM((own, depth), F32)],
        compiler_params=params(24),
        cost_estimate=pl.CostEstimate(flops=1200000000, bytes_accessed=11000000, transcendentals=0),
        name="token_grads",
    )(dz, w_in.T)
    grad_taps, grad_residues = pl.pallas_call(
        make_close_sums(scale),
        in_specs=[smem] * 3 + [vm] * 5,
        out_specs=[vm] * 2,
        out_shape=[
            jax.ShapeDtypeStruct((7, chans), F32),
            jax.ShapeDtypeStruct(rates.shape, F32),
        ],
        scratch_shapes=[pltpu.VMEM((128, 128), F32)],
        compiler_params=params(4),
        name="close_sums",
    )(xi, zi, yi, amp_mine, *parts)
    grad_weight = pl.pallas_call(
        make_close(scale),
        in_specs=[vm],
        out_specs=vm,
        out_shape=jax.ShapeDtypeStruct((fblk, 4 * piece), BF16),
        compiler_params=params(4),
        name="close_weight",
    )(last)
    return (output[None], grad_feats[None], grad_weight, grad_taps, grad_residues)


def solution(mesh):
    fine = Mesh(mesh.devices.reshape(4, 4, 4, 2, 2), ("x", "zl", "y", "zh", "core"))
    ctx = ("x", "zl", "y")
    dp = ("zh", "core")
    in_specs = (P(dp, ctx, None), P(), P(), P(ctx, None), P(ctx, None), P(dp, ctx, None))
    out_specs = (P(dp, ctx, None), P(dp, ctx, None), P(ctx, dp), P(), P(ctx, None))
    return jax.shard_map(local, mesh=fine, in_specs=in_specs, out_specs=out_specs, check_vma=False)
```

```python
import math

import jax
import jax.numpy as jnp
from jax import lax
from jax.experimental import pallas as pl
from jax.experimental.pallas import tpu as pltpu
from jax.sharding import Mesh, PartitionSpec as P

F32 = jnp.float32
BF16 = jnp.bfloat16
HALO = 16
EXT = 136
SEG = 17
PADC = 1024
MODES = 16
NT = (((1,), (1,)), ((), ()))


def rounded(a):
    return a.astype(BF16).astype(F32)


def make_project(g):
    def project(*refs):
        if g < 2:
            *ins, wt, zf, mix, wnext, sem = refs
            coming = pltpu.make_async_copy(wt.at[pl.ds((g + 1) * wnext.shape[0], wnext.shape[0])], wnext, sem)
            coming.start()
        else:
            *ins, zf, mix = refs
        tp, nexts, taps, tk, w = ins
        width, depth = w.shape
        zf[:, width:] = jnp.zeros((zf.shape[0], PADC - width), F32)
        rows = jnp.concatenate([tp[...], tk[...], nexts[:, 0:depth]], axis=0)
        for low, size in ((0, 512), (512, width - 512)):
            part = lax.dot_general(rows, w[low : low + size, :], NT, preferred_element_type=F32)
            zf[:, low : low + size] = rounded(part)

        def tile(ct, carry):
            lanes = pl.ds(pl.multiple_of(ct * 128, 128), 128)
            total = taps[g, 0:1, lanes] * zf[pl.ds(HALO, EXT), lanes]
            for j in range(1, 7):
                total = total + taps[g, j : j + 1, lanes] * zf[pl.ds(HALO - j, EXT), lanes]
            mix[:, lanes] = total
            return carry

        lax.fori_loop(0, PADC // 128, tile, 0)
        if g < 2:
            coming.wait()

    return project


def one_minus_exp(x):
    series = jnp.ones_like(x)
    for n in range(13, 1, -1):
        series = 1.0 - series * x * (1.0 / n)
    return jnp.where(x < 0.5, x * series, 1.0 - jnp.exp(-x))


def prepare(
    feats, cott, rates, residues, conv, wt, head, tail, block, taps, amp, tokens, cots, wfirst,
    held, turn, cbuf, rbuf, sbuf, vbuf, sems,
):
    count = rates.shape[0]
    width, own = cott.shape
    depth = feats.shape[1]
    copies = [
        pltpu.make_async_copy(rates, rbuf, sems.at[0]),
        pltpu.make_async_copy(residues, sbuf, sems.at[1]),
        pltpu.make_async_copy(cott, cbuf, sems.at[2]),
        pltpu.make_async_copy(conv, vbuf, sems.at[3]),
        pltpu.make_async_copy(feats.at[pl.ds(0, HALO)], head.at[:, pl.ds(0, depth)], sems.at[4]),
        pltpu.make_async_copy(feats.at[pl.ds(own - HALO, HALO)], tail, sems.at[5]),
        pltpu.make_async_copy(feats, tokens, sems.at[6]),
        pltpu.make_async_copy(wt.at[pl.ds(0, width)], wfirst, sems.at[7]),
    ]
    for copy in copies:
        copy.start()
    held[...] = jnp.zeros(held.shape, F32)
    turn[...] = jnp.zeros(turn.shape, F32)
    taps[...] = jnp.zeros(taps.shape, F32)
    copies[0].wait()
    copies[1].wait()
    size = jnp.sqrt(one_minus_exp(2.0 * rbuf[...]))
    amp[...] = size
    held[0:count, 0:MODES] = rbuf[...]
    held[0:count, MODES : 2 * MODES] = sbuf[...] * size
    block[...] = held[...].T[0 : 2 * MODES, 0:count]
    copies[2].wait()
    turn[0:width, :] = cbuf[...].astype(F32)
    for c in range(PADC // 128):
        part = turn[c * 128 : (c + 1) * 128, :].T
        cots[:, c * 128 : (c + 1) * 128] = part
        head[:, depth + c * 128 : depth + (c + 1) * 128] = part[0:HALO].astype(BF16)
    copies[3].wait()
    for g in range(3):
        taps[g, 0:7, 0:width] = vbuf[:, g * width : (g + 1) * width]
    for copy in copies[4:]:
        copy.wait()


def placed(me, refs, held, goal):
    wide = refs[0].shape[1]
    total = None
    for d, ref in enumerate(refs):
        held[...] = jnp.zeros(held.shape, F32)
        held[:, 0:wide] = ref[...]
        part = pltpu.roll(held[...], lax.rem(me + (4 - d), 4) * wide, 1)
        total = part if total is None else total + part
    return total[:, 0:goal]


def join_params(me, r0, r1, r2, r3, out, held):
    out[...] = placed(me[0], (r0, r1, r2, r3), held, out.shape[1])


def end_states(me, r0, r1, r2, r3, mq, mk, mv, cown, nexts, cots, rates, gains, es, ends, endb, ut, dt, held):
    joined = placed(me[0], (r0, r1, r2, r3), held, PADC)
    rates[...] = joined[0:MODES]
    gains[...] = joined[MODES : 2 * MODES]
    sub = lax.broadcasted_iota(jnp.int32, (8, 128), 0)
    subf = sub.astype(F32)
    fdepth = jnp.where(sub == 7, 0.0, (EXT - 8 - SEG) - SEG * subf)
    bdepth = jnp.where(sub == 0, 0.0, SEG * subf - 8.0)

    def tile(ct, carry):
        lanes = pl.ds(pl.multiple_of(ct * 128, 128), 128)
        ut[...] = rounded(mk[:, lanes] * mv[:, lanes])
        lane = pl.multiple_of(nexts.shape[1] - PADC + ct * 128, 128)
        after = nexts[:, pl.ds(lane, 128)].astype(F32)
        cot = jnp.concatenate([cown[:, lanes], after[0 : EXT - 128]], axis=0)
        cots[:, lanes] = cot
        dt[...] = rounded(cot * mq[:, lanes])
        rate = rates[:, lanes]
        decay = jnp.exp(-rate)
        for half in range(2):
            ks = range(half * 8, half * 8 + 8)
            al = [jnp.broadcast_to(decay[k : k + 1, :], (8, 128)) for k in ks]
            rl = [jnp.broadcast_to(rate[k : k + 1, :], (8, 128)) for k in ks]
            st = [jnp.zeros((8, 128), F32)] * 8
            snap = st
            for t in range(SEG):
                uv = ut[pl.ds(t, 8, stride=SEG), :]
                st = [a * s + uv for a, s in zip(al, st)]
                if t == 8:
                    snap = st
            for i, k in enumerate(ks):
                es[0, k, :, lanes] = st[i]
                full = jnp.where(sub == 7, snap[i], st[i]) * jnp.exp(-rl[i] * fdepth)
                ends[k : k + 1, lanes] = jnp.sum(full, axis=0, keepdims=True)
            st = [jnp.zeros((8, 128), F32)] * 8
            for t in range(SEG - 1, -1, -1):
                dv = dt[pl.ds(t, 8, stride=SEG), :]
                st = [a * s + dv for a, s in zip(al, st)]
                if t == 8:
                    snap = st
            for i, k in enumerate(ks):
                es[1, k, :, lanes] = st[i]
                full = jnp.where(sub == 0, snap[i], st[i]) * jnp.exp(-rl[i] * bdepth)
                ends[MODES + k : MODES + k + 1, lanes] = jnp.sum(full, axis=0, keepdims=True)
        return carry

    lax.fori_loop(0, PADC // 128, tile, 0)
    endb[...] = ends[...].astype(BF16)


def make_level(span):
    def level(index, own, r1, r2, r3, rates, total, totalb, prefix):
        me = index[0]
        rate = rates[...] * float(span)
        before = jnp.zeros((MODES, PADC), F32)
        after = before
        whole_f = before
        whole_b = before
        for d, ref in enumerate((own, r1, r2, r3)):
            m = lax.rem(me + (4 - d), 4)
            f = ref[0:MODES, :].astype(F32)
            b = ref[MODES : 2 * MODES, :].astype(F32)
            whole_f = whole_f + f * jnp.exp(-rate * (3 - m).astype(F32))
            whole_b = whole_b + b * jnp.exp(-rate * m.astype(F32))
            if d > 0:
                gf = me - 1 - m
                gb = m - me - 1
                wf = jnp.exp(-rate * jnp.maximum(gf, 0).astype(F32))
                wb = jnp.exp(-rate * jnp.maximum(gb, 0).astype(F32))
                before = before + jnp.where(gf >= 0, 1.0, 0.0) * (wf * f)
                after = after + jnp.where(gb >= 0, 1.0, 0.0) * (wb * b)
        prefix[0:MODES, :] = before
        prefix[MODES : 2 * MODES, :] = after
        total[0:MODES, :] = whole_f
        total[MODES : 2 * MODES, :] = whole_b
        totalb[0:MODES, :] = whole_f.astype(BF16)
        totalb[MODES : 2 * MODES, :] = whole_b.astype(BF16)

    return level


def finish(
    zi, yi, zq, zk, zv, mq, mk, mv, es, py, pz, px, taps, rates, reff, cots,
    outt, dz, dzb, sumb, sums, inc, ut, dt, longs, dps, dms, dzt,
):
    own = dz.shape[1]
    rate = rates[...]
    for back in range(2):
        part = pl.ds(back * MODES, MODES)
        near, mid = yi[0], zi[0]
        if back:
            near, mid = 3 - near, 3 - mid
        far = pz[part, :] + jnp.exp(-rate * (4 * own * mid).astype(F32)) * px[part, :]
        inc[part, :] = py[part, :] + jnp.exp(-rate * (own * near).astype(F32)) * far
    sub = lax.broadcasted_iota(jnp.int32, (8, 128), 0)
    ut[...] = rounded(mk[...] * mv[...])
    dt[...] = rounded(cots[...] * mq[...])
    decay = jnp.exp(-rate)
    gain = reff[...]
    for half in range(2):
        ks = range(half * 8, half * 8 + 8)
        al = [jnp.broadcast_to(decay[k : k + 1, :], (8, 128)) for k in ks]
        gl = [jnp.broadcast_to(gain[k : k + 1, :], (8, 128)) for k in ks]
        rl = [jnp.broadcast_to(rate[k : k + 1, :], (8, 128)) for k in ks]
        fwd = []
        bwd = []
        for i, k in enumerate(ks):
            jump = [jnp.exp(-float(SEG * m) * rl[i]) for m in (1, 2, 4)]
            x = jnp.where(sub == 0, inc[k : k + 1, :], pltpu.roll(es[0, k], 1, 0))
            for m, d in zip((1, 2, 4), jump):
                x = x + jnp.where(sub >= m, pltpu.roll(x, m, 0) * d, 0.0)
            fwd.append(x)
            x = jnp.where(
                sub == 7, inc[MODES + k : MODES + k + 1, :], pltpu.roll(es[1, k], 7, 0)
            )
            for m, d in zip((1, 2, 4), jump):
                x = x + jnp.where(sub < 8 - m, pltpu.roll(x, 8 - m, 0) * d, 0.0)
            bwd.append(x)
        gr = [jnp.zeros((8, 128), F32)] * 8
        st = fwd
        for t in range(SEG):
            uv = ut[pl.ds(t, 8, stride=SEG), :]
            dv = dt[pl.ds(t, 8, stride=SEG), :]
            if t >= 9:
                dv = jnp.where(sub < 7, dv, 0.0)
            st = [a * s + uv for a, s in zip(al, st)]
            gr = [q + dv * s for q, s in zip(gr, st)]
            total = sum(g * s for g, s in zip(gl, st))
            if half:
                total = total + longs[pl.ds(t, 8, stride=SEG), :]
            longs[pl.ds(t, 8, stride=SEG), :] = total
        for i, k in enumerate(ks):
            sums[24 + k : 25 + k, :] = jnp.sum(gr[i], axis=0, keepdims=True)
        st = bwd
        for t in range(SEG - 1, -1, -1):
            dv = dt[pl.ds(t, 8, stride=SEG), :]
            st = [a * s + dv for a, s in zip(al, st)]
            total = sum(g * s for g, s in zip(gl, st))
            if half:
                total = total + dps[pl.ds(t, 8, stride=SEG), :]
            dps[pl.ds(t, 8, stride=SEG), :] = total
    long_out = rounded(longs[...])
    dprod = rounded(dps[...])
    outt[...] = (mq[0:own, :] * long_out[0:own]).T.astype(BF16)
    dms[0] = rounded(cots[...] * long_out)
    dms[1] = rounded(dprod * mv[...])
    dms[2] = rounded(dprod * mk[...])
    ct = pl.program_id(0)
    for g, zg in enumerate((zq, zk, zv)):
        mine = dms[g, 0:own, :]
        total = taps[g, 0:1, :] * mine
        sums[8 * g : 8 * g + 1, :] = jnp.sum(mine * zg[pl.ds(HALO, own), :], axis=0, keepdims=True)
        for j in range(1, 7):
            total = total + taps[g, j : j + 1, :] * dms[g, pl.ds(j, own), :]
            sums[8 * g + j : 8 * g + j + 1, :] = jnp.sum(
                mine * zg[pl.ds(HALO - j, own), :], axis=0, keepdims=True
            )
        sums[8 * g + 7 : 8 * g + 8, :] = jnp.zeros((1, 128), F32)
        dz[g] = total.astype(BF16)
        dzt[g, pl.ds(pl.multiple_of(ct * 128, 128), 128), :] = total.T

    sumb[...] = sums[...].astype(BF16)

    @pl.when(ct == pl.num_programs(0) - 1)
    def _():
        piece = dzb.shape[1] // 2
        width = 16 * piece // 3
        for b in range(8):
            both = []
            for h in range(2):
                off = h * 8 * piece + (b % 2) * 4 * piece + (b // 2) * piece
                g, low = off // width, off % width
                size = min(piece, width - low)
                both.append(dzt[g, low : low + size, :])
                if size < piece:
                    both.append(dzt[g + 1, 0 : piece - size, :])
            dzb[b] = jnp.concatenate(both, axis=0).astype(BF16)


def token_grads(dz, wt, out, acc):
    g = pl.program_id(0)
    part = jnp.dot(dz[0, :, 0 : wt.shape[0]], wt[...], preferred_element_type=F32)

    @pl.when(g == 0)
    def _():
        acc[...] = part

    @pl.when(g > 0)
    def _():
        acc[...] += part

    @pl.when(g == pl.num_programs(0) - 1)
    def _():
        out[...] = acc[...].astype(BF16)


def weight_term(yi, ci, arrived, *refs):
    *tokens, term = refs
    me = yi[0]
    core = ci[0]
    chunk = term.shape[2]
    slots = (me, lax.bitwise_xor(me, 1), 3 - me, lax.bitwise_xor(3 - me, 1))
    pairs = []
    for half, c in ((0, core), (1, 1 - core)):
        for p in (0, 2):
            left = [arrived[slots[p + i] * 2 + c] for i in range(2)]
            pairs.append((jnp.concatenate(left, axis=1), tokens[4 * half + p : 4 * half + p + 2]))
    for j in range(4):
        total = None
        cols = slice(j * chunk, (j + 1) * chunk)
        for left, (one, two) in pairs:
            right = jnp.concatenate([one[:, cols], two[:, cols]], axis=0)
            part = jnp.dot(left, right, preferred_element_type=F32)
            total = part if total is None else total + part
        term[j] = total.astype(BF16)


def split_rows(got, blocks, turn):
    chans = got.shape[1]
    fblk = blocks.shape[1]
    piece = blocks.shape[2]
    turn[0:chans, :] = (
        got[0].astype(F32) + got[1].astype(F32) + got[2].astype(F32) + got[3].astype(F32)
    )
    turn[chans:, :] = jnp.zeros((turn.shape[0] - chans, turn.shape[1]), F32)
    flipped = turn[...].T
    for q in range(16):
        for h in range(2):
            part = flipped[q * fblk : (q + 1) * fblk, h * piece : (h + 1) * piece]
            blocks[2 * q + h] = part.astype(BF16)


def added(refs):
    total = refs[0][...].astype(F32)
    for ref in refs[1:]:
        total = total + ref[...].astype(F32)
    return total


def add_parts(*refs):
    refs[-1][...] = added(refs[:-1]).astype(BF16)


def make_close_sums(scale):
    def close_sums(xi, zi, yi, amp, *refs):
        *parts, grad_taps, grad_res, held = refs
        total = added(parts) * scale
        width = grad_taps.shape[1] // 3
        for g in range(3):
            grad_taps[:, g * width : (g + 1) * width] = total[8 * g : 8 * g + 7, 0:width]
        count = grad_res.shape[0]
        index = (xi[0] * 4 + zi[0]) * 4 + yi[0]
        moved = pltpu.roll(total[24:40, :], lax.rem(PADC - index * count, PADC), 1)
        held[...] = jnp.zeros(held.shape, F32)
        held[0:MODES, :] = moved[:, 0:128]
        grad_res[...] = held[...].T[0:count, 0:MODES] * amp[...]

    return close_sums


def make_close(scale):
    def close_weight(last, out):
        fblk, piece = last.shape[1:]
        for y in range(4):
            total = jnp.zeros((fblk, piece), F32)
            for z in range(4):
                for h in range(2):
                    total = total + last[(z * 4 + y) * 2 + h].astype(F32)
            out[:, y * piece : (y + 1) * piece] = (total * scale).astype(BF16)

    return close_weight


def ring(a, ax, d):
    return lax.ppermute(a, ax, [(i, (i + d) % 4) for i in range(4)])


def params(mb):
    return pltpu.CompilerParams(vmem_limit_bytes=int(mb * 1024 * 1024))


def local(tokens, w_in, conv_taps, residues, rates, cotangent):
    feats = tokens[0]
    cot = cotangent[0]
    own, width = cot.shape
    depth = feats.shape[1]
    chans = 3 * width
    count = 64
    piece = chans // 16
    fblk = depth // count
    ctx = ("x", "zl", "y")
    scale = 1.0 / math.sqrt(4 * count * own)
    smem = pl.BlockSpec(memory_space=pltpu.SMEM)
    vm = pl.BlockSpec(memory_space=pltpu.VMEM)
    names = ("x", "zl", "y", "core")
    feats, cot, rates, *where = lax.optimization_barrier(
        (feats, cot, rates, *[lax.axis_index(n) for n in names])
    )
    xi, zi, yi, ci = [w.reshape(1) for w in where]
    anywhere = pl.BlockSpec(memory_space=pl.ANY)
    head, tail, block, taps, amp_mine, tk, cown, wg = pl.pallas_call(
        prepare,
        in_specs=[anywhere] * 6,
        out_specs=[vm] * 8,
        out_shape=[
            jax.ShapeDtypeStruct((HALO, depth + PADC), BF16),
            jax.ShapeDtypeStruct((HALO, depth), BF16),
            jax.ShapeDtypeStruct((2 * MODES, width // count), F32),
            jax.ShapeDtypeStruct((3, 8, PADC), F32),
            jax.ShapeDtypeStruct(rates.shape, F32),
            jax.ShapeDtypeStruct((own, depth), BF16),
            jax.ShapeDtypeStruct((own, PADC), F32),
            jax.ShapeDtypeStruct((width, depth), BF16),
        ],
        scratch_shapes=[
            pltpu.VMEM((128, 128), F32),
            pltpu.VMEM((PADC, own), F32),
            pltpu.VMEM((width, own), BF16),
            pltpu.VMEM(rates.shape, F32),
            pltpu.VMEM(rates.shape, F32),
            pltpu.VMEM(conv_taps.shape, F32),
            pltpu.SemaphoreType.DMA((8,)),
        ],
        compiler_params=params(54),
        name="prepare",
    )(feats, cot.T, rates, residues, conv_taps, w_in.T)
    tprev = lax.ppermute(tail, ctx, [(i, i + 1) for i in range(count - 1)])
    nexts = lax.ppermute(head, ctx, [(i, i - 1) for i in range(1, count)])
    ext_rows = own + 2 * HALO
    project_out = [jax.ShapeDtypeStruct((ext_rows, PADC), F32), jax.ShapeDtypeStruct((EXT, PADC), F32)]
    project_cost = pl.CostEstimate(flops=500000000, bytes_accessed=4000000, transcendentals=0)
    held, each = block, width // count
    projected = []
    for g, (me, ax) in enumerate(((yi, "y"), (zi, "zl"), (xi, "x"))):
        blocks = [held] + [ring(held, ax, d) for d in (1, 2, 3)]
        more = g < 2
        done = pl.pallas_call(
            make_project(g),
            in_specs=[vm] * 5 + [anywhere] * more,
            out_specs=[vm] * (2 + more),
            out_shape=project_out + [jax.ShapeDtypeStruct((width, depth), BF16)] * more,
            scratch_shapes=[pltpu.SemaphoreType.DMA] * more,
            compiler_params=params((50, 50, 50)[g]),
            cost_estimate=project_cost,
            name="project",
        )(tprev, nexts, taps, tk, wg, *[w_in.T] * more)
        *blocks, zg, mg = lax.optimization_barrier((*blocks, done[0], done[1]))
        projected.append((zg, mg))
        if g == 2:
            break
        wg = done[2]
        each = 4 * each
        held = pl.pallas_call(
            join_params,
            in_specs=[smem] + [vm] * 4,
            out_specs=vm,
            out_shape=jax.ShapeDtypeStruct((2 * MODES, each), F32),
            scratch_shapes=[pltpu.VMEM((2 * MODES, 256), F32)],
            compiler_params=params(4),
            name="join_params",
        )(me, *blocks)
    (zq, mq), (zk, mk), (zv, mv) = projected
    cots, rate, gain, es, ends, endb = pl.pallas_call(
        end_states,
        in_specs=[smem] + [vm] * 9,
        out_specs=[vm] * 6,
        out_shape=[
            jax.ShapeDtypeStruct((EXT, PADC), F32),
            jax.ShapeDtypeStruct((MODES, PADC), F32),
            jax.ShapeDtypeStruct((MODES, PADC), F32),
            jax.ShapeDtypeStruct((2, MODES, 8, PADC), F32),
            jax.ShapeDtypeStruct((2 * MODES, PADC), F32),
            jax.ShapeDtypeStruct((2 * MODES, PADC), BF16),
        ],
        scratch_shapes=[
            pltpu.VMEM((EXT, 128), F32),
            pltpu.VMEM((EXT, 128), F32),
            pltpu.VMEM((2 * MODES, PADC), F32),
        ],
        compiler_params=params(16),
        cost_estimate=pl.CostEstimate(flops=20000000, bytes_accessed=3000000, transcendentals=0),
        name="end_states",
    )(xi, *blocks, mq, mk, mv, cown, nexts)

    prefixes = []
    total, sent = ends, endb
    for me, ax, span in ((yi, "y", own), (zi, "zl", 4 * own), (xi, "x", 16 * own)):
        near = [ring(sent, ax, d) for d in (1, 2, 3)]
        total, sent, prefix = pl.pallas_call(
            make_level(span),
            in_specs=[smem] + [vm] * 5,
            out_specs=[vm] * 3,
            out_shape=[
                jax.ShapeDtypeStruct((2 * MODES, PADC), F32),
                jax.ShapeDtypeStruct((2 * MODES, PADC), BF16),
                jax.ShapeDtypeStruct((2 * MODES, PADC), F32),
            ],
            compiler_params=params(8),
            name="level",
        )(me, total, *near, rate)
        prefixes.append(prefix)
        if ax == "zl":
            mine, _ = lax.optimization_barrier((feats, sent))
            pair = lax.ppermute(mine, "y", [(i, i ^ 1) for i in range(4)])
            opposite = lax.ppermute(mine, "y", [(i, 3 - i) for i in range(4)])
    pair, opposite, prefixes[2] = lax.optimization_barrier((pair, opposite, prefixes[2]))
    far = lax.ppermute(pair, "y", [(i, 3 - i) for i in range(4)])

    def swapped(a):
        return lax.ppermute(a, "core", [(0, 1), (1, 0)])

    def tiles(shape):
        lead = len(shape) - 1
        return pl.BlockSpec(shape, lambda k: (0,) * lead + (k,))

    outt, dz, dzb, sums = pl.pallas_call(
        finish,
        grid=(PADC // 128,),
        in_specs=[
            smem,
            smem,
            *[tiles((ext_rows, 128))] * 3,
            *[tiles((EXT, 128))] * 3,
            tiles((2, MODES, 8, 128)),
            tiles((2 * MODES, 128)),
            tiles((2 * MODES, 128)),
            tiles((2 * MODES, 128)),
            tiles((3, 8, 128)),
            tiles((MODES, 128)),
            tiles((MODES, 128)),
            tiles((EXT, 128)),
        ],
        out_specs=[
            pl.BlockSpec((128, own), lambda k: (k, 0)),
            tiles((3, own, 128)),
            pl.BlockSpec((8, 2 * piece, own), lambda k: (0, 0, 0)),
            tiles((40, 128)),
        ],
        out_shape=[
            jax.ShapeDtypeStruct((width, own), BF16),
            jax.ShapeDtypeStruct((3, own, PADC), BF16),
            jax.ShapeDtypeStruct((8, 2 * piece, own), BF16),
            jax.ShapeDtypeStruct((40, PADC), BF16),
        ],
        scratch_shapes=[
            pltpu.VMEM((40, 128), F32),
            pltpu.VMEM((2 * MODES, 128), F32),
            pltpu.VMEM((EXT, 128), F32),
            pltpu.VMEM((EXT, 128), F32),
            pltpu.VMEM((EXT, 128), F32),
            pltpu.VMEM((EXT, 128), F32),
            pltpu.VMEM((3, EXT, 128), F32),
            pltpu.VMEM((3, PADC, own), F32),
        ],
        compiler_params=params(24),
        cost_estimate=pl.CostEstimate(flops=200000000, bytes_accessed=10000000, transcendentals=0),
        name="finish",
    )(zi, yi, zq, zk, zv, mq, mk, mv, es, *prefixes, taps, rate, gain, cots)
    output = outt.T
    blocks_of = [mine, pair, opposite, far]
    mine, pair, opposite, _ = lax.optimization_barrier((mine, pair, opposite, sums))
    blocks_of = [mine, pair, opposite, far]
    theirs = [swapped(a) for a in blocks_of]

    def spread(a, ax):
        return [a] + [ring(a, ax, d) for d in (1, 2, 3)]

    def swap(a, ax):
        return [a, lax.ppermute(a, ax, [(0, 1), (1, 0)])]

    def summed(parts):
        return pl.pallas_call(
            add_parts,
            in_specs=[vm] * len(parts),
            out_specs=vm,
            out_shape=jax.ShapeDtypeStruct((40, PADC), BF16),
            compiler_params=params(4),
            name="add_parts",
        )(*parts)

    arrived = lax.all_to_all(dzb, ("y", "core"), split_axis=0, concat_axis=0, tiled=True)
    sums = summed(swap(sums, "core"))
    *theirs, sums = lax.optimization_barrier((*theirs, sums))
    parts = spread(sums, "zl")
    grad_feats = pl.pallas_call(
        token_grads,
        grid=(3,),
        in_specs=[
            pl.BlockSpec((1, own, PADC), lambda g: (g, 0, 0)),
            pl.BlockSpec((width, depth), lambda g: (g, 0)),
        ],
        out_specs=pl.BlockSpec((own, depth), lambda g: (0, 0)),
        out_shape=jax.ShapeDtypeStruct((own, depth), BF16),
        scratch_shapes=[pltpu.VMEM((own, depth), F32)],
        compiler_params=params(57),
        cost_estimate=pl.CostEstimate(flops=1200000000, bytes_accessed=11000000, transcendentals=0),
        name="token_grads",
    )(dz, w_in.T)
    *parts, grad_feats = lax.optimization_barrier((*parts, grad_feats))
    sums = summed(parts)
    arrived, sums = lax.optimization_barrier((arrived, sums))
    term = pl.pallas_call(
        weight_term,
        in_specs=[smem] * 2 + [vm] * 9,
        out_specs=vm,
        out_shape=jax.ShapeDtypeStruct((4, 2 * piece, depth // 4), BF16),
        compiler_params=params(24),
        cost_estimate=pl.CostEstimate(flops=1200000000, bytes_accessed=6000000, transcendentals=0),
        name="weight_term",
    )(yi, ci, arrived, *blocks_of, *theirs)
    got = lax.all_to_all(term, "x", 0, 0, tiled=True)
    sums, _ = lax.optimization_barrier((sums, term))
    sums = summed(swap(summed(spread(sums, "y")), "zh"))
    got, sums = lax.optimization_barrier((got, sums))
    blocks = pl.pallas_call(
        split_rows,
        in_specs=[vm],
        out_specs=vm,
        out_shape=jax.ShapeDtypeStruct((32, fblk, piece), BF16),
        scratch_shapes=[pltpu.VMEM((384, depth // 4), F32)],
        compiler_params=params(12),
        name="split_rows",
    )(got)
    last = lax.all_to_all(blocks, ("zl", "y", "zh"), 0, 0, tiled=True)
    sums, _ = lax.optimization_barrier((sums, blocks))
    parts = spread(sums, "x")
    grad_taps, grad_residues = pl.pallas_call(
        make_close_sums(scale),
        in_specs=[smem] * 3 + [vm] * 5,
        out_specs=[vm] * 2,
        out_shape=[
            jax.ShapeDtypeStruct((7, chans), F32),
            jax.ShapeDtypeStruct(rates.shape, F32),
        ],
        scratch_shapes=[pltpu.VMEM((128, 128), F32)],
        compiler_params=params(4),
        name="close_sums",
    )(xi, zi, yi, amp_mine, *parts)
    grad_weight = pl.pallas_call(
        make_close(scale),
        in_specs=[vm],
        out_specs=vm,
        out_shape=jax.ShapeDtypeStruct((fblk, 4 * piece), BF16),
        compiler_params=params(4),
        name="close_weight",
    )(last)
    return (output[None], grad_feats[None], grad_weight, grad_taps, grad_residues)


def solution(mesh):
    fine = Mesh(mesh.devices.reshape(4, 4, 4, 2, 2), ("x", "zl", "y", "zh", "core"))
    ctx = ("x", "zl", "y")
    dp = ("zh", "core")
    in_specs = (P(dp, ctx, None), P(), P(), P(ctx, None), P(ctx, None), P(dp, ctx, None))
    out_specs = (P(dp, ctx, None), P(dp, ctx, None), P(ctx, dp), P(), P(ctx, None))
    return jax.shard_map(local, mesh=fine, in_specs=in_specs, out_specs=out_specs, check_vma=False)
```

```python
import math

import jax
import jax.numpy as jnp
from jax import lax
from jax.experimental import pallas as pl
from jax.experimental.pallas import tpu as pltpu
from jax.sharding import Mesh, PartitionSpec as P

F32 = jnp.float32
BF16 = jnp.bfloat16
HALO = 16
EXT = 136
SEG = 17
PADC = 1024
MODES = 16
NT = (((1,), (1,)), ((), ()))


def rounded(a):
    return a.astype(BF16).astype(F32)


PARTS = 12


def part_copies(src, base, dst, sems):
    size = dst.shape[0] // PARTS
    return [
        pltpu.make_async_copy(
            src.at[pl.ds(base + i * size, size)], dst.at[pl.ds(i * size, size)], sems.at[i]
        )
        for i in range(PARTS)
    ]


def make_project(g):
    def project(*refs):
        if g < 2:
            *ins, wt, zf, mix, wnext, sems = refs
            coming = part_copies(wt, (g + 1) * wnext.shape[0], wnext, sems)
            for copy in coming:
                copy.start()
        else:
            *ins, zf, mix = refs
        tp, nexts, taps, tk, w = ins
        width, depth = w.shape
        zf[:, width:] = jnp.zeros((zf.shape[0], PADC - width), F32)
        rows = jnp.concatenate([tp[...], tk[...], nexts[:, 0:depth]], axis=0)
        for low, size in ((0, 512), (512, width - 512)):
            part = lax.dot_general(rows, w[low : low + size, :], NT, preferred_element_type=F32)
            zf[:, low : low + size] = rounded(part)

        def tile(ct, carry):
            lanes = pl.ds(pl.multiple_of(ct * 128, 128), 128)
            total = taps[g, 0:1, lanes] * zf[pl.ds(HALO, EXT), lanes]
            for j in range(1, 7):
                total = total + taps[g, j : j + 1, lanes] * zf[pl.ds(HALO - j, EXT), lanes]
            mix[:, lanes] = total
            return carry

        lax.fori_loop(0, PADC // 128, tile, 0)
        if g < 2:
            for copy in coming:
                copy.wait()

    return project


def one_minus_exp(x):
    series = jnp.ones_like(x)
    for n in range(13, 1, -1):
        series = 1.0 - series * x * (1.0 / n)
    return jnp.where(x < 0.5, x * series, 1.0 - jnp.exp(-x))


def prepare(
    feats, cott, rates, residues, conv, wt, head, tail, block, taps, amp, tokens, cots, wfirst,
    held, turn, cbuf, rbuf, sbuf, vbuf, sems, wsems,
):
    count = rates.shape[0]
    width, own = cott.shape
    depth = feats.shape[1]
    copies = [
        pltpu.make_async_copy(rates, rbuf, sems.at[0]),
        pltpu.make_async_copy(residues, sbuf, sems.at[1]),
        pltpu.make_async_copy(cott, cbuf, sems.at[2]),
        pltpu.make_async_copy(conv, vbuf, sems.at[3]),
        pltpu.make_async_copy(feats.at[pl.ds(0, HALO)], head.at[:, pl.ds(0, depth)], sems.at[4]),
        pltpu.make_async_copy(feats.at[pl.ds(own - HALO, HALO)], tail, sems.at[5]),
        pltpu.make_async_copy(feats, tokens, sems.at[6]),
        *part_copies(wt, 0, wfirst, wsems),
    ]
    for copy in copies:
        copy.start()
    held[...] = jnp.zeros(held.shape, F32)
    turn[...] = jnp.zeros(turn.shape, F32)
    taps[...] = jnp.zeros(taps.shape, F32)
    copies[0].wait()
    copies[1].wait()
    size = jnp.sqrt(one_minus_exp(2.0 * rbuf[...]))
    amp[...] = size
    held[0:count, 0:MODES] = rbuf[...]
    held[0:count, MODES : 2 * MODES] = sbuf[...] * size
    block[...] = held[...].T[0 : 2 * MODES, 0:count]
    copies[2].wait()
    turn[0:width, :] = cbuf[...].astype(F32)
    for c in range(PADC // 128):
        part = turn[c * 128 : (c + 1) * 128, :].T
        cots[:, c * 128 : (c + 1) * 128] = part
        head[:, depth + c * 128 : depth + (c + 1) * 128] = part[0:HALO].astype(BF16)
    copies[3].wait()
    for g in range(3):
        taps[g, 0:7, 0:width] = vbuf[:, g * width : (g + 1) * width]
    for copy in copies[4:]:
        copy.wait()


def placed(me, refs, held, goal):
    wide = refs[0].shape[1]
    total = None
    for d, ref in enumerate(refs):
        held[...] = jnp.zeros(held.shape, F32)
        held[:, 0:wide] = ref[...]
        part = pltpu.roll(held[...], lax.rem(me + (4 - d), 4) * wide, 1)
        total = part if total is None else total + part
    return total[:, 0:goal]


def join_params(me, r0, r1, r2, r3, out, held):
    out[...] = placed(me[0], (r0, r1, r2, r3), held, out.shape[1])


def end_states(me, r0, r1, r2, r3, mq, mk, mv, cown, nexts, cots, rates, gains, es, ends, endb, ut, dt, held):
    joined = placed(me[0], (r0, r1, r2, r3), held, PADC)
    rates[...] = joined[0:MODES]
    gains[...] = joined[MODES : 2 * MODES]
    sub = lax.broadcasted_iota(jnp.int32, (8, 128), 0)
    subf = sub.astype(F32)
    fdepth = jnp.where(sub == 7, 0.0, (EXT - 8 - SEG) - SEG * subf)
    bdepth = jnp.where(sub == 0, 0.0, SEG * subf - 8.0)

    def tile(ct, carry):
        lanes = pl.ds(pl.multiple_of(ct * 128, 128), 128)
        ut[...] = rounded(mk[:, lanes] * mv[:, lanes])
        lane = pl.multiple_of(nexts.shape[1] - PADC + ct * 128, 128)
        after = nexts[:, pl.ds(lane, 128)].astype(F32)
        cot = jnp.concatenate([cown[:, lanes], after[0 : EXT - 128]], axis=0)
        cots[:, lanes] = cot
        dt[...] = rounded(cot * mq[:, lanes])
        rate = rates[:, lanes]
        decay = jnp.exp(-rate)
        for half in range(2):
            ks = range(half * 8, half * 8 + 8)
            al = [jnp.broadcast_to(decay[k : k + 1, :], (8, 128)) for k in ks]
            rl = [jnp.broadcast_to(rate[k : k + 1, :], (8, 128)) for k in ks]
            st = [jnp.zeros((8, 128), F32)] * 8
            snap = st
            for t in range(SEG):
                uv = ut[pl.ds(t, 8, stride=SEG), :]
                st = [a * s + uv for a, s in zip(al, st)]
                if t == 8:
                    snap = st
            for i, k in enumerate(ks):
                es[0, k, :, lanes] = st[i]
                full = jnp.where(sub == 7, snap[i], st[i]) * jnp.exp(-rl[i] * fdepth)
                ends[k : k + 1, lanes] = jnp.sum(full, axis=0, keepdims=True)
            st = [jnp.zeros((8, 128), F32)] * 8
            for t in range(SEG - 1, -1, -1):
                dv = dt[pl.ds(t, 8, stride=SEG), :]
                st = [a * s + dv for a, s in zip(al, st)]
                if t == 8:
                    snap = st
            for i, k in enumerate(ks):
                es[1, k, :, lanes] = st[i]
                full = jnp.where(sub == 0, snap[i], st[i]) * jnp.exp(-rl[i] * bdepth)
                ends[MODES + k : MODES + k + 1, lanes] = jnp.sum(full, axis=0, keepdims=True)
        return carry

    lax.fori_loop(0, PADC // 128, tile, 0)
    endb[...] = ends[...].astype(BF16)


def make_level(span):
    def level(index, own, r1, r2, r3, rates, total, totalb, prefix):
        me = index[0]
        rate = rates[...] * float(span)
        before = jnp.zeros((MODES, PADC), F32)
        after = before
        whole_f = before
        whole_b = before
        for d, ref in enumerate((own, r1, r2, r3)):
            m = lax.rem(me + (4 - d), 4)
            f = ref[0:MODES, :].astype(F32)
            b = ref[MODES : 2 * MODES, :].astype(F32)
            whole_f = whole_f + f * jnp.exp(-rate * (3 - m).astype(F32))
            whole_b = whole_b + b * jnp.exp(-rate * m.astype(F32))
            if d > 0:
                gf = me - 1 - m
                gb = m - me - 1
                wf = jnp.exp(-rate * jnp.maximum(gf, 0).astype(F32))
                wb = jnp.exp(-rate * jnp.maximum(gb, 0).astype(F32))
                before = before + jnp.where(gf >= 0, 1.0, 0.0) * (wf * f)
                after = after + jnp.where(gb >= 0, 1.0, 0.0) * (wb * b)
        prefix[0:MODES, :] = before
        prefix[MODES : 2 * MODES, :] = after
        total[0:MODES, :] = whole_f
        total[MODES : 2 * MODES, :] = whole_b
        totalb[0:MODES, :] = whole_f.astype(BF16)
        totalb[MODES : 2 * MODES, :] = whole_b.astype(BF16)

    return level


def finish(
    zi, yi, zq, zk, zv, mq, mk, mv, es, py, pz, px, taps, rates, reff, cots,
    outt, dz, dzb, sumb, sums, inc, ut, dt, longs, dps, dms, dzt,
):
    own = dz.shape[1]
    rate = rates[...]
    for back in range(2):
        part = pl.ds(back * MODES, MODES)
        near, mid = yi[0], zi[0]
        if back:
            near, mid = 3 - near, 3 - mid
        far = pz[part, :] + jnp.exp(-rate * (4 * own * mid).astype(F32)) * px[part, :]
        inc[part, :] = py[part, :] + jnp.exp(-rate * (own * near).astype(F32)) * far
    sub = lax.broadcasted_iota(jnp.int32, (8, 128), 0)
    ut[...] = rounded(mk[...] * mv[...])
    dt[...] = rounded(cots[...] * mq[...])
    decay = jnp.exp(-rate)
    gain = reff[...]
    for half in range(2):
        ks = range(half * 8, half * 8 + 8)
        al = [jnp.broadcast_to(decay[k : k + 1, :], (8, 128)) for k in ks]
        gl = [jnp.broadcast_to(gain[k : k + 1, :], (8, 128)) for k in ks]
        rl = [jnp.broadcast_to(rate[k : k + 1, :], (8, 128)) for k in ks]
        fwd = []
        bwd = []
        for i, k in enumerate(ks):
            jump = [jnp.exp(-float(SEG * m) * rl[i]) for m in (1, 2, 4)]
            x = jnp.where(sub == 0, inc[k : k + 1, :], pltpu.roll(es[0, k], 1, 0))
            for m, d in zip((1, 2, 4), jump):
                x = x + jnp.where(sub >= m, pltpu.roll(x, m, 0) * d, 0.0)
            fwd.append(x)
            x = jnp.where(
                sub == 7, inc[MODES + k : MODES + k + 1, :], pltpu.roll(es[1, k], 7, 0)
            )
            for m, d in zip((1, 2, 4), jump):
                x = x + jnp.where(sub < 8 - m, pltpu.roll(x, 8 - m, 0) * d, 0.0)
            bwd.append(x)
        gr = [jnp.zeros((8, 128), F32)] * 8
        st = fwd
        for t in range(SEG):
            uv = ut[pl.ds(t, 8, stride=SEG), :]
            dv = dt[pl.ds(t, 8, stride=SEG), :]
            if t >= 9:
                dv = jnp.where(sub < 7, dv, 0.0)
            st = [a * s + uv for a, s in zip(al, st)]
            gr = [q + dv * s for q, s in zip(gr, st)]
            total = sum(g * s for g, s in zip(gl, st))
            if half:
                total = total + longs[pl.ds(t, 8, stride=SEG), :]
            longs[pl.ds(t, 8, stride=SEG), :] = total
        for i, k in enumerate(ks):
            sums[24 + k : 25 + k, :] = jnp.sum(gr[i], axis=0, keepdims=True)
        st = bwd
        for t in range(SEG - 1, -1, -1):
            dv = dt[pl.ds(t, 8, stride=SEG), :]
            st = [a * s + dv for a, s in zip(al, st)]
            total = sum(g * s for g, s in zip(gl, st))
            if half:
                total = total + dps[pl.ds(t, 8, stride=SEG), :]
            dps[pl.ds(t, 8, stride=SEG), :] = total
    long_out = rounded(longs[...])
    dprod = rounded(dps[...])
    outt[...] = (mq[0:own, :] * long_out[0:own]).T.astype(BF16)
    dms[0] = rounded(cots[...] * long_out)
    dms[1] = rounded(dprod * mv[...])
    dms[2] = rounded(dprod * mk[...])
    ct = pl.program_id(0)
    for g, zg in enumerate((zq, zk, zv)):
        mine = dms[g, 0:own, :]
        total = taps[g, 0:1, :] * mine
        sums[8 * g : 8 * g + 1, :] = jnp.sum(mine * zg[pl.ds(HALO, own), :], axis=0, keepdims=True)
        for j in range(1, 7):
            total = total + taps[g, j : j + 1, :] * dms[g, pl.ds(j, own), :]
            sums[8 * g + j : 8 * g + j + 1, :] = jnp.sum(
                mine * zg[pl.ds(HALO - j, own), :], axis=0, keepdims=True
            )
        sums[8 * g + 7 : 8 * g + 8, :] = jnp.zeros((1, 128), F32)
        dz[g] = total.astype(BF16)
        dzt[g, pl.ds(pl.multiple_of(ct * 128, 128), 128), :] = total.T

    sumb[...] = sums[...].astype(BF16)

    @pl.when(ct == pl.num_programs(0) - 1)
    def _():
        piece = dzb.shape[1] // 2
        width = 16 * piece // 3
        for b in range(8):
            both = []
            for h in range(2):
                off = h * 8 * piece + (b % 2) * 4 * piece + (b // 2) * piece
                g, low = off // width, off % width
                size = min(piece, width - low)
                both.append(dzt[g, low : low + size, :])
                if size < piece:
                    both.append(dzt[g + 1, 0 : piece - size, :])
            dzb[b] = jnp.concatenate(both, axis=0).astype(BF16)


def token_grads(dz, wt, out, dbuf, wbuf, dsem, sems):
    groups, width, depth = wbuf.shape
    dcopy = pltpu.make_async_copy(dz, dbuf, dsem)
    dcopy.start()
    coming = [part_copies(wt, g * width, wbuf.at[g], sems.at[g]) for g in range(groups)]
    for copies in coming:
        for copy in copies:
            copy.start()
    dcopy.wait()
    total = None
    for g in range(groups):
        for copy in coming[g]:
            copy.wait()
        part = jnp.dot(dbuf[g, :, 0:width], wbuf[g], preferred_element_type=F32)
        total = part if total is None else total + part
    out[...] = total.astype(BF16)


def weight_term(yi, ci, arrived, *refs):
    *tokens, term = refs
    me = yi[0]
    core = ci[0]
    chunk = term.shape[2]
    slots = (me, lax.bitwise_xor(me, 1), 3 - me, lax.bitwise_xor(3 - me, 1))
    pairs = []
    for half, c in ((0, core), (1, 1 - core)):
        for p in (0, 2):
            left = [arrived[slots[p + i] * 2 + c] for i in range(2)]
            pairs.append((jnp.concatenate(left, axis=1), tokens[4 * half + p : 4 * half + p + 2]))
    for j in range(4):
        total = None
        cols = slice(j * chunk, (j + 1) * chunk)
        for left, (one, two) in pairs:
            right = jnp.concatenate([one[:, cols], two[:, cols]], axis=0)
            part = jnp.dot(left, right, preferred_element_type=F32)
            total = part if total is None else total + part
        term[j] = total.astype(BF16)


def split_rows(got, blocks, turn):
    chans = got.shape[1]
    fblk = blocks.shape[1]
    piece = blocks.shape[2]
    turn[0:chans, :] = (
        got[0].astype(F32) + got[1].astype(F32) + got[2].astype(F32) + got[3].astype(F32)
    )
    turn[chans:, :] = jnp.zeros((turn.shape[0] - chans, turn.shape[1]), F32)
    flipped = turn[...].T
    for q in range(16):
        for h in range(2):
            part = flipped[q * fblk : (q + 1) * fblk, h * piece : (h + 1) * piece]
            blocks[2 * q + h] = part.astype(BF16)


def added(refs):
    total = refs[0][...].astype(F32)
    for ref in refs[1:]:
        total = total + ref[...].astype(F32)
    return total


def add_parts(*refs):
    refs[-1][...] = added(refs[:-1]).astype(BF16)


def make_close_sums(scale):
    def close_sums(xi, zi, yi, amp, *refs):
        *parts, grad_taps, grad_res, held = refs
        total = added(parts) * scale
        width = grad_taps.shape[1] // 3
        for g in range(3):
            grad_taps[:, g * width : (g + 1) * width] = total[8 * g : 8 * g + 7, 0:width]
        count = grad_res.shape[0]
        index = (xi[0] * 4 + zi[0]) * 4 + yi[0]
        moved = pltpu.roll(total[24:40, :], lax.rem(PADC - index * count, PADC), 1)
        held[...] = jnp.zeros(held.shape, F32)
        held[0:MODES, :] = moved[:, 0:128]
        grad_res[...] = held[...].T[0:count, 0:MODES] * amp[...]

    return close_sums


def make_close(scale):
    def close_weight(last, out):
        fblk, piece = last.shape[1:]
        for y in range(4):
            total = jnp.zeros((fblk, piece), F32)
            for z in range(4):
                for h in range(2):
                    total = total + last[(z * 4 + y) * 2 + h].astype(F32)
            out[:, y * piece : (y + 1) * piece] = (total * scale).astype(BF16)

    return close_weight


def ring(a, ax, d):
    return lax.ppermute(a, ax, [(i, (i + d) % 4) for i in range(4)])


def params(mb):
    return pltpu.CompilerParams(vmem_limit_bytes=int(mb * 1024 * 1024))


def local(tokens, w_in, conv_taps, residues, rates, cotangent):
    feats = tokens[0]
    cot = cotangent[0]
    own, width = cot.shape
    depth = feats.shape[1]
    chans = 3 * width
    count = 64
    piece = chans // 16
    fblk = depth // count
    ctx = ("x", "zl", "y")
    scale = 1.0 / math.sqrt(4 * count * own)
    smem = pl.BlockSpec(memory_space=pltpu.SMEM)
    vm = pl.BlockSpec(memory_space=pltpu.VMEM)
    free = pl.BlockSpec()
    names = ("x", "zl", "y", "core")
    feats, cot, rates, *where = lax.optimization_barrier(
        (feats, cot, rates, *[lax.axis_index(n) for n in names])
    )
    xi, zi, yi, ci = [w.reshape(1) for w in where]
    anywhere = pl.BlockSpec(memory_space=pl.ANY)
    head, tail, block, taps, amp_mine, tk, cown, wg = pl.pallas_call(
        prepare,
        in_specs=[anywhere] * 6,
        out_specs=[vm] * 8,
        out_shape=[
            jax.ShapeDtypeStruct((HALO, depth + PADC), BF16),
            jax.ShapeDtypeStruct((HALO, depth), BF16),
            jax.ShapeDtypeStruct((2 * MODES, width // count), F32),
            jax.ShapeDtypeStruct((3, 8, PADC), F32),
            jax.ShapeDtypeStruct(rates.shape, F32),
            jax.ShapeDtypeStruct((own, depth), BF16),
            jax.ShapeDtypeStruct((own, PADC), F32),
            jax.ShapeDtypeStruct((width, depth), BF16),
        ],
        scratch_shapes=[
            pltpu.VMEM((128, 128), F32),
            pltpu.VMEM((PADC, own), F32),
            pltpu.VMEM((width, own), BF16),
            pltpu.VMEM(rates.shape, F32),
            pltpu.VMEM(rates.shape, F32),
            pltpu.VMEM(conv_taps.shape, F32),
            pltpu.SemaphoreType.DMA((7,)),
            pltpu.SemaphoreType.DMA((PARTS,)),
        ],
        compiler_params=params(54),
        name="prepare",
    )(feats, cot.T, rates, residues, conv_taps, w_in.T)
    tprev = lax.ppermute(tail, ctx, [(i, i + 1) for i in range(count - 1)])
    nexts = lax.ppermute(head, ctx, [(i, i - 1) for i in range(1, count)])
    ext_rows = own + 2 * HALO
    project_out = [jax.ShapeDtypeStruct((ext_rows, PADC), F32), jax.ShapeDtypeStruct((EXT, PADC), F32)]
    project_cost = pl.CostEstimate(flops=500000000, bytes_accessed=4000000, transcendentals=0)
    held, each = block, width // count
    projected = []
    for g, (me, ax) in enumerate(((yi, "y"), (zi, "zl"), (xi, "x"))):
        blocks = [held] + [ring(held, ax, d) for d in (1, 2, 3)]
        more = g < 2
        done = pl.pallas_call(
            make_project(g),
            in_specs=[vm] * 5 + [anywhere] * more,
            out_specs=[vm] * (2 + more),
            out_shape=project_out + [jax.ShapeDtypeStruct((width, depth), BF16)] * more,
            scratch_shapes=[pltpu.SemaphoreType.DMA((PARTS,))] * more,
            compiler_params=params((50, 50, 50)[g]),
            cost_estimate=project_cost,
            name="project",
        )(tprev, nexts, taps, tk, wg, *[w_in.T] * more)
        *blocks, zg, mg = lax.optimization_barrier((*blocks, done[0], done[1]))
        projected.append((zg, mg))
        if g == 2:
            break
        wg = done[2]
        each = 4 * each
        held = pl.pallas_call(
            join_params,
            in_specs=[smem] + [vm] * 4,
            out_specs=vm,
            out_shape=jax.ShapeDtypeStruct((2 * MODES, each), F32),
            scratch_shapes=[pltpu.VMEM((2 * MODES, 256), F32)],
            compiler_params=params(4),
            name="join_params",
        )(me, *blocks)
    (zq, mq), (zk, mk), (zv, mv) = projected
    cots, rate, gain, es, ends, endb = pl.pallas_call(
        end_states,
        in_specs=[smem] + [vm] * 9,
        out_specs=[vm] * 6,
        out_shape=[
            jax.ShapeDtypeStruct((EXT, PADC), F32),
            jax.ShapeDtypeStruct((MODES, PADC), F32),
            jax.ShapeDtypeStruct((MODES, PADC), F32),
            jax.ShapeDtypeStruct((2, MODES, 8, PADC), F32),
            jax.ShapeDtypeStruct((2 * MODES, PADC), F32),
            jax.ShapeDtypeStruct((2 * MODES, PADC), BF16),
        ],
        scratch_shapes=[
            pltpu.VMEM((EXT, 128), F32),
            pltpu.VMEM((EXT, 128), F32),
            pltpu.VMEM((2 * MODES, PADC), F32),
        ],
        compiler_params=params(16),
        cost_estimate=pl.CostEstimate(flops=20000000, bytes_accessed=3000000, transcendentals=0),
        name="end_states",
    )(xi, *blocks, mq, mk, mv, cown, nexts)

    prefixes = []
    total, sent = ends, endb
    for me, ax, span in ((yi, "y", own), (zi, "zl", 4 * own), (xi, "x", 16 * own)):
        near = [ring(sent, ax, d) for d in (1, 2, 3)]
        total, sent, prefix = pl.pallas_call(
            make_level(span),
            in_specs=[smem] + [vm] * 5,
            out_specs=[vm] * 3,
            out_shape=[
                jax.ShapeDtypeStruct((2 * MODES, PADC), F32),
                jax.ShapeDtypeStruct((2 * MODES, PADC), BF16),
                jax.ShapeDtypeStruct((2 * MODES, PADC), F32),
            ],
            compiler_params=params(8),
            name="level",
        )(me, total, *near, rate)
        prefixes.append(prefix)
        if ax == "zl":
            mine, _ = lax.optimization_barrier((feats, sent))
            pair = lax.ppermute(mine, "y", [(i, i ^ 1) for i in range(4)])
            opposite = lax.ppermute(mine, "y", [(i, 3 - i) for i in range(4)])
    pair, opposite, prefixes[2] = lax.optimization_barrier((pair, opposite, prefixes[2]))
    far = lax.ppermute(pair, "y", [(i, 3 - i) for i in range(4)])

    def swapped(a):
        return lax.ppermute(a, "core", [(0, 1), (1, 0)])

    def tiles(shape):
        lead = len(shape) - 1
        return pl.BlockSpec(shape, lambda k: (0,) * lead + (k,))

    outt, dz, dzb, sums = pl.pallas_call(
        finish,
        grid=(PADC // 128,),
        in_specs=[
            smem,
            smem,
            *[tiles((ext_rows, 128))] * 3,
            *[tiles((EXT, 128))] * 3,
            tiles((2, MODES, 8, 128)),
            tiles((2 * MODES, 128)),
            tiles((2 * MODES, 128)),
            tiles((2 * MODES, 128)),
            tiles((3, 8, 128)),
            tiles((MODES, 128)),
            tiles((MODES, 128)),
            tiles((EXT, 128)),
        ],
        out_specs=[
            pl.BlockSpec((128, own), lambda k: (k, 0)),
            tiles((3, own, 128)),
            pl.BlockSpec((8, 2 * piece, own), lambda k: (0, 0, 0)),
            tiles((40, 128)),
        ],
        out_shape=[
            jax.ShapeDtypeStruct((width, own), BF16),
            jax.ShapeDtypeStruct((3, own, PADC), BF16),
            jax.ShapeDtypeStruct((8, 2 * piece, own), BF16),
            jax.ShapeDtypeStruct((40, PADC), BF16),
        ],
        scratch_shapes=[
            pltpu.VMEM((40, 128), F32),
            pltpu.VMEM((2 * MODES, 128), F32),
            pltpu.VMEM((EXT, 128), F32),
            pltpu.VMEM((EXT, 128), F32),
            pltpu.VMEM((EXT, 128), F32),
            pltpu.VMEM((EXT, 128), F32),
            pltpu.VMEM((3, EXT, 128), F32),
            pltpu.VMEM((3, PADC, own), F32),
        ],
        compiler_params=params(24),
        cost_estimate=pl.CostEstimate(flops=200000000, bytes_accessed=10000000, transcendentals=0),
        name="finish",
    )(zi, yi, zq, zk, zv, mq, mk, mv, es, *prefixes, taps, rate, gain, cots)
    output = outt.T
    blocks_of = [mine, pair, opposite, far]
    mine, pair, opposite, _ = lax.optimization_barrier((mine, pair, opposite, sums))
    blocks_of = [mine, pair, opposite, far]
    theirs = [swapped(a) for a in blocks_of]

    def spread(a, ax):
        return [a] + [ring(a, ax, d) for d in (1, 2, 3)]

    def swap(a, ax):
        return [a, lax.ppermute(a, ax, [(0, 1), (1, 0)])]

    def summed(parts):
        return pl.pallas_call(
            add_parts,
            in_specs=[free] * len(parts),
            out_specs=free,
            out_shape=jax.ShapeDtypeStruct((40, PADC), BF16),
            compiler_params=params(4),
            name="add_parts",
        )(*parts)

    arrived = lax.all_to_all(dzb, ("y", "core"), split_axis=0, concat_axis=0, tiled=True)
    sums = summed(swap(sums, "core"))
    *theirs, sums = lax.optimization_barrier((*theirs, sums))
    parts = spread(sums, "zl")
    sums = summed(parts)
    arrived, sums = lax.optimization_barrier((arrived, sums))
    term = pl.pallas_call(
        weight_term,
        in_specs=[smem] * 2 + [vm] + [free] * 8,
        out_specs=vm,
        out_shape=jax.ShapeDtypeStruct((4, 2 * piece, depth // 4), BF16),
        compiler_params=params(24),
        cost_estimate=pl.CostEstimate(flops=1200000000, bytes_accessed=6000000, transcendentals=0),
        name="weight_term",
    )(yi, ci, arrived, *blocks_of, *theirs)
    got = lax.all_to_all(term, "x", 0, 0, tiled=True)
    sums, _ = lax.optimization_barrier((sums, term))
    sums = summed(swap(summed(spread(sums, "y")), "zh"))
    got, sums = lax.optimization_barrier((got, sums))
    blocks = pl.pallas_call(
        split_rows,
        in_specs=[vm],
        out_specs=vm,
        out_shape=jax.ShapeDtypeStruct((32, fblk, piece), BF16),
        scratch_shapes=[pltpu.VMEM((384, depth // 4), F32)],
        compiler_params=params(12),
        name="split_rows",
    )(got)
    last = lax.all_to_all(blocks, ("zl", "y", "zh"), 0, 0, tiled=True)
    sums, _ = lax.optimization_barrier((sums, blocks))
    parts = spread(sums, "x")
    dz, _ = lax.optimization_barrier((dz, blocks))
    grad_feats = pl.pallas_call(
        token_grads,
        in_specs=[anywhere] * 2,
        out_specs=vm,
        out_shape=jax.ShapeDtypeStruct((own, depth), BF16),
        scratch_shapes=[
            pltpu.VMEM((3, own, PADC), BF16),
            pltpu.VMEM((3, width, depth), BF16),
            pltpu.SemaphoreType.DMA,
            pltpu.SemaphoreType.DMA((3, PARTS)),
        ],
        compiler_params=params(57),
        cost_estimate=pl.CostEstimate(flops=1200000000, bytes_accessed=11000000, transcendentals=0),
        name="token_grads",
    )(dz, w_in.T)
    *parts, grad_feats = lax.optimization_barrier((*parts, grad_feats))
    grad_taps, grad_residues = pl.pallas_call(
        make_close_sums(scale),
        in_specs=[smem] * 3 + [free] * 5,
        out_specs=[vm] * 2,
        out_shape=[
            jax.ShapeDtypeStruct((7, chans), F32),
            jax.ShapeDtypeStruct(rates.shape, F32),
        ],
        scratch_shapes=[pltpu.VMEM((128, 128), F32)],
        compiler_params=params(4),
        name="close_sums",
    )(xi, zi, yi, amp_mine, *parts)
    grad_weight = pl.pallas_call(
        make_close(scale),
        in_specs=[vm],
        out_specs=vm,
        out_shape=jax.ShapeDtypeStruct((fblk, 4 * piece), BF16),
        compiler_params=params(4),
        name="close_weight",
    )(last)
    return (output[None], grad_feats[None], grad_weight, grad_taps, grad_residues)


def solution(mesh):
    fine = Mesh(mesh.devices.reshape(4, 4, 4, 2, 2), ("x", "zl", "y", "zh", "core"))
    ctx = ("x", "zl", "y")
    dp = ("zh", "core")
    in_specs = (P(dp, ctx, None), P(), P(), P(ctx, None), P(ctx, None), P(dp, ctx, None))
    out_specs = (P(dp, ctx, None), P(dp, ctx, None), P(ctx, dp), P(), P(ctx, None))
    return jax.shard_map(local, mesh=fine, in_specs=in_specs, out_specs=out_specs, check_vma=False)
```

```python
import math

import jax
import jax.numpy as jnp
from jax import lax
from jax.experimental import pallas as pl
from jax.experimental.pallas import tpu as pltpu
from jax.sharding import Mesh, PartitionSpec as P

F32 = jnp.float32
BF16 = jnp.bfloat16
HALO = 16
EXT = 136
SEG = 17
PADC = 1024
MODES = 16
NT = (((1,), (1,)), ((), ()))


def rounded(a):
    return a.astype(BF16).astype(F32)


KBLK = 256


def make_project(part):
    def project(*refs):
        if part == 0:
            tp, nexts, feats, wt, acc, tk, wbuf, tsem, sems = refs
        else:
            tp, nexts, before, feats, wt, zq, zk, zv, tk, wbuf, tsem, sems, acc = refs
        steps, chans, _ = wbuf.shape
        low = part * steps * KBLK
        arrival = pltpu.make_async_copy(feats.at[:, pl.ds(low, steps * KBLK)], tk, tsem)
        arrival.start()
        copies = [
            pltpu.make_async_copy(wt.at[:, pl.ds(low + k * KBLK, KBLK)], wbuf.at[k], sems.at[k])
            for k in range(steps)
        ]
        for copy in copies:
            copy.start()
        arrival.wait()
        for k in range(steps):
            wide = slice(low + k * KBLK, low + (k + 1) * KBLK)
            rows = jnp.concatenate(
                [tp[:, wide], tk[:, k * KBLK : (k + 1) * KBLK], nexts[:, wide]], axis=0
            )
            copies[k].wait()
            total = lax.dot_general(rows, wbuf[k], NT, preferred_element_type=F32)
            if k > 0:
                total = acc[...] + total
            elif part == 1:
                total = before[...] + total
            if part == 0 or k < steps - 1:
                acc[...] = total
            else:
                width = chans // 3
                for g, z in enumerate((zq, zk, zv)):
                    z[:, 0:width] = rounded(total[:, g * width : (g + 1) * width])
                    z[:, width:] = jnp.zeros((z.shape[0], PADC - width), F32)

    return project


def mix_taps(taps, zq, zk, zv, mq, mk, mv):
    def tile(ct, carry):
        lanes = pl.ds(pl.multiple_of(ct * 128, 128), 128)
        for g, (z, m) in enumerate(((zq, mq), (zk, mk), (zv, mv))):
            total = taps[g, 0:1, lanes] * z[pl.ds(HALO, EXT), lanes]
            for j in range(1, 7):
                total = total + taps[g, j : j + 1, lanes] * z[pl.ds(HALO - j, EXT), lanes]
            m[:, lanes] = total
        return carry

    lax.fori_loop(0, PADC // 128, tile, 0)


def one_minus_exp(x):
    series = jnp.ones_like(x)
    for n in range(13, 1, -1):
        series = 1.0 - series * x * (1.0 / n)
    return jnp.where(x < 0.5, x * series, 1.0 - jnp.exp(-x))


def prepare(
    feats, cott, rates, residues, conv, head, tail, block, taps, amp, cots,
    held, turn, cbuf, rbuf, sbuf, vbuf, sems,
):
    count = rates.shape[0]
    width, own = cott.shape
    depth = feats.shape[1]
    copies = [
        pltpu.make_async_copy(rates, rbuf, sems.at[0]),
        pltpu.make_async_copy(residues, sbuf, sems.at[1]),
        pltpu.make_async_copy(cott, cbuf, sems.at[2]),
        pltpu.make_async_copy(conv, vbuf, sems.at[3]),
        pltpu.make_async_copy(feats.at[pl.ds(0, HALO)], head.at[:, pl.ds(0, depth)], sems.at[4]),
        pltpu.make_async_copy(feats.at[pl.ds(own - HALO, HALO)], tail, sems.at[5]),
    ]
    for copy in copies:
        copy.start()
    held[...] = jnp.zeros(held.shape, F32)
    turn[...] = jnp.zeros(turn.shape, F32)
    taps[...] = jnp.zeros(taps.shape, F32)
    copies[0].wait()
    copies[1].wait()
    size = jnp.sqrt(one_minus_exp(2.0 * rbuf[...]))
    amp[...] = size
    held[0:count, 0:MODES] = rbuf[...]
    held[0:count, MODES : 2 * MODES] = sbuf[...] * size
    block[...] = held[...].T[0 : 2 * MODES, 0:count]
    copies[2].wait()
    turn[0:width, :] = cbuf[...].astype(F32)
    for c in range(PADC // 128):
        part = turn[c * 128 : (c + 1) * 128, :].T
        cots[:, c * 128 : (c + 1) * 128] = part
        head[:, depth + c * 128 : depth + (c + 1) * 128] = part[0:HALO].astype(BF16)
    copies[3].wait()
    for g in range(3):
        taps[g, 0:7, 0:width] = vbuf[:, g * width : (g + 1) * width]
    for copy in copies[4:]:
        copy.wait()


def placed(me, refs, held, goal):
    wide = refs[0].shape[1]
    total = None
    for d, ref in enumerate(refs):
        held[...] = jnp.zeros(held.shape, F32)
        held[:, 0:wide] = ref[...]
        part = pltpu.roll(held[...], lax.rem(me + (4 - d), 4) * wide, 1)
        total = part if total is None else total + part
    return total[:, 0:goal]


def join_params(me, r0, r1, r2, r3, out, held):
    out[...] = placed(me[0], (r0, r1, r2, r3), held, out.shape[1])


def end_states(me, r0, r1, r2, r3, mq, mk, mv, cown, nexts, cots, rates, gains, es, ends, endb, ut, dt, held):
    joined = placed(me[0], (r0, r1, r2, r3), held, PADC)
    rates[...] = joined[0:MODES]
    gains[...] = joined[MODES : 2 * MODES]
    sub = lax.broadcasted_iota(jnp.int32, (8, 128), 0)
    subf = sub.astype(F32)
    fdepth = jnp.where(sub == 7, 0.0, (EXT - 8 - SEG) - SEG * subf)
    bdepth = jnp.where(sub == 0, 0.0, SEG * subf - 8.0)

    def tile(ct, carry):
        lanes = pl.ds(pl.multiple_of(ct * 128, 128), 128)
        ut[...] = rounded(mk[:, lanes] * mv[:, lanes])
        lane = pl.multiple_of(nexts.shape[1] - PADC + ct * 128, 128)
        after = nexts[:, pl.ds(lane, 128)].astype(F32)
        cot = jnp.concatenate([cown[:, lanes], after[0 : EXT - 128]], axis=0)
        cots[:, lanes] = cot
        dt[...] = rounded(cot * mq[:, lanes])
        rate = rates[:, lanes]
        decay = jnp.exp(-rate)
        for half in range(2):
            ks = range(half * 8, half * 8 + 8)
            al = [jnp.broadcast_to(decay[k : k + 1, :], (8, 128)) for k in ks]
            rl = [jnp.broadcast_to(rate[k : k + 1, :], (8, 128)) for k in ks]
            st = [jnp.zeros((8, 128), F32)] * 8
            snap = st
            for t in range(SEG):
                uv = ut[pl.ds(t, 8, stride=SEG), :]
                st = [a * s + uv for a, s in zip(al, st)]
                if t == 8:
                    snap = st
            for i, k in enumerate(ks):
                es[0, k, :, lanes] = st[i]
                full = jnp.where(sub == 7, snap[i], st[i]) * jnp.exp(-rl[i] * fdepth)
                ends[k : k + 1, lanes] = jnp.sum(full, axis=0, keepdims=True)
            st = [jnp.zeros((8, 128), F32)] * 8
            for t in range(SEG - 1, -1, -1):
                dv = dt[pl.ds(t, 8, stride=SEG), :]
                st = [a * s + dv for a, s in zip(al, st)]
                if t == 8:
                    snap = st
            for i, k in enumerate(ks):
                es[1, k, :, lanes] = st[i]
                full = jnp.where(sub == 0, snap[i], st[i]) * jnp.exp(-rl[i] * bdepth)
                ends[MODES + k : MODES + k + 1, lanes] = jnp.sum(full, axis=0, keepdims=True)
        return carry

    lax.fori_loop(0, PADC // 128, tile, 0)
    endb[...] = ends[...].astype(BF16)


def make_level(span):
    def level(index, own, r1, r2, r3, rates, total, totalb, prefix):
        me = index[0]
        rate = rates[...] * float(span)
        before = jnp.zeros((MODES, PADC), F32)
        after = before
        whole_f = before
        whole_b = before
        for d, ref in enumerate((own, r1, r2, r3)):
            m = lax.rem(me + (4 - d), 4)
            f = ref[0:MODES, :].astype(F32)
            b = ref[MODES : 2 * MODES, :].astype(F32)
            whole_f = whole_f + f * jnp.exp(-rate * (3 - m).astype(F32))
            whole_b = whole_b + b * jnp.exp(-rate * m.astype(F32))
            if d > 0:
                gf = me - 1 - m
                gb = m - me - 1
                wf = jnp.exp(-rate * jnp.maximum(gf, 0).astype(F32))
                wb = jnp.exp(-rate * jnp.maximum(gb, 0).astype(F32))
                before = before + jnp.where(gf >= 0, 1.0, 0.0) * (wf * f)
                after = after + jnp.where(gb >= 0, 1.0, 0.0) * (wb * b)
        prefix[0:MODES, :] = before
        prefix[MODES : 2 * MODES, :] = after
        total[0:MODES, :] = whole_f
        total[MODES : 2 * MODES, :] = whole_b
        totalb[0:MODES, :] = whole_f.astype(BF16)
        totalb[MODES : 2 * MODES, :] = whole_b.astype(BF16)

    return level


def finish(
    zi, yi, zq, zk, zv, mq, mk, mv, es, py, pz, px, taps, rates, reff, cots,
    outt, dz, dzb, sumb, sums, inc, ut, dt, longs, dps, dms, dzt,
):
    own = dz.shape[1]
    rate = rates[...]
    for back in range(2):
        part = pl.ds(back * MODES, MODES)
        near, mid = yi[0], zi[0]
        if back:
            near, mid = 3 - near, 3 - mid
        far = pz[part, :] + jnp.exp(-rate * (4 * own * mid).astype(F32)) * px[part, :]
        inc[part, :] = py[part, :] + jnp.exp(-rate * (own * near).astype(F32)) * far
    sub = lax.broadcasted_iota(jnp.int32, (8, 128), 0)
    ut[...] = rounded(mk[...] * mv[...])
    dt[...] = rounded(cots[...] * mq[...])
    decay = jnp.exp(-rate)
    gain = reff[...]
    for half in range(2):
        ks = range(half * 8, half * 8 + 8)
        al = [jnp.broadcast_to(decay[k : k + 1, :], (8, 128)) for k in ks]
        gl = [jnp.broadcast_to(gain[k : k + 1, :], (8, 128)) for k in ks]
        rl = [jnp.broadcast_to(rate[k : k + 1, :], (8, 128)) for k in ks]
        fwd = []
        bwd = []
        for i, k in enumerate(ks):
            jump = [jnp.exp(-float(SEG * m) * rl[i]) for m in (1, 2, 4)]
            x = jnp.where(sub == 0, inc[k : k + 1, :], pltpu.roll(es[0, k], 1, 0))
            for m, d in zip((1, 2, 4), jump):
                x = x + jnp.where(sub >= m, pltpu.roll(x, m, 0) * d, 0.0)
            fwd.append(x)
            x = jnp.where(
                sub == 7, inc[MODES + k : MODES + k + 1, :], pltpu.roll(es[1, k], 7, 0)
            )
            for m, d in zip((1, 2, 4), jump):
                x = x + jnp.where(sub < 8 - m, pltpu.roll(x, 8 - m, 0) * d, 0.0)
            bwd.append(x)
        gr = [jnp.zeros((8, 128), F32)] * 8
        st = fwd
        for t in range(SEG):
            uv = ut[pl.ds(t, 8, stride=SEG), :]
            dv = dt[pl.ds(t, 8, stride=SEG), :]
            if t >= 9:
                dv = jnp.where(sub < 7, dv, 0.0)
            st = [a * s + uv for a, s in zip(al, st)]
            gr = [q + dv * s for q, s in zip(gr, st)]
            total = sum(g * s for g, s in zip(gl, st))
            if half:
                total = total + longs[pl.ds(t, 8, stride=SEG), :]
            longs[pl.ds(t, 8, stride=SEG), :] = total
        for i, k in enumerate(ks):
            sums[24 + k : 25 + k, :] = jnp.sum(gr[i], axis=0, keepdims=True)
        st = bwd
        for t in range(SEG - 1, -1, -1):
            dv = dt[pl.ds(t, 8, stride=SEG), :]
            st = [a * s + dv for a, s in zip(al, st)]
            total = sum(g * s for g, s in zip(gl, st))
            if half:
                total = total + dps[pl.ds(t, 8, stride=SEG), :]
            dps[pl.ds(t, 8, stride=SEG), :] = total
    long_out = rounded(longs[...])
    dprod = rounded(dps[...])
    outt[...] = (mq[0:own, :] * long_out[0:own]).T.astype(BF16)
    dms[0] = rounded(cots[...] * long_out)
    dms[1] = rounded(dprod * mv[...])
    dms[2] = rounded(dprod * mk[...])
    ct = pl.program_id(0)
    for g, zg in enumerate((zq, zk, zv)):
        mine = dms[g, 0:own, :]
        total = taps[g, 0:1, :] * mine
        sums[8 * g : 8 * g + 1, :] = jnp.sum(mine * zg[pl.ds(HALO, own), :], axis=0, keepdims=True)
        for j in range(1, 7):
            total = total + taps[g, j : j + 1, :] * dms[g, pl.ds(j, own), :]
            sums[8 * g + j : 8 * g + j + 1, :] = jnp.sum(
                mine * zg[pl.ds(HALO - j, own), :], axis=0, keepdims=True
            )
        sums[8 * g + 7 : 8 * g + 8, :] = jnp.zeros((1, 128), F32)
        dz[g] = total.astype(BF16)
        dzt[g, pl.ds(pl.multiple_of(ct * 128, 128), 128), :] = total.T

    sumb[...] = sums[...].astype(BF16)

    @pl.when(ct == pl.num_programs(0) - 1)
    def _():
        piece = dzb.shape[1] // 2
        width = 16 * piece // 3
        for b in range(8):
            both = []
            for h in range(2):
                off = h * 8 * piece + (b % 2) * 4 * piece + (b // 2) * piece
                g, low = off // width, off % width
                size = min(piece, width - low)
                both.append(dzt[g, low : low + size, :])
                if size < piece:
                    both.append(dzt[g + 1, 0 : piece - size, :])
            dzb[b] = jnp.concatenate(both, axis=0).astype(BF16)


def token_grads(dz, wt, out, acc):
    g = pl.program_id(0)
    part = jnp.dot(dz[0, :, 0 : wt.shape[0]], wt[...], preferred_element_type=F32)

    @pl.when(g == 0)
    def _():
        acc[...] = part

    @pl.when(g > 0)
    def _():
        acc[...] += part

    @pl.when(g == pl.num_programs(0) - 1)
    def _():
        out[...] = acc[...].astype(BF16)


def weight_term(yi, ci, arrived, *refs):
    *tokens, term = refs
    me = yi[0]
    core = ci[0]
    chunk = term.shape[2]
    slots = (me, lax.bitwise_xor(me, 1), 3 - me, lax.bitwise_xor(3 - me, 1))
    pairs = []
    for half, c in ((0, core), (1, 1 - core)):
        for p in (0, 2):
            left = [arrived[slots[p + i] * 2 + c] for i in range(2)]
            pairs.append((jnp.concatenate(left, axis=1), tokens[4 * half + p : 4 * half + p + 2]))
    for j in range(4):
        total = None
        cols = slice(j * chunk, (j + 1) * chunk)
        for left, (one, two) in pairs:
            right = jnp.concatenate([one[:, cols], two[:, cols]], axis=0)
            part = jnp.dot(left, right, preferred_element_type=F32)
            total = part if total is None else total + part
        term[j] = total.astype(BF16)


def split_rows(got, blocks, turn):
    chans = got.shape[1]
    fblk = blocks.shape[1]
    piece = blocks.shape[2]
    turn[0:chans, :] = (
        got[0].astype(F32) + got[1].astype(F32) + got[2].astype(F32) + got[3].astype(F32)
    )
    turn[chans:, :] = jnp.zeros((turn.shape[0] - chans, turn.shape[1]), F32)
    flipped = turn[...].T
    for q in range(16):
        for h in range(2):
            part = flipped[q * fblk : (q + 1) * fblk, h * piece : (h + 1) * piece]
            blocks[2 * q + h] = part.astype(BF16)


def added(refs):
    total = refs[0][...].astype(F32)
    for ref in refs[1:]:
        total = total + ref[...].astype(F32)
    return total


def add_parts(*refs):
    refs[-1][...] = added(refs[:-1]).astype(BF16)


def make_close_sums(scale):
    def close_sums(xi, zi, yi, amp, *refs):
        *parts, grad_taps, grad_res, held = refs
        total = added(parts) * scale
        width = grad_taps.shape[1] // 3
        for g in range(3):
            grad_taps[:, g * width : (g + 1) * width] = total[8 * g : 8 * g + 7, 0:width]
        count = grad_res.shape[0]
        index = (xi[0] * 4 + zi[0]) * 4 + yi[0]
        moved = pltpu.roll(total[24:40, :], lax.rem(PADC - index * count, PADC), 1)
        held[...] = jnp.zeros(held.shape, F32)
        held[0:MODES, :] = moved[:, 0:128]
        grad_res[...] = held[...].T[0:count, 0:MODES] * amp[...]

    return close_sums


def make_close(scale):
    def close_weight(last, out):
        fblk, piece = last.shape[1:]
        for y in range(4):
            total = jnp.zeros((fblk, piece), F32)
            for z in range(4):
                for h in range(2):
                    total = total + last[(z * 4 + y) * 2 + h].astype(F32)
            out[:, y * piece : (y + 1) * piece] = (total * scale).astype(BF16)

    return close_weight


def ring(a, ax, d):
    return lax.ppermute(a, ax, [(i, (i + d) % 4) for i in range(4)])


def params(mb):
    return pltpu.CompilerParams(vmem_limit_bytes=int(mb * 1024 * 1024))


def local(tokens, w_in, conv_taps, residues, rates, cotangent):
    feats = tokens[0]
    cot = cotangent[0]
    own, width = cot.shape
    depth = feats.shape[1]
    chans = 3 * width
    count = 64
    piece = chans // 16
    fblk = depth // count
    ctx = ("x", "zl", "y")
    scale = 1.0 / math.sqrt(4 * count * own)
    smem = pl.BlockSpec(memory_space=pltpu.SMEM)
    vm = pl.BlockSpec(memory_space=pltpu.VMEM)
    free = pl.BlockSpec()
    names = ("x", "zl", "y", "core")
    feats, cot, rates, *where = lax.optimization_barrier(
        (feats, cot, rates, *[lax.axis_index(n) for n in names])
    )
    xi, zi, yi, ci = [w.reshape(1) for w in where]
    anywhere = pl.BlockSpec(memory_space=pl.ANY)
    head, tail, block, taps, amp_mine, cown = pl.pallas_call(
        prepare,
        in_specs=[anywhere] * 5,
        out_specs=[vm] * 6,
        out_shape=[
            jax.ShapeDtypeStruct((HALO, depth + PADC), BF16),
            jax.ShapeDtypeStruct((HALO, depth), BF16),
            jax.ShapeDtypeStruct((2 * MODES, width // count), F32),
            jax.ShapeDtypeStruct((3, 8, PADC), F32),
            jax.ShapeDtypeStruct(rates.shape, F32),
            jax.ShapeDtypeStruct((own, PADC), F32),
        ],
        scratch_shapes=[
            pltpu.VMEM((128, 128), F32),
            pltpu.VMEM((PADC, own), F32),
            pltpu.VMEM((width, own), BF16),
            pltpu.VMEM(rates.shape, F32),
            pltpu.VMEM(rates.shape, F32),
            pltpu.VMEM(conv_taps.shape, F32),
            pltpu.SemaphoreType.DMA((6,)),
        ],
        compiler_params=params(54),
        name="prepare",
    )(feats, cot.T, rates, residues, conv_taps)
    tprev = lax.ppermute(tail, ctx, [(i, i + 1) for i in range(count - 1)])
    nexts = lax.ppermute(head, ctx, [(i, i - 1) for i in range(1, count)])
    ext_rows = own + 2 * HALO
    steps = depth // KBLK // 2

    def project(part, *before):
        many = 3 if part else 1
        shape = (ext_rows, PADC) if part else (ext_rows, chans)
        return pl.pallas_call(
            make_project(part),
            in_specs=[vm] * (2 + part) + [anywhere] * 2,
            out_specs=[vm] * many,
            out_shape=[jax.ShapeDtypeStruct(shape, F32)] * many,
            scratch_shapes=[
                pltpu.VMEM((own, steps * KBLK), BF16),
                pltpu.VMEM((steps, chans, KBLK), BF16),
                pltpu.SemaphoreType.DMA,
                pltpu.SemaphoreType.DMA((steps,)),
                *[pltpu.VMEM((ext_rows, chans), F32)] * part,
            ],
            compiler_params=params((52, 51)[part]),
            cost_estimate=pl.CostEstimate(flops=800000000, bytes_accessed=6000000, transcendentals=0),
            name="project",
        )(tprev, nexts, *before, feats, w_in.T)

    def mixed(*zs):
        return pl.pallas_call(
            mix_taps,
            in_specs=[vm] * 4,
            out_specs=[vm] * 3,
            out_shape=[jax.ShapeDtypeStruct((EXT, PADC), F32)] * 3,
            compiler_params=params(8),
            cost_estimate=pl.CostEstimate(flops=800000000, bytes_accessed=6000000, transcendentals=0),
            name="mix_taps",
        )(taps, *zs)

    held, each = block, width // count
    work = []
    for g, (me, ax) in enumerate(((yi, "y"), (zi, "zl"), (xi, "x"))):
        blocks = [held] + [ring(held, ax, d) for d in (1, 2, 3)]
        work = project(0) if g == 0 else project(1, *work) if g == 1 else mixed(*work)
        *blocks, last_work = lax.optimization_barrier((*blocks, work[-1]))
        work = [*work[:-1], last_work]
        if g == 1:
            zq, zk, zv = work
        if g == 2:
            break
        each = 4 * each
        held = pl.pallas_call(
            join_params,
            in_specs=[smem] + [vm] * 4,
            out_specs=vm,
            out_shape=jax.ShapeDtypeStruct((2 * MODES, each), F32),
            scratch_shapes=[pltpu.VMEM((2 * MODES, 256), F32)],
            compiler_params=params(4),
            name="join_params",
        )(me, *blocks)
    mq, mk, mv = work
    cots, rate, gain, es, ends, endb = pl.pallas_call(
        end_states,
        in_specs=[smem] + [vm] * 9,
        out_specs=[vm] * 6,
        out_shape=[
            jax.ShapeDtypeStruct((EXT, PADC), F32),
            jax.ShapeDtypeStruct((MODES, PADC), F32),
            jax.ShapeDtypeStruct((MODES, PADC), F32),
            jax.ShapeDtypeStruct((2, MODES, 8, PADC), F32),
            jax.ShapeDtypeStruct((2 * MODES, PADC), F32),
            jax.ShapeDtypeStruct((2 * MODES, PADC), BF16),
        ],
        scratch_shapes=[
            pltpu.VMEM((EXT, 128), F32),
            pltpu.VMEM((EXT, 128), F32),
            pltpu.VMEM((2 * MODES, PADC), F32),
        ],
        compiler_params=params(16),
        cost_estimate=pl.CostEstimate(flops=20000000, bytes_accessed=3000000, transcendentals=0),
        name="end_states",
    )(xi, *blocks, mq, mk, mv, cown, nexts)

    prefixes = []
    total, sent = ends, endb
    for me, ax, span in ((yi, "y", own), (zi, "zl", 4 * own), (xi, "x", 16 * own)):
        near = [ring(sent, ax, d) for d in (1, 2, 3)]
        total, sent, prefix = pl.pallas_call(
            make_level(span),
            in_specs=[smem] + [vm] * 5,
            out_specs=[vm] * 3,
            out_shape=[
                jax.ShapeDtypeStruct((2 * MODES, PADC), F32),
                jax.ShapeDtypeStruct((2 * MODES, PADC), BF16),
                jax.ShapeDtypeStruct((2 * MODES, PADC), F32),
            ],
            compiler_params=params(8),
            name="level",
        )(me, total, *near, rate)
        prefixes.append(prefix)
        if ax == "zl":
            mine, _ = lax.optimization_barrier((feats, sent))
            pair = lax.ppermute(mine, "y", [(i, i ^ 1) for i in range(4)])
            opposite = lax.ppermute(mine, "y", [(i, 3 - i) for i in range(4)])
    pair, opposite, prefixes[2] = lax.optimization_barrier((pair, opposite, prefixes[2]))
    far = lax.ppermute(pair, "y", [(i, 3 - i) for i in range(4)])

    def swapped(a):
        return lax.ppermute(a, "core", [(0, 1), (1, 0)])

    def tiles(shape):
        lead = len(shape) - 1
        return pl.BlockSpec(shape, lambda k: (0,) * lead + (k,))

    outt, dz, dzb, sums = pl.pallas_call(
        finish,
        grid=(PADC // 128,),
        in_specs=[
            smem,
            smem,
            *[tiles((ext_rows, 128))] * 3,
            *[tiles((EXT, 128))] * 3,
            tiles((2, MODES, 8, 128)),
            tiles((2 * MODES, 128)),
            tiles((2 * MODES, 128)),
            tiles((2 * MODES, 128)),
            tiles((3, 8, 128)),
            tiles((MODES, 128)),
            tiles((MODES, 128)),
            tiles((EXT, 128)),
        ],
        out_specs=[
            pl.BlockSpec((128, own), lambda k: (k, 0)),
            tiles((3, own, 128)),
            pl.BlockSpec((8, 2 * piece, own), lambda k: (0, 0, 0)),
            tiles((40, 128)),
        ],
        out_shape=[
            jax.ShapeDtypeStruct((width, own), BF16),
            jax.ShapeDtypeStruct((3, own, PADC), BF16),
            jax.ShapeDtypeStruct((8, 2 * piece, own), BF16),
            jax.ShapeDtypeStruct((40, PADC), BF16),
        ],
        scratch_shapes=[
            pltpu.VMEM((40, 128), F32),
            pltpu.VMEM((2 * MODES, 128), F32),
            pltpu.VMEM((EXT, 128), F32),
            pltpu.VMEM((EXT, 128), F32),
            pltpu.VMEM((EXT, 128), F32),
            pltpu.VMEM((EXT, 128), F32),
            pltpu.VMEM((3, EXT, 128), F32),
            pltpu.VMEM((3, PADC, own), F32),
        ],
        compiler_params=params(50),
        cost_estimate=pl.CostEstimate(flops=200000000, bytes_accessed=10000000, transcendentals=0),
        name="finish",
    )(zi, yi, zq, zk, zv, mq, mk, mv, es, *prefixes, taps, rate, gain, cots)
    output = outt.T
    blocks_of = [mine, pair, opposite, far]
    mine, pair, opposite, _ = lax.optimization_barrier((mine, pair, opposite, sums))
    blocks_of = [mine, pair, opposite, far]
    theirs = [swapped(a) for a in blocks_of]

    def spread(a, ax):
        return [a] + [ring(a, ax, d) for d in (1, 2, 3)]

    def swap(a, ax):
        return [a, lax.ppermute(a, ax, [(0, 1), (1, 0)])]

    def summed(parts):
        return pl.pallas_call(
            add_parts,
            in_specs=[free] * len(parts),
            out_specs=free,
            out_shape=jax.ShapeDtypeStruct((40, PADC), BF16),
            compiler_params=params(4),
            name="add_parts",
        )(*parts)

    arrived = lax.all_to_all(dzb, ("y", "core"), split_axis=0, concat_axis=0, tiled=True)
    sums = summed(swap(sums, "core"))
    *theirs, sums = lax.optimization_barrier((*theirs, sums))
    parts = spread(sums, "zl")
    grad_feats = pl.pallas_call(
        token_grads,
        grid=(3,),
        in_specs=[
            pl.BlockSpec((1, own, PADC), lambda g: (g, 0, 0)),
            pl.BlockSpec((width, depth), lambda g: (g, 0)),
        ],
        out_specs=pl.BlockSpec((own, depth), lambda g: (0, 0)),
        out_shape=jax.ShapeDtypeStruct((own, depth), BF16),
        scratch_shapes=[pltpu.VMEM((own, depth), F32)],
        compiler_params=params(57),
        cost_estimate=pl.CostEstimate(flops=1200000000, bytes_accessed=11000000, transcendentals=0),
        name="token_grads",
    )(dz, w_in.T)
    *parts, grad_feats = lax.optimization_barrier((*parts, grad_feats))
    sums = summed(parts)
    arrived, sums = lax.optimization_barrier((arrived, sums))
    term = pl.pallas_call(
        weight_term,
        in_specs=[smem] * 2 + [vm] + [free] * 8,
        out_specs=vm,
        out_shape=jax.ShapeDtypeStruct((4, 2 * piece, depth // 4), BF16),
        compiler_params=params(24),
        cost_estimate=pl.CostEstimate(flops=1200000000, bytes_accessed=6000000, transcendentals=0),
        name="weight_term",
    )(yi, ci, arrived, *blocks_of, *theirs)
    got = lax.all_to_all(term, "x", 0, 0, tiled=True)
    sums, _ = lax.optimization_barrier((sums, term))
    sums = summed(swap(summed(spread(sums, "y")), "zh"))
    got, sums = lax.optimization_barrier((got, sums))
    blocks = pl.pallas_call(
        split_rows,
        in_specs=[vm],
        out_specs=vm,
        out_shape=jax.ShapeDtypeStruct((32, fblk, piece), BF16),
        scratch_shapes=[pltpu.VMEM((384, depth // 4), F32)],
        compiler_params=params(12),
        name="split_rows",
    )(got)
    last = lax.all_to_all(blocks, ("zl", "y", "zh"), 0, 0, tiled=True)
    sums, _ = lax.optimization_barrier((sums, blocks))
    parts = spread(sums, "x")
    grad_taps, grad_residues = pl.pallas_call(
        make_close_sums(scale),
        in_specs=[smem] * 3 + [free] * 5,
        out_specs=[vm] * 2,
        out_shape=[
            jax.ShapeDtypeStruct((7, chans), F32),
            jax.ShapeDtypeStruct(rates.shape, F32),
        ],
        scratch_shapes=[pltpu.VMEM((128, 128), F32)],
        compiler_params=params(4),
        name="close_sums",
    )(xi, zi, yi, amp_mine, *parts)
    grad_weight = pl.pallas_call(
        make_close(scale),
        in_specs=[vm],
        out_specs=vm,
        out_shape=jax.ShapeDtypeStruct((fblk, 4 * piece), BF16),
        compiler_params=params(4),
        name="close_weight",
    )(last)
    return (output[None], grad_feats[None], grad_weight, grad_taps, grad_residues)


def solution(mesh):
    fine = Mesh(mesh.devices.reshape(4, 4, 4, 2, 2), ("x", "zl", "y", "zh", "core"))
    ctx = ("x", "zl", "y")
    dp = ("zh", "core")
    in_specs = (P(dp, ctx, None), P(), P(), P(ctx, None), P(ctx, None), P(dp, ctx, None))
    out_specs = (P(dp, ctx, None), P(dp, ctx, None), P(ctx, dp), P(), P(ctx, None))
    return jax.shard_map(local, mesh=fine, in_specs=in_specs, out_specs=out_specs, check_vma=False)
```

```python
import math

import jax
import jax.numpy as jnp
from jax import lax
from jax.experimental import pallas as pl
from jax.experimental.pallas import tpu as pltpu
from jax.sharding import Mesh, PartitionSpec as P

F32 = jnp.float32
BF16 = jnp.bfloat16
HALO = 16
EXT = 136
SEG = 17
PADC = 1024
MODES = 16
NT = (((1,), (1,)), ((), ()))


def rounded(a):
    return a.astype(BF16).astype(F32)


KBLK = 256


def make_project(part):
    def project(*refs):
        if part == 0:
            tp, nexts, feats, wt, acc, tk, wbuf, tsem, sems = refs
        else:
            tp, nexts, before, feats, wt, zq, zk, zv, tk, wbuf, tsem, sems, acc = refs
        steps, chans, _ = wbuf.shape
        low = part * steps * KBLK
        arrival = pltpu.make_async_copy(feats.at[:, pl.ds(low, steps * KBLK)], tk, tsem)
        arrival.start()
        copies = [
            pltpu.make_async_copy(wt.at[:, pl.ds(low + k * KBLK, KBLK)], wbuf.at[k], sems.at[k])
            for k in range(steps)
        ]
        for copy in copies:
            copy.start()
        arrival.wait()
        for k in range(steps):
            wide = slice(low + k * KBLK, low + (k + 1) * KBLK)
            rows = jnp.concatenate(
                [tp[:, wide], tk[:, k * KBLK : (k + 1) * KBLK], nexts[:, wide]], axis=0
            )
            copies[k].wait()
            total = lax.dot_general(rows, wbuf[k], NT, preferred_element_type=F32)
            if k > 0:
                total = acc[...] + total
            elif part == 1:
                total = before[...] + total
            if part == 0 or k < steps - 1:
                acc[...] = total
            else:
                width = chans // 3
                for g, z in enumerate((zq, zk, zv)):
                    z[:, 0:width] = rounded(total[:, g * width : (g + 1) * width])
                    z[:, width:] = jnp.zeros((z.shape[0], PADC - width), F32)

    return project


def mix_taps(taps, zq, zk, zv, mq, mk, mv):
    def tile(ct, carry):
        lanes = pl.ds(pl.multiple_of(ct * 128, 128), 128)
        for g, (z, m) in enumerate(((zq, mq), (zk, mk), (zv, mv))):
            total = taps[g, 0:1, lanes] * z[pl.ds(HALO, EXT), lanes]
            for j in range(1, 7):
                total = total + taps[g, j : j + 1, lanes] * z[pl.ds(HALO - j, EXT), lanes]
            m[:, lanes] = total
        return carry

    lax.fori_loop(0, PADC // 128, tile, 0)


def one_minus_exp(x):
    series = jnp.ones_like(x)
    for n in range(13, 1, -1):
        series = 1.0 - series * x * (1.0 / n)
    return jnp.where(x < 0.5, x * series, 1.0 - jnp.exp(-x))


def prepare(
    feats, cott, rates, residues, conv, head, tail, block, taps, amp, cots,
    held, turn, cbuf, rbuf, sbuf, vbuf, sems,
):
    count = rates.shape[0]
    width, own = cott.shape
    depth = feats.shape[1]
    copies = [
        pltpu.make_async_copy(rates, rbuf, sems.at[0]),
        pltpu.make_async_copy(residues, sbuf, sems.at[1]),
        pltpu.make_async_copy(cott, cbuf, sems.at[2]),
        pltpu.make_async_copy(conv, vbuf, sems.at[3]),
        pltpu.make_async_copy(feats.at[pl.ds(0, HALO)], head.at[:, pl.ds(0, depth)], sems.at[4]),
        pltpu.make_async_copy(feats.at[pl.ds(own - HALO, HALO)], tail, sems.at[5]),
    ]
    for copy in copies:
        copy.start()
    held[...] = jnp.zeros(held.shape, F32)
    turn[...] = jnp.zeros(turn.shape, F32)
    taps[...] = jnp.zeros(taps.shape, F32)
    copies[0].wait()
    copies[1].wait()
    size = jnp.sqrt(one_minus_exp(2.0 * rbuf[...]))
    amp[...] = size
    held[0:count, 0:MODES] = rbuf[...]
    held[0:count, MODES : 2 * MODES] = sbuf[...] * size
    block[...] = held[...].T[0 : 2 * MODES, 0:count]
    copies[2].wait()
    turn[0:width, :] = cbuf[...].astype(F32)
    for c in range(PADC // 128):
        part = turn[c * 128 : (c + 1) * 128, :].T
        cots[:, c * 128 : (c + 1) * 128] = part
        head[:, depth + c * 128 : depth + (c + 1) * 128] = part[0:HALO].astype(BF16)
    copies[3].wait()
    for g in range(3):
        taps[g, 0:7, 0:width] = vbuf[:, g * width : (g + 1) * width]
    for copy in copies[4:]:
        copy.wait()


def placed(me, refs, held, goal):
    wide = refs[0].shape[1]
    total = None
    for d, ref in enumerate(refs):
        held[...] = jnp.zeros(held.shape, F32)
        held[:, 0:wide] = ref[...]
        part = pltpu.roll(held[...], lax.rem(me + (4 - d), 4) * wide, 1)
        total = part if total is None else total + part
    return total[:, 0:goal]


def join_params(me, r0, r1, r2, r3, out, held):
    out[...] = placed(me[0], (r0, r1, r2, r3), held, out.shape[1])


def end_states(me, r0, r1, r2, r3, mq, mk, mv, cown, nexts, cots, rates, gains, es, ends, endb, ut, dt, held):
    joined = placed(me[0], (r0, r1, r2, r3), held, PADC)
    rates[...] = joined[0:MODES]
    gains[...] = joined[MODES : 2 * MODES]
    sub = lax.broadcasted_iota(jnp.int32, (8, 128), 0)
    subf = sub.astype(F32)
    fdepth = jnp.where(sub == 7, 0.0, (EXT - 8 - SEG) - SEG * subf)
    bdepth = jnp.where(sub == 0, 0.0, SEG * subf - 8.0)

    def tile(ct, carry):
        lanes = pl.ds(pl.multiple_of(ct * 128, 128), 128)
        ut[...] = rounded(mk[:, lanes] * mv[:, lanes])
        lane = pl.multiple_of(nexts.shape[1] - PADC + ct * 128, 128)
        after = nexts[:, pl.ds(lane, 128)].astype(F32)
        cot = jnp.concatenate([cown[:, lanes], after[0 : EXT - 128]], axis=0)
        cots[:, lanes] = cot
        dt[...] = rounded(cot * mq[:, lanes])
        rate = rates[:, lanes]
        decay = jnp.exp(-rate)
        for half in range(2):
            ks = range(half * 8, half * 8 + 8)
            al = [jnp.broadcast_to(decay[k : k + 1, :], (8, 128)) for k in ks]
            rl = [jnp.broadcast_to(rate[k : k + 1, :], (8, 128)) for k in ks]
            st = [jnp.zeros((8, 128), F32)] * 8
            snap = st
            for t in range(SEG):
                uv = ut[pl.ds(t, 8, stride=SEG), :]
                st = [a * s + uv for a, s in zip(al, st)]
                if t == 8:
                    snap = st
            for i, k in enumerate(ks):
                es[0, k, :, lanes] = st[i]
                full = jnp.where(sub == 7, snap[i], st[i]) * jnp.exp(-rl[i] * fdepth)
                ends[k : k + 1, lanes] = jnp.sum(full, axis=0, keepdims=True)
            st = [jnp.zeros((8, 128), F32)] * 8
            for t in range(SEG - 1, -1, -1):
                dv = dt[pl.ds(t, 8, stride=SEG), :]
                st = [a * s + dv for a, s in zip(al, st)]
                if t == 8:
                    snap = st
            for i, k in enumerate(ks):
                es[1, k, :, lanes] = st[i]
                full = jnp.where(sub == 0, snap[i], st[i]) * jnp.exp(-rl[i] * bdepth)
                ends[MODES + k : MODES + k + 1, lanes] = jnp.sum(full, axis=0, keepdims=True)
        return carry

    lax.fori_loop(0, PADC // 128, tile, 0)
    endb[...] = ends[...].astype(BF16)


def make_level(span):
    def level(index, own, r1, r2, r3, rates, total, totalb, prefix):
        me = index[0]
        rate = rates[...] * float(span)
        before = jnp.zeros((MODES, PADC), F32)
        after = before
        whole_f = before
        whole_b = before
        for d, ref in enumerate((own, r1, r2, r3)):
            m = lax.rem(me + (4 - d), 4)
            f = ref[0:MODES, :].astype(F32)
            b = ref[MODES : 2 * MODES, :].astype(F32)
            whole_f = whole_f + f * jnp.exp(-rate * (3 - m).astype(F32))
            whole_b = whole_b + b * jnp.exp(-rate * m.astype(F32))
            if d > 0:
                gf = me - 1 - m
                gb = m - me - 1
                wf = jnp.exp(-rate * jnp.maximum(gf, 0).astype(F32))
                wb = jnp.exp(-rate * jnp.maximum(gb, 0).astype(F32))
                before = before + jnp.where(gf >= 0, 1.0, 0.0) * (wf * f)
                after = after + jnp.where(gb >= 0, 1.0, 0.0) * (wb * b)
        prefix[0:MODES, :] = before
        prefix[MODES : 2 * MODES, :] = after
        total[0:MODES, :] = whole_f
        total[MODES : 2 * MODES, :] = whole_b
        totalb[0:MODES, :] = whole_f.astype(BF16)
        totalb[MODES : 2 * MODES, :] = whole_b.astype(BF16)

    return level


def finish(
    zi, yi, zq, zk, zv, mq, mk, mv, es, py, pz, px, taps, rates, reff, cots,
    outt, dz, dzb, sumb, sums, inc, ut, dt, longs, dps, dms, dzt,
):
    own = dz.shape[1]
    rate = rates[...]
    for back in range(2):
        part = pl.ds(back * MODES, MODES)
        near, mid = yi[0], zi[0]
        if back:
            near, mid = 3 - near, 3 - mid
        far = pz[part, :] + jnp.exp(-rate * (4 * own * mid).astype(F32)) * px[part, :]
        inc[part, :] = py[part, :] + jnp.exp(-rate * (own * near).astype(F32)) * far
    sub = lax.broadcasted_iota(jnp.int32, (8, 128), 0)
    ut[...] = rounded(mk[...] * mv[...])
    dt[...] = rounded(cots[...] * mq[...])
    decay = jnp.exp(-rate)
    gain = reff[...]
    for half in range(2):
        ks = range(half * 8, half * 8 + 8)
        al = [jnp.broadcast_to(decay[k : k + 1, :], (8, 128)) for k in ks]
        gl = [jnp.broadcast_to(gain[k : k + 1, :], (8, 128)) for k in ks]
        rl = [jnp.broadcast_to(rate[k : k + 1, :], (8, 128)) for k in ks]
        fwd = []
        bwd = []
        for i, k in enumerate(ks):
            jump = [jnp.exp(-float(SEG * m) * rl[i]) for m in (1, 2, 4)]
            x = jnp.where(sub == 0, inc[k : k + 1, :], pltpu.roll(es[0, k], 1, 0))
            for m, d in zip((1, 2, 4), jump):
                x = x + jnp.where(sub >= m, pltpu.roll(x, m, 0) * d, 0.0)
            fwd.append(x)
            x = jnp.where(
                sub == 7, inc[MODES + k : MODES + k + 1, :], pltpu.roll(es[1, k], 7, 0)
            )
            for m, d in zip((1, 2, 4), jump):
                x = x + jnp.where(sub < 8 - m, pltpu.roll(x, 8 - m, 0) * d, 0.0)
            bwd.append(x)
        gr = [jnp.zeros((8, 128), F32)] * 8
        st = fwd
        for t in range(SEG):
            uv = ut[pl.ds(t, 8, stride=SEG), :]
            dv = dt[pl.ds(t, 8, stride=SEG), :]
            if t >= 9:
                dv = jnp.where(sub < 7, dv, 0.0)
            st = [a * s + uv for a, s in zip(al, st)]
            gr = [q + dv * s for q, s in zip(gr, st)]
            total = sum(g * s for g, s in zip(gl, st))
            if half:
                total = total + longs[pl.ds(t, 8, stride=SEG), :]
            longs[pl.ds(t, 8, stride=SEG), :] = total
        for i, k in enumerate(ks):
            sums[24 + k : 25 + k, :] = jnp.sum(gr[i], axis=0, keepdims=True)
        st = bwd
        for t in range(SEG - 1, -1, -1):
            dv = dt[pl.ds(t, 8, stride=SEG), :]
            st = [a * s + dv for a, s in zip(al, st)]
            total = sum(g * s for g, s in zip(gl, st))
            if half:
                total = total + dps[pl.ds(t, 8, stride=SEG), :]
            dps[pl.ds(t, 8, stride=SEG), :] = total
    long_out = rounded(longs[...])
    dprod = rounded(dps[...])
    outt[...] = (mq[0:own, :] * long_out[0:own]).T.astype(BF16)
    dms[0] = rounded(cots[...] * long_out)
    dms[1] = rounded(dprod * mv[...])
    dms[2] = rounded(dprod * mk[...])
    ct = pl.program_id(0)
    for g, zg in enumerate((zq, zk, zv)):
        mine = dms[g, 0:own, :]
        total = taps[g, 0:1, :] * mine
        sums[8 * g : 8 * g + 1, :] = jnp.sum(mine * zg[pl.ds(HALO, own), :], axis=0, keepdims=True)
        for j in range(1, 7):
            total = total + taps[g, j : j + 1, :] * dms[g, pl.ds(j, own), :]
            sums[8 * g + j : 8 * g + j + 1, :] = jnp.sum(
                mine * zg[pl.ds(HALO - j, own), :], axis=0, keepdims=True
            )
        sums[8 * g + 7 : 8 * g + 8, :] = jnp.zeros((1, 128), F32)
        dz[g] = total.astype(BF16)
        dzt[g, pl.ds(pl.multiple_of(ct * 128, 128), 128), :] = total.T

    sumb[...] = sums[...].astype(BF16)

    @pl.when(ct == pl.num_programs(0) - 1)
    def _():
        piece = dzb.shape[1] // 2
        width = 16 * piece // 3
        for b in range(8):
            both = []
            for h in range(2):
                off = h * 8 * piece + (b % 2) * 4 * piece + (b // 2) * piece
                g, low = off // width, off % width
                size = min(piece, width - low)
                both.append(dzt[g, low : low + size, :])
                if size < piece:
                    both.append(dzt[g + 1, 0 : piece - size, :])
            dzb[b] = jnp.concatenate(both, axis=0).astype(BF16)


def token_grads(dz, wt, out, acc):
    g = pl.program_id(0)
    part = jnp.dot(dz[0, :, 0 : wt.shape[0]], wt[...], preferred_element_type=F32)

    @pl.when(g == 0)
    def _():
        acc[...] = part

    @pl.when(g > 0)
    def _():
        acc[...] += part

    @pl.when(g == pl.num_programs(0) - 1)
    def _():
        out[...] = acc[...].astype(BF16)


def weight_term(xi, yi, ci, arrived, *refs):
    tokens, terms = refs[:8], refs[8:]
    me = yi[0]
    core = ci[0]
    chunk = terms[0].shape[1]
    slots = (me, lax.bitwise_xor(me, 1), 3 - me, lax.bitwise_xor(3 - me, 1))
    pairs = []
    for half, c in ((0, core), (1, 1 - core)):
        for p in (0, 2):
            left = [arrived[slots[p + i] * 2 + c] for i in range(2)]
            pairs.append((jnp.concatenate(left, axis=1), tokens[4 * half + p : 4 * half + p + 2]))
    for d, term in enumerate(terms):
        total = None
        cols = pl.ds(pl.multiple_of(lax.rem(xi[0] + d, 4) * chunk, 128), chunk)
        for left, (one, two) in pairs:
            right = jnp.concatenate([one[:, cols], two[:, cols]], axis=0)
            part = jnp.dot(left, right, preferred_element_type=F32)
            total = part if total is None else total + part
        term[...] = total.astype(BF16)


def split_rows(g0, g1, g2, g3, blocks, turn):
    chans = g0.shape[0]
    fblk = blocks.shape[1]
    piece = blocks.shape[2]
    turn[0:chans, :] = added((g0, g1, g2, g3))
    turn[chans:, :] = jnp.zeros((turn.shape[0] - chans, turn.shape[1]), F32)
    flipped = turn[...].T
    for q in range(16):
        for h in range(2):
            part = flipped[q * fblk : (q + 1) * fblk, h * piece : (h + 1) * piece]
            blocks[2 * q + h] = part.astype(BF16)


def added(refs):
    total = refs[0][...].astype(F32)
    for ref in refs[1:]:
        total = total + ref[...].astype(F32)
    return total


def add_parts(*refs):
    refs[-1][...] = added(refs[:-1]).astype(BF16)


def make_close_sums(scale):
    def close_sums(xi, zi, yi, amp, *refs):
        *parts, grad_taps, grad_res, held = refs
        total = added(parts) * scale
        width = grad_taps.shape[1] // 3
        for g in range(3):
            grad_taps[:, g * width : (g + 1) * width] = total[8 * g : 8 * g + 7, 0:width]
        count = grad_res.shape[0]
        index = (xi[0] * 4 + zi[0]) * 4 + yi[0]
        moved = pltpu.roll(total[24:40, :], lax.rem(PADC - index * count, PADC), 1)
        held[...] = jnp.zeros(held.shape, F32)
        held[0:MODES, :] = moved[:, 0:128]
        grad_res[...] = held[...].T[0:count, 0:MODES] * amp[...]

    return close_sums


def make_close(scale):
    def close_weight(last, out):
        fblk, piece = last.shape[1:]
        for y in range(4):
            total = jnp.zeros((fblk, piece), F32)
            for z in range(4):
                for h in range(2):
                    total = total + last[(z * 4 + y) * 2 + h].astype(F32)
            out[:, y * piece : (y + 1) * piece] = (total * scale).astype(BF16)

    return close_weight


def ring(a, ax, d):
    return lax.ppermute(a, ax, [(i, (i + d) % 4) for i in range(4)])


def params(mb):
    return pltpu.CompilerParams(vmem_limit_bytes=int(mb * 1024 * 1024))


def local(tokens, w_in, conv_taps, residues, rates, cotangent):
    feats = tokens[0]
    cot = cotangent[0]
    own, width = cot.shape
    depth = feats.shape[1]
    chans = 3 * width
    count = 64
    piece = chans // 16
    fblk = depth // count
    ctx = ("x", "zl", "y")
    scale = 1.0 / math.sqrt(4 * count * own)
    smem = pl.BlockSpec(memory_space=pltpu.SMEM)
    vm = pl.BlockSpec(memory_space=pltpu.VMEM)
    free = pl.BlockSpec()
    names = ("x", "zl", "y", "core")
    feats, cot, rates, *where = lax.optimization_barrier(
        (feats, cot, rates, *[lax.axis_index(n) for n in names])
    )
    xi, zi, yi, ci = [w.reshape(1) for w in where]
    anywhere = pl.BlockSpec(memory_space=pl.ANY)
    head, tail, block, taps, amp_mine, cown = pl.pallas_call(
        prepare,
        in_specs=[anywhere] * 5,
        out_specs=[vm] * 6,
        out_shape=[
            jax.ShapeDtypeStruct((HALO, depth + PADC), BF16),
            jax.ShapeDtypeStruct((HALO, depth), BF16),
            jax.ShapeDtypeStruct((2 * MODES, width // count), F32),
            jax.ShapeDtypeStruct((3, 8, PADC), F32),
            jax.ShapeDtypeStruct(rates.shape, F32),
            jax.ShapeDtypeStruct((own, PADC), F32),
        ],
        scratch_shapes=[
            pltpu.VMEM((128, 128), F32),
            pltpu.VMEM((PADC, own), F32),
            pltpu.VMEM((width, own), BF16),
            pltpu.VMEM(rates.shape, F32),
            pltpu.VMEM(rates.shape, F32),
            pltpu.VMEM(conv_taps.shape, F32),
            pltpu.SemaphoreType.DMA((6,)),
        ],
        compiler_params=params(54),
        name="prepare",
    )(feats, cot.T, rates, residues, conv_taps)
    tprev = lax.ppermute(tail, ctx, [(i, i + 1) for i in range(count - 1)])
    nexts = lax.ppermute(head, ctx, [(i, i - 1) for i in range(1, count)])
    ext_rows = own + 2 * HALO
    steps = depth // KBLK // 2

    def project(part, *before):
        many = 3 if part else 1
        shape = (ext_rows, PADC) if part else (ext_rows, chans)
        return pl.pallas_call(
            make_project(part),
            in_specs=[vm] * (2 + part) + [anywhere] * 2,
            out_specs=[vm] * many,
            out_shape=[jax.ShapeDtypeStruct(shape, F32)] * many,
            scratch_shapes=[
                pltpu.VMEM((own, steps * KBLK), BF16),
                pltpu.VMEM((steps, chans, KBLK), BF16),
                pltpu.SemaphoreType.DMA,
                pltpu.SemaphoreType.DMA((steps,)),
                *[pltpu.VMEM((ext_rows, chans), F32)] * part,
            ],
            compiler_params=params((52, 51)[part]),
            cost_estimate=pl.CostEstimate(flops=800000000, bytes_accessed=6000000, transcendentals=0),
            name="project",
        )(tprev, nexts, *before, feats, w_in.T)

    def mixed(*zs):
        return pl.pallas_call(
            mix_taps,
            in_specs=[vm] * 4,
            out_specs=[vm] * 3,
            out_shape=[jax.ShapeDtypeStruct((EXT, PADC), F32)] * 3,
            compiler_params=params(8),
            cost_estimate=pl.CostEstimate(flops=800000000, bytes_accessed=6000000, transcendentals=0),
            name="mix_taps",
        )(taps, *zs)

    held, each = block, width // count
    work = []
    for g, (me, ax) in enumerate(((yi, "y"), (zi, "zl"), (xi, "x"))):
        blocks = [held] + [ring(held, ax, d) for d in (1, 2, 3)]
        work = project(0) if g == 0 else project(1, *work) if g == 1 else mixed(*work)
        *blocks, last_work = lax.optimization_barrier((*blocks, work[-1]))
        work = [*work[:-1], last_work]
        if g == 1:
            zq, zk, zv = work
        if g == 2:
            break
        each = 4 * each
        held = pl.pallas_call(
            join_params,
            in_specs=[smem] + [vm] * 4,
            out_specs=vm,
            out_shape=jax.ShapeDtypeStruct((2 * MODES, each), F32),
            scratch_shapes=[pltpu.VMEM((2 * MODES, 256), F32)],
            compiler_params=params(4),
            name="join_params",
        )(me, *blocks)
    mq, mk, mv = work
    cots, rate, gain, es, ends, endb = pl.pallas_call(
        end_states,
        in_specs=[smem] + [vm] * 9,
        out_specs=[vm] * 6,
        out_shape=[
            jax.ShapeDtypeStruct((EXT, PADC), F32),
            jax.ShapeDtypeStruct((MODES, PADC), F32),
            jax.ShapeDtypeStruct((MODES, PADC), F32),
            jax.ShapeDtypeStruct((2, MODES, 8, PADC), F32),
            jax.ShapeDtypeStruct((2 * MODES, PADC), F32),
            jax.ShapeDtypeStruct((2 * MODES, PADC), BF16),
        ],
        scratch_shapes=[
            pltpu.VMEM((EXT, 128), F32),
            pltpu.VMEM((EXT, 128), F32),
            pltpu.VMEM((2 * MODES, PADC), F32),
        ],
        compiler_params=params(16),
        cost_estimate=pl.CostEstimate(flops=20000000, bytes_accessed=3000000, transcendentals=0),
        name="end_states",
    )(xi, *blocks, mq, mk, mv, cown, nexts)

    prefixes = []
    total, sent = ends, endb
    for me, ax, span in ((yi, "y", own), (zi, "zl", 4 * own), (xi, "x", 16 * own)):
        near = [ring(sent, ax, d) for d in (1, 2, 3)]
        total, sent, prefix = pl.pallas_call(
            make_level(span),
            in_specs=[smem] + [vm] * 5,
            out_specs=[vm] * 3,
            out_shape=[
                jax.ShapeDtypeStruct((2 * MODES, PADC), F32),
                jax.ShapeDtypeStruct((2 * MODES, PADC), BF16),
                jax.ShapeDtypeStruct((2 * MODES, PADC), F32),
            ],
            compiler_params=params(8),
            name="level",
        )(me, total, *near, rate)
        prefixes.append(prefix)
        if ax == "zl":
            mine, _ = lax.optimization_barrier((feats, sent))
            pair = lax.ppermute(mine, "y", [(i, i ^ 1) for i in range(4)])
            opposite = lax.ppermute(mine, "y", [(i, 3 - i) for i in range(4)])
    pair, opposite, prefixes[2] = lax.optimization_barrier((pair, opposite, prefixes[2]))
    far = lax.ppermute(pair, "y", [(i, 3 - i) for i in range(4)])

    def swapped(a):
        return lax.ppermute(a, "core", [(0, 1), (1, 0)])

    def tiles(shape):
        lead = len(shape) - 1
        return pl.BlockSpec(shape, lambda k: (0,) * lead + (k,))

    outt, dz, dzb, sums = pl.pallas_call(
        finish,
        grid=(PADC // 128,),
        in_specs=[
            smem,
            smem,
            *[tiles((ext_rows, 128))] * 3,
            *[tiles((EXT, 128))] * 3,
            tiles((2, MODES, 8, 128)),
            tiles((2 * MODES, 128)),
            tiles((2 * MODES, 128)),
            tiles((2 * MODES, 128)),
            tiles((3, 8, 128)),
            tiles((MODES, 128)),
            tiles((MODES, 128)),
            tiles((EXT, 128)),
        ],
        out_specs=[
            pl.BlockSpec((128, own), lambda k: (k, 0)),
            tiles((3, own, 128)),
            pl.BlockSpec((8, 2 * piece, own), lambda k: (0, 0, 0)),
            tiles((40, 128)),
        ],
        out_shape=[
            jax.ShapeDtypeStruct((width, own), BF16),
            jax.ShapeDtypeStruct((3, own, PADC), BF16),
            jax.ShapeDtypeStruct((8, 2 * piece, own), BF16),
            jax.ShapeDtypeStruct((40, PADC), BF16),
        ],
        scratch_shapes=[
            pltpu.VMEM((40, 128), F32),
            pltpu.VMEM((2 * MODES, 128), F32),
            pltpu.VMEM((EXT, 128), F32),
            pltpu.VMEM((EXT, 128), F32),
            pltpu.VMEM((EXT, 128), F32),
            pltpu.VMEM((EXT, 128), F32),
            pltpu.VMEM((3, EXT, 128), F32),
            pltpu.VMEM((3, PADC, own), F32),
        ],
        compiler_params=params(50),
        cost_estimate=pl.CostEstimate(flops=200000000, bytes_accessed=10000000, transcendentals=0),
        name="finish",
    )(zi, yi, zq, zk, zv, mq, mk, mv, es, *prefixes, taps, rate, gain, cots)
    output = outt.T
    blocks_of = [mine, pair, opposite, far]
    mine, pair, opposite, _ = lax.optimization_barrier((mine, pair, opposite, sums))
    blocks_of = [mine, pair, opposite, far]
    theirs = [swapped(a) for a in blocks_of]

    def spread(a, ax):
        return [a] + [ring(a, ax, d) for d in (1, 2, 3)]

    def swap(a, ax):
        return [a, lax.ppermute(a, ax, [(0, 1), (1, 0)])]

    def summed(parts):
        return pl.pallas_call(
            add_parts,
            in_specs=[free] * len(parts),
            out_specs=free,
            out_shape=jax.ShapeDtypeStruct((40, PADC), BF16),
            compiler_params=params(4),
            name="add_parts",
        )(*parts)

    arrived = lax.all_to_all(dzb, ("y", "core"), split_axis=0, concat_axis=0, tiled=True)
    sums = summed(swap(sums, "core"))
    *theirs, sums = lax.optimization_barrier((*theirs, sums))
    line = [(p % 4) * 2 + p // 4 for p in range(8)]
    turns = [[(line[p], line[(p + d) % 8]) for p in range(8)] for d in range(1, 8)]
    sums = summed([sums] + [lax.ppermute(sums, ("zl", "zh"), route) for route in turns])
    arrived, sums = lax.optimization_barrier((arrived, sums))
    terms = pl.pallas_call(
        weight_term,
        in_specs=[smem] * 3 + [vm] + [free] * 8,
        out_specs=[vm] * 4,
        out_shape=[jax.ShapeDtypeStruct((2 * piece, depth // 4), BF16)] * 4,
        compiler_params=params(24),
        cost_estimate=pl.CostEstimate(flops=1200000000, bytes_accessed=6000000, transcendentals=0),
        name="weight_term",
    )(xi, yi, ci, arrived, *blocks_of, *theirs)
    got = [terms[0]] + [ring(terms[d], "x", d) for d in (1, 2, 3)]
    sums, dz, _ = lax.optimization_barrier((sums, dz, terms[0]))
    parts = spread(sums, "y")
    grad_feats = pl.pallas_call(
        token_grads,
        grid=(3,),
        in_specs=[
            pl.BlockSpec((1, own, PADC), lambda g: (g, 0, 0)),
            pl.BlockSpec((width, depth), lambda g: (g, 0)),
        ],
        out_specs=pl.BlockSpec((own, depth), lambda g: (0, 0)),
        out_shape=jax.ShapeDtypeStruct((own, depth), BF16),
        scratch_shapes=[pltpu.VMEM((own, depth), F32)],
        compiler_params=params(57),
        cost_estimate=pl.CostEstimate(flops=1200000000, bytes_accessed=11000000, transcendentals=0),
        name="token_grads",
    )(dz, w_in.T)
    *parts, grad_feats = lax.optimization_barrier((*parts, grad_feats))
    sums = summed(parts)
    *got, grad_feats = lax.optimization_barrier((*got, grad_feats))
    blocks = pl.pallas_call(
        split_rows,
        in_specs=[vm] * 4,
        out_specs=vm,
        out_shape=jax.ShapeDtypeStruct((32, fblk, piece), BF16),
        scratch_shapes=[pltpu.VMEM((384, depth // 4), F32)],
        compiler_params=params(12),
        name="split_rows",
    )(*got)
    last = lax.all_to_all(blocks, ("zl", "y", "zh"), 0, 0, tiled=True)
    sums, _ = lax.optimization_barrier((sums, blocks))
    parts = spread(sums, "x")
    grad_taps, grad_residues = pl.pallas_call(
        make_close_sums(scale),
        in_specs=[smem] * 3 + [free] * 5,
        out_specs=[vm] * 2,
        out_shape=[
            jax.ShapeDtypeStruct((7, chans), F32),
            jax.ShapeDtypeStruct(rates.shape, F32),
        ],
        scratch_shapes=[pltpu.VMEM((128, 128), F32)],
        compiler_params=params(4),
        name="close_sums",
    )(xi, zi, yi, amp_mine, *parts)
    grad_weight = pl.pallas_call(
        make_close(scale),
        in_specs=[vm],
        out_specs=vm,
        out_shape=jax.ShapeDtypeStruct((fblk, 4 * piece), BF16),
        compiler_params=params(4),
        name="close_weight",
    )(last)
    return (output[None], grad_feats[None], grad_weight, grad_taps, grad_residues)


def solution(mesh):
    fine = Mesh(mesh.devices.reshape(4, 4, 4, 2, 2), ("x", "zl", "y", "zh", "core"))
    ctx = ("x", "zl", "y")
    dp = ("zh", "core")
    in_specs = (P(dp, ctx, None), P(), P(), P(ctx, None), P(ctx, None), P(dp, ctx, None))
    out_specs = (P(dp, ctx, None), P(dp, ctx, None), P(ctx, dp), P(), P(ctx, None))
    return jax.shard_map(local, mesh=fine, in_specs=in_specs, out_specs=out_specs, check_vma=False)
```

```python
import math

import jax
import jax.numpy as jnp
from jax import lax
from jax.experimental import pallas as pl
from jax.experimental.pallas import tpu as pltpu
from jax.sharding import Mesh, PartitionSpec as P

F32 = jnp.float32
BF16 = jnp.bfloat16
HALO = 16
EXT = 136
SEG = 17
PADC = 1024
MODES = 16
NT = (((1,), (1,)), ((), ()))


def rounded(a):
    return a.astype(BF16).astype(F32)


KBLK = 256


def make_project(part):
    def project(*refs):
        if part == 0:
            tp, nexts, feats, wt, acc, tk, wbuf, tsem, sems = refs
        else:
            tp, nexts, before, feats, wt, zq, zk, zv, tk, wbuf, tsem, sems, acc = refs
        steps, chans, _ = wbuf.shape
        low = part * steps * KBLK
        arrival = pltpu.make_async_copy(feats.at[:, pl.ds(low, steps * KBLK)], tk, tsem)
        arrival.start()
        copies = [
            pltpu.make_async_copy(wt.at[:, pl.ds(low + k * KBLK, KBLK)], wbuf.at[k], sems.at[k])
            for k in range(steps)
        ]
        for copy in copies:
            copy.start()
        arrival.wait()
        for k in range(steps):
            wide = slice(low + k * KBLK, low + (k + 1) * KBLK)
            rows = jnp.concatenate(
                [tp[:, wide], tk[:, k * KBLK : (k + 1) * KBLK], nexts[:, wide]], axis=0
            )
            copies[k].wait()
            total = lax.dot_general(rows, wbuf[k], NT, preferred_element_type=F32)
            if k > 0:
                total = acc[...] + total
            elif part == 1:
                total = before[...] + total
            if part == 0 or k < steps - 1:
                acc[...] = total
            else:
                width = chans // 3
                for g, z in enumerate((zq, zk, zv)):
                    z[:, 0:width] = rounded(total[:, g * width : (g + 1) * width])
                    z[:, width:] = jnp.zeros((z.shape[0], PADC - width), F32)

    return project


def mix_taps(taps, zq, zk, zv, mq, mk, mv):
    def tile(ct, carry):
        lanes = pl.ds(pl.multiple_of(ct * 128, 128), 128)
        for g, (z, m) in enumerate(((zq, mq), (zk, mk), (zv, mv))):
            total = taps[g, 0:1, lanes] * z[pl.ds(HALO, EXT), lanes]
            for j in range(1, 7):
                total = total + taps[g, j : j + 1, lanes] * z[pl.ds(HALO - j, EXT), lanes]
            m[:, lanes] = total
        return carry

    lax.fori_loop(0, PADC // 128, tile, 0)


def one_minus_exp(x):
    series = jnp.ones_like(x)
    for n in range(13, 1, -1):
        series = 1.0 - series * x * (1.0 / n)
    return jnp.where(x < 0.5, x * series, 1.0 - jnp.exp(-x))


def prepare(
    feats, cott, rates, residues, conv, head, tail, block, taps, amp, cots,
    held, turn, cbuf, rbuf, sbuf, vbuf, sems,
):
    count = rates.shape[0]
    width, own = cott.shape
    depth = feats.shape[1]
    copies = [
        pltpu.make_async_copy(rates, rbuf, sems.at[0]),
        pltpu.make_async_copy(residues, sbuf, sems.at[1]),
        pltpu.make_async_copy(cott, cbuf, sems.at[2]),
        pltpu.make_async_copy(conv, vbuf, sems.at[3]),
        pltpu.make_async_copy(feats.at[pl.ds(0, HALO)], head.at[:, pl.ds(0, depth)], sems.at[4]),
        pltpu.make_async_copy(feats.at[pl.ds(own - HALO, HALO)], tail, sems.at[5]),
    ]
    for copy in copies:
        copy.start()
    held[...] = jnp.zeros(held.shape, F32)
    turn[...] = jnp.zeros(turn.shape, F32)
    taps[...] = jnp.zeros(taps.shape, F32)
    copies[0].wait()
    copies[1].wait()
    size = jnp.sqrt(one_minus_exp(2.0 * rbuf[...]))
    amp[...] = size
    held[0:count, 0:MODES] = rbuf[...]
    held[0:count, MODES : 2 * MODES] = sbuf[...] * size
    block[...] = held[...].T[0 : 2 * MODES, 0:count]
    copies[2].wait()
    turn[0:width, :] = cbuf[...].astype(F32)
    for c in range(PADC // 128):
        part = turn[c * 128 : (c + 1) * 128, :].T
        cots[:, c * 128 : (c + 1) * 128] = part
        head[:, depth + c * 128 : depth + (c + 1) * 128] = part[0:HALO].astype(BF16)
    copies[3].wait()
    for g in range(3):
        taps[g, 0:7, 0:width] = vbuf[:, g * width : (g + 1) * width]
    for copy in copies[4:]:
        copy.wait()


def placed(me, refs, held, goal):
    wide = refs[0].shape[1]
    total = None
    for d, ref in enumerate(refs):
        held[...] = jnp.zeros(held.shape, F32)
        held[:, 0:wide] = ref[...]
        part = pltpu.roll(held[...], lax.rem(me + (4 - d), 4) * wide, 1)
        total = part if total is None else total + part
    return total[:, 0:goal]


def join_params(me, r0, r1, r2, r3, out, held):
    out[...] = placed(me[0], (r0, r1, r2, r3), held, out.shape[1])


def end_states(me, r0, r1, r2, r3, mq, mk, mv, cown, nexts, cots, rates, gains, es, ends, endb, ut, dt, held):
    joined = placed(me[0], (r0, r1, r2, r3), held, PADC)
    rates[...] = joined[0:MODES]
    gains[...] = joined[MODES : 2 * MODES]
    sub = lax.broadcasted_iota(jnp.int32, (8, 128), 0)
    subf = sub.astype(F32)
    fdepth = jnp.where(sub == 7, 0.0, (EXT - 8 - SEG) - SEG * subf)
    bdepth = jnp.where(sub == 0, 0.0, SEG * subf - 8.0)

    def tile(ct, carry):
        lanes = pl.ds(pl.multiple_of(ct * 128, 128), 128)
        ut[...] = rounded(mk[:, lanes] * mv[:, lanes])
        lane = pl.multiple_of(nexts.shape[1] - PADC + ct * 128, 128)
        after = nexts[:, pl.ds(lane, 128)].astype(F32)
        cot = jnp.concatenate([cown[:, lanes], after[0 : EXT - 128]], axis=0)
        cots[:, lanes] = cot
        dt[...] = rounded(cot * mq[:, lanes])
        rate = rates[:, lanes]
        decay = jnp.exp(-rate)
        for half in range(2):
            ks = range(half * 8, half * 8 + 8)
            al = [jnp.broadcast_to(decay[k : k + 1, :], (8, 128)) for k in ks]
            rl = [jnp.broadcast_to(rate[k : k + 1, :], (8, 128)) for k in ks]
            st = [jnp.zeros((8, 128), F32)] * 8
            snap = st
            for t in range(SEG):
                uv = ut[pl.ds(t, 8, stride=SEG), :]
                st = [a * s + uv for a, s in zip(al, st)]
                if t == 8:
                    snap = st
            for i, k in enumerate(ks):
                es[0, k, :, lanes] = st[i]
                full = jnp.where(sub == 7, snap[i], st[i]) * jnp.exp(-rl[i] * fdepth)
                ends[k : k + 1, lanes] = jnp.sum(full, axis=0, keepdims=True)
            st = [jnp.zeros((8, 128), F32)] * 8
            for t in range(SEG - 1, -1, -1):
                dv = dt[pl.ds(t, 8, stride=SEG), :]
                st = [a * s + dv for a, s in zip(al, st)]
                if t == 8:
                    snap = st
            for i, k in enumerate(ks):
                es[1, k, :, lanes] = st[i]
                full = jnp.where(sub == 0, snap[i], st[i]) * jnp.exp(-rl[i] * bdepth)
                ends[MODES + k : MODES + k + 1, lanes] = jnp.sum(full, axis=0, keepdims=True)
        return carry

    lax.fori_loop(0, PADC // 128, tile, 0)
    endb[...] = ends[...].astype(BF16)


def make_level(span):
    def level(index, own, r1, r2, r3, rates, total, totalb, prefix):
        me = index[0]
        rate = rates[...] * float(span)
        before = jnp.zeros((MODES, PADC), F32)
        after = before
        whole_f = before
        whole_b = before
        for d, ref in enumerate((own, r1, r2, r3)):
            m = lax.rem(me + (4 - d), 4)
            f = ref[0:MODES, :].astype(F32)
            b = ref[MODES : 2 * MODES, :].astype(F32)
            whole_f = whole_f + f * jnp.exp(-rate * (3 - m).astype(F32))
            whole_b = whole_b + b * jnp.exp(-rate * m.astype(F32))
            if d > 0:
                gf = me - 1 - m
                gb = m - me - 1
                wf = jnp.exp(-rate * jnp.maximum(gf, 0).astype(F32))
                wb = jnp.exp(-rate * jnp.maximum(gb, 0).astype(F32))
                before = before + jnp.where(gf >= 0, 1.0, 0.0) * (wf * f)
                after = after + jnp.where(gb >= 0, 1.0, 0.0) * (wb * b)
        prefix[0:MODES, :] = before
        prefix[MODES : 2 * MODES, :] = after
        total[0:MODES, :] = whole_f
        total[MODES : 2 * MODES, :] = whole_b
        totalb[0:MODES, :] = whole_f.astype(BF16)
        totalb[MODES : 2 * MODES, :] = whole_b.astype(BF16)

    return level


def finish(
    zi, yi, zq, zk, zv, mq, mk, mv, es, py, pz, px, taps, rates, reff, cots,
    outt, dz, dzb, sumb, sums, inc, ut, dt, longs, dps, dms, dzt,
):
    own = dz.shape[1]
    rate = rates[...]
    for back in range(2):
        part = pl.ds(back * MODES, MODES)
        near, mid = yi[0], zi[0]
        if back:
            near, mid = 3 - near, 3 - mid
        far = pz[part, :] + jnp.exp(-rate * (4 * own * mid).astype(F32)) * px[part, :]
        inc[part, :] = py[part, :] + jnp.exp(-rate * (own * near).astype(F32)) * far
    sub = lax.broadcasted_iota(jnp.int32, (8, 128), 0)
    ut[...] = rounded(mk[...] * mv[...])
    dt[...] = rounded(cots[...] * mq[...])
    decay = jnp.exp(-rate)
    gain = reff[...]
    for half in range(2):
        ks = range(half * 8, half * 8 + 8)
        al = [jnp.broadcast_to(decay[k : k + 1, :], (8, 128)) for k in ks]
        gl = [jnp.broadcast_to(gain[k : k + 1, :], (8, 128)) for k in ks]
        rl = [jnp.broadcast_to(rate[k : k + 1, :], (8, 128)) for k in ks]
        fwd = []
        bwd = []
        for i, k in enumerate(ks):
            jump = [jnp.exp(-float(SEG * m) * rl[i]) for m in (1, 2, 4)]
            x = jnp.where(sub == 0, inc[k : k + 1, :], pltpu.roll(es[0, k], 1, 0))
            for m, d in zip((1, 2, 4), jump):
                x = x + jnp.where(sub >= m, pltpu.roll(x, m, 0) * d, 0.0)
            fwd.append(x)
            x = jnp.where(
                sub == 7, inc[MODES + k : MODES + k + 1, :], pltpu.roll(es[1, k], 7, 0)
            )
            for m, d in zip((1, 2, 4), jump):
                x = x + jnp.where(sub < 8 - m, pltpu.roll(x, 8 - m, 0) * d, 0.0)
            bwd.append(x)
        gr = [jnp.zeros((8, 128), F32)] * 8
        st = fwd
        for t in range(SEG):
            uv = ut[pl.ds(t, 8, stride=SEG), :]
            dv = dt[pl.ds(t, 8, stride=SEG), :]
            if t >= 9:
                dv = jnp.where(sub < 7, dv, 0.0)
            st = [a * s + uv for a, s in zip(al, st)]
            gr = [q + dv * s for q, s in zip(gr, st)]
            total = sum(g * s for g, s in zip(gl, st))
            if half:
                total = total + longs[pl.ds(t, 8, stride=SEG), :]
            longs[pl.ds(t, 8, stride=SEG), :] = total
        for i, k in enumerate(ks):
            sums[24 + k : 25 + k, :] = jnp.sum(gr[i], axis=0, keepdims=True)
        st = bwd
        for t in range(SEG - 1, -1, -1):
            dv = dt[pl.ds(t, 8, stride=SEG), :]
            st = [a * s + dv for a, s in zip(al, st)]
            total = sum(g * s for g, s in zip(gl, st))
            if half:
                total = total + dps[pl.ds(t, 8, stride=SEG), :]
            dps[pl.ds(t, 8, stride=SEG), :] = total
    long_out = rounded(longs[...])
    dprod = rounded(dps[...])
    outt[...] = (mq[0:own, :] * long_out[0:own]).T.astype(BF16)
    dms[0] = rounded(cots[...] * long_out)
    dms[1] = rounded(dprod * mv[...])
    dms[2] = rounded(dprod * mk[...])
    ct = pl.program_id(0)
    for g, zg in enumerate((zq, zk, zv)):
        mine = dms[g, 0:own, :]
        total = taps[g, 0:1, :] * mine
        sums[8 * g : 8 * g + 1, :] = jnp.sum(mine * zg[pl.ds(HALO, own), :], axis=0, keepdims=True)
        for j in range(1, 7):
            total = total + taps[g, j : j + 1, :] * dms[g, pl.ds(j, own), :]
            sums[8 * g + j : 8 * g + j + 1, :] = jnp.sum(
                mine * zg[pl.ds(HALO - j, own), :], axis=0, keepdims=True
            )
        sums[8 * g + 7 : 8 * g + 8, :] = jnp.zeros((1, 128), F32)
        dz[g] = total.astype(BF16)
        dzt[g, pl.ds(pl.multiple_of(ct * 128, 128), 128), :] = total.T

    sumb[...] = sums[...].astype(BF16)

    @pl.when(ct == pl.num_programs(0) - 1)
    def _():
        piece = dzb.shape[1] // 2
        width = 16 * piece // 3
        for b in range(8):
            both = []
            for h in range(2):
                off = h * 8 * piece + (b % 2) * 4 * piece + (b // 2) * piece
                g, low = off // width, off % width
                size = min(piece, width - low)
                both.append(dzt[g, low : low + size, :])
                if size < piece:
                    both.append(dzt[g + 1, 0 : piece - size, :])
            dzb[b] = jnp.concatenate(both, axis=0).astype(BF16)


def token_grads(dz, wt, out, acc):
    g = pl.program_id(0)
    part = jnp.dot(dz[0, :, 0 : wt.shape[0]], wt[...], preferred_element_type=F32)

    @pl.when(g == 0)
    def _():
        acc[...] = part

    @pl.when(g > 0)
    def _():
        acc[...] += part

    @pl.when(g == pl.num_programs(0) - 1)
    def _():
        out[...] = acc[...].astype(BF16)


def weight_term(xi, yi, ci, arrived, *refs):
    tokens, terms = refs[:8], refs[8:]
    me = yi[0]
    core = ci[0]
    chunk = terms[0].shape[1]
    slots = (me, lax.bitwise_xor(me, 1), 3 - me, lax.bitwise_xor(3 - me, 1))
    pairs = []
    for half, c in ((0, core), (1, 1 - core)):
        for p in (0, 2):
            left = [arrived[slots[p + i] * 2 + c] for i in range(2)]
            pairs.append((jnp.concatenate(left, axis=1), tokens[4 * half + p : 4 * half + p + 2]))
    for d, term in enumerate(terms):
        total = None
        cols = pl.ds(pl.multiple_of(lax.rem(xi[0] + d, 4) * chunk, 128), chunk)
        for left, (one, two) in pairs:
            right = jnp.concatenate([one[:, cols], two[:, cols]], axis=0)
            part = jnp.dot(left, right, preferred_element_type=F32)
            total = part if total is None else total + part
        term[...] = total.astype(BF16)


def split_rows(g0, g1, g2, g3, blocks, turn):
    chans = g0.shape[0]
    fblk = blocks.shape[1]
    piece = blocks.shape[2]
    turn[0:chans, :] = added((g0, g1, g2, g3))
    turn[chans:, :] = jnp.zeros((turn.shape[0] - chans, turn.shape[1]), F32)
    flipped = turn[...].T
    for q in range(16):
        for h in range(2):
            part = flipped[q * fblk : (q + 1) * fblk, h * piece : (h + 1) * piece]
            blocks[2 * q + h] = part.astype(BF16)


def added(refs):
    total = refs[0][...].astype(F32)
    for ref in refs[1:]:
        total = total + ref[...].astype(F32)
    return total


def add_parts(*refs):
    refs[-1][...] = added(refs[:-1]).astype(BF16)


def make_close_sums(scale):
    def close_sums(xi, zi, yi, amp, *refs):
        *parts, grad_taps, grad_res, held = refs
        total = added(parts) * scale
        width = grad_taps.shape[1] // 3
        for g in range(3):
            grad_taps[:, g * width : (g + 1) * width] = total[8 * g : 8 * g + 7, 0:width]
        count = grad_res.shape[0]
        index = (xi[0] * 4 + zi[0]) * 4 + yi[0]
        moved = pltpu.roll(total[24:40, :], lax.rem(PADC - index * count, PADC), 1)
        held[...] = jnp.zeros(held.shape, F32)
        held[0:MODES, :] = moved[:, 0:128]
        grad_res[...] = held[...].T[0:count, 0:MODES] * amp[...]

    return close_sums


def make_close(scale):
    def close_weight(last, out):
        fblk, piece = last.shape[1:]
        for y in range(4):
            total = jnp.zeros((fblk, piece), F32)
            for z in range(4):
                for h in range(2):
                    total = total + last[(z * 4 + y) * 2 + h].astype(F32)
            out[:, y * piece : (y + 1) * piece] = (total * scale).astype(BF16)

    return close_weight


def ring(a, ax, d):
    return lax.ppermute(a, ax, [(i, (i + d) % 4) for i in range(4)])


def params(mb):
    return pltpu.CompilerParams(vmem_limit_bytes=int(mb * 1024 * 1024))


def local(tokens, w_in, conv_taps, residues, rates, cotangent):
    feats = tokens[0]
    cot = cotangent[0]
    own, width = cot.shape
    depth = feats.shape[1]
    chans = 3 * width
    count = 64
    piece = chans // 16
    fblk = depth // count
    ctx = ("x", "zl", "y")
    scale = 1.0 / math.sqrt(4 * count * own)
    smem = pl.BlockSpec(memory_space=pltpu.SMEM)
    vm = pl.BlockSpec(memory_space=pltpu.VMEM)
    free = pl.BlockSpec()
    names = ("x", "zl", "y", "core")
    feats, cot, rates, *where = lax.optimization_barrier(
        (feats, cot, rates, *[lax.axis_index(n) for n in names])
    )
    xi, zi, yi, ci = [w.reshape(1) for w in where]
    anywhere = pl.BlockSpec(memory_space=pl.ANY)
    head, tail, block, taps, amp_mine, cown = pl.pallas_call(
        prepare,
        in_specs=[anywhere] * 5,
        out_specs=[vm] * 6,
        out_shape=[
            jax.ShapeDtypeStruct((HALO, depth + PADC), BF16),
            jax.ShapeDtypeStruct((HALO, depth), BF16),
            jax.ShapeDtypeStruct((2 * MODES, width // count), F32),
            jax.ShapeDtypeStruct((3, 8, PADC), F32),
            jax.ShapeDtypeStruct(rates.shape, F32),
            jax.ShapeDtypeStruct((own, PADC), F32),
        ],
        scratch_shapes=[
            pltpu.VMEM((128, 128), F32),
            pltpu.VMEM((PADC, own), F32),
            pltpu.VMEM((width, own), BF16),
            pltpu.VMEM(rates.shape, F32),
            pltpu.VMEM(rates.shape, F32),
            pltpu.VMEM(conv_taps.shape, F32),
            pltpu.SemaphoreType.DMA((6,)),
        ],
        compiler_params=params(54),
        name="prepare",
    )(feats, cot.T, rates, residues, conv_taps)
    tprev = lax.ppermute(tail, ctx, [(i, i + 1) for i in range(count - 1)])
    nexts = lax.ppermute(head, ctx, [(i, i - 1) for i in range(1, count)])
    ext_rows = own + 2 * HALO
    steps = depth // KBLK // 2

    def project(part, *before):
        many = 3 if part else 1
        shape = (ext_rows, PADC) if part else (ext_rows, chans)
        return pl.pallas_call(
            make_project(part),
            in_specs=[vm] * (2 + part) + [anywhere] * 2,
            out_specs=[vm] * many,
            out_shape=[jax.ShapeDtypeStruct(shape, F32)] * many,
            scratch_shapes=[
                pltpu.VMEM((own, steps * KBLK), BF16),
                pltpu.VMEM((steps, chans, KBLK), BF16),
                pltpu.SemaphoreType.DMA,
                pltpu.SemaphoreType.DMA((steps,)),
                *[pltpu.VMEM((ext_rows, chans), F32)] * part,
            ],
            compiler_params=params((52, 51)[part]),
            cost_estimate=pl.CostEstimate(flops=800000000, bytes_accessed=6000000, transcendentals=0),
            name="project",
        )(tprev, nexts, *before, feats, w_in.T)

    def mixed(*zs):
        return pl.pallas_call(
            mix_taps,
            in_specs=[vm] * 4,
            out_specs=[vm] * 3,
            out_shape=[jax.ShapeDtypeStruct((EXT, PADC), F32)] * 3,
            compiler_params=params(8),
            cost_estimate=pl.CostEstimate(flops=800000000, bytes_accessed=6000000, transcendentals=0),
            name="mix_taps",
        )(taps, *zs)

    held, each = block, width // count
    work = []
    for g, (me, ax) in enumerate(((yi, "y"), (zi, "zl"), (xi, "x"))):
        blocks = [held] + [ring(held, ax, d) for d in (1, 2, 3)]
        work = project(0) if g == 0 else project(1, *work) if g == 1 else mixed(*work)
        *blocks, last_work = lax.optimization_barrier((*blocks, work[-1]))
        work = [*work[:-1], last_work]
        if g == 1:
            zq, zk, zv = work
        if g == 2:
            break
        each = 4 * each
        held = pl.pallas_call(
            join_params,
            in_specs=[smem] + [vm] * 4,
            out_specs=vm,
            out_shape=jax.ShapeDtypeStruct((2 * MODES, each), F32),
            scratch_shapes=[pltpu.VMEM((2 * MODES, 256), F32)],
            compiler_params=params(4),
            name="join_params",
        )(me, *blocks)
    mq, mk, mv = work
    cots, rate, gain, es, ends, endb = pl.pallas_call(
        end_states,
        in_specs=[smem] + [vm] * 9,
        out_specs=[vm] * 6,
        out_shape=[
            jax.ShapeDtypeStruct((EXT, PADC), F32),
            jax.ShapeDtypeStruct((MODES, PADC), F32),
            jax.ShapeDtypeStruct((MODES, PADC), F32),
            jax.ShapeDtypeStruct((2, MODES, 8, PADC), F32),
            jax.ShapeDtypeStruct((2 * MODES, PADC), F32),
            jax.ShapeDtypeStruct((2 * MODES, PADC), BF16),
        ],
        scratch_shapes=[
            pltpu.VMEM((EXT, 128), F32),
            pltpu.VMEM((EXT, 128), F32),
            pltpu.VMEM((2 * MODES, PADC), F32),
        ],
        compiler_params=params(16),
        cost_estimate=pl.CostEstimate(flops=20000000, bytes_accessed=3000000, transcendentals=0),
        name="end_states",
    )(xi, *blocks, mq, mk, mv, cown, nexts)

    prefixes = []
    total, sent = ends, endb
    for me, ax, span in ((yi, "y", own), (zi, "zl", 4 * own), (xi, "x", 16 * own)):
        near = [ring(sent, ax, d) for d in (1, 2, 3)]
        total, sent, prefix = pl.pallas_call(
            make_level(span),
            in_specs=[smem] + [vm] * 5,
            out_specs=[vm] * 3,
            out_shape=[
                jax.ShapeDtypeStruct((2 * MODES, PADC), F32),
                jax.ShapeDtypeStruct((2 * MODES, PADC), BF16),
                jax.ShapeDtypeStruct((2 * MODES, PADC), F32),
            ],
            compiler_params=params(8),
            name="level",
        )(me, total, *near, rate)
        prefixes.append(prefix)
        if ax == "zl":
            mine, _ = lax.optimization_barrier((feats, sent))
            pair = lax.ppermute(mine, "y", [(i, i ^ 1) for i in range(4)])
            opposite = lax.ppermute(mine, "y", [(i, 3 - i) for i in range(4)])
    pair, opposite, prefixes[2] = lax.optimization_barrier((pair, opposite, prefixes[2]))
    far = lax.ppermute(pair, "y", [(i, 3 - i) for i in range(4)])

    def swapped(a):
        return lax.ppermute(a, "core", [(0, 1), (1, 0)])

    def tiles(shape):
        lead = len(shape) - 1
        return pl.BlockSpec(shape, lambda k: (0,) * lead + (k,))

    outt, dz, dzb, sums = pl.pallas_call(
        finish,
        grid=(PADC // 128,),
        in_specs=[
            smem,
            smem,
            *[tiles((ext_rows, 128))] * 3,
            *[tiles((EXT, 128))] * 3,
            tiles((2, MODES, 8, 128)),
            tiles((2 * MODES, 128)),
            tiles((2 * MODES, 128)),
            tiles((2 * MODES, 128)),
            tiles((3, 8, 128)),
            tiles((MODES, 128)),
            tiles((MODES, 128)),
            tiles((EXT, 128)),
        ],
        out_specs=[
            pl.BlockSpec((128, own), lambda k: (k, 0)),
            tiles((3, own, 128)),
            pl.BlockSpec((8, 2 * piece, own), lambda k: (0, 0, 0)),
            tiles((40, 128)),
        ],
        out_shape=[
            jax.ShapeDtypeStruct((width, own), BF16),
            jax.ShapeDtypeStruct((3, own, PADC), BF16),
            jax.ShapeDtypeStruct((8, 2 * piece, own), BF16),
            jax.ShapeDtypeStruct((40, PADC), BF16),
        ],
        scratch_shapes=[
            pltpu.VMEM((40, 128), F32),
            pltpu.VMEM((2 * MODES, 128), F32),
            pltpu.VMEM((EXT, 128), F32),
            pltpu.VMEM((EXT, 128), F32),
            pltpu.VMEM((EXT, 128), F32),
            pltpu.VMEM((EXT, 128), F32),
            pltpu.VMEM((3, EXT, 128), F32),
            pltpu.VMEM((3, PADC, own), F32),
        ],
        compiler_params=params(50),
        cost_estimate=pl.CostEstimate(flops=200000000, bytes_accessed=10000000, transcendentals=0),
        name="finish",
    )(zi, yi, zq, zk, zv, mq, mk, mv, es, *prefixes, taps, rate, gain, cots)
    output = outt.T
    blocks_of = [mine, pair, opposite, far]
    mine, pair, opposite, _ = lax.optimization_barrier((mine, pair, opposite, sums))
    blocks_of = [mine, pair, opposite, far]
    theirs = [swapped(a) for a in blocks_of]

    def spread(a, ax):
        return [a] + [ring(a, ax, d) for d in (1, 2, 3)]

    def swap(a, ax):
        return [a, lax.ppermute(a, ax, [(0, 1), (1, 0)])]

    def summed(parts):
        return pl.pallas_call(
            add_parts,
            in_specs=[free] * len(parts),
            out_specs=free,
            out_shape=jax.ShapeDtypeStruct((40, PADC), BF16),
            compiler_params=params(4),
            name="add_parts",
        )(*parts)

    arrived = lax.all_to_all(dzb, ("y", "core"), split_axis=0, concat_axis=0, tiled=True)
    sums = summed(swap(sums, "core"))
    *theirs, sums = lax.optimization_barrier((*theirs, sums))
    parts = spread(sums, "zl")
    grad_feats = pl.pallas_call(
        token_grads,
        grid=(3,),
        in_specs=[
            pl.BlockSpec((1, own, PADC), lambda g: (g, 0, 0)),
            pl.BlockSpec((width, depth), lambda g: (g, 0)),
        ],
        out_specs=pl.BlockSpec((own, depth), lambda g: (0, 0)),
        out_shape=jax.ShapeDtypeStruct((own, depth), BF16),
        scratch_shapes=[pltpu.VMEM((own, depth), F32)],
        compiler_params=params(57),
        cost_estimate=pl.CostEstimate(flops=1200000000, bytes_accessed=11000000, transcendentals=0),
        name="token_grads",
    )(dz, w_in.T)
    *parts, grad_feats = lax.optimization_barrier((*parts, grad_feats))
    sums = summed(parts)
    arrived, sums = lax.optimization_barrier((arrived, sums))
    terms = pl.pallas_call(
        weight_term,
        in_specs=[smem] * 3 + [vm] + [free] * 8,
        out_specs=[vm] * 4,
        out_shape=[jax.ShapeDtypeStruct((2 * piece, depth // 4), BF16)] * 4,
        compiler_params=params(24),
        cost_estimate=pl.CostEstimate(flops=1200000000, bytes_accessed=6000000, transcendentals=0),
        name="weight_term",
    )(xi, yi, ci, arrived, *blocks_of, *theirs)
    got = [terms[0]] + [ring(terms[d], "x", d) for d in (1, 2, 3)]
    sums, _ = lax.optimization_barrier((sums, terms[0]))
    sums = summed(swap(summed(spread(sums, "y")), "zh"))
    *got, sums = lax.optimization_barrier((*got, sums))
    blocks = pl.pallas_call(
        split_rows,
        in_specs=[vm] * 4,
        out_specs=vm,
        out_shape=jax.ShapeDtypeStruct((32, fblk, piece), BF16),
        scratch_shapes=[pltpu.VMEM((384, depth // 4), F32)],
        compiler_params=params(12),
        name="split_rows",
    )(*got)
    last = lax.all_to_all(blocks, ("zl", "y", "zh"), 0, 0, tiled=True)
    sums, _ = lax.optimization_barrier((sums, blocks))
    parts = spread(sums, "x")
    grad_taps, grad_residues = pl.pallas_call(
        make_close_sums(scale),
        in_specs=[smem] * 3 + [free] * 5,
        out_specs=[vm] * 2,
        out_shape=[
            jax.ShapeDtypeStruct((7, chans), F32),
            jax.ShapeDtypeStruct(rates.shape, F32),
        ],
        scratch_shapes=[pltpu.VMEM((128, 128), F32)],
        compiler_params=params(4),
        name="close_sums",
    )(xi, zi, yi, amp_mine, *parts)
    grad_weight = pl.pallas_call(
        make_close(scale),
        in_specs=[vm],
        out_specs=vm,
        out_shape=jax.ShapeDtypeStruct((fblk, 4 * piece), BF16),
        compiler_params=params(4),
        name="close_weight",
    )(last)
    return (output[None], grad_feats[None], grad_weight, grad_taps, grad_residues)


def solution(mesh):
    fine = Mesh(mesh.devices.reshape(4, 4, 4, 2, 2), ("x", "zl", "y", "zh", "core"))
    ctx = ("x", "zl", "y")
    dp = ("zh", "core")
    in_specs = (P(dp, ctx, None), P(), P(), P(ctx, None), P(ctx, None), P(dp, ctx, None))
    out_specs = (P(dp, ctx, None), P(dp, ctx, None), P(ctx, dp), P(), P(ctx, None))
    return jax.shard_map(local, mesh=fine, in_specs=in_specs, out_specs=out_specs, check_vma=False)
```

```python
import math

import jax
import jax.numpy as jnp
from jax import lax
from jax.experimental import pallas as pl
from jax.experimental.pallas import tpu as pltpu
from jax.sharding import Mesh, PartitionSpec as P

F32 = jnp.float32
BF16 = jnp.bfloat16
HALO = 16
EXT = 136
SEG = 17
PADC = 1024
MODES = 16
NT = (((1,), (1,)), ((), ()))


def rounded(a):
    return a.astype(BF16).astype(F32)


KBLK = 256


def make_project(part):
    def project(*refs):
        if part == 0:
            tp, nexts, feats, wt, acc, tk, wbuf, tsem, sems = refs
        else:
            tp, nexts, before, feats, wt, zq, zk, zv, tk, wbuf, tsem, sems, acc = refs
        steps, chans, _ = wbuf.shape
        low = part * steps * KBLK
        arrival = pltpu.make_async_copy(feats.at[:, pl.ds(low, steps * KBLK)], tk, tsem)
        arrival.start()
        copies = [
            pltpu.make_async_copy(wt.at[:, pl.ds(low + k * KBLK, KBLK)], wbuf.at[k], sems.at[k])
            for k in range(steps)
        ]
        for copy in copies:
            copy.start()
        arrival.wait()
        for k in range(steps):
            wide = slice(low + k * KBLK, low + (k + 1) * KBLK)
            rows = jnp.concatenate(
                [tp[:, wide], tk[:, k * KBLK : (k + 1) * KBLK], nexts[:, wide]], axis=0
            )
            copies[k].wait()
            total = lax.dot_general(rows, wbuf[k], NT, preferred_element_type=F32)
            if k > 0:
                total = acc[...] + total
            elif part == 1:
                total = before[...] + total
            if part == 0 or k < steps - 1:
                acc[...] = total
            else:
                width = chans // 3
                for g, z in enumerate((zq, zk, zv)):
                    z[:, 0:width] = rounded(total[:, g * width : (g + 1) * width])
                    z[:, width:] = jnp.zeros((z.shape[0], PADC - width), F32)

    return project


def mix_taps(taps, zq, zk, zv, mq, mk, mv):
    def tile(ct, carry):
        lanes = pl.ds(pl.multiple_of(ct * 128, 128), 128)
        for g, (z, m) in enumerate(((zq, mq), (zk, mk), (zv, mv))):
            total = taps[g, 0:1, lanes] * z[pl.ds(HALO, EXT), lanes]
            for j in range(1, 7):
                total = total + taps[g, j : j + 1, lanes] * z[pl.ds(HALO - j, EXT), lanes]
            m[:, lanes] = total
        return carry

    lax.fori_loop(0, PADC // 128, tile, 0)


def one_minus_exp(x):
    series = jnp.ones_like(x)
    for n in range(13, 1, -1):
        series = 1.0 - series * x * (1.0 / n)
    return jnp.where(x < 0.5, x * series, 1.0 - jnp.exp(-x))


def prepare(
    feats, cott, rates, residues, conv, head, tail, block, taps, amp, cots,
    held, turn, cbuf, rbuf, sbuf, vbuf, sems,
):
    count = rates.shape[0]
    width, own = cott.shape
    depth = feats.shape[1]
    copies = [
        pltpu.make_async_copy(rates, rbuf, sems.at[0]),
        pltpu.make_async_copy(residues, sbuf, sems.at[1]),
        pltpu.make_async_copy(cott, cbuf, sems.at[2]),
        pltpu.make_async_copy(conv, vbuf, sems.at[3]),
        pltpu.make_async_copy(feats.at[pl.ds(0, HALO)], head.at[:, pl.ds(0, depth)], sems.at[4]),
        pltpu.make_async_copy(feats.at[pl.ds(own - HALO, HALO)], tail, sems.at[5]),
    ]
    for copy in copies:
        copy.start()
    held[...] = jnp.zeros(held.shape, F32)
    turn[...] = jnp.zeros(turn.shape, F32)
    taps[...] = jnp.zeros(taps.shape, F32)
    copies[0].wait()
    copies[1].wait()
    size = jnp.sqrt(one_minus_exp(2.0 * rbuf[...]))
    amp[...] = size
    held[0:count, 0:MODES] = rbuf[...]
    held[0:count, MODES : 2 * MODES] = sbuf[...] * size
    block[...] = held[...].T[0 : 2 * MODES, 0:count]
    copies[2].wait()
    turn[0:width, :] = cbuf[...].astype(F32)
    for c in range(PADC // 128):
        part = turn[c * 128 : (c + 1) * 128, :].T
        cots[:, c * 128 : (c + 1) * 128] = part
        head[:, depth + c * 128 : depth + (c + 1) * 128] = part[0:HALO].astype(BF16)
    copies[3].wait()
    for g in range(3):
        taps[g, 0:7, 0:width] = vbuf[:, g * width : (g + 1) * width]
    for copy in copies[4:]:
        copy.wait()


def placed(me, refs, held, goal):
    wide = refs[0].shape[1]
    total = None
    for d, ref in enumerate(refs):
        held[...] = jnp.zeros(held.shape, F32)
        held[:, 0:wide] = ref[...]
        part = pltpu.roll(held[...], lax.rem(me + (4 - d), 4) * wide, 1)
        total = part if total is None else total + part
    return total[:, 0:goal]


def join_params(me, r0, r1, r2, r3, out, held):
    out[...] = placed(me[0], (r0, r1, r2, r3), held, out.shape[1])


def end_states(me, r0, r1, r2, r3, mq, mk, mv, cown, nexts, cots, rates, gains, es, ends, endb, ut, dt, held):
    joined = placed(me[0], (r0, r1, r2, r3), held, PADC)
    rates[...] = joined[0:MODES]
    gains[...] = joined[MODES : 2 * MODES]
    sub = lax.broadcasted_iota(jnp.int32, (8, 128), 0)
    subf = sub.astype(F32)
    fdepth = jnp.where(sub == 7, 0.0, (EXT - 8 - SEG) - SEG * subf)
    bdepth = jnp.where(sub == 0, 0.0, SEG * subf - 8.0)

    def tile(ct, carry):
        lanes = pl.ds(pl.multiple_of(ct * 128, 128), 128)
        ut[...] = rounded(mk[:, lanes] * mv[:, lanes])
        lane = pl.multiple_of(nexts.shape[1] - PADC + ct * 128, 128)
        after = nexts[:, pl.ds(lane, 128)].astype(F32)
        cot = jnp.concatenate([cown[:, lanes], after[0 : EXT - 128]], axis=0)
        cots[:, lanes] = cot
        dt[...] = rounded(cot * mq[:, lanes])
        rate = rates[:, lanes]
        decay = jnp.exp(-rate)
        for half in range(2):
            ks = range(half * 8, half * 8 + 8)
            al = [jnp.broadcast_to(decay[k : k + 1, :], (8, 128)) for k in ks]
            rl = [jnp.broadcast_to(rate[k : k + 1, :], (8, 128)) for k in ks]
            st = [jnp.zeros((8, 128), F32)] * 8
            snap = st
            for t in range(SEG):
                uv = ut[pl.ds(t, 8, stride=SEG), :]
                st = [a * s + uv for a, s in zip(al, st)]
                if t == 8:
                    snap = st
            for i, k in enumerate(ks):
                es[0, k, :, lanes] = st[i]
                full = jnp.where(sub == 7, snap[i], st[i]) * jnp.exp(-rl[i] * fdepth)
                ends[k : k + 1, lanes] = jnp.sum(full, axis=0, keepdims=True)
            st = [jnp.zeros((8, 128), F32)] * 8
            for t in range(SEG - 1, -1, -1):
                dv = dt[pl.ds(t, 8, stride=SEG), :]
                st = [a * s + dv for a, s in zip(al, st)]
                if t == 8:
                    snap = st
            for i, k in enumerate(ks):
                es[1, k, :, lanes] = st[i]
                full = jnp.where(sub == 0, snap[i], st[i]) * jnp.exp(-rl[i] * bdepth)
                ends[MODES + k : MODES + k + 1, lanes] = jnp.sum(full, axis=0, keepdims=True)
        return carry

    lax.fori_loop(0, PADC // 128, tile, 0)
    endb[...] = ends[...].astype(BF16)


def make_level(span):
    def level(index, own, r1, r2, r3, rates, total, totalb, prefix):
        me = index[0]
        rate = rates[...] * float(span)
        before = jnp.zeros((MODES, PADC), F32)
        after = before
        whole_f = before
        whole_b = before
        for d, ref in enumerate((own, r1, r2, r3)):
            m = lax.rem(me + (4 - d), 4)
            f = ref[0:MODES, :].astype(F32)
            b = ref[MODES : 2 * MODES, :].astype(F32)
            whole_f = whole_f + f * jnp.exp(-rate * (3 - m).astype(F32))
            whole_b = whole_b + b * jnp.exp(-rate * m.astype(F32))
            if d > 0:
                gf = me - 1 - m
                gb = m - me - 1
                wf = jnp.exp(-rate * jnp.maximum(gf, 0).astype(F32))
                wb = jnp.exp(-rate * jnp.maximum(gb, 0).astype(F32))
                before = before + jnp.where(gf >= 0, 1.0, 0.0) * (wf * f)
                after = after + jnp.where(gb >= 0, 1.0, 0.0) * (wb * b)
        prefix[0:MODES, :] = before
        prefix[MODES : 2 * MODES, :] = after
        total[0:MODES, :] = whole_f
        total[MODES : 2 * MODES, :] = whole_b
        totalb[0:MODES, :] = whole_f.astype(BF16)
        totalb[MODES : 2 * MODES, :] = whole_b.astype(BF16)

    return level


def finish(
    zi, yi, zq, zk, zv, mq, mk, mv, es, py, pz, px, taps, rates, reff, cots,
    outt, dz, dzb, sumb, sums, inc, ut, dt, longs, dps, dms, dzt,
):
    own = dz.shape[1]
    rate = rates[...]
    for back in range(2):
        part = pl.ds(back * MODES, MODES)
        near, mid = yi[0], zi[0]
        if back:
            near, mid = 3 - near, 3 - mid
        far = pz[part, :] + jnp.exp(-rate * (4 * own * mid).astype(F32)) * px[part, :]
        inc[part, :] = py[part, :] + jnp.exp(-rate * (own * near).astype(F32)) * far
    sub = lax.broadcasted_iota(jnp.int32, (8, 128), 0)
    ut[...] = rounded(mk[...] * mv[...])
    dt[...] = rounded(cots[...] * mq[...])
    decay = jnp.exp(-rate)
    gain = reff[...]
    for half in range(2):
        ks = range(half * 8, half * 8 + 8)
        al = [jnp.broadcast_to(decay[k : k + 1, :], (8, 128)) for k in ks]
        gl = [jnp.broadcast_to(gain[k : k + 1, :], (8, 128)) for k in ks]
        rl = [jnp.broadcast_to(rate[k : k + 1, :], (8, 128)) for k in ks]
        fwd = []
        bwd = []
        for i, k in enumerate(ks):
            jump = [jnp.exp(-float(SEG * m) * rl[i]) for m in (1, 2, 4)]
            x = jnp.where(sub == 0, inc[k : k + 1, :], pltpu.roll(es[0, k], 1, 0))
            for m, d in zip((1, 2, 4), jump):
                x = x + jnp.where(sub >= m, pltpu.roll(x, m, 0) * d, 0.0)
            fwd.append(x)
            x = jnp.where(
                sub == 7, inc[MODES + k : MODES + k + 1, :], pltpu.roll(es[1, k], 7, 0)
            )
            for m, d in zip((1, 2, 4), jump):
                x = x + jnp.where(sub < 8 - m, pltpu.roll(x, 8 - m, 0) * d, 0.0)
            bwd.append(x)
        gr = [jnp.zeros((8, 128), F32)] * 8
        st = fwd
        for t in range(SEG):
            uv = ut[pl.ds(t, 8, stride=SEG), :]
            dv = dt[pl.ds(t, 8, stride=SEG), :]
            if t >= 9:
                dv = jnp.where(sub < 7, dv, 0.0)
            st = [a * s + uv for a, s in zip(al, st)]
            gr = [q + dv * s for q, s in zip(gr, st)]
            total = sum(g * s for g, s in zip(gl, st))
            if half:
                total = total + longs[pl.ds(t, 8, stride=SEG), :]
            longs[pl.ds(t, 8, stride=SEG), :] = total
        for i, k in enumerate(ks):
            sums[24 + k : 25 + k, :] = jnp.sum(gr[i], axis=0, keepdims=True)
        st = bwd
        for t in range(SEG - 1, -1, -1):
            dv = dt[pl.ds(t, 8, stride=SEG), :]
            st = [a * s + dv for a, s in zip(al, st)]
            total = sum(g * s for g, s in zip(gl, st))
            if half:
                total = total + dps[pl.ds(t, 8, stride=SEG), :]
            dps[pl.ds(t, 8, stride=SEG), :] = total
    long_out = rounded(longs[...])
    dprod = rounded(dps[...])
    outt[...] = (mq[0:own, :] * long_out[0:own]).T.astype(BF16)
    dms[0] = rounded(cots[...] * long_out)
    dms[1] = rounded(dprod * mv[...])
    dms[2] = rounded(dprod * mk[...])
    ct = pl.program_id(0)
    for g, zg in enumerate((zq, zk, zv)):
        mine = dms[g, 0:own, :]
        total = taps[g, 0:1, :] * mine
        sums[8 * g : 8 * g + 1, :] = jnp.sum(mine * zg[pl.ds(HALO, own), :], axis=0, keepdims=True)
        for j in range(1, 7):
            total = total + taps[g, j : j + 1, :] * dms[g, pl.ds(j, own), :]
            sums[8 * g + j : 8 * g + j + 1, :] = jnp.sum(
                mine * zg[pl.ds(HALO - j, own), :], axis=0, keepdims=True
            )
        sums[8 * g + 7 : 8 * g + 8, :] = jnp.zeros((1, 128), F32)
        dz[g] = total.astype(BF16)
        dzt[g, pl.ds(pl.multiple_of(ct * 128, 128), 128), :] = total.T

    sumb[...] = sums[...].astype(BF16)

    @pl.when(ct == pl.num_programs(0) - 1)
    def _():
        piece = dzb.shape[1] // 2
        width = 16 * piece // 3
        for b in range(8):
            both = []
            for h in range(2):
                off = h * 8 * piece + (b % 2) * 4 * piece + (b // 2) * piece
                g, low = off // width, off % width
                size = min(piece, width - low)
                both.append(dzt[g, low : low + size, :])
                if size < piece:
                    both.append(dzt[g + 1, 0 : piece - size, :])
            dzb[b] = jnp.concatenate(both, axis=0).astype(BF16)


def token_grads(dz, wt, out, acc):
    g = pl.program_id(0)
    part = jnp.dot(dz[0, :, 0 : wt.shape[0]], wt[...], preferred_element_type=F32)

    @pl.when(g == 0)
    def _():
        acc[...] = part

    @pl.when(g > 0)
    def _():
        acc[...] += part

    @pl.when(g == pl.num_programs(0) - 1)
    def _():
        out[...] = acc[...].astype(BF16)


def weight_term(xi, yi, ci, arrived, *refs):
    tokens, terms = refs[:8], refs[8:]
    me = yi[0]
    core = ci[0]
    chunk = terms[0].shape[1]
    slots = (me, lax.bitwise_xor(me, 1), 3 - me, lax.bitwise_xor(3 - me, 1))
    pairs = []
    for half, c in ((0, core), (1, 1 - core)):
        for p in (0, 2):
            left = [arrived[slots[p + i] * 2 + c] for i in range(2)]
            pairs.append((jnp.concatenate(left, axis=1), tokens[4 * half + p : 4 * half + p + 2]))
    for d, term in enumerate(terms):
        total = None
        cols = pl.ds(pl.multiple_of(lax.rem(xi[0] + d, 4) * chunk, 128), chunk)
        for left, (one, two) in pairs:
            right = jnp.concatenate([one[:, cols], two[:, cols]], axis=0)
            part = jnp.dot(left, right, preferred_element_type=F32)
            total = part if total is None else total + part
        term[...] = total.astype(BF16)


def split_rows(g0, g1, g2, g3, blocks, turn):
    chans = g0.shape[0]
    fblk = blocks.shape[1]
    piece = blocks.shape[2]
    turn[0:chans, :] = added((g0, g1, g2, g3))
    turn[chans:, :] = jnp.zeros((turn.shape[0] - chans, turn.shape[1]), F32)
    flipped = turn[...].T
    for q in range(16):
        for h in range(2):
            part = flipped[q * fblk : (q + 1) * fblk, h * piece : (h + 1) * piece]
            blocks[2 * q + h] = part.astype(BF16)


def added(refs):
    total = refs[0][...].astype(F32)
    for ref in refs[1:]:
        total = total + ref[...].astype(F32)
    return total


def add_parts(*refs):
    refs[-1][...] = added(refs[:-1]).astype(BF16)


def make_close_sums(scale):
    def close_sums(xi, zi, yi, amp, *refs):
        *parts, grad_taps, grad_res, held = refs
        total = added(parts) * scale
        width = grad_taps.shape[1] // 3
        for g in range(3):
            grad_taps[:, g * width : (g + 1) * width] = total[8 * g : 8 * g + 7, 0:width]
        count = grad_res.shape[0]
        index = (xi[0] * 4 + zi[0]) * 4 + yi[0]
        moved = pltpu.roll(total[24:40, :], lax.rem(PADC - index * count, PADC), 1)
        held[...] = jnp.zeros(held.shape, F32)
        held[0:MODES, :] = moved[:, 0:128]
        grad_res[...] = held[...].T[0:count, 0:MODES] * amp[...]

    return close_sums


def make_close(scale):
    def close_weight(last, out):
        fblk, piece = last.shape[1:]
        for y in range(4):
            total = jnp.zeros((fblk, piece), F32)
            for z in range(4):
                for h in range(2):
                    total = total + last[(z * 4 + y) * 2 + h].astype(F32)
            out[:, y * piece : (y + 1) * piece] = (total * scale).astype(BF16)

    return close_weight


def ring(a, ax, d):
    return lax.ppermute(a, ax, [(i, (i + d) % 4) for i in range(4)])


def params(mb):
    return pltpu.CompilerParams(vmem_limit_bytes=int(mb * 1024 * 1024))


def local(tokens, w_in, conv_taps, residues, rates, cotangent):
    feats = tokens[0]
    cot = cotangent[0]
    own, width = cot.shape
    depth = feats.shape[1]
    chans = 3 * width
    count = 64
    piece = chans // 16
    fblk = depth // count
    ctx = ("x", "zl", "y")
    scale = 1.0 / math.sqrt(4 * count * own)
    smem = pl.BlockSpec(memory_space=pltpu.SMEM)
    vm = pl.BlockSpec(memory_space=pltpu.VMEM)
    free = pl.BlockSpec()
    names = ("x", "zl", "y", "core")
    feats, cot, rates, *where = lax.optimization_barrier(
        (feats, cot, rates, *[lax.axis_index(n) for n in names])
    )
    xi, zi, yi, ci = [w.reshape(1) for w in where]
    anywhere = pl.BlockSpec(memory_space=pl.ANY)
    head, tail, block, taps, amp_mine, cown = pl.pallas_call(
        prepare,
        in_specs=[anywhere] * 5,
        out_specs=[vm] * 6,
        out_shape=[
            jax.ShapeDtypeStruct((HALO, depth + PADC), BF16),
            jax.ShapeDtypeStruct((HALO, depth), BF16),
            jax.ShapeDtypeStruct((2 * MODES, width // count), F32),
            jax.ShapeDtypeStruct((3, 8, PADC), F32),
            jax.ShapeDtypeStruct(rates.shape, F32),
            jax.ShapeDtypeStruct((own, PADC), F32),
        ],
        scratch_shapes=[
            pltpu.VMEM((128, 128), F32),
            pltpu.VMEM((PADC, own), F32),
            pltpu.VMEM((width, own), BF16),
            pltpu.VMEM(rates.shape, F32),
            pltpu.VMEM(rates.shape, F32),
            pltpu.VMEM(conv_taps.shape, F32),
            pltpu.SemaphoreType.DMA((6,)),
        ],
        compiler_params=params(54),
        name="prepare",
    )(feats, cot.T, rates, residues, conv_taps)
    ext_rows = own + 2 * HALO
    steps = depth // KBLK // 2

    def project(part, *before):
        many = 3 if part else 1
        shape = (ext_rows, PADC) if part else (ext_rows, chans)
        return pl.pallas_call(
            make_project(part),
            in_specs=[vm] * (2 + part) + [anywhere] * 2,
            out_specs=[vm] * many,
            out_shape=[jax.ShapeDtypeStruct(shape, F32)] * many,
            scratch_shapes=[
                pltpu.VMEM((own, steps * KBLK), BF16),
                pltpu.VMEM((steps, chans, KBLK), BF16),
                pltpu.SemaphoreType.DMA,
                pltpu.SemaphoreType.DMA((steps,)),
                *[pltpu.VMEM((ext_rows, chans), F32)] * part,
            ],
            compiler_params=params((52, 51)[part]),
            cost_estimate=pl.CostEstimate(flops=800000000, bytes_accessed=6000000, transcendentals=0),
            name="project",
        )(tprev, nexts, *before, feats, w_in.T)

    def mixed(*zs):
        return pl.pallas_call(
            mix_taps,
            in_specs=[vm] * 4,
            out_specs=[vm] * 3,
            out_shape=[jax.ShapeDtypeStruct((EXT, PADC), F32)] * 3,
            compiler_params=params(8),
            cost_estimate=pl.CostEstimate(flops=800000000, bytes_accessed=6000000, transcendentals=0),
            name="mix_taps",
        )(taps, *zs)

    held, each = block, width // count
    work = []
    for g, (me, ax) in enumerate(((yi, "y"), (zi, "zl"), (xi, "x"))):
        if g == 1:
            head, tail, held = lax.optimization_barrier((head, tail, held))
            tprev = lax.ppermute(tail, ctx, [(i, i + 1) for i in range(count - 1)])
            nexts = lax.ppermute(head, ctx, [(i, i - 1) for i in range(1, count)])
        blocks = [held] + [ring(held, ax, d) for d in (1, 2, 3)]
        if g > 0:
            work = project(g - 1, *work)
            *blocks, last_work = lax.optimization_barrier((*blocks, work[-1]))
            work = [*work[:-1], last_work]
        if g == 2:
            break
        each = 4 * each
        held = pl.pallas_call(
            join_params,
            in_specs=[smem] + [vm] * 4,
            out_specs=vm,
            out_shape=jax.ShapeDtypeStruct((2 * MODES, each), F32),
            scratch_shapes=[pltpu.VMEM((2 * MODES, 256), F32)],
            compiler_params=params(4),
            name="join_params",
        )(me, *blocks)
    zq, zk, zv = work
    mq, mk, mv = mixed(*work)
    cots, rate, gain, es, ends, endb = pl.pallas_call(
        end_states,
        in_specs=[smem] + [vm] * 9,
        out_specs=[vm] * 6,
        out_shape=[
            jax.ShapeDtypeStruct((EXT, PADC), F32),
            jax.ShapeDtypeStruct((MODES, PADC), F32),
            jax.ShapeDtypeStruct((MODES, PADC), F32),
            jax.ShapeDtypeStruct((2, MODES, 8, PADC), F32),
            jax.ShapeDtypeStruct((2 * MODES, PADC), F32),
            jax.ShapeDtypeStruct((2 * MODES, PADC), BF16),
        ],
        scratch_shapes=[
            pltpu.VMEM((EXT, 128), F32),
            pltpu.VMEM((EXT, 128), F32),
            pltpu.VMEM((2 * MODES, PADC), F32),
        ],
        compiler_params=params(16),
        cost_estimate=pl.CostEstimate(flops=20000000, bytes_accessed=3000000, transcendentals=0),
        name="end_states",
    )(xi, *blocks, mq, mk, mv, cown, nexts)

    prefixes = []
    total, sent = ends, endb
    for me, ax, span in ((yi, "y", own), (zi, "zl", 4 * own), (xi, "x", 16 * own)):
        near = [ring(sent, ax, d) for d in (1, 2, 3)]
        total, sent, prefix = pl.pallas_call(
            make_level(span),
            in_specs=[smem] + [vm] * 5,
            out_specs=[vm] * 3,
            out_shape=[
                jax.ShapeDtypeStruct((2 * MODES, PADC), F32),
                jax.ShapeDtypeStruct((2 * MODES, PADC), BF16),
                jax.ShapeDtypeStruct((2 * MODES, PADC), F32),
            ],
            compiler_params=params(8),
            name="level",
        )(me, total, *near, rate)
        prefixes.append(prefix)
        if ax == "zl":
            mine, _ = lax.optimization_barrier((feats, sent))
            pair = lax.ppermute(mine, "y", [(i, i ^ 1) for i in range(4)])
            opposite = lax.ppermute(mine, "y", [(i, 3 - i) for i in range(4)])
    pair, opposite, prefixes[2] = lax.optimization_barrier((pair, opposite, prefixes[2]))
    far = lax.ppermute(pair, "y", [(i, 3 - i) for i in range(4)])

    def swapped(a):
        return lax.ppermute(a, "core", [(0, 1), (1, 0)])

    def tiles(shape):
        lead = len(shape) - 1
        return pl.BlockSpec(shape, lambda k: (0,) * lead + (k,))

    outt, dz, dzb, sums = pl.pallas_call(
        finish,
        grid=(PADC // 128,),
        in_specs=[
            smem,
            smem,
            *[tiles((ext_rows, 128))] * 3,
            *[tiles((EXT, 128))] * 3,
            tiles((2, MODES, 8, 128)),
            tiles((2 * MODES, 128)),
            tiles((2 * MODES, 128)),
            tiles((2 * MODES, 128)),
            tiles((3, 8, 128)),
            tiles((MODES, 128)),
            tiles((MODES, 128)),
            tiles((EXT, 128)),
        ],
        out_specs=[
            pl.BlockSpec((128, own), lambda k: (k, 0)),
            tiles((3, own, 128)),
            pl.BlockSpec((8, 2 * piece, own), lambda k: (0, 0, 0)),
            tiles((40, 128)),
        ],
        out_shape=[
            jax.ShapeDtypeStruct((width, own), BF16),
            jax.ShapeDtypeStruct((3, own, PADC), BF16),
            jax.ShapeDtypeStruct((8, 2 * piece, own), BF16),
            jax.ShapeDtypeStruct((40, PADC), BF16),
        ],
        scratch_shapes=[
            pltpu.VMEM((40, 128), F32),
            pltpu.VMEM((2 * MODES, 128), F32),
            pltpu.VMEM((EXT, 128), F32),
            pltpu.VMEM((EXT, 128), F32),
            pltpu.VMEM((EXT, 128), F32),
            pltpu.VMEM((EXT, 128), F32),
            pltpu.VMEM((3, EXT, 128), F32),
            pltpu.VMEM((3, PADC, own), F32),
        ],
        compiler_params=params(50),
        cost_estimate=pl.CostEstimate(flops=200000000, bytes_accessed=10000000, transcendentals=0),
        name="finish",
    )(zi, yi, zq, zk, zv, mq, mk, mv, es, *prefixes, taps, rate, gain, cots)
    output = outt.T
    blocks_of = [mine, pair, opposite, far]
    mine, pair, opposite, _ = lax.optimization_barrier((mine, pair, opposite, sums))
    blocks_of = [mine, pair, opposite, far]
    theirs = [swapped(a) for a in blocks_of]

    def spread(a, ax):
        return [a] + [ring(a, ax, d) for d in (1, 2, 3)]

    def swap(a, ax):
        return [a, lax.ppermute(a, ax, [(0, 1), (1, 0)])]

    def summed(parts):
        return pl.pallas_call(
            add_parts,
            in_specs=[free] * len(parts),
            out_specs=free,
            out_shape=jax.ShapeDtypeStruct((40, PADC), BF16),
            compiler_params=params(4),
            name="add_parts",
        )(*parts)

    arrived = lax.all_to_all(dzb, ("y", "core"), split_axis=0, concat_axis=0, tiled=True)
    sums = summed(swap(sums, "core"))
    *theirs, sums = lax.optimization_barrier((*theirs, sums))
    parts = spread(sums, "zl")
    grad_feats = pl.pallas_call(
        token_grads,
        grid=(3,),
        in_specs=[
            pl.BlockSpec((1, own, PADC), lambda g: (g, 0, 0)),
            pl.BlockSpec((width, depth), lambda g: (g, 0)),
        ],
        out_specs=pl.BlockSpec((own, depth), lambda g: (0, 0)),
        out_shape=jax.ShapeDtypeStruct((own, depth), BF16),
        scratch_shapes=[pltpu.VMEM((own, depth), F32)],
        compiler_params=params(57),
        cost_estimate=pl.CostEstimate(flops=1200000000, bytes_accessed=11000000, transcendentals=0),
        name="token_grads",
    )(dz, w_in.T)
    *parts, grad_feats = lax.optimization_barrier((*parts, grad_feats))
    sums = summed(parts)
    arrived, sums = lax.optimization_barrier((arrived, sums))
    terms = pl.pallas_call(
        weight_term,
        in_specs=[smem] * 3 + [vm] + [free] * 8,
        out_specs=[vm] * 4,
        out_shape=[jax.ShapeDtypeStruct((2 * piece, depth // 4), BF16)] * 4,
        compiler_params=params(24),
        cost_estimate=pl.CostEstimate(flops=1200000000, bytes_accessed=6000000, transcendentals=0),
        name="weight_term",
    )(xi, yi, ci, arrived, *blocks_of, *theirs)
    got = [terms[0]] + [ring(terms[d], "x", d) for d in (1, 2, 3)]
    sums, _ = lax.optimization_barrier((sums, terms[0]))
    sums = summed(swap(summed(spread(sums, "y")), "zh"))
    *got, sums = lax.optimization_barrier((*got, sums))
    blocks = pl.pallas_call(
        split_rows,
        in_specs=[vm] * 4,
        out_specs=vm,
        out_shape=jax.ShapeDtypeStruct((32, fblk, piece), BF16),
        scratch_shapes=[pltpu.VMEM((384, depth // 4), F32)],
        compiler_params=params(12),
        name="split_rows",
    )(*got)
    last = lax.all_to_all(blocks, ("zl", "y", "zh"), 0, 0, tiled=True)
    sums, _ = lax.optimization_barrier((sums, blocks))
    parts = spread(sums, "x")
    grad_taps, grad_residues = pl.pallas_call(
        make_close_sums(scale),
        in_specs=[smem] * 3 + [free] * 5,
        out_specs=[vm] * 2,
        out_shape=[
            jax.ShapeDtypeStruct((7, chans), F32),
            jax.ShapeDtypeStruct(rates.shape, F32),
        ],
        scratch_shapes=[pltpu.VMEM((128, 128), F32)],
        compiler_params=params(4),
        name="close_sums",
    )(xi, zi, yi, amp_mine, *parts)
    grad_weight = pl.pallas_call(
        make_close(scale),
        in_specs=[vm],
        out_specs=vm,
        out_shape=jax.ShapeDtypeStruct((fblk, 4 * piece), BF16),
        compiler_params=params(4),
        name="close_weight",
    )(last)
    return (output[None], grad_feats[None], grad_weight, grad_taps, grad_residues)


def solution(mesh):
    fine = Mesh(mesh.devices.reshape(4, 4, 4, 2, 2), ("x", "zl", "y", "zh", "core"))
    ctx = ("x", "zl", "y")
    dp = ("zh", "core")
    in_specs = (P(dp, ctx, None), P(), P(), P(ctx, None), P(ctx, None), P(dp, ctx, None))
    out_specs = (P(dp, ctx, None), P(dp, ctx, None), P(ctx, dp), P(), P(ctx, None))
    return jax.shard_map(local, mesh=fine, in_specs=in_specs, out_specs=out_specs, check_vma=False)
```

```python
import math

import jax
import jax.numpy as jnp
from jax import lax
from jax.experimental import pallas as pl
from jax.experimental.pallas import tpu as pltpu
from jax.sharding import Mesh, PartitionSpec as P

F32 = jnp.float32
BF16 = jnp.bfloat16
HALO = 16
EXT = 136
SEG = 17
PADC = 1024
MODES = 16
NT = (((1,), (1,)), ((), ()))


def rounded(a):
    return a.astype(BF16).astype(F32)


KBLK = 256


def make_project(part):
    def project(*refs):
        if part == 0:
            tp, nexts, feats, wt, acc, tk, wbuf, tsem, sems = refs
        else:
            tp, nexts, before, feats, wt, zq, zk, zv, tk, wbuf, tsem, sems, acc = refs
        steps, chans, _ = wbuf.shape
        low = part * steps * KBLK
        arrival = pltpu.make_async_copy(feats.at[:, pl.ds(low, steps * KBLK)], tk, tsem)
        arrival.start()
        copies = [
            pltpu.make_async_copy(wt.at[:, pl.ds(low + k * KBLK, KBLK)], wbuf.at[k], sems.at[k])
            for k in range(steps)
        ]
        for copy in copies:
            copy.start()
        arrival.wait()
        for k in range(steps):
            wide = slice(low + k * KBLK, low + (k + 1) * KBLK)
            rows = jnp.concatenate(
                [tp[:, wide], tk[:, k * KBLK : (k + 1) * KBLK], nexts[:, wide]], axis=0
            )
            copies[k].wait()
            total = lax.dot_general(rows, wbuf[k], NT, preferred_element_type=F32)
            if k > 0:
                total = acc[...] + total
            elif part == 1:
                total = before[...] + total
            if part == 0 or k < steps - 1:
                acc[...] = total
            else:
                width = chans // 3
                for g, z in enumerate((zq, zk, zv)):
                    z[:, 0:width] = rounded(total[:, g * width : (g + 1) * width])
                    z[:, width:] = jnp.zeros((z.shape[0], PADC - width), F32)

    return project


def mix_taps(taps, zq, zk, zv, mq, mk, mv):
    def tile(ct, carry):
        lanes = pl.ds(pl.multiple_of(ct * 128, 128), 128)
        for g, (z, m) in enumerate(((zq, mq), (zk, mk), (zv, mv))):
            total = taps[g, 0:1, lanes] * z[pl.ds(HALO, EXT), lanes]
            for j in range(1, 7):
                total = total + taps[g, j : j + 1, lanes] * z[pl.ds(HALO - j, EXT), lanes]
            m[:, lanes] = total
        return carry

    lax.fori_loop(0, PADC // 128, tile, 0)


def one_minus_exp(x):
    series = jnp.ones_like(x)
    for n in range(13, 1, -1):
        series = 1.0 - series * x * (1.0 / n)
    return jnp.where(x < 0.5, x * series, 1.0 - jnp.exp(-x))


def prepare(
    feats, cott, rates, residues, conv, head, tail, block, taps, amp, cots,
    held, turn, cbuf, rbuf, sbuf, vbuf, sems,
):
    count = rates.shape[0]
    width, own = cott.shape
    depth = feats.shape[1]
    copies = [
        pltpu.make_async_copy(rates, rbuf, sems.at[0]),
        pltpu.make_async_copy(residues, sbuf, sems.at[1]),
        pltpu.make_async_copy(cott, cbuf, sems.at[2]),
        pltpu.make_async_copy(conv, vbuf, sems.at[3]),
        pltpu.make_async_copy(feats.at[pl.ds(0, HALO)], head.at[:, pl.ds(0, depth)], sems.at[4]),
        pltpu.make_async_copy(feats.at[pl.ds(own - HALO, HALO)], tail, sems.at[5]),
    ]
    for copy in copies:
        copy.start()
    held[...] = jnp.zeros(held.shape, F32)
    turn[...] = jnp.zeros(turn.shape, F32)
    taps[...] = jnp.zeros(taps.shape, F32)
    copies[0].wait()
    copies[1].wait()
    size = jnp.sqrt(one_minus_exp(2.0 * rbuf[...]))
    amp[...] = size
    held[0:count, 0:MODES] = rbuf[...]
    held[0:count, MODES : 2 * MODES] = sbuf[...] * size
    block[...] = held[...].T[0 : 2 * MODES, 0:count]
    copies[2].wait()
    turn[0:width, :] = cbuf[...].astype(F32)
    for c in range(PADC // 128):
        part = turn[c * 128 : (c + 1) * 128, :].T
        cots[:, c * 128 : (c + 1) * 128] = part
        head[:, depth + c * 128 : depth + (c + 1) * 128] = part[0:HALO].astype(BF16)
    copies[3].wait()
    for g in range(3):
        taps[g, 0:7, 0:width] = vbuf[:, g * width : (g + 1) * width]
    for copy in copies[4:]:
        copy.wait()


def placed(me, refs, held, goal):
    wide = refs[0].shape[1]
    total = None
    for d, ref in enumerate(refs):
        held[...] = jnp.zeros(held.shape, F32)
        held[:, 0:wide] = ref[...]
        part = pltpu.roll(held[...], lax.rem(me + (4 - d), 4) * wide, 1)
        total = part if total is None else total + part
    return total[:, 0:goal]


def join_params(me, r0, r1, r2, r3, out, held):
    out[...] = placed(me[0], (r0, r1, r2, r3), held, out.shape[1])


def end_states(me, r0, r1, r2, r3, mq, mk, mv, cown, nexts, cots, rates, gains, es, ends, endb, ut, dt, held):
    joined = placed(me[0], (r0, r1, r2, r3), held, PADC)
    rates[...] = joined[0:MODES]
    gains[...] = joined[MODES : 2 * MODES]
    sub = lax.broadcasted_iota(jnp.int32, (8, 128), 0)
    subf = sub.astype(F32)
    fdepth = jnp.where(sub == 7, 0.0, (EXT - 8 - SEG) - SEG * subf)
    bdepth = jnp.where(sub == 0, 0.0, SEG * subf - 8.0)

    def tile(ct, carry):
        lanes = pl.ds(pl.multiple_of(ct * 128, 128), 128)
        ut[0:EXT, :] = rounded(mk[:, lanes] * mv[:, lanes])
        lane = pl.multiple_of(nexts.shape[1] - PADC + ct * 128, 128)
        after = nexts[:, pl.ds(lane, 128)].astype(F32)
        cot = jnp.concatenate([cown[:, lanes], after[0 : EXT - 128]], axis=0)
        cots[:, lanes] = cot
        dt[0:EXT, :] = rounded(cot * mq[:, lanes])
        rate = rates[:, lanes]
        decay = jnp.exp(-rate)
        for half in range(2):
            ks = range(half * 8, half * 8 + 8)
            al = [jnp.broadcast_to(decay[k : k + 1, :], (8, 128)) for k in ks]
            rl = [jnp.broadcast_to(rate[k : k + 1, :], (8, 128)) for k in ks]
            st = [jnp.zeros((8, 128), F32)] * 8
            snap = st
            for t in range(SEG):
                uv = ut[pl.ds(t, 8, stride=SEG), :]
                st = [a * s + uv for a, s in zip(al, st)]
                if t == 8:
                    snap = st
            for i, k in enumerate(ks):
                es[0, k, :, lanes] = st[i]
                full = jnp.where(sub == 7, snap[i], st[i]) * jnp.exp(-rl[i] * fdepth)
                ends[k : k + 1, lanes] = jnp.sum(full, axis=0, keepdims=True)
            st = [jnp.zeros((8, 128), F32)] * 8
            for t in range(SEG - 1, -1, -1):
                dv = dt[pl.ds(t, 8, stride=SEG), :]
                st = [a * s + dv for a, s in zip(al, st)]
                if t == 8:
                    snap = st
            for i, k in enumerate(ks):
                es[1, k, :, lanes] = st[i]
                full = jnp.where(sub == 0, snap[i], st[i]) * jnp.exp(-rl[i] * bdepth)
                ends[MODES + k : MODES + k + 1, lanes] = jnp.sum(full, axis=0, keepdims=True)
        return carry

    lax.fori_loop(0, PADC // 128, tile, 0)
    endb[...] = ends[...].astype(BF16)


def make_level(span):
    def level(index, own, r1, r2, r3, rates, total, totalb, prefix):
        me = index[0]
        rate = rates[...] * float(span)
        before = jnp.zeros((MODES, PADC), F32)
        after = before
        whole_f = before
        whole_b = before
        for d, ref in enumerate((own, r1, r2, r3)):
            m = lax.rem(me + (4 - d), 4)
            f = ref[0:MODES, :].astype(F32)
            b = ref[MODES : 2 * MODES, :].astype(F32)
            whole_f = whole_f + f * jnp.exp(-rate * (3 - m).astype(F32))
            whole_b = whole_b + b * jnp.exp(-rate * m.astype(F32))
            if d > 0:
                gf = me - 1 - m
                gb = m - me - 1
                wf = jnp.exp(-rate * jnp.maximum(gf, 0).astype(F32))
                wb = jnp.exp(-rate * jnp.maximum(gb, 0).astype(F32))
                before = before + jnp.where(gf >= 0, 1.0, 0.0) * (wf * f)
                after = after + jnp.where(gb >= 0, 1.0, 0.0) * (wb * b)
        prefix[0:MODES, :] = before
        prefix[MODES : 2 * MODES, :] = after
        total[0:MODES, :] = whole_f
        total[MODES : 2 * MODES, :] = whole_b
        totalb[0:MODES, :] = whole_f.astype(BF16)
        totalb[MODES : 2 * MODES, :] = whole_b.astype(BF16)

    return level


def finish(
    zi, yi, zq, zk, zv, mq, mk, mv, es, py, pz, px, taps, rates, reff, cots,
    outt, dz, dzb, sumb, sums, inc, ut, dt, longs, dps, dms, dzt,
):
    own = dz.shape[1]
    rate = rates[...]
    for back in range(2):
        part = pl.ds(back * MODES, MODES)
        near, mid = yi[0], zi[0]
        if back:
            near, mid = 3 - near, 3 - mid
        far = pz[part, :] + jnp.exp(-rate * (4 * own * mid).astype(F32)) * px[part, :]
        inc[part, :] = py[part, :] + jnp.exp(-rate * (own * near).astype(F32)) * far
    sub = lax.broadcasted_iota(jnp.int32, (8, 128), 0)
    ut[0:EXT, :] = rounded(mk[...] * mv[...])
    dt[0:EXT, :] = rounded(cots[...] * mq[...])
    decay = jnp.exp(-rate)
    gain = reff[...]
    for half in range(2):
        ks = range(half * 8, half * 8 + 8)
        al = [jnp.broadcast_to(decay[k : k + 1, :], (8, 128)) for k in ks]
        gl = [jnp.broadcast_to(gain[k : k + 1, :], (8, 128)) for k in ks]
        rl = [jnp.broadcast_to(rate[k : k + 1, :], (8, 128)) for k in ks]
        fwd = []
        bwd = []
        for i, k in enumerate(ks):
            jump = [jnp.exp(-float(SEG * m) * rl[i]) for m in (1, 2, 4)]
            x = jnp.where(sub == 0, inc[k : k + 1, :], pltpu.roll(es[0, k], 1, 0))
            for m, d in zip((1, 2, 4), jump):
                x = x + jnp.where(sub >= m, pltpu.roll(x, m, 0) * d, 0.0)
            fwd.append(x)
            x = jnp.where(
                sub == 7, inc[MODES + k : MODES + k + 1, :], pltpu.roll(es[1, k], 7, 0)
            )
            for m, d in zip((1, 2, 4), jump):
                x = x + jnp.where(sub < 8 - m, pltpu.roll(x, 8 - m, 0) * d, 0.0)
            bwd.append(x)
        gr = [jnp.zeros((8, 128), F32)] * 8
        st = fwd
        for t in range(SEG):
            uv = ut[pl.ds(t, 8, stride=SEG), :]
            dv = dt[pl.ds(t, 8, stride=SEG), :]
            if t >= 9:
                dv = jnp.where(sub < 7, dv, 0.0)
            st = [a * s + uv for a, s in zip(al, st)]
            gr = [q + dv * s for q, s in zip(gr, st)]
            total = sum(g * s for g, s in zip(gl, st))
            if half:
                total = total + longs[pl.ds(t, 8, stride=SEG), :]
            longs[pl.ds(t, 8, stride=SEG), :] = total
        for i, k in enumerate(ks):
            sums[24 + k : 25 + k, :] = jnp.sum(gr[i], axis=0, keepdims=True)
        st = bwd
        for t in range(SEG - 1, -1, -1):
            dv = dt[pl.ds(t, 8, stride=SEG), :]
            st = [a * s + dv for a, s in zip(al, st)]
            total = sum(g * s for g, s in zip(gl, st))
            if half:
                total = total + dps[pl.ds(t, 8, stride=SEG), :]
            dps[pl.ds(t, 8, stride=SEG), :] = total
    long_out = rounded(longs[0:EXT, :])
    dprod = rounded(dps[0:EXT, :])
    outt[...] = (mq[0:own, :] * long_out[0:own]).T.astype(BF16)
    dms[0] = rounded(cots[...] * long_out)
    dms[1] = rounded(dprod * mv[...])
    dms[2] = rounded(dprod * mk[...])
    ct = pl.program_id(0)
    for g, zg in enumerate((zq, zk, zv)):
        mine = dms[g, 0:own, :]
        total = taps[g, 0:1, :] * mine
        sums[8 * g : 8 * g + 1, :] = jnp.sum(mine * zg[pl.ds(HALO, own), :], axis=0, keepdims=True)
        for j in range(1, 7):
            total = total + taps[g, j : j + 1, :] * dms[g, pl.ds(j, own), :]
            sums[8 * g + j : 8 * g + j + 1, :] = jnp.sum(
                mine * zg[pl.ds(HALO - j, own), :], axis=0, keepdims=True
            )
        sums[8 * g + 7 : 8 * g + 8, :] = jnp.zeros((1, 128), F32)
        dz[g] = total.astype(BF16)
        dzt[g, pl.ds(pl.multiple_of(ct * 128, 128), 128), :] = total.T

    sumb[...] = sums[...].astype(BF16)

    @pl.when(ct == pl.num_programs(0) - 1)
    def _():
        piece = dzb.shape[1] // 2
        width = 16 * piece // 3
        for b in range(8):
            both = []
            for h in range(2):
                off = h * 8 * piece + (b % 2) * 4 * piece + (b // 2) * piece
                g, low = off // width, off % width
                size = min(piece, width - low)
                both.append(dzt[g, low : low + size, :])
                if size < piece:
                    both.append(dzt[g + 1, 0 : piece - size, :])
            dzb[b] = jnp.concatenate(both, axis=0).astype(BF16)


def token_grads(dz, wt, out, acc):
    g = pl.program_id(0)
    part = jnp.dot(dz[0, :, 0 : wt.shape[0]], wt[...], preferred_element_type=F32)

    @pl.when(g == 0)
    def _():
        acc[...] = part

    @pl.when(g > 0)
    def _():
        acc[...] += part

    @pl.when(g == pl.num_programs(0) - 1)
    def _():
        out[...] = acc[...].astype(BF16)


def weight_term(xi, yi, ci, arrived, *refs):
    tokens, terms = refs[:8], refs[8:]
    me = yi[0]
    core = ci[0]
    chunk = terms[0].shape[1]
    slots = (me, lax.bitwise_xor(me, 1), 3 - me, lax.bitwise_xor(3 - me, 1))
    pairs = []
    for half, c in ((0, core), (1, 1 - core)):
        for p in (0, 2):
            left = [arrived[slots[p + i] * 2 + c] for i in range(2)]
            pairs.append((jnp.concatenate(left, axis=1), tokens[4 * half + p : 4 * half + p + 2]))
    for d, term in enumerate(terms):
        total = None
        cols = pl.ds(pl.multiple_of(lax.rem(xi[0] + d, 4) * chunk, 128), chunk)
        for left, (one, two) in pairs:
            right = jnp.concatenate([one[:, cols], two[:, cols]], axis=0)
            part = jnp.dot(left, right, preferred_element_type=F32)
            total = part if total is None else total + part
        term[...] = total.astype(BF16)


def split_rows(g0, g1, g2, g3, blocks, turn):
    chans = g0.shape[0]
    fblk = blocks.shape[1]
    piece = blocks.shape[2]
    turn[0:chans, :] = added((g0, g1, g2, g3))
    turn[chans:, :] = jnp.zeros((turn.shape[0] - chans, turn.shape[1]), F32)
    flipped = turn[...].T
    for q in range(16):
        for h in range(2):
            part = flipped[q * fblk : (q + 1) * fblk, h * piece : (h + 1) * piece]
            blocks[2 * q + h] = part.astype(BF16)


def added(refs):
    total = refs[0][...].astype(F32)
    for ref in refs[1:]:
        total = total + ref[...].astype(F32)
    return total


def add_parts(*refs):
    refs[-1][...] = added(refs[:-1]).astype(BF16)


def make_close_sums(scale):
    def close_sums(xi, zi, yi, amp, *refs):
        *parts, grad_taps, grad_res, held = refs
        total = added(parts) * scale
        width = grad_taps.shape[1] // 3
        for g in range(3):
            grad_taps[:, g * width : (g + 1) * width] = total[8 * g : 8 * g + 7, 0:width]
        count = grad_res.shape[0]
        index = (xi[0] * 4 + zi[0]) * 4 + yi[0]
        moved = pltpu.roll(total[24:40, :], lax.rem(PADC - index * count, PADC), 1)
        held[...] = jnp.zeros(held.shape, F32)
        held[0:MODES, :] = moved[:, 0:128]
        grad_res[...] = held[...].T[0:count, 0:MODES] * amp[...]

    return close_sums


def make_close(scale):
    def close_weight(last, out):
        fblk, piece = last.shape[1:]
        for y in range(4):
            total = jnp.zeros((fblk, piece), F32)
            for z in range(4):
                for h in range(2):
                    total = total + last[(z * 4 + y) * 2 + h].astype(F32)
            out[:, y * piece : (y + 1) * piece] = (total * scale).astype(BF16)

    return close_weight


def ring(a, ax, d):
    return lax.ppermute(a, ax, [(i, (i + d) % 4) for i in range(4)])


def params(mb):
    return pltpu.CompilerParams(vmem_limit_bytes=int(mb * 1024 * 1024))


def local(tokens, w_in, conv_taps, residues, rates, cotangent):
    feats = tokens[0]
    cot = cotangent[0]
    own, width = cot.shape
    depth = feats.shape[1]
    chans = 3 * width
    count = 64
    piece = chans // 16
    fblk = depth // count
    ctx = ("x", "zl", "y")
    scale = 1.0 / math.sqrt(4 * count * own)
    smem = pl.BlockSpec(memory_space=pltpu.SMEM)
    vm = pl.BlockSpec(memory_space=pltpu.VMEM)
    free = pl.BlockSpec()
    names = ("x", "zl", "y", "core")
    feats, cot, rates, *where = lax.optimization_barrier(
        (feats, cot, rates, *[lax.axis_index(n) for n in names])
    )
    xi, zi, yi, ci = [w.reshape(1) for w in where]
    anywhere = pl.BlockSpec(memory_space=pl.ANY)
    head, tail, block, taps, amp_mine, cown = pl.pallas_call(
        prepare,
        in_specs=[anywhere] * 5,
        out_specs=[vm] * 6,
        out_shape=[
            jax.ShapeDtypeStruct((HALO, depth + PADC), BF16),
            jax.ShapeDtypeStruct((HALO, depth), BF16),
            jax.ShapeDtypeStruct((2 * MODES, width // count), F32),
            jax.ShapeDtypeStruct((3, 8, PADC), F32),
            jax.ShapeDtypeStruct(rates.shape, F32),
            jax.ShapeDtypeStruct((own, PADC), F32),
        ],
        scratch_shapes=[
            pltpu.VMEM((128, 128), F32),
            pltpu.VMEM((PADC, own), F32),
            pltpu.VMEM((width, own), BF16),
            pltpu.VMEM(rates.shape, F32),
            pltpu.VMEM(rates.shape, F32),
            pltpu.VMEM(conv_taps.shape, F32),
            pltpu.SemaphoreType.DMA((6,)),
        ],
        compiler_params=params(54),
        name="prepare",
    )(feats, cot.T, rates, residues, conv_taps)
    tprev = lax.ppermute(tail, ctx, [(i, i + 1) for i in range(count - 1)])
    nexts = lax.ppermute(head, ctx, [(i, i - 1) for i in range(1, count)])
    ext_rows = own + 2 * HALO
    steps = depth // KBLK // 2

    def project(part, *before):
        many = 3 if part else 1
        shape = (ext_rows, PADC) if part else (ext_rows, chans)
        return pl.pallas_call(
            make_project(part),
            in_specs=[vm] * (2 + part) + [anywhere] * 2,
            out_specs=[vm] * many,
            out_shape=[jax.ShapeDtypeStruct(shape, F32)] * many,
            scratch_shapes=[
                pltpu.VMEM((own, steps * KBLK), BF16),
                pltpu.VMEM((steps, chans, KBLK), BF16),
                pltpu.SemaphoreType.DMA,
                pltpu.SemaphoreType.DMA((steps,)),
                *[pltpu.VMEM((ext_rows, chans), F32)] * part,
            ],
            compiler_params=params((52, 51)[part]),
            cost_estimate=pl.CostEstimate(flops=800000000, bytes_accessed=6000000, transcendentals=0),
            name="project",
        )(tprev, nexts, *before, feats, w_in.T)

    def mixed(*zs):
        return pl.pallas_call(
            mix_taps,
            in_specs=[vm] * 4,
            out_specs=[vm] * 3,
            out_shape=[jax.ShapeDtypeStruct((EXT, PADC), F32)] * 3,
            compiler_params=params(8),
            cost_estimate=pl.CostEstimate(flops=800000000, bytes_accessed=6000000, transcendentals=0),
            name="mix_taps",
        )(taps, *zs)

    held, each = block, width // count
    work = []
    for g, (me, ax) in enumerate(((yi, "y"), (zi, "zl"), (xi, "x"))):
        blocks = [held] + [ring(held, ax, d) for d in (1, 2, 3)]
        work = project(0) if g == 0 else project(1, *work) if g == 1 else mixed(*work)
        *blocks, last_work = lax.optimization_barrier((*blocks, work[-1]))
        work = [*work[:-1], last_work]
        if g == 1:
            zq, zk, zv = work
        if g == 2:
            break
        each = 4 * each
        held = pl.pallas_call(
            join_params,
            in_specs=[smem] + [vm] * 4,
            out_specs=vm,
            out_shape=jax.ShapeDtypeStruct((2 * MODES, each), F32),
            scratch_shapes=[pltpu.VMEM((2 * MODES, 256), F32)],
            compiler_params=params(4),
            name="join_params",
        )(me, *blocks)
    mq, mk, mv = work
    cots, rate, gain, es, ends, endb = pl.pallas_call(
        end_states,
        in_specs=[smem] + [vm] * 9,
        out_specs=[vm] * 6,
        out_shape=[
            jax.ShapeDtypeStruct((EXT, PADC), F32),
            jax.ShapeDtypeStruct((MODES, PADC), F32),
            jax.ShapeDtypeStruct((MODES, PADC), F32),
            jax.ShapeDtypeStruct((2, MODES, 8, PADC), F32),
            jax.ShapeDtypeStruct((2 * MODES, PADC), F32),
            jax.ShapeDtypeStruct((2 * MODES, PADC), BF16),
        ],
        scratch_shapes=[
            pltpu.VMEM((EXT + 24, 128), F32),
            pltpu.VMEM((EXT + 24, 128), F32),
            pltpu.VMEM((2 * MODES, PADC), F32),
        ],
        compiler_params=params(16),
        cost_estimate=pl.CostEstimate(flops=20000000, bytes_accessed=3000000, transcendentals=0),
        name="end_states",
    )(xi, *blocks, mq, mk, mv, cown, nexts)

    prefixes = []
    total, sent = ends, endb
    for me, ax, span in ((yi, "y", own), (zi, "zl", 4 * own), (xi, "x", 16 * own)):
        near = [ring(sent, ax, d) for d in (1, 2, 3)]
        total, sent, prefix = pl.pallas_call(
            make_level(span),
            in_specs=[smem] + [vm] * 5,
            out_specs=[vm] * 3,
            out_shape=[
                jax.ShapeDtypeStruct((2 * MODES, PADC), F32),
                jax.ShapeDtypeStruct((2 * MODES, PADC), BF16),
                jax.ShapeDtypeStruct((2 * MODES, PADC), F32),
            ],
            compiler_params=params(8),
            name="level",
        )(me, total, *near, rate)
        prefixes.append(prefix)
        if ax == "zl":
            mine, _ = lax.optimization_barrier((feats, sent))
            pair = lax.ppermute(mine, "y", [(i, i ^ 1) for i in range(4)])
            opposite = lax.ppermute(mine, "y", [(i, 3 - i) for i in range(4)])
    pair, opposite, prefixes[2] = lax.optimization_barrier((pair, opposite, prefixes[2]))
    far = lax.ppermute(pair, "y", [(i, 3 - i) for i in range(4)])

    def swapped(a):
        return lax.ppermute(a, "core", [(0, 1), (1, 0)])

    def tiles(shape):
        lead = len(shape) - 1
        return pl.BlockSpec(shape, lambda k: (0,) * lead + (k,))

    outt, dz, dzb, sums = pl.pallas_call(
        finish,
        grid=(PADC // 128,),
        in_specs=[
            smem,
            smem,
            *[tiles((ext_rows, 128))] * 3,
            *[tiles((EXT, 128))] * 3,
            tiles((2, MODES, 8, 128)),
            tiles((2 * MODES, 128)),
            tiles((2 * MODES, 128)),
            tiles((2 * MODES, 128)),
            tiles((3, 8, 128)),
            tiles((MODES, 128)),
            tiles((MODES, 128)),
            tiles((EXT, 128)),
        ],
        out_specs=[
            pl.BlockSpec((128, own), lambda k: (k, 0)),
            tiles((3, own, 128)),
            pl.BlockSpec((8, 2 * piece, own), lambda k: (0, 0, 0)),
            tiles((40, 128)),
        ],
        out_shape=[
            jax.ShapeDtypeStruct((width, own), BF16),
            jax.ShapeDtypeStruct((3, own, PADC), BF16),
            jax.ShapeDtypeStruct((8, 2 * piece, own), BF16),
            jax.ShapeDtypeStruct((40, PADC), BF16),
        ],
        scratch_shapes=[
            pltpu.VMEM((40, 128), F32),
            pltpu.VMEM((2 * MODES, 128), F32),
            pltpu.VMEM((EXT + 24, 128), F32),
            pltpu.VMEM((EXT + 24, 128), F32),
            pltpu.VMEM((EXT + 24, 128), F32),
            pltpu.VMEM((EXT + 24, 128), F32),
            pltpu.VMEM((3, EXT, 128), F32),
            pltpu.VMEM((3, PADC, own), F32),
        ],
        compiler_params=params(50),
        cost_estimate=pl.CostEstimate(flops=200000000, bytes_accessed=10000000, transcendentals=0),
        name="finish",
    )(zi, yi, zq, zk, zv, mq, mk, mv, es, *prefixes, taps, rate, gain, cots)
    output = outt.T
    blocks_of = [mine, pair, opposite, far]
    mine, pair, opposite, _ = lax.optimization_barrier((mine, pair, opposite, sums))
    blocks_of = [mine, pair, opposite, far]
    theirs = [swapped(a) for a in blocks_of]

    def spread(a, ax):
        return [a] + [ring(a, ax, d) for d in (1, 2, 3)]

    def swap(a, ax):
        return [a, lax.ppermute(a, ax, [(0, 1), (1, 0)])]

    def summed(parts):
        return pl.pallas_call(
            add_parts,
            in_specs=[free] * len(parts),
            out_specs=free,
            out_shape=jax.ShapeDtypeStruct((40, PADC), BF16),
            compiler_params=params(4),
            name="add_parts",
        )(*parts)

    arrived = lax.all_to_all(dzb, ("y", "core"), split_axis=0, concat_axis=0, tiled=True)
    sums = summed(swap(sums, "core"))
    *theirs, sums = lax.optimization_barrier((*theirs, sums))
    parts = spread(sums, "zl")
    grad_feats = pl.pallas_call(
        token_grads,
        grid=(3,),
        in_specs=[
            pl.BlockSpec((1, own, PADC), lambda g: (g, 0, 0)),
            pl.BlockSpec((width, depth), lambda g: (g, 0)),
        ],
        out_specs=pl.BlockSpec((own, depth), lambda g: (0, 0)),
        out_shape=jax.ShapeDtypeStruct((own, depth), BF16),
        scratch_shapes=[pltpu.VMEM((own, depth), F32)],
        compiler_params=params(57),
        cost_estimate=pl.CostEstimate(flops=1200000000, bytes_accessed=11000000, transcendentals=0),
        name="token_grads",
    )(dz, w_in.T)
    *parts, grad_feats = lax.optimization_barrier((*parts, grad_feats))
    sums = summed(parts)
    arrived, sums = lax.optimization_barrier((arrived, sums))
    terms = pl.pallas_call(
        weight_term,
        in_specs=[smem] * 3 + [vm] + [free] * 8,
        out_specs=[vm] * 4,
        out_shape=[jax.ShapeDtypeStruct((2 * piece, depth // 4), BF16)] * 4,
        compiler_params=params(24),
        cost_estimate=pl.CostEstimate(flops=1200000000, bytes_accessed=6000000, transcendentals=0),
        name="weight_term",
    )(xi, yi, ci, arrived, *blocks_of, *theirs)
    got = [terms[0]] + [ring(terms[d], "x", d) for d in (1, 2, 3)]
    sums, _ = lax.optimization_barrier((sums, terms[0]))
    sums = summed(swap(summed(spread(sums, "y")), "zh"))
    *got, sums = lax.optimization_barrier((*got, sums))
    blocks = pl.pallas_call(
        split_rows,
        in_specs=[vm] * 4,
        out_specs=vm,
        out_shape=jax.ShapeDtypeStruct((32, fblk, piece), BF16),
        scratch_shapes=[pltpu.VMEM((384, depth // 4), F32)],
        compiler_params=params(12),
        name="split_rows",
    )(*got)
    last = lax.all_to_all(blocks, ("zl", "y", "zh"), 0, 0, tiled=True)
    sums, _ = lax.optimization_barrier((sums, blocks))
    parts = spread(sums, "x")
    grad_taps, grad_residues = pl.pallas_call(
        make_close_sums(scale),
        in_specs=[smem] * 3 + [free] * 5,
        out_specs=[vm] * 2,
        out_shape=[
            jax.ShapeDtypeStruct((7, chans), F32),
            jax.ShapeDtypeStruct(rates.shape, F32),
        ],
        scratch_shapes=[pltpu.VMEM((128, 128), F32)],
        compiler_params=params(4),
        name="close_sums",
    )(xi, zi, yi, amp_mine, *parts)
    grad_weight = pl.pallas_call(
        make_close(scale),
        in_specs=[vm],
        out_specs=vm,
        out_shape=jax.ShapeDtypeStruct((fblk, 4 * piece), BF16),
        compiler_params=params(4),
        name="close_weight",
    )(last)
    return (output[None], grad_feats[None], grad_weight, grad_taps, grad_residues)


def solution(mesh):
    fine = Mesh(mesh.devices.reshape(4, 4, 4, 2, 2), ("x", "zl", "y", "zh", "core"))
    ctx = ("x", "zl", "y")
    dp = ("zh", "core")
    in_specs = (P(dp, ctx, None), P(), P(), P(ctx, None), P(ctx, None), P(dp, ctx, None))
    out_specs = (P(dp, ctx, None), P(dp, ctx, None), P(ctx, dp), P(), P(ctx, None))
    return jax.shard_map(local, mesh=fine, in_specs=in_specs, out_specs=out_specs, check_vma=False)
```

```python
import math

import jax
import jax.numpy as jnp
from jax import lax
from jax.experimental import pallas as pl
from jax.experimental.pallas import tpu as pltpu
from jax.sharding import Mesh, PartitionSpec as P

F32 = jnp.float32
BF16 = jnp.bfloat16
HALO = 16
EXT = 136
SEG = 17
PADC = 1024
MODES = 16
NT = (((1,), (1,)), ((), ()))


def rounded(a):
    return a.astype(BF16).astype(F32)


KBLK = 256


def make_project(part):
    def project(*refs):
        if part == 0:
            tp, nexts, feats, wt, acc, tk, wbuf, tsem, sems = refs
        else:
            tp, nexts, before, feats, wt, zq, zk, zv, tk, wbuf, tsem, sems, acc = refs
        steps, chans, _ = wbuf.shape
        low = part * steps * KBLK
        arrival = pltpu.make_async_copy(feats.at[:, pl.ds(low, steps * KBLK)], tk, tsem)
        arrival.start()
        copies = [
            pltpu.make_async_copy(wt.at[:, pl.ds(low + k * KBLK, KBLK)], wbuf.at[k], sems.at[k])
            for k in range(steps)
        ]
        for copy in copies:
            copy.start()
        arrival.wait()
        for k in range(steps):
            wide = slice(low + k * KBLK, low + (k + 1) * KBLK)
            rows = jnp.concatenate(
                [tp[:, wide], tk[:, k * KBLK : (k + 1) * KBLK], nexts[:, wide]], axis=0
            )
            copies[k].wait()
            total = lax.dot_general(rows, wbuf[k], NT, preferred_element_type=F32)
            if k > 0:
                total = acc[...] + total
            elif part == 1:
                total = before[...] + total
            if part == 0 or k < steps - 1:
                acc[...] = total
            else:
                width = chans // 3
                for g, z in enumerate((zq, zk, zv)):
                    z[:, 0:width] = rounded(total[:, g * width : (g + 1) * width])
                    z[:, width:] = jnp.zeros((z.shape[0], PADC - width), F32)

    return project


def mix_taps(taps, zq, zk, zv, mq, mk, mv):
    def tile(ct, carry):
        lanes = pl.ds(pl.multiple_of(ct * 128, 128), 128)
        for g, (z, m) in enumerate(((zq, mq), (zk, mk), (zv, mv))):
            total = taps[g, 0:1, lanes] * z[pl.ds(HALO, EXT), lanes]
            for j in range(1, 7):
                total = total + taps[g, j : j + 1, lanes] * z[pl.ds(HALO - j, EXT), lanes]
            m[:, lanes] = total
        return carry

    lax.fori_loop(0, PADC // 128, tile, 0)


def one_minus_exp(x):
    series = jnp.ones_like(x)
    for n in range(13, 1, -1):
        series = 1.0 - series * x * (1.0 / n)
    return jnp.where(x < 0.5, x * series, 1.0 - jnp.exp(-x))


def prepare(
    feats, cott, rates, residues, conv, head, tail, block, taps, amp, cots,
    held, turn, cbuf, rbuf, sbuf, vbuf, sems,
):
    count = rates.shape[0]
    width, own = cott.shape
    depth = feats.shape[1]
    copies = [
        pltpu.make_async_copy(rates, rbuf, sems.at[0]),
        pltpu.make_async_copy(residues, sbuf, sems.at[1]),
        pltpu.make_async_copy(cott, cbuf, sems.at[2]),
        pltpu.make_async_copy(conv, vbuf, sems.at[3]),
        pltpu.make_async_copy(feats.at[pl.ds(0, HALO)], head.at[:, pl.ds(0, depth)], sems.at[4]),
        pltpu.make_async_copy(feats.at[pl.ds(own - HALO, HALO)], tail, sems.at[5]),
    ]
    for copy in copies:
        copy.start()
    held[...] = jnp.zeros(held.shape, F32)
    turn[...] = jnp.zeros(turn.shape, F32)
    taps[...] = jnp.zeros(taps.shape, F32)
    copies[0].wait()
    copies[1].wait()
    size = jnp.sqrt(one_minus_exp(2.0 * rbuf[...]))
    amp[...] = size
    held[0:count, 0:MODES] = rbuf[...]
    held[0:count, MODES : 2 * MODES] = sbuf[...] * size
    block[...] = held[...].T[0 : 2 * MODES, 0:count]
    copies[2].wait()
    turn[0:width, :] = cbuf[...].astype(F32)
    for c in range(PADC // 128):
        part = turn[c * 128 : (c + 1) * 128, :].T
        cots[:, c * 128 : (c + 1) * 128] = part
        head[:, depth + c * 128 : depth + (c + 1) * 128] = part[0:HALO].astype(BF16)
    copies[3].wait()
    for g in range(3):
        taps[g, 0:7, 0:width] = vbuf[:, g * width : (g + 1) * width]
    for copy in copies[4:]:
        copy.wait()


def placed(me, refs, held, goal):
    wide = refs[0].shape[1]
    total = None
    for d, ref in enumerate(refs):
        held[...] = jnp.zeros(held.shape, F32)
        held[:, 0:wide] = ref[...]
        part = pltpu.roll(held[...], lax.rem(me + (4 - d), 4) * wide, 1)
        total = part if total is None else total + part
    return total[:, 0:goal]


def join_params(me, r0, r1, r2, r3, out, held):
    out[...] = placed(me[0], (r0, r1, r2, r3), held, out.shape[1])


def end_states(me, r0, r1, r2, r3, mq, mk, mv, cown, nexts, cots, rates, gains, es, ends, endb, ut, dt, held):
    joined = placed(me[0], (r0, r1, r2, r3), held, PADC)
    rates[...] = joined[0:MODES]
    gains[...] = joined[MODES : 2 * MODES]
    sub = lax.broadcasted_iota(jnp.int32, (8, 128), 0)
    subf = sub.astype(F32)
    fdepth = jnp.where(sub == 7, 0.0, (EXT - 8 - SEG) - SEG * subf)
    bdepth = jnp.where(sub == 0, 0.0, SEG * subf - 8.0)

    def tile(ct, carry):
        lanes = pl.ds(pl.multiple_of(ct * 128, 128), 128)
        ut[0:EXT, :] = rounded(mk[:, lanes] * mv[:, lanes])
        lane = pl.multiple_of(nexts.shape[1] - PADC + ct * 128, 128)
        after = nexts[:, pl.ds(lane, 128)].astype(F32)
        cot = jnp.concatenate([cown[:, lanes], after[0 : EXT - 128]], axis=0)
        cots[:, lanes] = cot
        dt[0:EXT, :] = rounded(cot * mq[:, lanes])
        rate = rates[:, lanes]
        decay = jnp.exp(-rate)
        for half in range(2):
            ks = range(half * 8, half * 8 + 8)
            al = [jnp.broadcast_to(decay[k : k + 1, :], (8, 128)) for k in ks]
            rl = [jnp.broadcast_to(rate[k : k + 1, :], (8, 128)) for k in ks]
            st = [jnp.zeros((8, 128), F32)] * 8
            snap = st
            for t in range(SEG):
                uv = ut[pl.ds(t, 8, stride=SEG), :]
                st = [a * s + uv for a, s in zip(al, st)]
                if t == 8:
                    snap = st
            for i, k in enumerate(ks):
                es[0, k, :, lanes] = st[i]
                full = jnp.where(sub == 7, snap[i], st[i]) * jnp.exp(-rl[i] * fdepth)
                ends[k : k + 1, lanes] = jnp.sum(full, axis=0, keepdims=True)
            st = [jnp.zeros((8, 128), F32)] * 8
            for t in range(SEG - 1, -1, -1):
                dv = dt[pl.ds(t, 8, stride=SEG), :]
                st = [a * s + dv for a, s in zip(al, st)]
                if t == 8:
                    snap = st
            for i, k in enumerate(ks):
                es[1, k, :, lanes] = st[i]
                full = jnp.where(sub == 0, snap[i], st[i]) * jnp.exp(-rl[i] * bdepth)
                ends[MODES + k : MODES + k + 1, lanes] = jnp.sum(full, axis=0, keepdims=True)
        return carry

    lax.fori_loop(0, PADC // 128, tile, 0)
    endb[...] = ends[...].astype(BF16)


def make_level(span):
    def level(index, own, r1, r2, r3, rates, total, totalb, prefix):
        me = index[0]
        rate = rates[...] * float(span)
        before = jnp.zeros((MODES, PADC), F32)
        after = before
        whole_f = before
        whole_b = before
        for d, ref in enumerate((own, r1, r2, r3)):
            m = lax.rem(me + (4 - d), 4)
            f = ref[0:MODES, :].astype(F32)
            b = ref[MODES : 2 * MODES, :].astype(F32)
            whole_f = whole_f + f * jnp.exp(-rate * (3 - m).astype(F32))
            whole_b = whole_b + b * jnp.exp(-rate * m.astype(F32))
            if d > 0:
                gf = me - 1 - m
                gb = m - me - 1
                wf = jnp.exp(-rate * jnp.maximum(gf, 0).astype(F32))
                wb = jnp.exp(-rate * jnp.maximum(gb, 0).astype(F32))
                before = before + jnp.where(gf >= 0, 1.0, 0.0) * (wf * f)
                after = after + jnp.where(gb >= 0, 1.0, 0.0) * (wb * b)
        prefix[0:MODES, :] = before
        prefix[MODES : 2 * MODES, :] = after
        total[0:MODES, :] = whole_f
        total[MODES : 2 * MODES, :] = whole_b
        totalb[0:MODES, :] = whole_f.astype(BF16)
        totalb[MODES : 2 * MODES, :] = whole_b.astype(BF16)

    return level


def finish(
    zi, yi, zq, zk, zv, mq, mk, mv, es, py, pz, px, taps, rates, reff, cots,
    outt, dz, dzb, sumb, sums, inc, ut, dt, longs, dps, dms, dzt,
):
    own = dz.shape[1]
    rate = rates[...]
    for back in range(2):
        part = pl.ds(back * MODES, MODES)
        near, mid = yi[0], zi[0]
        if back:
            near, mid = 3 - near, 3 - mid
        far = pz[part, :] + jnp.exp(-rate * (4 * own * mid).astype(F32)) * px[part, :]
        inc[part, :] = py[part, :] + jnp.exp(-rate * (own * near).astype(F32)) * far
    sub = lax.broadcasted_iota(jnp.int32, (8, 128), 0)
    ut[0:EXT, :] = rounded(mk[...] * mv[...])
    dt[0:EXT, :] = rounded(cots[...] * mq[...])
    decay = jnp.exp(-rate)
    gain = reff[...]
    for half in range(2):
        ks = range(half * 8, half * 8 + 8)
        al = [jnp.broadcast_to(decay[k : k + 1, :], (8, 128)) for k in ks]
        gl = [jnp.broadcast_to(gain[k : k + 1, :], (8, 128)) for k in ks]
        rl = [jnp.broadcast_to(rate[k : k + 1, :], (8, 128)) for k in ks]
        fwd = []
        bwd = []
        for i, k in enumerate(ks):
            jump = [jnp.exp(-float(SEG * m) * rl[i]) for m in (1, 2, 4)]
            x = jnp.where(sub == 0, inc[k : k + 1, :], pltpu.roll(es[0, k], 1, 0))
            for m, d in zip((1, 2, 4), jump):
                x = x + jnp.where(sub >= m, pltpu.roll(x, m, 0) * d, 0.0)
            fwd.append(x)
            x = jnp.where(
                sub == 7, inc[MODES + k : MODES + k + 1, :], pltpu.roll(es[1, k], 7, 0)
            )
            for m, d in zip((1, 2, 4), jump):
                x = x + jnp.where(sub < 8 - m, pltpu.roll(x, 8 - m, 0) * d, 0.0)
            bwd.append(x)
        gr = [jnp.zeros((8, 128), F32)] * 8
        st = fwd
        for t in range(SEG):
            uv = ut[pl.ds(t, 8, stride=SEG), :]
            dv = dt[pl.ds(t, 8, stride=SEG), :]
            if t >= 9:
                dv = jnp.where(sub < 7, dv, 0.0)
            st = [a * s + uv for a, s in zip(al, st)]
            gr = [q + dv * s for q, s in zip(gr, st)]
            total = sum(g * s for g, s in zip(gl, st))
            if half:
                total = total + longs[pl.ds(t, 8, stride=SEG), :]
            longs[pl.ds(t, 8, stride=SEG), :] = total
        for i, k in enumerate(ks):
            sums[24 + k : 25 + k, :] = jnp.sum(gr[i], axis=0, keepdims=True)
        st = bwd
        for t in range(SEG - 1, -1, -1):
            dv = dt[pl.ds(t, 8, stride=SEG), :]
            st = [a * s + dv for a, s in zip(al, st)]
            total = sum(g * s for g, s in zip(gl, st))
            if half:
                total = total + dps[pl.ds(t, 8, stride=SEG), :]
            dps[pl.ds(t, 8, stride=SEG), :] = total
    long_out = rounded(longs[0:EXT, :])
    dprod = rounded(dps[0:EXT, :])
    outt[...] = (mq[0:own, :] * long_out[0:own]).T.astype(BF16)
    dms[0] = rounded(cots[...] * long_out)
    dms[1] = rounded(dprod * mv[...])
    dms[2] = rounded(dprod * mk[...])
    ct = pl.program_id(0)
    for g, zg in enumerate((zq, zk, zv)):
        mine = dms[g, 0:own, :]
        total = taps[g, 0:1, :] * mine
        sums[8 * g : 8 * g + 1, :] = jnp.sum(mine * zg[pl.ds(HALO, own), :], axis=0, keepdims=True)
        for j in range(1, 7):
            total = total + taps[g, j : j + 1, :] * dms[g, pl.ds(j, own), :]
            sums[8 * g + j : 8 * g + j + 1, :] = jnp.sum(
                mine * zg[pl.ds(HALO - j, own), :], axis=0, keepdims=True
            )
        sums[8 * g + 7 : 8 * g + 8, :] = jnp.zeros((1, 128), F32)
        dz[g] = total.astype(BF16)
        dzt[g, pl.ds(pl.multiple_of(ct * 128, 128), 128), :] = total.T

    sumb[...] = sums[...].astype(BF16)

    @pl.when(ct == pl.num_programs(0) - 1)
    def _():
        piece = dzb.shape[1] // 2
        width = 16 * piece // 3
        for b in range(8):
            both = []
            for h in range(2):
                off = h * 8 * piece + (b % 2) * 4 * piece + (b // 2) * piece
                g, low = off // width, off % width
                size = min(piece, width - low)
                both.append(dzt[g, low : low + size, :])
                if size < piece:
                    both.append(dzt[g + 1, 0 : piece - size, :])
            dzb[b] = jnp.concatenate(both, axis=0).astype(BF16)


def token_grads(dz, wt, out, acc):
    g = pl.program_id(0)
    part = jnp.dot(dz[0, :, 0 : wt.shape[0]], wt[...], preferred_element_type=F32)

    @pl.when(g == 0)
    def _():
        acc[...] = part

    @pl.when(g > 0)
    def _():
        acc[...] += part

    @pl.when(g == pl.num_programs(0) - 1)
    def _():
        out[...] = acc[...].astype(BF16)


def weight_term(xi, yi, ci, arrived, *refs):
    tokens, terms = refs[:8], refs[8:]
    me = yi[0]
    core = ci[0]
    chunk = terms[0].shape[1]
    slots = (me, lax.bitwise_xor(me, 1), 3 - me, lax.bitwise_xor(3 - me, 1))
    pairs = []
    for half, c in ((0, core), (1, 1 - core)):
        for p in (0, 2):
            left = [arrived[slots[p + i] * 2 + c] for i in range(2)]
            pairs.append((jnp.concatenate(left, axis=1), tokens[4 * half + p : 4 * half + p + 2]))
    for d, term in enumerate(terms):
        total = None
        cols = pl.ds(pl.multiple_of(lax.rem(xi[0] + d, 4) * chunk, 128), chunk)
        for left, (one, two) in pairs:
            right = jnp.concatenate([one[:, cols], two[:, cols]], axis=0)
            part = jnp.dot(left, right, preferred_element_type=F32)
            total = part if total is None else total + part
        term[...] = total.astype(BF16)


def split_rows(g0, g1, g2, g3, blocks, turn):
    chans = g0.shape[0]
    fblk = blocks.shape[1]
    piece = blocks.shape[2]
    turn[0:chans, :] = added((g0, g1, g2, g3))
    turn[chans:, :] = jnp.zeros((turn.shape[0] - chans, turn.shape[1]), F32)
    flipped = turn[...].T
    for q in range(16):
        for h in range(2):
            part = flipped[q * fblk : (q + 1) * fblk, h * piece : (h + 1) * piece]
            blocks[2 * q + h] = part.astype(BF16)


def added(refs):
    total = refs[0][...].astype(F32)
    for ref in refs[1:]:
        total = total + ref[...].astype(F32)
    return total


def add_parts(*refs):
    refs[-1][...] = added(refs[:-1]).astype(BF16)


def make_close_sums(scale):
    def close_sums(xi, zi, yi, amp, *refs):
        *parts, grad_taps, grad_res, held = refs
        total = added(parts) * scale
        width = grad_taps.shape[1] // 3
        for g in range(3):
            grad_taps[:, g * width : (g + 1) * width] = total[8 * g : 8 * g + 7, 0:width]
        count = grad_res.shape[0]
        index = (xi[0] * 4 + zi[0]) * 4 + yi[0]
        moved = pltpu.roll(total[24:40, :], lax.rem(PADC - index * count, PADC), 1)
        held[...] = jnp.zeros(held.shape, F32)
        held[0:MODES, :] = moved[:, 0:128]
        grad_res[...] = held[...].T[0:count, 0:MODES] * amp[...]

    return close_sums


def make_close(scale):
    def close_weight(last, out):
        fblk, piece = last.shape[1:]
        for y in range(4):
            total = jnp.zeros((fblk, piece), F32)
            for z in range(4):
                for h in range(2):
                    total = total + last[(z * 4 + y) * 2 + h].astype(F32)
            out[:, y * piece : (y + 1) * piece] = (total * scale).astype(BF16)

    return close_weight


def ring(a, ax, d):
    return lax.ppermute(a, ax, [(i, (i + d) % 4) for i in range(4)])


def params(mb):
    return pltpu.CompilerParams(vmem_limit_bytes=int(mb * 1024 * 1024))


def local(tokens, w_in, conv_taps, residues, rates, cotangent):
    feats = tokens[0]
    cot = cotangent[0]
    own, width = cot.shape
    depth = feats.shape[1]
    chans = 3 * width
    count = 64
    piece = chans // 16
    fblk = depth // count
    ctx = ("x", "zl", "y")
    scale = 1.0 / math.sqrt(4 * count * own)
    smem = pl.BlockSpec(memory_space=pltpu.SMEM)
    vm = pl.BlockSpec(memory_space=pltpu.VMEM)
    free = pl.BlockSpec()
    names = ("x", "zl", "y", "core")
    feats, cot, rates, *where = lax.optimization_barrier(
        (feats, cot, rates, *[lax.axis_index(n) for n in names])
    )
    xi, zi, yi, ci = [w.reshape(1) for w in where]
    anywhere = pl.BlockSpec(memory_space=pl.ANY)
    head, tail, block, taps, amp_mine, cown = pl.pallas_call(
        prepare,
        in_specs=[anywhere] * 5,
        out_specs=[vm] * 6,
        out_shape=[
            jax.ShapeDtypeStruct((HALO, depth + PADC), BF16),
            jax.ShapeDtypeStruct((HALO, depth), BF16),
            jax.ShapeDtypeStruct((2 * MODES, width // count), F32),
            jax.ShapeDtypeStruct((3, 8, PADC), F32),
            jax.ShapeDtypeStruct(rates.shape, F32),
            jax.ShapeDtypeStruct((own, PADC), F32),
        ],
        scratch_shapes=[
            pltpu.VMEM((128, 128), F32),
            pltpu.VMEM((PADC, own), F32),
            pltpu.VMEM((width, own), BF16),
            pltpu.VMEM(rates.shape, F32),
            pltpu.VMEM(rates.shape, F32),
            pltpu.VMEM(conv_taps.shape, F32),
            pltpu.SemaphoreType.DMA((6,)),
        ],
        compiler_params=params(54),
        name="prepare",
    )(feats, cot.T, rates, residues, conv_taps)
    tprev = lax.ppermute(tail, ctx, [(i, i + 1) for i in range(count - 1)])
    nexts = lax.ppermute(head, ctx, [(i, i - 1) for i in range(1, count)])
    ext_rows = own + 2 * HALO
    steps = depth // KBLK // 2

    def project(part, *before):
        many = 3 if part else 1
        shape = (ext_rows, PADC) if part else (ext_rows, chans)
        return pl.pallas_call(
            make_project(part),
            in_specs=[vm] * (2 + part) + [anywhere] * 2,
            out_specs=[vm] * many,
            out_shape=[jax.ShapeDtypeStruct(shape, F32)] * many,
            scratch_shapes=[
                pltpu.VMEM((own, steps * KBLK), BF16),
                pltpu.VMEM((steps, chans, KBLK), BF16),
                pltpu.SemaphoreType.DMA,
                pltpu.SemaphoreType.DMA((steps,)),
                *[pltpu.VMEM((ext_rows, chans), F32)] * part,
            ],
            compiler_params=params((52, 51)[part]),
            cost_estimate=pl.CostEstimate(flops=800000000, bytes_accessed=6000000, transcendentals=0),
            name="project",
        )(tprev, nexts, *before, feats, w_in.T)

    def mixed(*zs):
        return pl.pallas_call(
            mix_taps,
            in_specs=[vm] * 4,
            out_specs=[vm] * 3,
            out_shape=[jax.ShapeDtypeStruct((EXT, PADC), F32)] * 3,
            compiler_params=params(8),
            cost_estimate=pl.CostEstimate(flops=800000000, bytes_accessed=6000000, transcendentals=0),
            name="mix_taps",
        )(taps, *zs)

    held, each = block, width // count
    work = []
    for g, (me, ax) in enumerate(((yi, "y"), (zi, "zl"), (xi, "x"))):
        blocks = [held] + [ring(held, ax, d) for d in (1, 2, 3)]
        work = project(0) if g == 0 else project(1, *work) if g == 1 else mixed(*work)
        *blocks, last_work = lax.optimization_barrier((*blocks, work[-1]))
        work = [*work[:-1], last_work]
        if g == 1:
            zq, zk, zv = work
        if g == 2:
            break
        each = 4 * each
        held = pl.pallas_call(
            join_params,
            in_specs=[smem] + [vm] * 4,
            out_specs=vm,
            out_shape=jax.ShapeDtypeStruct((2 * MODES, each), F32),
            scratch_shapes=[pltpu.VMEM((2 * MODES, 256), F32)],
            compiler_params=params(4),
            name="join_params",
        )(me, *blocks)
    mq, mk, mv = work
    cots, rate, gain, es, ends, endb = pl.pallas_call(
        end_states,
        in_specs=[smem] + [vm] * 9,
        out_specs=[vm] * 6,
        out_shape=[
            jax.ShapeDtypeStruct((EXT, PADC), F32),
            jax.ShapeDtypeStruct((MODES, PADC), F32),
            jax.ShapeDtypeStruct((MODES, PADC), F32),
            jax.ShapeDtypeStruct((2, MODES, 8, PADC), F32),
            jax.ShapeDtypeStruct((2 * MODES, PADC), F32),
            jax.ShapeDtypeStruct((2 * MODES, PADC), BF16),
        ],
        scratch_shapes=[
            pltpu.VMEM((EXT + 24, 128), F32),
            pltpu.VMEM((EXT + 24, 128), F32),
            pltpu.VMEM((2 * MODES, PADC), F32),
        ],
        compiler_params=params(16),
        cost_estimate=pl.CostEstimate(flops=20000000, bytes_accessed=3000000, transcendentals=0),
        name="end_states",
    )(xi, *blocks, mq, mk, mv, cown, nexts)

    prefixes = []
    total, sent = ends, endb
    for me, ax, span in ((yi, "y", own), (zi, "zl", 4 * own), (xi, "x", 16 * own)):
        near = [ring(sent, ax, d) for d in (1, 2, 3)]
        total, sent, prefix = pl.pallas_call(
            make_level(span),
            in_specs=[smem] + [vm] * 5,
            out_specs=[vm] * 3,
            out_shape=[
                jax.ShapeDtypeStruct((2 * MODES, PADC), F32),
                jax.ShapeDtypeStruct((2 * MODES, PADC), BF16),
                jax.ShapeDtypeStruct((2 * MODES, PADC), F32),
            ],
            compiler_params=params(8),
            name="level",
        )(me, total, *near, rate)
        prefixes.append(prefix)
        if ax == "zl":
            mine, _ = lax.optimization_barrier((feats, sent))
            pair = lax.ppermute(mine, "y", [(i, i ^ 1) for i in range(4)])
            opposite = lax.ppermute(mine, "y", [(i, 3 - i) for i in range(4)])
    pair, opposite, prefixes[2] = lax.optimization_barrier((pair, opposite, prefixes[2]))
    far = lax.ppermute(pair, "y", [(i, 3 - i) for i in range(4)])

    def swapped(a):
        return lax.ppermute(a, "core", [(0, 1), (1, 0)])

    def tiles(shape):
        lead = len(shape) - 1
        return pl.BlockSpec(shape, lambda k: (0,) * lead + (k,))

    outt, dz, dzb, sums = pl.pallas_call(
        finish,
        grid=(PADC // 128,),
        in_specs=[
            smem,
            smem,
            *[tiles((ext_rows, 128))] * 3,
            *[tiles((EXT, 128))] * 3,
            tiles((2, MODES, 8, 128)),
            tiles((2 * MODES, 128)),
            tiles((2 * MODES, 128)),
            tiles((2 * MODES, 128)),
            tiles((3, 8, 128)),
            tiles((MODES, 128)),
            tiles((MODES, 128)),
            tiles((EXT, 128)),
        ],
        out_specs=[
            pl.BlockSpec((128, own), lambda k: (k, 0)),
            tiles((3, own, 128)),
            pl.BlockSpec((8, 2 * piece, own), lambda k: (0, 0, 0)),
            tiles((40, 128)),
        ],
        out_shape=[
            jax.ShapeDtypeStruct((width, own), BF16),
            jax.ShapeDtypeStruct((3, own, PADC), BF16),
            jax.ShapeDtypeStruct((8, 2 * piece, own), BF16),
            jax.ShapeDtypeStruct((40, PADC), BF16),
        ],
        scratch_shapes=[
            pltpu.VMEM((40, 128), F32),
            pltpu.VMEM((2 * MODES, 128), F32),
            pltpu.VMEM((EXT + 24, 128), F32),
            pltpu.VMEM((EXT + 24, 128), F32),
            pltpu.VMEM((EXT + 24, 128), F32),
            pltpu.VMEM((EXT + 24, 128), F32),
            pltpu.VMEM((3, EXT, 128), F32),
            pltpu.VMEM((3, PADC, own), F32),
        ],
        compiler_params=params(50),
        cost_estimate=pl.CostEstimate(flops=200000000, bytes_accessed=10000000, transcendentals=0),
        name="finish",
    )(zi, yi, zq, zk, zv, mq, mk, mv, es, *prefixes, taps, rate, gain, cots)
    output = outt.T
    blocks_of = [mine, pair, opposite, far]
    mine, pair, opposite, _ = lax.optimization_barrier((mine, pair, opposite, sums))
    blocks_of = [mine, pair, opposite, far]
    theirs = [swapped(a) for a in blocks_of]

    def spread(a, ax):
        return [a] + [ring(a, ax, d) for d in (1, 2, 3)]

    def swap(a, ax):
        return [a, lax.ppermute(a, ax, [(0, 1), (1, 0)])]

    def summed(parts):
        return pl.pallas_call(
            add_parts,
            in_specs=[free] * len(parts),
            out_specs=free,
            out_shape=jax.ShapeDtypeStruct((40, PADC), BF16),
            compiler_params=params(4),
            name="add_parts",
        )(*parts)

    arrived = lax.all_to_all(dzb, ("y", "core"), split_axis=0, concat_axis=0, tiled=True)
    sums = summed(swap(sums, "core"))
    *theirs, sums = lax.optimization_barrier((*theirs, sums))
    parts = spread(sums, "zl")
    grad_feats = pl.pallas_call(
        token_grads,
        grid=(3,),
        in_specs=[
            pl.BlockSpec((1, own, PADC), lambda g: (g, 0, 0)),
            pl.BlockSpec((width, depth), lambda g: (g, 0)),
        ],
        out_specs=pl.BlockSpec((own, depth), lambda g: (0, 0)),
        out_shape=jax.ShapeDtypeStruct((own, depth), BF16),
        scratch_shapes=[pltpu.VMEM((own, depth), F32)],
        compiler_params=params(57),
        cost_estimate=pl.CostEstimate(flops=1200000000, bytes_accessed=11000000, transcendentals=0),
        name="token_grads",
    )(dz, w_in.T)
    *parts, grad_feats = lax.optimization_barrier((*parts, grad_feats))
    sums = summed(parts)
    arrived, sums = lax.optimization_barrier((arrived, sums))
    terms = pl.pallas_call(
        weight_term,
        in_specs=[smem] * 3 + [vm] + [free] * 8,
        out_specs=[vm] * 4,
        out_shape=[jax.ShapeDtypeStruct((2 * piece, depth // 4), BF16)] * 4,
        compiler_params=params(24),
        cost_estimate=pl.CostEstimate(flops=1200000000, bytes_accessed=6000000, transcendentals=0),
        name="weight_term",
    )(xi, yi, ci, arrived, *blocks_of, *theirs)
    got = [terms[0]] + [ring(terms[d], "x", d) for d in (1, 2, 3)]
    sums, _ = lax.optimization_barrier((sums, terms[0]))
    sums = summed(spread(sums, "y"))
    *got, sums = lax.optimization_barrier((*got, sums))
    parts = swap(sums, "zh")
    blocks = pl.pallas_call(
        split_rows,
        in_specs=[vm] * 4,
        out_specs=vm,
        out_shape=jax.ShapeDtypeStruct((32, fblk, piece), BF16),
        scratch_shapes=[pltpu.VMEM((384, depth // 4), F32)],
        compiler_params=params(12),
        name="split_rows",
    )(*got)
    last = lax.all_to_all(blocks, ("zl", "y", "zh"), 0, 0, tiled=True)
    *parts, _ = lax.optimization_barrier((*parts, blocks))
    parts = spread(summed(parts), "x")
    grad_taps, grad_residues = pl.pallas_call(
        make_close_sums(scale),
        in_specs=[smem] * 3 + [free] * 5,
        out_specs=[vm] * 2,
        out_shape=[
            jax.ShapeDtypeStruct((7, chans), F32),
            jax.ShapeDtypeStruct(rates.shape, F32),
        ],
        scratch_shapes=[pltpu.VMEM((128, 128), F32)],
        compiler_params=params(4),
        name="close_sums",
    )(xi, zi, yi, amp_mine, *parts)
    grad_weight = pl.pallas_call(
        make_close(scale),
        in_specs=[vm],
        out_specs=vm,
        out_shape=jax.ShapeDtypeStruct((fblk, 4 * piece), BF16),
        compiler_params=params(4),
        name="close_weight",
    )(last)
    return (output[None], grad_feats[None], grad_weight, grad_taps, grad_residues)


def solution(mesh):
    fine = Mesh(mesh.devices.reshape(4, 4, 4, 2, 2), ("x", "zl", "y", "zh", "core"))
    ctx = ("x", "zl", "y")
    dp = ("zh", "core")
    in_specs = (P(dp, ctx, None), P(), P(), P(ctx, None), P(ctx, None), P(dp, ctx, None))
    out_specs = (P(dp, ctx, None), P(dp, ctx, None), P(ctx, dp), P(), P(ctx, None))
    return jax.shard_map(local, mesh=fine, in_specs=in_specs, out_specs=out_specs, check_vma=False)
```
